32 devices in a mesh: dp: 8 (over y, x, core), patch: 4 (over z).
Axes of the slice: x: 2, y: 2, z: 4, core: 2. Of those that a mesh axis runs over, the one named last changes fastest.
Arguments:
- pixels: bfloat16 [256, 196, 768], P(('dp', 'patch')), may hold values from -6 to 6
- shuffle: int32 [256, 196], P(('dp', 'patch')), may hold values from 0 to 195, each once within a row
- vis_len: int32 [256], P(('dp', 'patch')), may hold values from 20 to 80, as said below
- block_owner: int32 [192], replicated, may hold values from 0 to 191, each once
- weights: float32 [192, 256, 256], P('dp'), may hold values from -0.21875 to 0.21875
- vectors: float32 [20480], P('dp')
- vec_moment: float32 [20480], P('dp'), may hold values from -1.9073486e-05 to 1.9073486e-05
- vec_second: float32 [20480], P('dp'), may hold values from 1.3768946e-13 to 5.5075784e-13
- left_stat: float32 [192, 256, 256], P('dp')
- right_stat: float32 [192, 256, 256], P('dp')
- left_root: float32 [192, 256, 256], P('dp')
- right_root: float32 [192, 256, 256], P('dp')
Outputs:
- loss_sum: float32 [], replicated
- masked_count: float32 [], replicated
- grad_norm: float32 [], replicated
- grads_clipped: float32 [192, 256, 256], P('dp')
- left_new: float32 [192, 256, 256], P('dp')
- right_new: float32 [192, 256, 256], P('dp')
- weights_new: float32 [192, 256, 256], P('dp')
- moment_new: float32 [20480], P('dp')
- second_new: float32 [20480], P('dp')
- vectors_new: float32 [20480], P('dp')
The draws below stay inside these ranges and needn't reach their ends.
Inputs may be any that keep to these rules, and one draw needn't show every extreme that they name: `shuffle`: each row is an order of the 196 patches; its first vis_len entries are the visible ones. `vis_len`: at least one image has exactly 80 visible patches. `block_owner`: A permutation of the slots; a slot whose entry is 177 or more holds no tile.
All inputs are finite; a program needn't handle non-finite values.
Results may differ from the reference program's by a relative error of at most 0.0096.
Values may be sent and summed in bfloat16 or wider, within the bound.
No kernel may reach another device: no remote copies, remote signals or barrier semaphores. Data moves between devices by JAX's collectives and lax.ppermute only.
A program may use at most 384 MiB of HBM per device.

```python
import math
import jax
import jax.numpy as jnp
from jax import lax

D = 768
HE = 12
FE = 3072
E = 512
HD = 16
FD = 2048
PIX = 768
POS = 196
VMAX = 80
BS = 256
STEP = 10
B_DEV = 8
IMAGES = 256
NBLK = 177
SLOTS = 192
NVEC = 20480
NPARAM = 11620352


def draw_vis_len(key, part):
    key = jax.random.fold_in(key, 11)
    lowest = VMAX // 4
    spread = max(1, (VMAX - lowest) // 6)
    position = jnp.arange(IMAGES, dtype=jnp.int32)
    centre = VMAX - position * (VMAX - lowest) // (IMAGES - 1)
    noise = jax.random.randint(jax.random.fold_in(key, 1), (IMAGES,), -spread, spread + 1)
    lengths = jnp.clip(centre + noise, lowest, VMAX)
    chosen = jax.random.randint(jax.random.fold_in(key, 2), (), 0, IMAGES)
    return jnp.where(position == chosen, VMAX, lengths).astype(jnp.int32)


def draw_vectors(key, part):
    normal_draw = jax.random.truncated_normal(jax.random.fold_in(key, 21), -3.0, 3.0, (NVEC,), jnp.float32)
    position = jnp.arange(NVEC)
    start_dec = 11 * D + FE + 2 * E
    bounds = [(D, 2 * D), (6 * D, 7 * D), (9 * D + FE, 10 * D + FE), (start_dec, start_dec + E), (start_dec + 5 * E, start_dec + 6 * E), (start_dec + 8 * E + FD, start_dec + 9 * E + FD)]
    gain_mask = jnp.zeros((NVEC,), jnp.bool_)
    for range_start, range_end in bounds:
        gain_mask = gain_mask | (position >= range_start) & (position < range_end)
    return jnp.where(gain_mask, 1.0 + 0.15 * normal_draw, 0.3 * normal_draw).astype(jnp.float32)


def symmetric_tile(key, diag_low, diag_high, scale_value):
    normal_draw = jax.random.normal(jax.random.fold_in(key, 31), (SLOTS, BS, BS), jnp.float32)
    diagonal = jnp.exp(jax.random.uniform(jax.random.fold_in(key, 32), (SLOTS, BS, 1), jnp.float32, jnp.log(diag_low), jnp.log(diag_high)))
    identity = (jnp.arange(BS)[:, None] == jnp.arange(BS)[None, :]).astype(jnp.float32)
    off_part = 0.15 / BS ** 0.5 * (normal_draw + jnp.swapaxes(normal_draw, 1, 2))
    return (scale_value * (diagonal * identity + off_part)).astype(jnp.float32)


def stat_scale():
    return 0.0001 * BS / NPARAM


def draw_left_stat(key, part):
    return symmetric_tile(jax.random.fold_in(key, 41), 1.0, 4.0, stat_scale())


def draw_right_stat(key, part):
    return symmetric_tile(jax.random.fold_in(key, 42), 1.0, 4.0, stat_scale())


def draw_left_root(key, part):
    return symmetric_tile(jax.random.fold_in(key, 43), 0.5, 2.0, 2.0 * stat_scale() ** (-0.25))


def draw_right_root(key, part):
    return symmetric_tile(jax.random.fold_in(key, 44), 0.5, 2.0, 2.0 * stat_scale() ** (-0.25))


def shard_levels(rng, shape, cuts, least, top_value):
    def one(axis_at, parts):
        heights = jax.random.uniform(jax.random.fold_in(jax.random.fold_in(rng, 6), axis_at), (parts,), jnp.float32, least / len(cuts), top_value / len(cuts))
        return jnp.repeat(jnp.exp(heights), shape[axis_at] // parts).reshape((-1,) + (1,) * (len(shape) - axis_at - 1))

    gain = one(*cuts[0])
    for cut in cuts[1:]:
        gain = gain * one(*cut)
    return gain


def bell_draw(own_key, dims, scale, most, shards=(), held_as=jnp.bfloat16):
    drawn = jax.random.normal(own_key, dims, jnp.float32) * scale
    if len(shards) > 0:
        drawn = shard_levels(own_key, dims, shards, -0.22, 0.18) * drawn
    return jnp.clip(drawn, min=-most, max=most).astype(held_as)


def setup_inputs(seed: int = 0) -> dict:
    arg_keys = jax.random.split(jax.random.key(seed), 13)
    return {
        "pixels": bell_draw(arg_keys[0], (IMAGES, POS, PIX), 1.0, 6.0, ((0, 32),)),
        "shuffle": jax.vmap(lambda own: jax.random.permutation(own, POS))(jax.random.split(arg_keys[1], IMAGES)).reshape((IMAGES, POS)).astype(jnp.int32),
        "vis_len": draw_vis_len(jax.random.fold_in(arg_keys[12], 71), 0),
        "block_owner": jax.random.permutation(arg_keys[3], SLOTS).astype(jnp.int32),
        "weights": bell_draw(arg_keys[4], (SLOTS, BS, BS), D ** -0.5, 0.21875, ((0, 8),), jnp.float32),
        "vectors": draw_vectors(jax.random.fold_in(arg_keys[12], 71), 0),
        "vec_moment": bell_draw(arg_keys[6], (NVEC,), (0.0044 / NPARAM ** 0.5), 1.9073486328125e-05, ((0, 8),), jnp.float32),
        "vec_second": jnp.clip(jnp.exp(math.log(5.507578442788541e-13) - 1.3862944 * jax.random.uniform(arg_keys[7], (NVEC,), jnp.float32) ** shard_levels(arg_keys[7], (NVEC,), ((0, 8),), -0.2, 0.2)), 1.3768946106971353e-13, 5.507578442788541e-13),
        "left_stat": draw_left_stat(jax.random.fold_in(arg_keys[12], 71), 0),
        "right_stat": draw_right_stat(jax.random.fold_in(arg_keys[12], 71), 0),
        "left_root": draw_left_root(jax.random.fold_in(arg_keys[12], 71), 0),
        "right_root": draw_right_root(jax.random.fold_in(arg_keys[12], 71), 0),
    }


EXACT_DOT = lax.Precision.HIGHEST
EPS_NORM = 1e-06
EPS_ROOT = 1e-06
EPS_ADAM = 1e-08
CLIP_NORM = 0.01
RATE_MATRIX = 0.03
DECAY_MATRIX = 0.05
BETA_STAT = 0.5
BETA_FIRST = 0.9
BETA_SECOND = 0.999
RATE_VECTOR = 0.1
NEG_LARGE = -1e+30

@jax.custom_vjp
def low(v):
    return lax.optimization_barrier(v.astype(jnp.bfloat16)).astype(jnp.float32)

@jax.custom_vjp
def low_back(v):
    return v

def low_keep(v):
    return (low(v), None)

def low_pass(kept, grad):
    return (grad,)

def back_keep(v):
    return (v, None)

def back_low(kept, grad):
    return (low(grad),)
low.defvjp(low_keep, low_pass)
low_back.defvjp(back_keep, back_low)

def cut_up(vector, lengths):
    pieces = []
    offset = 0
    for length in lengths:
        pieces.append(vector[offset:offset + length])
        offset += length
    return pieces

def matrix_shapes():
    return [(PIX, D), (D, 3 * D), (D, D), (D, FE), (FE, D), (D, E), (E, 3 * E), (E, E), (E, FD), (FD, E), (E, PIX)]

def assemble(blocks):
    matrices = []
    offset = 0
    for row_count, col_count in matrix_shapes():
        row_tiles, col_tiles = (row_count // BS, col_count // BS)
        tile_grid = blocks[offset:offset + row_tiles * col_tiles].reshape(row_tiles, col_tiles, BS, BS)
        matrices.append(tile_grid.transpose(0, 2, 1, 3).reshape(row_count, col_count))
        offset += row_tiles * col_tiles
    return matrices

def disassemble(matrices):
    pieces = []
    for matrix in matrices:
        row_count, col_count = matrix.shape
        tile_grid = matrix.reshape(row_count // BS, BS, col_count // BS, BS).transpose(0, 2, 1, 3)
        pieces.append(tile_grid.reshape(-1, BS, BS))
    return jnp.concatenate(pieces, axis=0)

def sinusoid(count, model_width):
    half_width = model_width // 2
    frequency = jnp.exp(jnp.arange(half_width, dtype=jnp.float32) * (-jnp.log(10000.0) / half_width))
    angles = jnp.arange(count, dtype=jnp.float32)[:, None] * frequency[None, :]
    return jnp.concatenate([jnp.sin(angles), jnp.cos(angles)], axis=1)

def layer_norm(inputs, gain_vec, shift_vec):
    centred = inputs - lax.optimization_barrier(jnp.mean(inputs, axis=-1, keepdims=True))
    spread = lax.optimization_barrier(jnp.mean(centred * centred, axis=-1, keepdims=True))
    return centred * lax.rsqrt(spread + EPS_NORM) * gain_vec + shift_vec

def target_norm(pixel_rows):
    centred = pixel_rows - lax.optimization_barrier(jnp.mean(pixel_rows, axis=-1, keepdims=True))
    return centred * lax.rsqrt(lax.optimization_barrier(jnp.mean(centred * centred, axis=-1, keepdims=True)) + EPS_NORM)

def linear(inputs, matrix, bias_vec):
    return low_back(jnp.dot(low(inputs), matrix, precision=EXACT_DOT) + bias_vec)

def position_rank(shuffle):
    indices = jnp.arange(POS, dtype=jnp.int32)
    matches = shuffle[:, :, None] == indices[None, None, :]
    return lax.optimization_barrier(jnp.sum(jnp.where(matches, indices[None, :, None], 0), axis=1)).astype(jnp.int32)

def take_rows(source, indices):
    return jax.vmap(lambda one_image, one_index: one_image[one_index])(source, indices)

def transformer_block(residual_in, vector, matrices, head_count, key_valid):
    w_qkv, w_out, w_up, w_down = matrices
    model_width = residual_in.shape[-1]
    hidden = w_up.shape[1]
    gain_one, shift_one, bias_query, bias_value, bias_out, gain_two, shift_two, bias_up, bias_down = cut_up(vector, [model_width] * 7 + [hidden, model_width])
    normed = layer_norm(residual_in, gain_one, shift_one)
    projected = linear(normed, w_qkv, jnp.concatenate([bias_query, jnp.zeros_like(bias_query), bias_value]))
    batch_size, seq_length = (residual_in.shape[0], residual_in.shape[1])
    head_size = model_width // head_count
    queries, keys_in, values = [low(portion.reshape(batch_size, seq_length, head_count, head_size)) for portion in jnp.split(projected, 3, axis=-1)]
    scores = low_back(jnp.einsum('bqhd,bkhd->bhqk', queries, keys_in, precision=EXACT_DOT) * head_size ** (-0.5))
    scores = jnp.where(key_valid[:, None, None, :], scores, NEG_LARGE)
    probs_low = low(jax.nn.softmax(scores, axis=-1))
    attended = low_back(jnp.einsum('bhqk,bkhd->bqhd', probs_low, values, precision=EXACT_DOT))
    residual_mid = residual_in + linear(attended.reshape(batch_size, seq_length, model_width), w_out, bias_out)
    activation = jax.nn.gelu(linear(layer_norm(residual_mid, gain_two, shift_two), w_up, bias_up), approximate=False)
    return residual_mid + linear(activation, w_down, bias_down)

def group_loss(matrices, vector, pixel_rows, shuffle, lengths):
    w_embed, enc_qkv, enc_out, enc_up, enc_down, w_proj, dec_qkv, dec_out, dec_up, dec_down, w_head = [low(matrix) for matrix in matrices]
    bias_embed, enc_vector, enc_gain, enc_shift, bias_proj, mask_token, dec_vector, dec_gain, dec_shift, bias_head = cut_up(low(vector), [D, 8 * D + FE, D, D, E, E, 8 * E + FD, E, E, PIX])
    images = pixel_rows.shape[0]
    visible_ids = shuffle[:, :VMAX]
    embedded = linear(take_rows(pixel_rows, visible_ids), w_embed, bias_embed) + sinusoid(POS, D)[visible_ids]
    key_valid = jnp.arange(VMAX, dtype=jnp.int32)[None, :] < lengths[:, None]
    encoded = transformer_block(embedded, enc_vector, (enc_qkv, enc_out, enc_up, enc_down), HE, key_valid)
    latent = linear(layer_norm(encoded, enc_gain, enc_shift), w_proj, bias_proj)
    ranked = position_rank(shuffle)
    visible = ranked < lengths[:, None]
    placed = take_rows(latent, jnp.minimum(ranked, VMAX - 1))
    decoded = jnp.where(visible[:, :, None], placed, mask_token) + sinusoid(POS, E)
    decoded = transformer_block(decoded, dec_vector, (dec_qkv, dec_out, dec_up, dec_down), HD, jnp.ones((images, POS), jnp.bool_))
    predicted = linear(layer_norm(decoded, dec_gain, dec_shift), w_head, bias_head)
    patch_error = lax.optimization_barrier(jnp.mean((predicted - target_norm(pixel_rows)) ** 2, axis=-1))
    return jnp.sum(jnp.where(visible, 0.0, patch_error))

def reference(pixels, shuffle, vis_len, block_owner, weights, vectors, vec_moment, vec_second, left_stat, right_stat, left_root, right_root):
    slot_index = jnp.arange(SLOTS, dtype=jnp.int32)
    slot_of_block = lax.optimization_barrier(jnp.sum(jnp.where(block_owner[None, :] == slot_index[:NBLK, None], slot_index[None, :], 0), axis=1)).astype(jnp.int32)
    matrices = assemble(weights[slot_of_block])
    masked_count = jnp.sum(POS - vis_len).astype(jnp.float32)
    inverse_count = 1.0 / masked_count
    groups = IMAGES // B_DEV
    group_input = (pixels.reshape(groups, B_DEV, POS, PIX), shuffle.reshape(groups, B_DEV, POS), vis_len.reshape(groups, B_DEV))

    def accumulate(carry, one_group):
        grad_mats, grad_vec, loss_total = carry
        pixel_group, shuffle_group, length_group = one_group
        pixel_float = pixel_group.astype(jnp.float32)
        group_value, pull_back = jax.vjp(lambda mats_in, vec_in: group_loss(mats_in, vec_in, pixel_float, shuffle_group, length_group), matrices, vectors)
        delta_mats, delta_vec = pull_back(inverse_count)
        summed = [acc_one + acc_two for acc_one, acc_two in zip(grad_mats, delta_mats)]
        return ((summed, grad_vec + delta_vec, loss_total + group_value), None)
    initial = ([jnp.zeros_like(matrix) for matrix in matrices], jnp.zeros_like(vectors), jnp.zeros((), jnp.float32))
    (grad_mats, grad_vec, loss_sum), unused = lax.scan(accumulate, initial, group_input)
    grad_blocks = jnp.concatenate([disassemble(grad_mats), jnp.zeros((SLOTS - NBLK, BS, BS), jnp.float32)], axis=0)
    grad_slots = grad_blocks[block_owner]
    grad_norm = jnp.sqrt(jnp.sum(grad_slots * grad_slots) + jnp.sum(grad_vec * grad_vec))
    factor = jnp.minimum(1.0, CLIP_NORM / grad_norm)
    clipped = grad_slots * factor
    clipped_vec = grad_vec * factor
    left_new = BETA_STAT * left_stat + (1.0 - BETA_STAT) * jnp.einsum('sik,sjk->sij', clipped, clipped, precision=EXACT_DOT)
    right_new = BETA_STAT * right_stat + (1.0 - BETA_STAT) * jnp.einsum('ski,skj->sij', clipped, clipped, precision=EXACT_DOT)
    direction = jnp.einsum('sij,sjk->sik', jnp.einsum('sij,sjk->sik', left_root, clipped, precision=EXACT_DOT), right_root, precision=EXACT_DOT)
    direction = direction * lax.rsqrt(lax.optimization_barrier(jnp.mean(direction * direction, axis=(1, 2), keepdims=True)) + EPS_ROOT)
    weights_new = weights - RATE_MATRIX * (direction + DECAY_MATRIX * weights)
    moment_new = BETA_FIRST * vec_moment + (1.0 - BETA_FIRST) * clipped_vec
    second_new = BETA_SECOND * vec_second + (1.0 - BETA_SECOND) * clipped_vec * clipped_vec
    corrected = moment_new / (1.0 - BETA_FIRST ** STEP)
    second_scaled = second_new / (1.0 - BETA_SECOND ** STEP)
    vectors_new = vectors - RATE_VECTOR * corrected / (jnp.sqrt(second_scaled) + EPS_ADAM)
    return (loss_sum, masked_count, grad_norm, clipped, left_new, right_new, weights_new, moment_new, second_new, vectors_new)
```

```python
import functools
import math

import jax
import jax.numpy as jnp
import numpy as np
from jax import lax
from jax.experimental import pallas as pl
from jax.experimental.pallas import tpu as pltpu
from jax.sharding import PartitionSpec as P

D = 768
HE = 12
FE = 3072
E = 512
HD = 16
FD = 2048
PIX = 768
POS = 196
VMAX = 80
BS = 256
STEP = 10
NBLK = 177

SD = 208

EPS_NORM = 1e-06
EPS_ROOT = 1e-06
EPS_ADAM = 1e-08
CLIP_NORM = 0.01
RATE_MATRIX = 0.03
DECAY_MATRIX = 0.05
BETA_STAT = 0.5
BETA_FIRST = 0.9
BETA_SECOND = 0.999
RATE_VECTOR = 0.1
NEG_LARGE = -1e30
LOG2E = math.log2(math.e)

BF = jnp.bfloat16
F32 = jnp.float32
VMEM_LIMIT = 60 * 1024 * 1024

T_EMBED, T_EQKV, T_EOUT, T_EUP, T_EDOWN, T_PROJ = 0, 9, 36, 45, 81, 117
T_DQKV, T_DOUT, T_DUP, T_DDOWN, T_HEAD = 123, 135, 139, 155, 171

V_EMBED = 0
V_ENC = D
V_ENORM = V_ENC + 9 * D + FE
V_PROJ = V_ENORM + 2 * D
V_MASK = V_PROJ + E
V_DEC = V_MASK + E
V_DNORM = V_DEC + 9 * E + FD
V_HEAD = V_DNORM + 2 * E
V_ALL = V_HEAD + PIX


def layer_offsets(start, width, hidden):
    names = ["g1", "s1", "bqkv", "bo", "g2", "s2", "bu", "bd"]
    sizes = [width, width, 3 * width, width, width, width, hidden, width]
    offsets = {}
    for name, size in zip(names, sizes):
        offsets[name] = start
        start += size
    return offsets


def mm(a, b):
    return jnp.dot(a, b, preferred_element_type=F32)


def mm_nt(a, b):
    return lax.dot_general(a, b, (((1,), (1,)), ((), ())), preferred_element_type=F32)


def mm_tn(a, b):
    return lax.dot_general(a, b, (((0,), (0,)), ((), ())), preferred_element_type=F32)


def fold8(x):
    rows, cols = x.shape
    return jnp.sum(x.reshape(rows // 8, 8, cols), axis=0)


def gelu_pair(u):
    t = 1.0 / (1.0 + (0.3275911 * math.sqrt(0.5)) * jnp.abs(u))
    e = jnp.exp2((-0.5 * LOG2E) * (u * u))
    poly = t * (
        0.5 * 0.254829592
        + t * (-0.5 * 0.284496736 + t * (0.5 * 1.421413741 + t * (-0.5 * 1.453152027 + t * (0.5 * 1.061405429))))
    )
    tail = poly * e
    phi = jnp.where(u >= 0, 1.0 - tail, tail)
    return u * phi, phi + u * (e * (1.0 / math.sqrt(2.0 * math.pi)))


def norm_parts(x):
    centred = x - jnp.mean(x, axis=-1, keepdims=True)
    inverse = lax.rsqrt(jnp.mean(centred * centred, axis=-1, keepdims=True) + EPS_NORM)
    return centred * inverse, inverse


def row_loop(rows, step, body, carry=0, unroll=2):
    count = rows // step

    def one(i, c):
        return body(pl.ds(pl.multiple_of(i * step, step), step), c)

    return lax.fori_loop(0, count, one, carry, unroll=unroll if count % unroll == 0 else 1)


def norm_forward(x_ref, gain, shift, out_ref):
    def body(sl, c):
        normed, _ = norm_parts(x_ref[sl, :])
        out_ref[sl, :] = (normed * gain + shift).astype(BF)
        return c

    row_loop(x_ref.shape[0], 16, body)


def norm_backward(x_ref, dy_ref, gain, out_ref, add):
    width = x_ref.shape[1]

    def body(sl, c):
        d_gain, d_shift = c
        normed, inverse = norm_parts(x_ref[sl, :])
        dy = dy_ref[sl, :]
        dn = dy * gain
        mean_one = jnp.mean(dn, axis=-1, keepdims=True)
        mean_two = jnp.mean(dn * normed, axis=-1, keepdims=True)
        dx = inverse * (dn - mean_one - normed * mean_two)
        out_ref[sl, :] = out_ref[sl, :] + dx if add else dx
        return (d_gain + fold8(dy * normed), d_shift + fold8(dy))

    zero = jnp.zeros((8, width), F32)
    return row_loop(x_ref.shape[0], 16, body, (zero, zero))


def col_loop(count, body):
    def one(j, c):
        body(j, pl.ds(pl.multiple_of(j * BS, BS), BS))
        return c

    lax.fori_loop(0, count, one, 0)


def vec_at(vec_ref, start, j):
    return vec_ref[:, pl.ds(pl.multiple_of(start + j * BS, BS), BS)]


def head_mask(head, head_size):
    lane = lax.broadcasted_iota(jnp.int32, (1, BS), 1)
    inside = (lane >= head * head_size) & (lane < (head + 1) * head_size)
    return jnp.where(inside, 1.0, 0.0).astype(BF)


def scores_of(k_masked, q, head_size, valid):
    scores = mm_nt(k_masked, q) * (head_size**-0.5 * LOG2E)
    return jnp.where(valid, scores, NEG_LARGE)


def attention_forward(qkv_ref, att_ref, lse_ref, image, seq, width, head_size, valid):
    rows = pl.ds(pl.multiple_of(image * seq, 16), seq)
    per = BS // head_size

    def group(g, c):
        def part(which):
            return qkv_ref[rows, pl.ds(pl.multiple_of(which * width + g * BS, BS), BS)]

        q, k, v = part(0), part(1), part(2)
        v_t = v.T
        outs, logs = [], []
        for h in range(per):
            scores = scores_of(k * head_mask(h, head_size), q, head_size, valid)
            top = jnp.max(scores, axis=0, keepdims=True)
            e = jnp.exp2(scores - top)
            total = jnp.sum(e, axis=0, keepdims=True)
            out = mm(v_t[h * head_size : (h + 1) * head_size, :], e.astype(BF))
            outs.append(out * (1.0 / total))
            logs.append(top + jnp.log2(total))
        att_ref[rows, pl.ds(pl.multiple_of(g * BS, BS), BS)] = jnp.concatenate(outs, axis=0).T.astype(BF)
        lse_ref[image, g] = jnp.concatenate(logs, axis=0)
        return c

    lax.fori_loop(0, width // BS, group, 0)


def attention_backward(qkv_ref, datt_ref, lse_ref, dqkv_ref, image, seq, width, head_size, valid):
    rows = pl.ds(pl.multiple_of(image * seq, 16), seq)
    per = BS // head_size
    scale = head_size**-0.5

    def group(g, c):
        def cols(which):
            return pl.ds(pl.multiple_of(which * width + g * BS, BS), BS)

        q, k, v = qkv_ref[rows, cols(0)], qkv_ref[rows, cols(1)], qkv_ref[rows, cols(2)]
        d_out = datt_ref[rows, cols(0)]
        lse = lse_ref[image, g]
        q_t, k_t, d_out_t = q.T, k.T, d_out.T
        d_q, d_k, d_v = [], [], []
        for h in range(per):
            mask = head_mask(h, head_size)
            part = slice(h * head_size, (h + 1) * head_size)
            probs = jnp.exp2(scores_of(k * mask, q, head_size, valid) - lse[h : h + 1, :])
            d_probs = mm_nt(v * mask, d_out)
            delta = jnp.sum(probs * d_probs, axis=0, keepdims=True)
            d_scores = (probs * (d_probs - delta)).astype(BF)
            d_v.append(mm_nt(d_out_t[part, :], probs.astype(BF)))
            d_k.append(mm_nt(q_t[part, :], d_scores))
            d_q.append(mm(k_t[part, :], d_scores))
        dqkv_ref[rows, cols(0)] = (jnp.concatenate(d_q, axis=0).T * scale).astype(BF)
        dqkv_ref[rows, cols(1)] = (jnp.concatenate(d_k, axis=0).T * scale).astype(BF)
        dqkv_ref[rows, cols(2)] = jnp.concatenate(d_v, axis=0).T.astype(BF)
        return c

    lax.fori_loop(0, width // BS, group, 0)


def fetch_tiles(row_ref, wg_ref, first, dst, sem):
    row_tiles, col_tiles = dst.shape[0] // BS, dst.shape[1] // BS
    for i in range(row_tiles):
        for j in range(col_tiles):
            start = pl.multiple_of(row_ref[first + i * col_tiles + j], 16)
            pltpu.make_async_copy(
                wg_ref.at[pl.ds(start, BS), :],
                dst.at[i * BS : (i + 1) * BS, j * BS : (j + 1) * BS],
                sem,
            ).start()


def await_tiles(dst, sem):
    pltpu.make_async_copy(dst, dst, sem).wait()


def fetch_all(first_step, row_ref, wg_ref, sems, matrices):
    @pl.when(first_step)
    def _():
        for i, (first, dst) in enumerate(matrices):
            fetch_tiles(row_ref, wg_ref, first, dst, sems.at[i])

    def ready(i):
        @pl.when(first_step)
        def _():
            await_tiles(matrices[i][1], sems.at[i])

    return ready


def qkv_forward(h_ref, w_ref, vec_ref, start, out_ref):
    def body(j, cols):
        out_ref[:, cols] = (mm(h_ref[...], w_ref[:, cols]) + vec_at(vec_ref, start, j)).astype(BF)

    col_loop(w_ref.shape[1] // BS, body)


def add_linear(x_ref, h_ref, w_ref, vec_ref, start, out_ref):
    def body(j, cols):
        out_ref[:, cols] = x_ref[:, cols] + (mm(h_ref[...], w_ref[:, cols]) + vec_at(vec_ref, start, j))

    col_loop(w_ref.shape[1] // BS, body)


def up_forward(h_ref, w_ref, vec_ref, start, act_ref, slope_ref):
    def body(j, cols):
        act, slope = gelu_pair(mm(h_ref[...], w_ref[:, cols]) + vec_at(vec_ref, start, j))
        act_ref[:, cols] = act.astype(BF)
        slope_ref[:, cols] = slope.astype(BF)

    col_loop(w_ref.shape[1] // BS, body)


def back_linear(g_ref, w_ref, out_ref):
    def body(j, cols):
        out_ref[:, cols] = mm_nt(g_ref[...], w_ref[cols, :])

    col_loop(w_ref.shape[0] // BS, body)


def back_up(g_ref, w_ref, slope_ref, du_ref, sum_ref, start):
    def body(j, cols):
        du = (mm_nt(g_ref[...], w_ref[cols, :]) * slope_ref[:, cols].astype(F32)).astype(BF)
        du_ref[:, cols] = du
        at = pl.ds(pl.multiple_of(start + j * BS, BS), BS)
        sum_ref[:, at] = sum_ref[:, at] + fold8(du.astype(F32))

    col_loop(w_ref.shape[0] // BS, body)


def round_and_sum(x_ref, out_ref, sum_ref, start):
    width = x_ref.shape[1]

    def body(sl, c):
        low = x_ref[sl, :].astype(BF)
        out_ref[sl, :] = low
        return c + fold8(low.astype(F32))

    total = row_loop(x_ref.shape[0], 16, body, jnp.zeros((8, width), F32))
    sum_ref[:, start : start + width] = sum_ref[:, start : start + width] + total


def sum_rows(x_ref, sum_ref, start):
    width = x_ref.shape[1]

    def body(sl, c):
        return c + fold8(x_ref[sl, :].astype(F32))

    total = row_loop(x_ref.shape[0], 16, body, jnp.zeros((8, width), F32))
    sum_ref[:, start : start + width] = sum_ref[:, start : start + width] + total


def add_sum(sum_ref, start, value):
    stop = start + value.shape[1]
    sum_ref[:, start:stop] = sum_ref[:, start:stop] + value


def order_kernel(shuffle_ref, pixels_ref, sin_d_ref, sin_e_ref, all_ref, visible_ref, pos_d_ref, pos_e_ref):
    ids = shuffle_ref[0]
    pick = jnp.where(ids == lax.broadcasted_iota(jnp.int32, (SD, POS), 1), 1.0, 0.0).astype(BF)
    ordered = mm(pick, pixels_ref[0]).astype(BF)
    all_ref[0] = ordered
    visible_ref[0] = ordered[:VMAX, :]
    few = pick[:VMAX, :]
    pos_d_ref[0] = mm(few, sin_d_ref[0]) + mm(few, sin_d_ref[1])
    pos_e_ref[0] = mm(pick, sin_e_ref[0]) + mm(pick, sin_e_ref[1])


def sinusoid_parts(count, width):
    half = width // 2
    frequency = np.exp(np.arange(half) * (-np.log(10000.0) / half))
    angles = np.arange(count)[:, None] * frequency[None, :]
    table = np.concatenate([np.sin(angles), np.cos(angles)], axis=1).astype(np.float32)
    high = table.astype(jnp.bfloat16)
    low = (table - high.astype(np.float32)).astype(jnp.bfloat16)
    return np.stack([high, low])


def order_patches(pixels, shuffle):
    images = pixels.shape[0]
    ids = jnp.pad(shuffle, ((0, 0), (0, SD - POS)), constant_values=-1)[:, :, None]

    def image(*dims):
        return pl.BlockSpec((1,) + dims, lambda b: (b,) + (0,) * len(dims))

    def whole(*dims):
        return pl.BlockSpec(dims, lambda b: (0,) * len(dims))

    return pl.pallas_call(
        order_kernel,
        grid=(images,),
        in_specs=[image(SD, 1), image(POS, PIX), whole(2, POS, D), whole(2, POS, E)],
        out_specs=[image(SD, PIX), image(VMAX, PIX), image(VMAX, D), image(SD, E)],
        out_shape=[
            jax.ShapeDtypeStruct((images, SD, PIX), BF),
            jax.ShapeDtypeStruct((images, VMAX, PIX), BF),
            jax.ShapeDtypeStruct((images, VMAX, D), F32),
            jax.ShapeDtypeStruct((images, SD, E), F32),
        ],
        compiler_params=pltpu.CompilerParams(vmem_limit_bytes=VMEM_LIMIT),
        name="order_patches",
    )(ids, pixels, jnp.asarray(sinusoid_parts(POS, D)), jnp.asarray(sinusoid_parts(POS, E)))


def group_call(kernel, steps, prefetch, in_arrays, out_list, scratch, name, flops):
    def spec(shape, kind):
        if kind == "any":
            return pl.BlockSpec(memory_space=pl.ANY)
        if kind == "rows":
            block = (shape[0] // steps,) + tuple(shape[1:])
            return pl.BlockSpec(block, lambda i, *_: (i,) + (0,) * (len(shape) - 1))
        return pl.BlockSpec(tuple(shape), lambda i, *_: (0,) * len(shape))

    return pl.pallas_call(
        kernel,
        grid_spec=pltpu.PrefetchScalarGridSpec(
            num_scalar_prefetch=len(prefetch),
            grid=(steps,),
            in_specs=[spec(a.shape, kind) for a, kind in in_arrays],
            out_specs=[spec(shape, kind) for shape, _, kind in out_list],
            scratch_shapes=scratch,
        ),
        out_shape=[jax.ShapeDtypeStruct(shape, dtype) for shape, dtype, _ in out_list],
        compiler_params=pltpu.CompilerParams(
            vmem_limit_bytes=VMEM_LIMIT, dimension_semantics=("arbitrary",)
        ),
        cost_estimate=pl.CostEstimate(
            flops=flops,
            bytes_accessed=sum(math.prod(s) * jnp.dtype(t).itemsize for s, t, _ in out_list) * 2,
            transcendentals=0,
        ),
        name=name,
    )(*prefetch, *[a for a, _ in in_arrays])


ENC = layer_offsets(V_ENC, D, FE)
DEC = layer_offsets(V_DEC, E, FD)


def encoder_forward_kernel(
    row_ref, len_ref, wg_ref, vec_ref, pix_ref, pos_ref,
    x0_ref, h1_ref, qkv_ref, lse_ref, att_ref, mid_ref, h2_ref, act_ref, slope_ref, x1_ref, hn_ref, latent_ref,
    w_embed, w_qkv, w_out, w_up, w_down, w_proj, sems,
):
    step = pl.program_id(0)
    images = lse_ref.shape[0]
    ready = fetch_all(
        step == 0,
        row_ref,
        wg_ref,
        sems,
        [
            (T_EMBED, w_embed),
            (T_EQKV, w_qkv),
            (T_EOUT, w_out),
            (T_EUP, w_up),
            (T_EDOWN, w_down),
            (T_PROJ, w_proj),
        ],
    )

    def vec(start, size=D):
        return vec_ref[:, start : start + size]

    ready(0)
    add_linear(pos_ref, pix_ref, w_embed, vec_ref, V_EMBED, x0_ref)
    norm_forward(x0_ref, vec(ENC["g1"]), vec(ENC["s1"]), h1_ref)
    ready(1)
    qkv_forward(h1_ref, w_qkv, vec_ref, ENC["bqkv"], qkv_ref)

    def one(image, c):
        valid = lax.broadcasted_iota(jnp.int32, (VMAX, 1), 0) < len_ref[step * images + image]
        attention_forward(qkv_ref, att_ref, lse_ref, image, VMAX, D, D // HE, valid)
        return c

    lax.fori_loop(0, images, one, 0)
    ready(2)
    add_linear(x0_ref, att_ref, w_out, vec_ref, ENC["bo"], mid_ref)
    norm_forward(mid_ref, vec(ENC["g2"]), vec(ENC["s2"]), h2_ref)
    ready(3)
    up_forward(h2_ref, w_up, vec_ref, ENC["bu"], act_ref, slope_ref)
    ready(4)
    add_linear(mid_ref, act_ref, w_down, vec_ref, ENC["bd"], x1_ref)
    norm_forward(x1_ref, vec(V_ENORM), vec(V_ENORM + D), hn_ref)
    ready(5)

    def project(j, cols):
        latent_ref[:, cols] = mm(hn_ref[...], w_proj[:, cols]) + vec_at(vec_ref, V_PROJ, j)

    col_loop(E // BS, project)


def encoder_forward(tile_rows, vis_len, gathered, vector, visible_pix, pos_d, steps):
    images = vis_len.shape[0]
    rows = images * VMAX
    outs = [
        ((rows, D), F32, "rows"),
        ((rows, D), BF, "rows"),
        ((rows, 3 * D), BF, "rows"),
        ((images, D // BS, BS * HE // D, VMAX), F32, "rows"),
        ((rows, D), BF, "rows"),
        ((rows, D), F32, "rows"),
        ((rows, D), BF, "rows"),
        ((rows, FE), BF, "rows"),
        ((rows, FE), BF, "rows"),
        ((rows, D), F32, "rows"),
        ((rows, D), BF, "rows"),
        ((rows, E), F32, "rows"),
    ]
    scratch = [pltpu.VMEM(s, BF) for s in [(PIX, D), (D, 3 * D), (D, D), (D, FE), (FE, D), (D, E)]]
    return group_call(
        encoder_forward_kernel,
        steps,
        (tile_rows, vis_len),
        [
            (gathered, "any"),
            (vector, "whole"),
            (visible_pix.reshape(rows, PIX), "rows"),
            (pos_d.reshape(rows, D), "rows"),
        ],
        outs,
        scratch + [pltpu.SemaphoreType.DMA((6,))],
        "encoder_forward",
        2 * rows * (PIX * D + 4 * D * D + 2 * D * FE + D * E),
    )


DS = layer_offsets(0, E, FD)
DS_NORM = 9 * E + FD
DS_HEAD = DS_NORM + 2 * E
DS_MASK = DS_HEAD + PIX
DS_LOSS = DS_MASK + E
DS_ALL = DS_LOSS + PIX


def decoder_kernel(
    row_ref, len_ref, wg_ref, vec_ref, latent_ref, pos_ref, pix_ref,
    h1_ref, dqkv_ref, att_ref, gproj_ref, h2_ref, du_ref, act_ref, gdown_ref, hn_ref, gpred_ref, glat_ref, sum_ref,
    w_qkv, w_out, w_up, w_down, w_head, x0, qkv, lse, mid, slope, x1, pred, dy, grad, datt, sems,
):
    step = pl.program_id(0)
    images = lse.shape[0]
    ready = fetch_all(
        step == 0,
        row_ref,
        wg_ref,
        sems,
        [(T_DQKV, w_qkv), (T_DOUT, w_out), (T_DUP, w_up), (T_DDOWN, w_down), (T_HEAD, w_head)],
    )

    @pl.when(step == 0)
    def _():
        sum_ref[...] = jnp.zeros_like(sum_ref)

    def vec(start, size=E):
        return vec_ref[:, start : start + size]

    def length(image):
        return len_ref[step * images + image]

    chunk = 16
    order = lax.broadcasted_iota(jnp.int32, (chunk, 1), 0)
    token = vec(V_MASK)

    def place(image, c):
        def head_rows(i, c):
            at = pl.ds(pl.multiple_of(image * SD + i * chunk, chunk), chunk)
            got = latent_ref[pl.ds(pl.multiple_of(image * VMAX + i * chunk, chunk), chunk), :]
            x0[at, :] = jnp.where(i * chunk + order < length(image), got, token) + pos_ref[at, :]
            return c

        def tail_rows(i, c):
            at = pl.ds(pl.multiple_of(image * SD + i * chunk, chunk), chunk)
            x0[at, :] = token + pos_ref[at, :]
            return c

        lax.fori_loop(0, VMAX // chunk, head_rows, 0)
        lax.fori_loop(VMAX // chunk, SD // chunk, tail_rows, 0)
        return c

    lax.fori_loop(0, images, place, 0)
    norm_forward(x0, vec(DEC["g1"]), vec(DEC["s1"]), h1_ref)
    ready(0)
    qkv_forward(h1_ref, w_qkv, vec_ref, DEC["bqkv"], qkv)
    valid = lax.broadcasted_iota(jnp.int32, (SD, 1), 0) < POS

    def attend(image, c):
        attention_forward(qkv, att_ref, lse, image, SD, E, E // HD, valid)
        return c

    lax.fori_loop(0, images, attend, 0)
    ready(1)
    add_linear(x0, att_ref, w_out, vec_ref, DEC["bo"], mid)
    norm_forward(mid, vec(DEC["g2"]), vec(DEC["s2"]), h2_ref)
    ready(2)
    up_forward(h2_ref, w_up, vec_ref, DEC["bu"], act_ref, slope)
    ready(3)
    add_linear(mid, act_ref, w_down, vec_ref, DEC["bd"], x1)
    norm_forward(x1, vec(V_DNORM), vec(V_DNORM + E), hn_ref)
    ready(4)

    def predict(j, cols):
        pred[:, cols] = mm(hn_ref[...], w_head[:, cols]) + vec_at(vec_ref, V_HEAD, j)

    col_loop(PIX // BS, predict)

    def errors(image, c):
        def one(i, c):
            loss, bias = c
            at = pl.ds(pl.multiple_of(image * SD + i * chunk, chunk), chunk)
            target, _ = norm_parts(pix_ref[at, :].astype(F32))
            place_in = i * chunk + order
            masked = (place_in >= length(image)) & (place_in < POS)
            residual = jnp.where(masked, pred[at, :] - target, 0.0)
            low = (residual * (2.0 / PIX)).astype(BF)
            gpred_ref[at, :] = low
            return (loss + fold8(residual * residual), bias + fold8(low.astype(F32)))

        return lax.fori_loop(0, SD // chunk, one, c)

    zero = jnp.zeros((8, PIX), F32)
    loss, bias = lax.fori_loop(0, images, errors, (zero, zero))
    add_sum(sum_ref, DS_LOSS, loss)
    add_sum(sum_ref, DS_HEAD, bias)

    back_linear(gpred_ref, w_head, dy)
    d_gain, d_shift = norm_backward(x1, dy, vec(V_DNORM), grad, False)
    add_sum(sum_ref, DS_NORM, d_gain)
    add_sum(sum_ref, DS_NORM + E, d_shift)
    round_and_sum(grad, gdown_ref, sum_ref, DS["bd"])
    back_up(gdown_ref, w_down, slope, du_ref, sum_ref, DS["bu"])
    back_linear(du_ref, w_up, dy)
    d_gain, d_shift = norm_backward(mid, dy, vec(DEC["g2"]), grad, True)
    add_sum(sum_ref, DS["g2"], d_gain)
    add_sum(sum_ref, DS["s2"], d_shift)
    round_and_sum(grad, gproj_ref, sum_ref, DS["bo"])

    def back_out(j, cols):
        datt[:, cols] = mm_nt(gproj_ref[...], w_out[cols, :]).astype(BF)

    col_loop(E // BS, back_out)

    def attend_back(image, c):
        attention_backward(qkv, datt, lse, dqkv_ref, image, SD, E, E // HD, valid)
        return c

    lax.fori_loop(0, images, attend_back, 0)
    sum_rows(dqkv_ref, sum_ref, DS["bqkv"])
    back_linear(dqkv_ref, w_qkv, dy)
    d_gain, d_shift = norm_backward(x0, dy, vec(DEC["g1"]), grad, True)
    add_sum(sum_ref, DS["g1"], d_gain)
    add_sum(sum_ref, DS["s1"], d_shift)

    def unplace(image, c):
        def head_rows(i, c):
            got = grad[pl.ds(pl.multiple_of(image * SD + i * chunk, chunk), chunk), :]
            seen = i * chunk + order < length(image)
            at = pl.ds(pl.multiple_of(image * VMAX + i * chunk, chunk), chunk)
            glat_ref[at, :] = jnp.where(seen, got, 0.0).astype(BF)
            return c + fold8(jnp.where(seen, 0.0, got))

        def tail_rows(i, c):
            got = grad[pl.ds(pl.multiple_of(image * SD + i * chunk, chunk), chunk), :]
            return c + fold8(jnp.where(i * chunk + order < POS, got, 0.0))

        c = lax.fori_loop(0, VMAX // chunk, head_rows, c)
        return lax.fori_loop(VMAX // chunk, SD // chunk, tail_rows, c)

    add_sum(sum_ref, DS_MASK, lax.fori_loop(0, images, unplace, jnp.zeros((8, E), F32)))


def decoder(tile_rows, vis_len, gathered, vector, latent, pos_e, ordered, steps):
    images = vis_len.shape[0]
    rows = images * SD
    part = rows // steps
    outs = [
        ((rows, E), BF, "rows"),
        ((rows, 3 * E), BF, "rows"),
        ((rows, E), BF, "rows"),
        ((rows, E), BF, "rows"),
        ((rows, E), BF, "rows"),
        ((rows, FD), BF, "rows"),
        ((rows, FD), BF, "rows"),
        ((rows, E), BF, "rows"),
        ((rows, E), BF, "rows"),
        ((rows, PIX), BF, "rows"),
        ((images * VMAX, E), BF, "rows"),
        ((8, DS_ALL), F32, "whole"),
    ]
    scratch = [pltpu.VMEM(s, BF) for s in [(E, 3 * E), (E, E), (E, FD), (FD, E), (E, PIX)]]
    scratch += [
        pltpu.VMEM((part, E), F32),
        pltpu.VMEM((part, 3 * E), BF),
        pltpu.VMEM((images // steps, E // BS, BS * HD // E, SD), F32),
        pltpu.VMEM((part, E), F32),
        pltpu.VMEM((part, FD), BF),
        pltpu.VMEM((part, E), F32),
        pltpu.VMEM((part, PIX), F32),
        pltpu.VMEM((part, E), F32),
        pltpu.VMEM((part, E), F32),
        pltpu.VMEM((part, E), BF),
        pltpu.SemaphoreType.DMA((5,)),
    ]
    return group_call(
        decoder_kernel,
        steps,
        (tile_rows, vis_len),
        [
            (gathered, "any"),
            (vector, "whole"),
            (latent, "rows"),
            (pos_e.reshape(rows, E), "rows"),
            (ordered.reshape(rows, PIX), "rows"),
        ],
        outs,
        scratch,
        "decoder",
        4 * rows * (4 * E * E + 2 * E * FD + E * PIX),
    )


EM_BD, EM_BU = 0, D
EM_G2, EM_S2 = D + FE, 2 * D + FE
EM_BO, EM_NORM = 3 * D + FE, 4 * D + FE
EM_PROJ = 6 * D + FE
EM_ALL = EM_PROJ + E
EA_QKV, EA_G1, EA_S1, EA_EMBED, EA_ALL = 0, 3 * D, 4 * D, 5 * D, 6 * D


def encoder_mlp_back_kernel(
    row_ref, wg_ref, vec_ref, glat_ref, x1_ref, mid_ref, slope_ref,
    gdown_ref, du_ref, grad_ref, gproj_ref, sum_ref,
    w_proj, w_down, w_up, dy, sems,
):
    step = pl.program_id(0)
    ready = fetch_all(
        step == 0, row_ref, wg_ref, sems, [(T_PROJ, w_proj), (T_EDOWN, w_down), (T_EUP, w_up)]
    )

    @pl.when(step == 0)
    def _():
        sum_ref[...] = jnp.zeros_like(sum_ref)

    def vec(start):
        return vec_ref[:, start : start + D]

    sum_rows(glat_ref, sum_ref, EM_PROJ)
    ready(0)
    back_linear(glat_ref, w_proj, dy)
    d_gain, d_shift = norm_backward(x1_ref, dy, vec(V_ENORM), grad_ref, False)
    add_sum(sum_ref, EM_NORM, d_gain)
    add_sum(sum_ref, EM_NORM + D, d_shift)
    round_and_sum(grad_ref, gdown_ref, sum_ref, EM_BD)
    ready(1)
    back_up(gdown_ref, w_down, slope_ref, du_ref, sum_ref, EM_BU)
    ready(2)
    back_linear(du_ref, w_up, dy)
    d_gain, d_shift = norm_backward(mid_ref, dy, vec(ENC["g2"]), grad_ref, True)
    add_sum(sum_ref, EM_G2, d_gain)
    add_sum(sum_ref, EM_S2, d_shift)
    round_and_sum(grad_ref, gproj_ref, sum_ref, EM_BO)


def encoder_mlp_back(tile_rows, gathered, vector, glat, x1, mid, slope, steps):
    rows = x1.shape[0]
    part = rows // steps
    outs = [
        ((rows, D), BF, "rows"),
        ((rows, FE), BF, "rows"),
        ((rows, D), F32, "rows"),
        ((rows, D), BF, "rows"),
        ((8, EM_ALL), F32, "whole"),
    ]
    scratch = [pltpu.VMEM(s, BF) for s in [(D, E), (FE, D), (D, FE)]]
    scratch += [pltpu.VMEM((part, D), F32), pltpu.SemaphoreType.DMA((3,))]
    return group_call(
        encoder_mlp_back_kernel,
        steps,
        (tile_rows,),
        [
            (gathered, "any"),
            (vector, "whole"),
            (glat, "rows"),
            (x1, "rows"),
            (mid, "rows"),
            (slope, "rows"),
        ],
        outs,
        scratch,
        "encoder_mlp_back",
        2 * rows * (D * E + 2 * D * FE),
    )


def encoder_attention_back_kernel(
    row_ref, len_ref, wg_ref, vec_ref, gproj_ref, grad_in_ref, qkv_ref, lse_ref, x0_ref,
    dqkv_ref, gembed_ref, sum_ref,
    w_out, w_qkv, dy, grad, datt, sems,
):
    step = pl.program_id(0)
    images = lse_ref.shape[0]
    ready = fetch_all(step == 0, row_ref, wg_ref, sems, [(T_EOUT, w_out), (T_EQKV, w_qkv)])

    @pl.when(step == 0)
    def _():
        sum_ref[...] = jnp.zeros_like(sum_ref)

    ready(0)

    def back_out(j, cols):
        datt[:, cols] = mm_nt(gproj_ref[...], w_out[cols, :]).astype(BF)

    col_loop(D // BS, back_out)

    def attend_back(image, c):
        valid = lax.broadcasted_iota(jnp.int32, (VMAX, 1), 0) < len_ref[step * images + image]
        attention_backward(qkv_ref, datt, lse_ref, dqkv_ref, image, VMAX, D, D // HE, valid)
        return c

    lax.fori_loop(0, images, attend_back, 0)
    sum_rows(dqkv_ref, sum_ref, EA_QKV)
    ready(1)
    back_linear(dqkv_ref, w_qkv, dy)
    grad[...] = grad_in_ref[...]
    gain = vec_ref[:, ENC["g1"] : ENC["g1"] + D]
    d_gain, d_shift = norm_backward(x0_ref, dy, gain, grad, True)
    add_sum(sum_ref, EA_G1, d_gain)
    add_sum(sum_ref, EA_S1, d_shift)
    round_and_sum(grad, gembed_ref, sum_ref, EA_EMBED)


def encoder_attention_back(tile_rows, vis_len, gathered, vector, gproj, grad, qkv, lse, x0, steps):
    rows = x0.shape[0]
    part = rows // steps
    outs = [((rows, 3 * D), BF, "rows"), ((rows, D), BF, "rows"), ((8, EA_ALL), F32, "whole")]
    scratch = [pltpu.VMEM(s, BF) for s in [(D, D), (D, 3 * D)]]
    scratch += [pltpu.VMEM((part, D), F32), pltpu.VMEM((part, D), F32), pltpu.VMEM((part, D), BF)]
    return group_call(
        encoder_attention_back_kernel,
        steps,
        (tile_rows, vis_len),
        [
            (gathered, "any"),
            (vector, "whole"),
            (gproj, "rows"),
            (grad, "rows"),
            (qkv, "rows"),
            (lse, "rows"),
            (x0, "rows"),
        ],
        outs,
        scratch + [pltpu.SemaphoreType.DMA((2,))],
        "encoder_attention_back",
        2 * rows * 4 * D * D,
    )


def weight_grad_kernel(parts, cut, extra, index_ref, x_ref, g_ref, *refs):
    outs = refs[extra : extra + min(parts, 2)]
    total = refs[-1]
    col_tiles = g_ref.shape[1] // BS
    x_t = x_ref[...].T

    def body(j, cols):
        total[:, cols] = mm(x_t, g_ref[:, cols])

    col_loop(col_tiles, body)
    for p in range(parts):
        start = pl.multiple_of((p ^ index_ref[0]) * cut, cut)
        for j in range(col_tiles):
            outs[p % 2][p // 2, j] = total[pl.ds(start, cut), j * BS : (j + 1) * BS].astype(BF)


def weight_grad(index, parts, count, first, x, g, buffers):
    cut = BS // parts
    rows, width = x.shape
    col_tiles = g.shape[1] // BS
    assert first % col_tiles == 0
    held = min(parts, 2)
    shape = jax.ShapeDtypeStruct((parts // held, count, cut, BS), BF)
    given = list(buffers or [])
    out_spec = pl.BlockSpec(
        (parts // held, col_tiles, cut, BS), lambda i, *_: (0, first // col_tiles + i, 0, 0)
    )
    return pl.pallas_call(
        functools.partial(weight_grad_kernel, parts, cut, len(given)),
        grid_spec=pltpu.PrefetchScalarGridSpec(
            num_scalar_prefetch=1,
            grid=(width // BS,),
            in_specs=[
                pl.BlockSpec((rows, BS), lambda i, *_: (0, i)),
                pl.BlockSpec(g.shape, lambda i, *_: (0, 0)),
            ]
            + [pl.BlockSpec(memory_space=pl.ANY)] * len(given),
            out_specs=[out_spec] * held,
            scratch_shapes=[pltpu.VMEM((BS, g.shape[1]), F32)],
        ),
        out_shape=[shape] * held,
        input_output_aliases={3 + i: i for i in range(len(given))},
        compiler_params=pltpu.CompilerParams(vmem_limit_bytes=VMEM_LIMIT),
        cost_estimate=pl.CostEstimate(
            flops=2 * rows * width * g.shape[1],
            bytes_accessed=2 * rows * (width + g.shape[1]) + 2 * width * g.shape[1],
            transcendentals=0,
        ),
        name="weight_grad",
    )(index, x, g, *given)


def seed_kernel(parts, index_ref, vec_ref, *outs):
    at = pl.program_id(0)
    for p in range(parts):
        got = vec_ref[p ^ index_ref[0]]
        outs[p % 2][p // 2, 0] = jnp.where(at == 0, got, 0.0).astype(BF)


def seed_buffers(index, parts, count, first, vector_tile):
    cut = BS // parts
    held = min(parts, 2)
    shape = jax.ShapeDtypeStruct((parts // held, count, cut, BS), BF)
    return pl.pallas_call(
        functools.partial(seed_kernel, parts),
        grid_spec=pltpu.PrefetchScalarGridSpec(
            num_scalar_prefetch=1,
            grid=(count - first,),
            in_specs=[pl.BlockSpec(vector_tile.shape, lambda i, *_: (0, 0, 0))],
            out_specs=[pl.BlockSpec((parts // held, 1, cut, BS), lambda i, *_: (0, first + i, 0, 0))] * held,
        ),
        out_shape=[shape] * held,
        name="seed_buffers",
    )(index, vector_tile)


def low_sum(a, b):
    return (a.astype(F32) + b.astype(F32)).astype(BF)


def swap_bit(x, bit, size):
    return lax.ppermute(x, "dp", [(i, i ^ (1 << bit)) for i in range(size)])


def reduce_dp(buffers, parts):
    if parts == 1:
        return buffers[0][0]
    bits = parts.bit_length() - 1
    whole = low_sum(buffers[0], swap_bit(buffers[1], 0, parts))
    count = whole.shape[1]
    whole = whole.reshape((2,) * (bits - 1) + whole.shape[1:])
    results = []
    for half in range(2):
        lo, hi = (0, count // 2) if half == 0 else (count // 2, count)
        current = whole[..., lo:hi, :, :]
        left = list(range(bits - 1, 0, -1))
        order = left[::-1] if half == 0 else left
        for bit in order:
            axis = left.index(bit)
            left = [b for b in left if b != bit]
            keep = lax.index_in_dim(current, 0, axis, keepdims=False)
            send = lax.index_in_dim(current, 1, axis, keepdims=False)
            current = low_sum(keep, swap_bit(send, bit, parts))
        results.append(current)
    return jnp.concatenate(results, axis=0)


def shift_patch(x, shift, size):
    return lax.ppermute(x, "patch", [(i, (i + shift) % size) for i in range(size)])


def reduce_patch(x, groups):
    if groups == 1:
        return x
    me = lax.axis_index("patch")
    pieces = x.reshape((groups, x.shape[0] // groups) + x.shape[1:])
    total = lax.dynamic_index_in_dim(pieces, me, 0, keepdims=False).astype(F32)
    for k in range(1, groups):
        piece = lax.dynamic_index_in_dim(pieces, (me + k) % groups, 0, keepdims=False)
        total = total + shift_patch(piece, k, groups).astype(F32)
    total = total.astype(BF)
    return jnp.concatenate([total] + [shift_patch(total, k, groups) for k in range(1, groups)], axis=0)


def place_after(position, count, groups):
    if groups == 1:
        return position
    size = count // groups
    me = lax.axis_index("patch")
    return (me - position // size) % groups * size + position % size


def sum_all(x, parts, groups):
    for bit in range(groups.bit_length() - 1):
        x = x + lax.ppermute(x, "patch", [(i, i ^ (1 << bit)) for i in range(groups)])
    return sum_dp(x, parts)


def sum_dp(x, parts):
    for bit in range(parts.bit_length() - 1):
        x = x + swap_bit(x, bit, parts)
    return x


def split_low(x):
    high = x.astype(BF)
    return high, (x - high.astype(F32)).astype(BF)


def tile_kernel(
    scale_ref, grad_ref, w_ref, left_stat_ref, right_stat_ref, left_root_ref, right_root_ref,
    clipped_ref, left_new_ref, right_new_ref, w_new_ref,
):
    scale = scale_ref[0]
    for t in range(w_ref.shape[0]):
        grad = grad_ref[:, t].reshape(BS, BS)
        clipped_ref[t] = grad.astype(F32) * scale
        square = (1.0 - BETA_STAT) * scale * scale
        left_new_ref[t] = BETA_STAT * left_stat_ref[t] + square * mm_nt(grad, grad)
        right_new_ref[t] = BETA_STAT * right_stat_ref[t] + square * mm_tn(grad, grad)
        high, low = split_low(left_root_ref[t])
        half = (mm(high, grad) + mm(low, grad)) * scale
        half_high, half_low = split_low(half)
        high, low = split_low(right_root_ref[t])
        direction = mm(half_high, high) + (mm(half_high, low) + mm(half_low, high))
        direction = direction * lax.rsqrt(jnp.mean(direction * direction) + EPS_ROOT)
        w_new_ref[t] = w_ref[t] - RATE_MATRIX * (direction + DECAY_MATRIX * w_ref[t])


def tile_update(scale, grads, states):
    parts, slots, cut, _ = grads.shape
    per = 2 if slots % 2 == 0 else 1
    tile = pl.BlockSpec((per, BS, BS), lambda i, *_: (i, 0, 0))
    return pl.pallas_call(
        tile_kernel,
        grid_spec=pltpu.PrefetchScalarGridSpec(
            num_scalar_prefetch=1,
            grid=(slots // per,),
            in_specs=[pl.BlockSpec((parts, per, cut, BS), lambda i, *_: (0, i, 0, 0))] + [tile] * 5,
            out_specs=[tile] * 4,
        ),
        out_shape=[jax.ShapeDtypeStruct((slots, BS, BS), F32)] * 4,
        compiler_params=pltpu.CompilerParams(vmem_limit_bytes=VMEM_LIMIT),
        name="tile_update",
    )(scale.reshape(1), grads, *states)


def vector_update(clipped, vectors, moment, second):
    moment_new = BETA_FIRST * moment + (1.0 - BETA_FIRST) * clipped
    second_new = BETA_SECOND * second + (1.0 - BETA_SECOND) * clipped * clipped
    corrected = moment_new / (1.0 - BETA_FIRST**STEP)
    scaled = second_new / (1.0 - BETA_SECOND**STEP)
    vectors_new = vectors - RATE_VECTOR * corrected / (jnp.sqrt(scaled) + EPS_ADAM)
    return moment_new, second_new, vectors_new


ENC_ORDER = [(T_EUP, 3, 12), (T_EDOWN, 12, 3)]
CHUNKS = [
    [(T_DUP, 2, 8), (T_DDOWN, 8, 2), (T_DOUT, 2, 2), (T_DQKV, 2, 6), (T_HEAD, 2, 3), (T_PROJ, 3, 2)],
    [(T_EUP, 3, 12), (T_EDOWN, 12, 3)],
    [(T_EQKV, 3, 9), (T_EOUT, 3, 3), (T_EMBED, 3, 3)],
]


def chunk_sizes(groups):
    unit = max(2, groups)
    sizes = []
    for i, chunk in enumerate(CHUNKS):
        used = sum(r * c for _, r, c in chunk) + (2 if i == len(CHUNKS) - 1 else 0)
        sizes.append(-(-used // unit) * unit)
    return sizes


def tile_places(sizes):
    chunk_of = np.zeros(NBLK + 2, np.int32)
    place_of = np.zeros(NBLK + 2, np.int32)
    for i, chunk in enumerate(CHUNKS):
        at = 0
        for first, row_tiles, col_tiles in chunk:
            for t in range(row_tiles * col_tiles):
                chunk_of[first + t], place_of[first + t] = i, at + t
            at += row_tiles * col_tiles
    chunk_of[NBLK:] = len(CHUNKS) - 1
    place_of[NBLK + 1] = at
    place_of[NBLK] = at + 1
    return chunk_of, place_of, at


def shards(parts, groups, pixels, shuffle, vis_len, block_owner, weights, vectors, vec_moment, vec_second,
           left_stat, right_stat, left_root, right_root):
    slots = weights.shape[0]
    own = vectors.shape[0]
    index = lax.axis_index("dp").astype(jnp.int32).reshape(1)
    images = pixels.shape[0]

    vector_rows = -(-own // (16 * BS)) * 16
    mine = jnp.concatenate(
        [
            weights.astype(BF).reshape(slots * BS, BS),
            jnp.pad(vectors.astype(BF), (0, vector_rows * BS - own)).reshape(vector_rows, BS),
        ]
    )
    gathered = lax.all_gather(mine, "dp", axis=0, tiled=True)
    stride = mine.shape[0]
    slot_index = jnp.arange(block_owner.shape[0], dtype=jnp.int32)
    slot_of_block = jnp.sum(
        jnp.where(block_owner[None, :] == jnp.arange(NBLK, dtype=jnp.int32)[:, None], slot_index[None, :], 0),
        axis=1,
    )
    tile_rows = slot_of_block // slots * stride + slot_of_block % slots * BS
    vector = gathered.reshape(parts, stride, BS)[:, slots * BS :].reshape(parts, vector_rows * BS)
    vector = vector[:, :own].reshape(-1).astype(F32)
    enc_key, dec_key = 4 * D, 4 * D + (8 * D + FE - 3 * D) + 2 * D + 2 * E + 3 * E
    vector = jnp.concatenate(
        [vector[:enc_key], jnp.zeros(D, F32), vector[enc_key:dec_key], jnp.zeros(E, F32), vector[dec_key:]]
    ).reshape(1, V_ALL)

    ordered, visible_pix, pos_d, pos_e = order_patches(pixels, shuffle)
    (x0, h1, qkv, lse, att, mid, h2, act, slope, x1, hn, latent) = encoder_forward(
        tile_rows, vis_len, gathered, vector, visible_pix, pos_d, 2
    )
    (d_h1, d_dqkv, d_att, d_gproj, d_h2, d_du, d_act, d_gdown, d_hn, d_gpred, glat, d_sums) = decoder(
        tile_rows, vis_len, gathered, vector, latent, pos_e, ordered, 4
    )
    sizes = chunk_sizes(groups)
    chunk_of, place_of, vector_place = tile_places(sizes)

    def gradients(chunk, pairs, buffers=None):
        at = 0
        for x, g in pairs:
            buffers = weight_grad(index, parts, sizes[chunk], at, x, g, buffers)
            at += x.shape[1] // BS * (g.shape[1] // BS)
        return reduce_patch(reduce_dp(buffers, parts), groups)

    first = gradients(
        0, [(d_h2, d_du), (d_act, d_gdown), (d_att, d_gproj), (d_h1, d_dqkv), (d_hn, d_gpred), (hn, glat)]
    )
    gdown, du, grad_mid, gproj, m_sums = encoder_mlp_back(tile_rows, gathered, vector, glat, x1, mid, slope, 2)
    second = gradients(1, [(h2, du), (act, gdown)])
    dqkv, gembed, a_sums = encoder_attention_back(
        tile_rows, vis_len, gathered, vector, gproj, grad_mid, qkv, lse, x0, 2
    )

    d_sums, m_sums, a_sums = (jnp.sum(s, axis=0) for s in (d_sums, m_sums, a_sums))

    def cut(sums, start, size):
        return sums[start : start + size]

    grad_vector = jnp.concatenate(
        [
            cut(a_sums, EA_EMBED, D),
            cut(a_sums, EA_G1, 2 * D),
            cut(a_sums, EA_QKV, D),
            cut(a_sums, EA_QKV + 2 * D, D),
            cut(m_sums, EM_BO, D),
            cut(m_sums, EM_G2, 2 * D),
            cut(m_sums, EM_BU, FE),
            cut(m_sums, EM_BD, D),
            cut(m_sums, EM_NORM, 2 * D),
            cut(m_sums, EM_PROJ, E),
            cut(d_sums, DS_MASK, E),
            cut(d_sums, DS["g1"], 2 * E),
            cut(d_sums, DS["bqkv"], E),
            cut(d_sums, DS["bqkv"] + 2 * E, E),
            cut(d_sums, DS["bo"], E),
            cut(d_sums, DS["g2"], 2 * E),
            cut(d_sums, DS["bu"], FD),
            cut(d_sums, DS["bd"], E),
            cut(d_sums, DS_NORM, 2 * E),
            cut(d_sums, DS_HEAD, PIX),
        ]
    )
    rows_cut = BS // parts
    vector_tile = jnp.pad(grad_vector.reshape(parts, own), ((0, 0), (0, rows_cut * BS - own)))
    seeded = seed_buffers(index, parts, sizes[2], vector_place, vector_tile.reshape(parts, rows_cut, BS))
    third = gradients(2, [(h1, dqkv), (att, gproj), (visible_pix.reshape(-1, PIX), gembed)], seeded)

    reduced = jnp.concatenate([first, second, third], axis=0)
    starts = np.cumsum([0] + sizes)
    where = jnp.zeros(NBLK + 2, jnp.int32)
    for i, size in enumerate(sizes):
        here = starts[i] + place_after(jnp.asarray(place_of), size, groups)
        where = jnp.where(jnp.asarray(chunk_of == i), here, where)
    wide = reduced.astype(F32)
    squares = sum_dp(jnp.sum(wide * wide), parts)
    totals = jnp.stack([jnp.sum(cut(d_sums, DS_LOSS, PIX)) / PIX, jnp.sum(POS - vis_len).astype(F32)])
    totals = sum_all(totals, parts, groups)
    loss_sum, masked_count = totals[0], totals[1]
    grad_norm = jnp.sqrt(squares) / masked_count
    scale = jnp.minimum(1.0, CLIP_NORM / grad_norm) / masked_count

    slot_rows = reduced[where[jnp.minimum(block_owner, NBLK)]]
    if parts > 1:
        slot_rows = lax.all_to_all(slot_rows, "dp", 0, 0, tiled=True)
    grads = slot_rows.reshape(parts, slots, rows_cut, BS)
    clipped, left_new, right_new, weights_new = tile_update(
        scale, grads, (weights, left_stat, right_stat, left_root, right_root)
    )
    own_vector = lax.dynamic_index_in_dim(reduced, where[NBLK + 1], 0, keepdims=False)
    own_vector = own_vector.reshape(-1)[:own].astype(F32) * scale
    moment_new, second_new, vectors_new = vector_update(own_vector, vectors, vec_moment, vec_second)
    return (
        loss_sum,
        masked_count,
        grad_norm,
        clipped,
        left_new,
        right_new,
        weights_new,
        moment_new,
        second_new,
        vectors_new,
    )


def solution(mesh):
    both = ("dp", "patch")
    tiles = P("dp", None, None)
    return jax.shard_map(
        functools.partial(shards, mesh.shape["dp"], mesh.shape["patch"]),
        mesh=mesh,
        in_specs=(P(both, None, None), P(both, None), P(both), P())
        + (tiles, P("dp"), P("dp"), P("dp"))
        + (tiles,) * 4,
        out_specs=(P(), P(), P()) + (tiles,) * 4 + (P("dp"),) * 3,
        check_vma=False,
    )
```

```python
import functools
import math

import jax
import jax.numpy as jnp
import numpy as np
from jax import lax
from jax.experimental import pallas as pl
from jax.experimental.pallas import tpu as pltpu
from jax.sharding import PartitionSpec as P

D = 768
HE = 12
FE = 3072
E = 512
HD = 16
FD = 2048
PIX = 768
POS = 196
VMAX = 80
BS = 256
STEP = 10
NBLK = 177

SD = 208

EPS_NORM = 1e-06
EPS_ROOT = 1e-06
EPS_ADAM = 1e-08
CLIP_NORM = 0.01
RATE_MATRIX = 0.03
DECAY_MATRIX = 0.05
BETA_STAT = 0.5
BETA_FIRST = 0.9
BETA_SECOND = 0.999
RATE_VECTOR = 0.1
NEG_LARGE = -1e30
LOG2E = math.log2(math.e)

BF = jnp.bfloat16
F32 = jnp.float32
VMEM_LIMIT = 60 * 1024 * 1024

T_EMBED, T_EQKV, T_EOUT, T_EUP, T_EDOWN, T_PROJ = 0, 9, 36, 45, 81, 117
T_DQKV, T_DOUT, T_DUP, T_DDOWN, T_HEAD = 123, 135, 139, 155, 171

V_EMBED = 0
V_ENC = D
V_ENORM = V_ENC + 9 * D + FE
V_PROJ = V_ENORM + 2 * D
V_MASK = V_PROJ + E
V_DEC = V_MASK + E
V_DNORM = V_DEC + 9 * E + FD
V_HEAD = V_DNORM + 2 * E
V_ALL = V_HEAD + PIX


def layer_offsets(start, width, hidden):
    names = ["g1", "s1", "bqkv", "bo", "g2", "s2", "bu", "bd"]
    sizes = [width, width, 3 * width, width, width, width, hidden, width]
    offsets = {}
    for name, size in zip(names, sizes):
        offsets[name] = start
        start += size
    return offsets


def mm(a, b):
    return jnp.dot(a, b, preferred_element_type=F32)


def mm_nt(a, b):
    return lax.dot_general(a, b, (((1,), (1,)), ((), ())), preferred_element_type=F32)


def mm_tn(a, b):
    return lax.dot_general(a, b, (((0,), (0,)), ((), ())), preferred_element_type=F32)


def fold8(x):
    rows, cols = x.shape
    return jnp.sum(x.reshape(rows // 8, 8, cols), axis=0)


def gelu_pair(u):
    t = 1.0 / (1.0 + (0.3275911 * math.sqrt(0.5)) * jnp.abs(u))
    e = jnp.exp2((-0.5 * LOG2E) * (u * u))
    poly = t * (
        0.5 * 0.254829592
        + t * (-0.5 * 0.284496736 + t * (0.5 * 1.421413741 + t * (-0.5 * 1.453152027 + t * (0.5 * 1.061405429))))
    )
    tail = poly * e
    phi = jnp.where(u >= 0, 1.0 - tail, tail)
    return u * phi, phi + u * (e * (1.0 / math.sqrt(2.0 * math.pi)))


def norm_parts(x):
    centred = x - jnp.mean(x, axis=-1, keepdims=True)
    inverse = lax.rsqrt(jnp.mean(centred * centred, axis=-1, keepdims=True) + EPS_NORM)
    return centred * inverse, inverse


def loop(lower, upper, body, carry, most=26):
    count = upper - lower
    unroll = max(u for u in range(1, min(most, count) + 1) if count % u == 0)
    return lax.fori_loop(lower, upper, body, carry, unroll=unroll)


def row_loop(rows, step, body, carry=0):
    count = rows // step

    def one(i, c):
        return body(pl.ds(pl.multiple_of(i * step, step), step), c)

    return loop(0, count, one, carry)


def norm_forward(x_ref, gain, shift, out_ref):
    def body(sl, c):
        normed, _ = norm_parts(x_ref[sl, :])
        out_ref[sl, :] = (normed * gain + shift).astype(BF)
        return c

    row_loop(x_ref.shape[0], 16, body)


def norm_backward(x_ref, dy_ref, gain, out_ref, add):
    width = x_ref.shape[1]

    def body(sl, c):
        d_gain, d_shift = c
        normed, inverse = norm_parts(x_ref[sl, :])
        dy = dy_ref[sl, :]
        dn = dy * gain
        mean_one = jnp.mean(dn, axis=-1, keepdims=True)
        mean_two = jnp.mean(dn * normed, axis=-1, keepdims=True)
        dx = inverse * (dn - mean_one - normed * mean_two)
        out_ref[sl, :] = out_ref[sl, :] + dx if add else dx
        return (d_gain + fold8(dy * normed), d_shift + fold8(dy))

    zero = jnp.zeros((8, width), F32)
    return row_loop(x_ref.shape[0], 16, body, (zero, zero))


def col_loop(count, body):
    def one(j, c):
        body(j, pl.ds(pl.multiple_of(j * BS, BS), BS))
        return c

    loop(0, count, one, 0, 4)


def vec_at(vec_ref, start, j):
    return vec_ref[:, pl.ds(pl.multiple_of(start + j * BS, BS), BS)]


def head_mask(head, head_size):
    lane = lax.broadcasted_iota(jnp.int32, (1, BS), 1)
    inside = (lane >= head * head_size) & (lane < (head + 1) * head_size)
    return jnp.where(inside, 1.0, 0.0).astype(BF)


def scores_of(k_masked, q, head_size, valid):
    scores = mm_nt(k_masked, q) * (head_size**-0.5 * LOG2E)
    return jnp.where(valid, scores, NEG_LARGE)


def attention_forward(qkv_ref, att_ref, lse_ref, image, seq, width, head_size, valid):
    rows = pl.ds(pl.multiple_of(image * seq, 16), seq)
    per = BS // head_size

    def group(g, c):
        def part(which):
            return qkv_ref[rows, pl.ds(pl.multiple_of(which * width + g * BS, BS), BS)]

        q, k, v = part(0), part(1), part(2)
        v_t = v.T
        outs, logs = [], []
        for h in range(per):
            scores = scores_of(k * head_mask(h, head_size), q, head_size, valid)
            top = jnp.max(scores, axis=0, keepdims=True)
            e = jnp.exp2(scores - top)
            total = jnp.sum(e, axis=0, keepdims=True)
            out = mm(v_t[h * head_size : (h + 1) * head_size, :], e.astype(BF))
            outs.append(out * (1.0 / total))
            logs.append(top + jnp.log2(total))
        att_ref[rows, pl.ds(pl.multiple_of(g * BS, BS), BS)] = jnp.concatenate(outs, axis=0).T.astype(BF)
        lse_ref[image, g] = jnp.concatenate(logs, axis=0)
        return c

    loop(0, width // BS, group, 0)


def attention_backward(qkv_ref, datt_ref, lse_ref, dqkv_ref, image, seq, width, head_size, valid):
    rows = pl.ds(pl.multiple_of(image * seq, 16), seq)
    per = BS // head_size
    scale = head_size**-0.5

    def group(g, c):
        def cols(which):
            return pl.ds(pl.multiple_of(which * width + g * BS, BS), BS)

        q, k, v = qkv_ref[rows, cols(0)], qkv_ref[rows, cols(1)], qkv_ref[rows, cols(2)]
        d_out = datt_ref[rows, cols(0)]
        lse = lse_ref[image, g]
        q_t, k_t, d_out_t = q.T, k.T, d_out.T
        d_q, d_k, d_v = [], [], []
        for h in range(per):
            mask = head_mask(h, head_size)
            part = slice(h * head_size, (h + 1) * head_size)
            probs = jnp.exp2(scores_of(k * mask, q, head_size, valid) - lse[h : h + 1, :])
            d_probs = mm_nt(v * mask, d_out)
            delta = jnp.sum(probs * d_probs, axis=0, keepdims=True)
            d_scores = (probs * (d_probs - delta)).astype(BF)
            d_v.append(mm_nt(d_out_t[part, :], probs.astype(BF)))
            d_k.append(mm_nt(q_t[part, :], d_scores))
            d_q.append(mm(k_t[part, :], d_scores))
        dqkv_ref[rows, cols(0)] = (jnp.concatenate(d_q, axis=0).T * scale).astype(BF)
        dqkv_ref[rows, cols(1)] = (jnp.concatenate(d_k, axis=0).T * scale).astype(BF)
        dqkv_ref[rows, cols(2)] = jnp.concatenate(d_v, axis=0).T.astype(BF)
        return c

    loop(0, width // BS, group, 0)


def fetch_tiles(row_ref, wg_ref, first, dst, sem):
    row_tiles, col_tiles = dst.shape[0] // BS, dst.shape[1] // BS
    for i in range(row_tiles):
        for j in range(col_tiles):
            start = pl.multiple_of(row_ref[first + i * col_tiles + j], 16)
            pltpu.make_async_copy(
                wg_ref.at[pl.ds(start, BS), :],
                dst.at[i * BS : (i + 1) * BS, j * BS : (j + 1) * BS],
                sem,
            ).start()


def await_tiles(dst, sem):
    pltpu.make_async_copy(dst, dst, sem).wait()


def fetch_all(first_step, row_ref, wg_ref, sems, matrices):
    @pl.when(first_step)
    def _():
        for i, (first, dst) in enumerate(matrices):
            fetch_tiles(row_ref, wg_ref, first, dst, sems.at[i])

    def ready(i):
        @pl.when(first_step)
        def _():
            await_tiles(matrices[i][1], sems.at[i])

    return ready


def qkv_forward(h_ref, w_ref, vec_ref, start, out_ref):
    def body(j, cols):
        out_ref[:, cols] = (mm(h_ref[...], w_ref[:, cols]) + vec_at(vec_ref, start, j)).astype(BF)

    col_loop(w_ref.shape[1] // BS, body)


def add_linear(x_ref, h_ref, w_ref, vec_ref, start, out_ref):
    def body(j, cols):
        out_ref[:, cols] = x_ref[:, cols] + (mm(h_ref[...], w_ref[:, cols]) + vec_at(vec_ref, start, j))

    col_loop(w_ref.shape[1] // BS, body)


def up_forward(h_ref, w_ref, vec_ref, start, act_ref, slope_ref):
    def body(j, cols):
        act, slope = gelu_pair(mm(h_ref[...], w_ref[:, cols]) + vec_at(vec_ref, start, j))
        act_ref[:, cols] = act.astype(BF)
        slope_ref[:, cols] = slope.astype(BF)

    col_loop(w_ref.shape[1] // BS, body)


def back_linear(g_ref, w_ref, out_ref):
    def body(j, cols):
        out_ref[:, cols] = mm_nt(g_ref[...], w_ref[cols, :])

    col_loop(w_ref.shape[0] // BS, body)


def back_up(g_ref, w_ref, slope_ref, du_ref, sum_ref, start):
    def body(j, cols):
        du = (mm_nt(g_ref[...], w_ref[cols, :]) * slope_ref[:, cols].astype(F32)).astype(BF)
        du_ref[:, cols] = du
        at = pl.ds(pl.multiple_of(start + j * BS, BS), BS)
        sum_ref[:, at] = sum_ref[:, at] + fold8(du.astype(F32))

    col_loop(w_ref.shape[0] // BS, body)


def round_and_sum(x_ref, out_ref, sum_ref, start):
    width = x_ref.shape[1]

    def body(sl, c):
        low = x_ref[sl, :].astype(BF)
        out_ref[sl, :] = low
        return c + fold8(low.astype(F32))

    total = row_loop(x_ref.shape[0], 16, body, jnp.zeros((8, width), F32))
    sum_ref[:, start : start + width] = sum_ref[:, start : start + width] + total


def sum_rows(x_ref, sum_ref, start):
    width = x_ref.shape[1]

    def body(sl, c):
        return c + fold8(x_ref[sl, :].astype(F32))

    total = row_loop(x_ref.shape[0], 16, body, jnp.zeros((8, width), F32))
    sum_ref[:, start : start + width] = sum_ref[:, start : start + width] + total


def add_sum(sum_ref, start, value):
    stop = start + value.shape[1]
    sum_ref[:, start:stop] = sum_ref[:, start:stop] + value


def order_kernel(shuffle_ref, pixels_ref, sin_d_ref, sin_e_ref, all_ref, visible_ref, pos_d_ref, pos_e_ref):
    ids = shuffle_ref[0]
    pick = jnp.where(ids == lax.broadcasted_iota(jnp.int32, (SD, POS), 1), 1.0, 0.0).astype(BF)
    ordered = mm(pick, pixels_ref[0]).astype(BF)
    all_ref[0] = ordered
    visible_ref[0] = ordered[:VMAX, :]
    few = pick[:VMAX, :]
    pos_d_ref[0] = mm(few, sin_d_ref[0]) + mm(few, sin_d_ref[1])
    pos_e_ref[0] = mm(pick, sin_e_ref[0]) + mm(pick, sin_e_ref[1])


def sinusoid_parts(count, width):
    half = width // 2
    frequency = np.exp(np.arange(half) * (-np.log(10000.0) / half))
    angles = np.arange(count)[:, None] * frequency[None, :]
    table = np.concatenate([np.sin(angles), np.cos(angles)], axis=1).astype(np.float32)
    high = table.astype(jnp.bfloat16)
    low = (table - high.astype(np.float32)).astype(jnp.bfloat16)
    return np.stack([high, low])


def order_patches(pixels, shuffle):
    images = pixels.shape[0]
    ids = jnp.pad(shuffle, ((0, 0), (0, SD - POS)), constant_values=-1)[:, :, None]

    def image(*dims):
        return pl.BlockSpec((1,) + dims, lambda b: (b,) + (0,) * len(dims))

    def whole(*dims):
        return pl.BlockSpec(dims, lambda b: (0,) * len(dims))

    return pl.pallas_call(
        order_kernel,
        grid=(images,),
        in_specs=[image(SD, 1), image(POS, PIX), whole(2, POS, D), whole(2, POS, E)],
        out_specs=[image(SD, PIX), image(VMAX, PIX), image(VMAX, D), image(SD, E)],
        out_shape=[
            jax.ShapeDtypeStruct((images, SD, PIX), BF),
            jax.ShapeDtypeStruct((images, VMAX, PIX), BF),
            jax.ShapeDtypeStruct((images, VMAX, D), F32),
            jax.ShapeDtypeStruct((images, SD, E), F32),
        ],
        compiler_params=pltpu.CompilerParams(vmem_limit_bytes=VMEM_LIMIT),
        name="order_patches",
    )(ids, pixels, jnp.asarray(sinusoid_parts(POS, D)), jnp.asarray(sinusoid_parts(POS, E)))


def group_call(kernel, steps, prefetch, in_arrays, out_list, scratch, name, flops):
    def spec(shape, kind):
        if kind == "any":
            return pl.BlockSpec(memory_space=pl.ANY)
        if kind == "rows":
            block = (shape[0] // steps,) + tuple(shape[1:])
            return pl.BlockSpec(block, lambda i, *_: (i,) + (0,) * (len(shape) - 1))
        return pl.BlockSpec(tuple(shape), lambda i, *_: (0,) * len(shape))

    return pl.pallas_call(
        kernel,
        grid_spec=pltpu.PrefetchScalarGridSpec(
            num_scalar_prefetch=len(prefetch),
            grid=(steps,),
            in_specs=[spec(a.shape, kind) for a, kind in in_arrays],
            out_specs=[spec(shape, kind) for shape, _, kind in out_list],
            scratch_shapes=scratch,
        ),
        out_shape=[jax.ShapeDtypeStruct(shape, dtype) for shape, dtype, _ in out_list],
        compiler_params=pltpu.CompilerParams(
            vmem_limit_bytes=VMEM_LIMIT, dimension_semantics=("arbitrary",)
        ),
        cost_estimate=pl.CostEstimate(
            flops=flops,
            bytes_accessed=sum(math.prod(s) * jnp.dtype(t).itemsize for s, t, _ in out_list) * 2,
            transcendentals=0,
        ),
        name=name,
    )(*prefetch, *[a for a, _ in in_arrays])


ENC = layer_offsets(V_ENC, D, FE)
DEC = layer_offsets(V_DEC, E, FD)


def encoder_forward_kernel(
    row_ref, len_ref, wg_ref, vec_ref, pix_ref, pos_ref,
    x0_ref, h1_ref, qkv_ref, lse_ref, att_ref, mid_ref, h2_ref, act_ref, slope_ref, x1_ref, hn_ref, latent_ref,
    w_embed, w_qkv, w_out, w_up, w_down, w_proj, sems,
):
    step = pl.program_id(0)
    images = lse_ref.shape[0]
    ready = fetch_all(
        step == 0,
        row_ref,
        wg_ref,
        sems,
        [
            (T_EMBED, w_embed),
            (T_EQKV, w_qkv),
            (T_EOUT, w_out),
            (T_EUP, w_up),
            (T_EDOWN, w_down),
            (T_PROJ, w_proj),
        ],
    )

    def vec(start, size=D):
        return vec_ref[:, start : start + size]

    ready(0)
    add_linear(pos_ref, pix_ref, w_embed, vec_ref, V_EMBED, x0_ref)
    norm_forward(x0_ref, vec(ENC["g1"]), vec(ENC["s1"]), h1_ref)
    ready(1)
    qkv_forward(h1_ref, w_qkv, vec_ref, ENC["bqkv"], qkv_ref)

    def one(image, c):
        valid = lax.broadcasted_iota(jnp.int32, (VMAX, 1), 0) < len_ref[step * images + image]
        attention_forward(qkv_ref, att_ref, lse_ref, image, VMAX, D, D // HE, valid)
        return c

    lax.fori_loop(0, images, one, 0)
    ready(2)
    add_linear(x0_ref, att_ref, w_out, vec_ref, ENC["bo"], mid_ref)
    norm_forward(mid_ref, vec(ENC["g2"]), vec(ENC["s2"]), h2_ref)
    ready(3)
    up_forward(h2_ref, w_up, vec_ref, ENC["bu"], act_ref, slope_ref)
    ready(4)
    add_linear(mid_ref, act_ref, w_down, vec_ref, ENC["bd"], x1_ref)
    norm_forward(x1_ref, vec(V_ENORM), vec(V_ENORM + D), hn_ref)
    ready(5)

    def project(j, cols):
        latent_ref[:, cols] = mm(hn_ref[...], w_proj[:, cols]) + vec_at(vec_ref, V_PROJ, j)

    col_loop(E // BS, project)


def encoder_forward(tile_rows, vis_len, gathered, vector, visible_pix, pos_d, steps):
    images = vis_len.shape[0]
    rows = images * VMAX
    outs = [
        ((rows, D), F32, "rows"),
        ((rows, D), BF, "rows"),
        ((rows, 3 * D), BF, "rows"),
        ((images, D // BS, BS * HE // D, VMAX), F32, "rows"),
        ((rows, D), BF, "rows"),
        ((rows, D), F32, "rows"),
        ((rows, D), BF, "rows"),
        ((rows, FE), BF, "rows"),
        ((rows, FE), BF, "rows"),
        ((rows, D), F32, "rows"),
        ((rows, D), BF, "rows"),
        ((rows, E), F32, "rows"),
    ]
    scratch = [pltpu.VMEM(s, BF) for s in [(PIX, D), (D, 3 * D), (D, D), (D, FE), (FE, D), (D, E)]]
    return group_call(
        encoder_forward_kernel,
        steps,
        (tile_rows, vis_len),
        [
            (gathered, "any"),
            (vector, "whole"),
            (visible_pix.reshape(rows, PIX), "rows"),
            (pos_d.reshape(rows, D), "rows"),
        ],
        outs,
        scratch + [pltpu.SemaphoreType.DMA((6,))],
        "encoder_forward",
        2 * rows * (PIX * D + 4 * D * D + 2 * D * FE + D * E),
    )


DS = layer_offsets(0, E, FD)
DS_NORM = 9 * E + FD
DS_HEAD = DS_NORM + 2 * E
DS_MASK = DS_HEAD + PIX
DS_LOSS = DS_MASK + E
DS_ALL = DS_LOSS + PIX


def decoder_kernel(
    row_ref, len_ref, wg_ref, vec_ref, latent_ref, pos_ref, pix_ref,
    h1_ref, dqkv_ref, att_ref, gproj_ref, h2_ref, du_ref, act_ref, gdown_ref, hn_ref, gpred_ref, glat_ref, sum_ref,
    w_qkv, w_out, w_up, w_down, w_head, x0, qkv, lse, mid, slope, x1, pred, dy, grad, datt, sems,
):
    step = pl.program_id(0)
    images = lse.shape[0]
    ready = fetch_all(
        step == 0,
        row_ref,
        wg_ref,
        sems,
        [(T_DQKV, w_qkv), (T_DOUT, w_out), (T_DUP, w_up), (T_DDOWN, w_down), (T_HEAD, w_head)],
    )

    @pl.when(step == 0)
    def _():
        sum_ref[...] = jnp.zeros_like(sum_ref)

    def vec(start, size=E):
        return vec_ref[:, start : start + size]

    def length(image):
        return len_ref[step * images + image]

    chunk = 16
    order = lax.broadcasted_iota(jnp.int32, (chunk, 1), 0)
    token = vec(V_MASK)

    def place(image, c):
        def head_rows(i, c):
            at = pl.ds(pl.multiple_of(image * SD + i * chunk, chunk), chunk)
            got = latent_ref[pl.ds(pl.multiple_of(image * VMAX + i * chunk, chunk), chunk), :]
            x0[at, :] = jnp.where(i * chunk + order < length(image), got, token) + pos_ref[at, :]
            return c

        def tail_rows(i, c):
            at = pl.ds(pl.multiple_of(image * SD + i * chunk, chunk), chunk)
            x0[at, :] = token + pos_ref[at, :]
            return c

        loop(0, VMAX // chunk, head_rows, 0)
        loop(VMAX // chunk, SD // chunk, tail_rows, 0)
        return c

    lax.fori_loop(0, images, place, 0)
    norm_forward(x0, vec(DEC["g1"]), vec(DEC["s1"]), h1_ref)
    ready(0)
    qkv_forward(h1_ref, w_qkv, vec_ref, DEC["bqkv"], qkv)
    valid = lax.broadcasted_iota(jnp.int32, (SD, 1), 0) < POS

    def attend(image, c):
        attention_forward(qkv, att_ref, lse, image, SD, E, E // HD, valid)
        return c

    lax.fori_loop(0, images, attend, 0)
    ready(1)
    add_linear(x0, att_ref, w_out, vec_ref, DEC["bo"], mid)
    norm_forward(mid, vec(DEC["g2"]), vec(DEC["s2"]), h2_ref)
    ready(2)
    up_forward(h2_ref, w_up, vec_ref, DEC["bu"], act_ref, slope)
    ready(3)
    add_linear(mid, act_ref, w_down, vec_ref, DEC["bd"], x1)
    norm_forward(x1, vec(V_DNORM), vec(V_DNORM + E), hn_ref)
    ready(4)

    def predict(j, cols):
        pred[:, cols] = mm(hn_ref[...], w_head[:, cols]) + vec_at(vec_ref, V_HEAD, j)

    col_loop(PIX // BS, predict)

    def errors(image, c):
        def one(i, c):
            loss, bias = c
            at = pl.ds(pl.multiple_of(image * SD + i * chunk, chunk), chunk)
            target, _ = norm_parts(pix_ref[at, :].astype(F32))
            place_in = i * chunk + order
            masked = (place_in >= length(image)) & (place_in < POS)
            residual = jnp.where(masked, pred[at, :] - target, 0.0)
            low = (residual * (2.0 / PIX)).astype(BF)
            gpred_ref[at, :] = low
            return (loss + fold8(residual * residual), bias + fold8(low.astype(F32)))

        return loop(0, SD // chunk, one, c)

    zero = jnp.zeros((8, PIX), F32)
    loss, bias = lax.fori_loop(0, images, errors, (zero, zero))
    add_sum(sum_ref, DS_LOSS, loss)
    add_sum(sum_ref, DS_HEAD, bias)

    back_linear(gpred_ref, w_head, dy)
    d_gain, d_shift = norm_backward(x1, dy, vec(V_DNORM), grad, False)
    add_sum(sum_ref, DS_NORM, d_gain)
    add_sum(sum_ref, DS_NORM + E, d_shift)
    round_and_sum(grad, gdown_ref, sum_ref, DS["bd"])
    back_up(gdown_ref, w_down, slope, du_ref, sum_ref, DS["bu"])
    back_linear(du_ref, w_up, dy)
    d_gain, d_shift = norm_backward(mid, dy, vec(DEC["g2"]), grad, True)
    add_sum(sum_ref, DS["g2"], d_gain)
    add_sum(sum_ref, DS["s2"], d_shift)
    round_and_sum(grad, gproj_ref, sum_ref, DS["bo"])

    def back_out(j, cols):
        datt[:, cols] = mm_nt(gproj_ref[...], w_out[cols, :]).astype(BF)

    col_loop(E // BS, back_out)

    def attend_back(image, c):
        attention_backward(qkv, datt, lse, dqkv_ref, image, SD, E, E // HD, valid)
        return c

    lax.fori_loop(0, images, attend_back, 0)
    sum_rows(dqkv_ref, sum_ref, DS["bqkv"])
    back_linear(dqkv_ref, w_qkv, dy)
    d_gain, d_shift = norm_backward(x0, dy, vec(DEC["g1"]), grad, True)
    add_sum(sum_ref, DS["g1"], d_gain)
    add_sum(sum_ref, DS["s1"], d_shift)

    def unplace(image, c):
        def head_rows(i, c):
            got = grad[pl.ds(pl.multiple_of(image * SD + i * chunk, chunk), chunk), :]
            seen = i * chunk + order < length(image)
            at = pl.ds(pl.multiple_of(image * VMAX + i * chunk, chunk), chunk)
            glat_ref[at, :] = jnp.where(seen, got, 0.0).astype(BF)
            return c + fold8(jnp.where(seen, 0.0, got))

        def tail_rows(i, c):
            got = grad[pl.ds(pl.multiple_of(image * SD + i * chunk, chunk), chunk), :]
            return c + fold8(jnp.where(i * chunk + order < POS, got, 0.0))

        c = loop(0, VMAX // chunk, head_rows, c)
        return loop(VMAX // chunk, SD // chunk, tail_rows, c)

    add_sum(sum_ref, DS_MASK, lax.fori_loop(0, images, unplace, jnp.zeros((8, E), F32)))


def decoder(tile_rows, vis_len, gathered, vector, latent, pos_e, ordered, steps):
    images = vis_len.shape[0]
    rows = images * SD
    part = rows // steps
    outs = [
        ((rows, E), BF, "rows"),
        ((rows, 3 * E), BF, "rows"),
        ((rows, E), BF, "rows"),
        ((rows, E), BF, "rows"),
        ((rows, E), BF, "rows"),
        ((rows, FD), BF, "rows"),
        ((rows, FD), BF, "rows"),
        ((rows, E), BF, "rows"),
        ((rows, E), BF, "rows"),
        ((rows, PIX), BF, "rows"),
        ((images * VMAX, E), BF, "rows"),
        ((8, DS_ALL), F32, "whole"),
    ]
    scratch = [pltpu.VMEM(s, BF) for s in [(E, 3 * E), (E, E), (E, FD), (FD, E), (E, PIX)]]
    scratch += [
        pltpu.VMEM((part, E), F32),
        pltpu.VMEM((part, 3 * E), BF),
        pltpu.VMEM((images // steps, E // BS, BS * HD // E, SD), F32),
        pltpu.VMEM((part, E), F32),
        pltpu.VMEM((part, FD), BF),
        pltpu.VMEM((part, E), F32),
        pltpu.VMEM((part, PIX), F32),
        pltpu.VMEM((part, E), F32),
        pltpu.VMEM((part, E), F32),
        pltpu.VMEM((part, E), BF),
        pltpu.SemaphoreType.DMA((5,)),
    ]
    return group_call(
        decoder_kernel,
        steps,
        (tile_rows, vis_len),
        [
            (gathered, "any"),
            (vector, "whole"),
            (latent, "rows"),
            (pos_e.reshape(rows, E), "rows"),
            (ordered.reshape(rows, PIX), "rows"),
        ],
        outs,
        scratch,
        "decoder",
        4 * rows * (4 * E * E + 2 * E * FD + E * PIX),
    )


EM_BD, EM_BU = 0, D
EM_G2, EM_S2 = D + FE, 2 * D + FE
EM_BO, EM_NORM = 3 * D + FE, 4 * D + FE
EM_PROJ = 6 * D + FE
EM_ALL = EM_PROJ + E
EA_QKV, EA_G1, EA_S1, EA_EMBED, EA_ALL = 0, 3 * D, 4 * D, 5 * D, 6 * D


def encoder_mlp_back_kernel(
    row_ref, wg_ref, vec_ref, glat_ref, x1_ref, mid_ref, slope_ref,
    gdown_ref, du_ref, grad_ref, gproj_ref, sum_ref,
    w_proj, w_down, w_up, dy, sems,
):
    step = pl.program_id(0)
    ready = fetch_all(
        step == 0, row_ref, wg_ref, sems, [(T_PROJ, w_proj), (T_EDOWN, w_down), (T_EUP, w_up)]
    )

    @pl.when(step == 0)
    def _():
        sum_ref[...] = jnp.zeros_like(sum_ref)

    def vec(start):
        return vec_ref[:, start : start + D]

    sum_rows(glat_ref, sum_ref, EM_PROJ)
    ready(0)
    back_linear(glat_ref, w_proj, dy)
    d_gain, d_shift = norm_backward(x1_ref, dy, vec(V_ENORM), grad_ref, False)
    add_sum(sum_ref, EM_NORM, d_gain)
    add_sum(sum_ref, EM_NORM + D, d_shift)
    round_and_sum(grad_ref, gdown_ref, sum_ref, EM_BD)
    ready(1)
    back_up(gdown_ref, w_down, slope_ref, du_ref, sum_ref, EM_BU)
    ready(2)
    back_linear(du_ref, w_up, dy)
    d_gain, d_shift = norm_backward(mid_ref, dy, vec(ENC["g2"]), grad_ref, True)
    add_sum(sum_ref, EM_G2, d_gain)
    add_sum(sum_ref, EM_S2, d_shift)
    round_and_sum(grad_ref, gproj_ref, sum_ref, EM_BO)


def encoder_mlp_back(tile_rows, gathered, vector, glat, x1, mid, slope, steps):
    rows = x1.shape[0]
    part = rows // steps
    outs = [
        ((rows, D), BF, "rows"),
        ((rows, FE), BF, "rows"),
        ((rows, D), F32, "rows"),
        ((rows, D), BF, "rows"),
        ((8, EM_ALL), F32, "whole"),
    ]
    scratch = [pltpu.VMEM(s, BF) for s in [(D, E), (FE, D), (D, FE)]]
    scratch += [pltpu.VMEM((part, D), F32), pltpu.SemaphoreType.DMA((3,))]
    return group_call(
        encoder_mlp_back_kernel,
        steps,
        (tile_rows,),
        [
            (gathered, "any"),
            (vector, "whole"),
            (glat, "rows"),
            (x1, "rows"),
            (mid, "rows"),
            (slope, "rows"),
        ],
        outs,
        scratch,
        "encoder_mlp_back",
        2 * rows * (D * E + 2 * D * FE),
    )


def encoder_attention_back_kernel(
    row_ref, len_ref, wg_ref, vec_ref, gproj_ref, grad_in_ref, qkv_ref, lse_ref, x0_ref,
    dqkv_ref, gembed_ref, sum_ref,
    w_out, w_qkv, dy, grad, datt, sems,
):
    step = pl.program_id(0)
    images = lse_ref.shape[0]
    ready = fetch_all(step == 0, row_ref, wg_ref, sems, [(T_EOUT, w_out), (T_EQKV, w_qkv)])

    @pl.when(step == 0)
    def _():
        sum_ref[...] = jnp.zeros_like(sum_ref)

    ready(0)

    def back_out(j, cols):
        datt[:, cols] = mm_nt(gproj_ref[...], w_out[cols, :]).astype(BF)

    col_loop(D // BS, back_out)

    def attend_back(image, c):
        valid = lax.broadcasted_iota(jnp.int32, (VMAX, 1), 0) < len_ref[step * images + image]
        attention_backward(qkv_ref, datt, lse_ref, dqkv_ref, image, VMAX, D, D // HE, valid)
        return c

    lax.fori_loop(0, images, attend_back, 0)
    sum_rows(dqkv_ref, sum_ref, EA_QKV)
    ready(1)
    back_linear(dqkv_ref, w_qkv, dy)
    grad[...] = grad_in_ref[...]
    gain = vec_ref[:, ENC["g1"] : ENC["g1"] + D]
    d_gain, d_shift = norm_backward(x0_ref, dy, gain, grad, True)
    add_sum(sum_ref, EA_G1, d_gain)
    add_sum(sum_ref, EA_S1, d_shift)
    round_and_sum(grad, gembed_ref, sum_ref, EA_EMBED)


def encoder_attention_back(tile_rows, vis_len, gathered, vector, gproj, grad, qkv, lse, x0, steps):
    rows = x0.shape[0]
    part = rows // steps
    outs = [((rows, 3 * D), BF, "rows"), ((rows, D), BF, "rows"), ((8, EA_ALL), F32, "whole")]
    scratch = [pltpu.VMEM(s, BF) for s in [(D, D), (D, 3 * D)]]
    scratch += [pltpu.VMEM((part, D), F32), pltpu.VMEM((part, D), F32), pltpu.VMEM((part, D), BF)]
    return group_call(
        encoder_attention_back_kernel,
        steps,
        (tile_rows, vis_len),
        [
            (gathered, "any"),
            (vector, "whole"),
            (gproj, "rows"),
            (grad, "rows"),
            (qkv, "rows"),
            (lse, "rows"),
            (x0, "rows"),
        ],
        outs,
        scratch + [pltpu.SemaphoreType.DMA((2,))],
        "encoder_attention_back",
        2 * rows * 4 * D * D,
    )


def weight_grad_kernel(parts, cut, extra, index_ref, x_ref, g_ref, *refs):
    outs = refs[extra : extra + min(parts, 2)]
    x_t, total = refs[-2:]
    row_tiles, col_tiles = x_ref.shape[1] // BS, g_ref.shape[1] // BS

    @pl.when(pl.program_id(1) == 0)
    def _():
        x_t[...] = x_ref[...].T

    total[...] = mm(x_t[...], g_ref[...])
    for p in range(parts):
        for i in range(row_tiles):
            start = pl.multiple_of(i * BS + (p ^ index_ref[0]) * cut, cut)
            for j in range(col_tiles):
                got = total[pl.ds(start, cut), j * BS : (j + 1) * BS]
                outs[p % 2][p // 2, i * col_tiles + j] = got.astype(BF)


def weight_grad(index, parts, count, first, x, g, block, buffers):
    cut = BS // parts
    rows, width = x.shape
    row_tiles, col_tiles = block
    size = row_tiles * col_tiles
    across = g.shape[1] // (col_tiles * BS)
    assert first % size == 0
    held = min(parts, 2)
    shape = jax.ShapeDtypeStruct((parts // held, count, cut, BS), BF)
    given = list(buffers or [])
    out_spec = pl.BlockSpec(
        (parts // held, size, cut, BS), lambda i, j, *_: (0, first // size + i * across + j, 0, 0)
    )
    return pl.pallas_call(
        functools.partial(weight_grad_kernel, parts, cut, len(given)),
        grid_spec=pltpu.PrefetchScalarGridSpec(
            num_scalar_prefetch=1,
            grid=(width // (row_tiles * BS), across),
            in_specs=[
                pl.BlockSpec((rows, row_tiles * BS), lambda i, j, *_: (0, i)),
                pl.BlockSpec((rows, col_tiles * BS), lambda i, j, *_: (0, j)),
            ]
            + [pl.BlockSpec(memory_space=pl.ANY)] * len(given),
            out_specs=[out_spec] * held,
            scratch_shapes=[
                pltpu.VMEM((row_tiles * BS, rows), BF),
                pltpu.VMEM((row_tiles * BS, col_tiles * BS), F32),
            ],
        ),
        out_shape=[shape] * held,
        input_output_aliases={3 + i: i for i in range(len(given))},
        compiler_params=pltpu.CompilerParams(vmem_limit_bytes=VMEM_LIMIT),
        cost_estimate=pl.CostEstimate(
            flops=2 * rows * width * g.shape[1],
            bytes_accessed=2 * rows * (width + g.shape[1]) + 2 * width * g.shape[1],
            transcendentals=0,
        ),
        name="weight_grad",
    )(index, x, g, *given)


def seed_kernel(parts, index_ref, vec_ref, *outs):
    at = pl.program_id(0)
    for p in range(parts):
        got = vec_ref[p ^ index_ref[0]]
        outs[p % 2][p // 2, 0] = jnp.where(at == 0, got, 0.0).astype(BF)


def seed_buffers(index, parts, count, first, vector_tile):
    cut = BS // parts
    held = min(parts, 2)
    shape = jax.ShapeDtypeStruct((parts // held, count, cut, BS), BF)
    return pl.pallas_call(
        functools.partial(seed_kernel, parts),
        grid_spec=pltpu.PrefetchScalarGridSpec(
            num_scalar_prefetch=1,
            grid=(count - first,),
            in_specs=[pl.BlockSpec(vector_tile.shape, lambda i, *_: (0, 0, 0))],
            out_specs=[pl.BlockSpec((parts // held, 1, cut, BS), lambda i, *_: (0, first + i, 0, 0))] * held,
        ),
        out_shape=[shape] * held,
        name="seed_buffers",
    )(index, vector_tile)


def low_sum(a, b):
    return (a.astype(F32) + b.astype(F32)).astype(BF)


def swap_bit(x, bit, size):
    return lax.ppermute(x, "dp", [(i, i ^ (1 << bit)) for i in range(size)])


def reduce_core(buffers, parts):
    if parts == 1:
        return [buffers[0][0]] * 2, []
    whole = low_sum(buffers[0], swap_bit(buffers[1], 0, parts))
    bits = list(range(parts.bit_length() - 2, 0, -1))
    whole = whole.reshape((2,) * len(bits) + whole.shape[1:])
    count = whole.shape[-3]
    return [whole[..., : count // 2, :, :], whole[..., count // 2 :, :, :]], [bits, bits]


def reduce_chips(state, parts, steps):
    halves, left = list(state[0]), list(state[1])
    for half in range(2 if parts > 1 else 0):
        for _ in range(min(steps, len(left[half]))):
            bit = left[half][-1 if half == 0 else 0]
            axis = left[half].index(bit)
            keep = lax.index_in_dim(halves[half], 0, axis, keepdims=False)
            send = lax.index_in_dim(halves[half], 1, axis, keepdims=False)
            halves[half] = low_sum(keep, swap_bit(send, bit, parts))
            left[half] = [b for b in left[half] if b != bit]
    return halves, left


def reduce_end(state, parts, groups):
    halves, _ = reduce_chips(state, parts, 99)
    whole = jnp.concatenate(halves, axis=0) if parts > 1 else halves[0]
    return reduce_patch(whole, groups)


def shift_patch(x, shift, size):
    return lax.ppermute(x, "patch", [(i, (i + shift) % size) for i in range(size)])


def reduce_patch(x, groups):
    if groups == 1:
        return x
    me = lax.axis_index("patch")
    pieces = x.reshape((groups, x.shape[0] // groups) + x.shape[1:])
    total = lax.dynamic_index_in_dim(pieces, me, 0, keepdims=False).astype(F32)
    for k in range(1, groups):
        piece = lax.dynamic_index_in_dim(pieces, (me + k) % groups, 0, keepdims=False)
        total = total + shift_patch(piece, k, groups).astype(F32)
    total = total.astype(BF)
    return jnp.concatenate([total] + [shift_patch(total, k, groups) for k in range(1, groups)], axis=0)


def place_after(position, count, groups):
    if groups == 1:
        return position
    size = count // groups
    me = lax.axis_index("patch")
    return (me - position // size) % groups * size + position % size


def sum_all(x, parts, groups):
    for bit in range(groups.bit_length() - 1):
        x = x + lax.ppermute(x, "patch", [(i, i ^ (1 << bit)) for i in range(groups)])
    return sum_dp(x, parts)


def sum_dp(x, parts):
    for bit in range(parts.bit_length() - 1):
        x = x + swap_bit(x, bit, parts)
    return x


def split_low(x):
    high = x.astype(BF)
    return high, (x - high.astype(F32)).astype(BF)


def tile_kernel(
    scale_ref, grad_ref, w_ref, left_stat_ref, right_stat_ref, left_root_ref, right_root_ref,
    clipped_ref, left_new_ref, right_new_ref, w_new_ref,
):
    scale = scale_ref[0]
    for t in range(w_ref.shape[0]):
        grad = grad_ref[:, t].reshape(BS, BS)
        clipped_ref[t] = grad.astype(F32) * scale
        square = (1.0 - BETA_STAT) * scale * scale
        left_new_ref[t] = BETA_STAT * left_stat_ref[t] + square * mm_nt(grad, grad)
        right_new_ref[t] = BETA_STAT * right_stat_ref[t] + square * mm_tn(grad, grad)
        high, low = split_low(left_root_ref[t])
        half = (mm(high, grad) + mm(low, grad)) * scale
        half_high, half_low = split_low(half)
        high, low = split_low(right_root_ref[t])
        direction = mm(half_high, high) + (mm(half_high, low) + mm(half_low, high))
        direction = direction * lax.rsqrt(jnp.mean(direction * direction) + EPS_ROOT)
        w_new_ref[t] = w_ref[t] - RATE_MATRIX * (direction + DECAY_MATRIX * w_ref[t])


def tile_update(scale, grads, states):
    parts, slots, cut, _ = grads.shape
    per = 2 if slots % 2 == 0 else 1
    tile = pl.BlockSpec((per, BS, BS), lambda i, *_: (i, 0, 0))
    return pl.pallas_call(
        tile_kernel,
        grid_spec=pltpu.PrefetchScalarGridSpec(
            num_scalar_prefetch=1,
            grid=(slots // per,),
            in_specs=[pl.BlockSpec((parts, per, cut, BS), lambda i, *_: (0, i, 0, 0))] + [tile] * 5,
            out_specs=[tile] * 4,
        ),
        out_shape=[jax.ShapeDtypeStruct((slots, BS, BS), F32)] * 4,
        compiler_params=pltpu.CompilerParams(vmem_limit_bytes=VMEM_LIMIT),
        name="tile_update",
    )(scale.reshape(1), grads, *states)


def vector_update(clipped, vectors, moment, second):
    moment_new = BETA_FIRST * moment + (1.0 - BETA_FIRST) * clipped
    second_new = BETA_SECOND * second + (1.0 - BETA_SECOND) * clipped * clipped
    corrected = moment_new / (1.0 - BETA_FIRST**STEP)
    scaled = second_new / (1.0 - BETA_SECOND**STEP)
    vectors_new = vectors - RATE_VECTOR * corrected / (jnp.sqrt(scaled) + EPS_ADAM)
    return moment_new, second_new, vectors_new


CHUNKS = [
    [
        (T_DUP, 2, 8, (2, 4)),
        (T_DDOWN, 8, 2, (4, 2)),
        (T_DOUT, 2, 2, (2, 2)),
        (T_DQKV, 2, 6, (2, 3)),
        (T_HEAD, 2, 3, (2, 3)),
        (T_PROJ, 3, 2, (3, 2)),
    ],
    [(T_EUP, 3, 12, (3, 4)), (T_EDOWN, 12, 3, (4, 3)), (T_EOUT, 3, 3, (3, 3))],
    [(T_EQKV, 3, 9, (3, 3)), (T_EMBED, 3, 3, (3, 3))],
]


def chunk_sizes(groups):
    unit = max(2, groups)
    sizes = []
    for i, chunk in enumerate(CHUNKS):
        used = sum(r * c for _, r, c, _ in chunk) + (2 if i == len(CHUNKS) - 1 else 0)
        sizes.append(-(-used // unit) * unit)
    return sizes


def tile_places(sizes):
    chunk_of = np.zeros(NBLK + 2, np.int32)
    place_of = np.zeros(NBLK + 2, np.int32)
    for i, chunk in enumerate(CHUNKS):
        at = 0
        for first, row_tiles, col_tiles, (high, wide) in chunk:
            for r in range(row_tiles):
                for c in range(col_tiles):
                    block = r // high * (col_tiles // wide) + c // wide
                    chunk_of[first + r * col_tiles + c] = i
                    place_of[first + r * col_tiles + c] = at + block * high * wide + r % high * wide + c % wide
            at += row_tiles * col_tiles
    chunk_of[NBLK:] = len(CHUNKS) - 1
    place_of[NBLK + 1] = at
    place_of[NBLK] = at + 1
    return chunk_of, place_of


def shards(parts, groups, pixels, shuffle, vis_len, block_owner, weights, vectors, vec_moment, vec_second,
           left_stat, right_stat, left_root, right_root):
    slots = weights.shape[0]
    own = vectors.shape[0]
    index = lax.axis_index("dp").astype(jnp.int32).reshape(1)
    images = pixels.shape[0]

    vector_rows = -(-own // (16 * BS)) * 16
    mine = jnp.concatenate(
        [
            weights.astype(BF).reshape(slots * BS, BS),
            jnp.pad(vectors.astype(BF), (0, vector_rows * BS - own)).reshape(vector_rows, BS),
        ]
    )
    gathered = lax.all_gather(mine, "dp", axis=0, tiled=True)
    stride = mine.shape[0]
    slot_index = jnp.arange(block_owner.shape[0], dtype=jnp.int32)
    slot_of_block = jnp.sum(
        jnp.where(block_owner[None, :] == jnp.arange(NBLK, dtype=jnp.int32)[:, None], slot_index[None, :], 0),
        axis=1,
    )
    tile_rows = slot_of_block // slots * stride + slot_of_block % slots * BS
    vector = gathered.reshape(parts, stride, BS)[:, slots * BS :].reshape(parts, vector_rows * BS)
    vector = vector[:, :own].reshape(-1).astype(F32)
    enc_key, dec_key = 4 * D, 4 * D + (8 * D + FE - 3 * D) + 2 * D + 2 * E + 3 * E
    vector = jnp.concatenate(
        [vector[:enc_key], jnp.zeros(D, F32), vector[enc_key:dec_key], jnp.zeros(E, F32), vector[dec_key:]]
    ).reshape(1, V_ALL)

    ordered, visible_pix, pos_d, pos_e = order_patches(pixels, shuffle)
    (x0, h1, qkv, lse, att, mid, h2, act, slope, x1, hn, latent) = encoder_forward(
        tile_rows, vis_len, gathered, vector, visible_pix, pos_d, 2
    )
    (d_h1, d_dqkv, d_att, d_gproj, d_h2, d_du, d_act, d_gdown, d_hn, d_gpred, glat, d_sums) = decoder(
        tile_rows, vis_len, gathered, vector, latent, pos_e, ordered, 4
    )
    sizes = chunk_sizes(groups)
    chunk_of, place_of = tile_places(sizes)

    rows_cut = BS // parts

    def gradients(chunk, pairs, vector_tile=None):
        used = sum(r * c for _, r, c, _ in CHUNKS[chunk])
        at, buffers = 0, None
        if sizes[chunk] > used:
            if vector_tile is None:
                vector_tile = jnp.zeros((parts, rows_cut, BS), F32)
            buffers = seed_buffers(index, parts, sizes[chunk], used, vector_tile)
        for (x, g), (_, row_tiles, col_tiles, block) in zip(pairs, CHUNKS[chunk]):
            buffers = weight_grad(index, parts, sizes[chunk], at, x, g, block, buffers)
            at += row_tiles * col_tiles
        return buffers

    buffers0 = gradients(
        0, [(d_h2, d_du), (d_act, d_gdown), (d_att, d_gproj), (d_h1, d_dqkv), (d_hn, d_gpred), (hn, glat)]
    )
    glat, buffers0 = lax.optimization_barrier((glat, buffers0))
    gdown, du, grad_mid, gproj, m_sums = encoder_mlp_back(tile_rows, gathered, vector, glat, x1, mid, slope, 2)
    state0 = reduce_core(buffers0, parts)
    gdown, du, gproj, halves = lax.optimization_barrier((gdown, du, gproj, state0[0]))
    state0 = (halves, state0[1])
    buffers1 = gradients(1, [(h2, du), (act, gdown), (att, gproj)])
    state0 = reduce_chips(state0, parts, 1)
    gproj, buffers1 = lax.optimization_barrier((gproj, buffers1))
    dqkv, gembed, a_sums = encoder_attention_back(
        tile_rows, vis_len, gathered, vector, gproj, grad_mid, qkv, lse, x0, 2
    )
    state1 = reduce_core(buffers1, parts)
    dqkv, gembed, halves0, halves1 = lax.optimization_barrier((dqkv, gembed, state0[0], state1[0]))
    state0, state1 = (halves0, state0[1]), (halves1, state1[1])

    d_sums, m_sums, a_sums = (jnp.sum(s, axis=0) for s in (d_sums, m_sums, a_sums))

    def cut(sums, start, size):
        return sums[start : start + size]

    grad_vector = jnp.concatenate(
        [
            cut(a_sums, EA_EMBED, D),
            cut(a_sums, EA_G1, 2 * D),
            cut(a_sums, EA_QKV, D),
            cut(a_sums, EA_QKV + 2 * D, D),
            cut(m_sums, EM_BO, D),
            cut(m_sums, EM_G2, 2 * D),
            cut(m_sums, EM_BU, FE),
            cut(m_sums, EM_BD, D),
            cut(m_sums, EM_NORM, 2 * D),
            cut(m_sums, EM_PROJ, E),
            cut(d_sums, DS_MASK, E),
            cut(d_sums, DS["g1"], 2 * E),
            cut(d_sums, DS["bqkv"], E),
            cut(d_sums, DS["bqkv"] + 2 * E, E),
            cut(d_sums, DS["bo"], E),
            cut(d_sums, DS["g2"], 2 * E),
            cut(d_sums, DS["bu"], FD),
            cut(d_sums, DS["bd"], E),
            cut(d_sums, DS_NORM, 2 * E),
            cut(d_sums, DS_HEAD, PIX),
        ]
    )
    vector_tile = jnp.pad(grad_vector.reshape(parts, own), ((0, 0), (0, rows_cut * BS - own)))
    vector_tile = vector_tile.reshape(parts, rows_cut, BS)
    buffers2 = gradients(2, [(h1, dqkv), (visible_pix.reshape(-1, PIX), gembed)], vector_tile)
    first = reduce_end(state0, parts, groups)
    second = reduce_end(state1, parts, groups)
    third = reduce_end(reduce_core(buffers2, parts), parts, groups)

    reduced = jnp.concatenate([first, second, third], axis=0)
    starts = np.cumsum([0] + sizes)
    where = jnp.zeros(NBLK + 2, jnp.int32)
    for i, size in enumerate(sizes):
        here = starts[i] + place_after(jnp.asarray(place_of), size, groups)
        where = jnp.where(jnp.asarray(chunk_of == i), here, where)
    wide = reduced.astype(F32)
    squares = sum_dp(jnp.sum(wide * wide), parts)
    totals = jnp.stack([jnp.sum(cut(d_sums, DS_LOSS, PIX)) / PIX, jnp.sum(POS - vis_len).astype(F32)])
    totals = sum_all(totals, parts, groups)
    loss_sum, masked_count = totals[0], totals[1]
    grad_norm = jnp.sqrt(squares) / masked_count
    scale = jnp.minimum(1.0, CLIP_NORM / grad_norm) / masked_count

    slot_rows = reduced[where[jnp.minimum(block_owner, NBLK)]]
    if parts > 1:
        slot_rows = lax.all_to_all(slot_rows, "dp", 0, 0, tiled=True)
    grads = slot_rows.reshape(parts, slots, rows_cut, BS)
    clipped, left_new, right_new, weights_new = tile_update(
        scale, grads, (weights, left_stat, right_stat, left_root, right_root)
    )
    own_vector = lax.dynamic_index_in_dim(reduced, where[NBLK + 1], 0, keepdims=False)
    own_vector = own_vector.reshape(-1)[:own].astype(F32) * scale
    moment_new, second_new, vectors_new = vector_update(own_vector, vectors, vec_moment, vec_second)
    return (
        loss_sum,
        masked_count,
        grad_norm,
        clipped,
        left_new,
        right_new,
        weights_new,
        moment_new,
        second_new,
        vectors_new,
    )


def solution(mesh):
    both = ("dp", "patch")
    tiles = P("dp", None, None)
    return jax.shard_map(
        functools.partial(shards, mesh.shape["dp"], mesh.shape["patch"]),
        mesh=mesh,
        in_specs=(P(both, None, None), P(both, None), P(both), P())
        + (tiles, P("dp"), P("dp"), P("dp"))
        + (tiles,) * 4,
        out_specs=(P(), P(), P()) + (tiles,) * 4 + (P("dp"),) * 3,
        check_vma=False,
    )
```

```python
import functools
import math

import jax
import jax.numpy as jnp
import numpy as np
from jax import lax
from jax.experimental import pallas as pl
from jax.experimental.pallas import tpu as pltpu
from jax.sharding import PartitionSpec as P

D = 768
HE = 12
FE = 3072
E = 512
HD = 16
FD = 2048
PIX = 768
POS = 196
VMAX = 80
BS = 256
STEP = 10
NBLK = 177

SD = 208

EPS_NORM = 1e-06
EPS_ROOT = 1e-06
EPS_ADAM = 1e-08
CLIP_NORM = 0.01
RATE_MATRIX = 0.03
DECAY_MATRIX = 0.05
BETA_STAT = 0.5
BETA_FIRST = 0.9
BETA_SECOND = 0.999
RATE_VECTOR = 0.1
NEG_LARGE = -1e30
LOG2E = math.log2(math.e)

BF = jnp.bfloat16
F32 = jnp.float32
VMEM_LIMIT = 60 * 1024 * 1024

T_EMBED, T_EQKV, T_EOUT, T_EUP, T_EDOWN, T_PROJ = 0, 9, 36, 45, 81, 117
T_DQKV, T_DOUT, T_DUP, T_DDOWN, T_HEAD = 123, 135, 139, 155, 171

V_EMBED = 0
V_ENC = D
V_ENORM = V_ENC + 9 * D + FE
V_PROJ = V_ENORM + 2 * D
V_MASK = V_PROJ + E
V_DEC = V_MASK + E
V_DNORM = V_DEC + 9 * E + FD
V_HEAD = V_DNORM + 2 * E
V_ALL = V_HEAD + PIX


def layer_offsets(start, width, hidden):
    names = ["g1", "s1", "bqkv", "bo", "g2", "s2", "bu", "bd"]
    sizes = [width, width, 3 * width, width, width, width, hidden, width]
    offsets = {}
    for name, size in zip(names, sizes):
        offsets[name] = start
        start += size
    return offsets


def mm(a, b):
    return jnp.dot(a, b, preferred_element_type=F32)


def mm_nt(a, b):
    return lax.dot_general(a, b, (((1,), (1,)), ((), ())), preferred_element_type=F32)


def mm_tn(a, b):
    return lax.dot_general(a, b, (((0,), (0,)), ((), ())), preferred_element_type=F32)


def fold8(x):
    rows, cols = x.shape
    return jnp.sum(x.reshape(rows // 8, 8, cols), axis=0)


def gelu_pair(u):
    t = 1.0 / (1.0 + (0.3275911 * math.sqrt(0.5)) * jnp.abs(u))
    e = jnp.exp2((-0.5 * LOG2E) * (u * u))
    poly = t * (
        0.5 * 0.254829592
        + t * (-0.5 * 0.284496736 + t * (0.5 * 1.421413741 + t * (-0.5 * 1.453152027 + t * (0.5 * 1.061405429))))
    )
    tail = poly * e
    phi = jnp.where(u >= 0, 1.0 - tail, tail)
    return u * phi, phi + u * (e * (1.0 / math.sqrt(2.0 * math.pi)))


def norm_parts(x):
    centred = x - jnp.mean(x, axis=-1, keepdims=True)
    inverse = lax.rsqrt(jnp.mean(centred * centred, axis=-1, keepdims=True) + EPS_NORM)
    return centred * inverse, inverse


def loop(lower, upper, body, carry, most=26):
    count = upper - lower
    unroll = max(u for u in range(1, min(most, count) + 1) if count % u == 0)
    return lax.fori_loop(lower, upper, body, carry, unroll=unroll)


def row_loop(rows, step, body, carry=0):
    count = rows // step

    def one(i, c):
        return body(pl.ds(pl.multiple_of(i * step, step), step), c)

    return loop(0, count, one, carry)


def norm_forward(x_ref, gain, shift, out_ref):
    def body(sl, c):
        normed, _ = norm_parts(x_ref[sl, :])
        out_ref[sl, :] = (normed * gain + shift).astype(BF)
        return c

    row_loop(x_ref.shape[0], 16, body)


def norm_backward(x_ref, dy_ref, gain, out_ref, add):
    width = x_ref.shape[1]

    def body(sl, c):
        d_gain, d_shift = c
        normed, inverse = norm_parts(x_ref[sl, :])
        dy = dy_ref[sl, :]
        dn = dy * gain
        mean_one = jnp.mean(dn, axis=-1, keepdims=True)
        mean_two = jnp.mean(dn * normed, axis=-1, keepdims=True)
        dx = inverse * (dn - mean_one - normed * mean_two)
        out_ref[sl, :] = out_ref[sl, :] + dx if add else dx
        return (d_gain + fold8(dy * normed), d_shift + fold8(dy))

    zero = jnp.zeros((8, width), F32)
    return row_loop(x_ref.shape[0], 16, body, (zero, zero))


def col_loop(count, body):
    def one(j, c):
        body(j, pl.ds(pl.multiple_of(j * BS, BS), BS))
        return c

    loop(0, count, one, 0, 4)


def vec_at(vec_ref, start, j):
    return vec_ref[:, pl.ds(pl.multiple_of(start + j * BS, BS), BS)]


def head_mask(head, head_size):
    lane = lax.broadcasted_iota(jnp.int32, (1, BS), 1)
    inside = (lane >= head * head_size) & (lane < (head + 1) * head_size)
    return jnp.where(inside, 1.0, 0.0).astype(BF)


def scores_of(k_masked, q, head_size, valid):
    scores = mm_nt(k_masked, q) * (head_size**-0.5 * LOG2E)
    return jnp.where(valid, scores, NEG_LARGE)


def attention_forward(qkv_ref, att_ref, lse_ref, image, seq, width, head_size, valid):
    rows = pl.ds(pl.multiple_of(image * seq, 16), seq)
    per = BS // head_size

    def group(g, c):
        def part(which):
            return qkv_ref[rows, pl.ds(pl.multiple_of(which * width + g * BS, BS), BS)]

        q, k, v = part(0), part(1), part(2)
        v_t = v.T
        outs, logs = [], []
        for h in range(per):
            scores = scores_of(k * head_mask(h, head_size), q, head_size, valid)
            top = jnp.max(scores, axis=0, keepdims=True)
            e = jnp.exp2(scores - top)
            total = jnp.sum(e, axis=0, keepdims=True)
            out = mm(v_t[h * head_size : (h + 1) * head_size, :], e.astype(BF))
            outs.append(out * (1.0 / total))
            logs.append(top + jnp.log2(total))
        att_ref[rows, pl.ds(pl.multiple_of(g * BS, BS), BS)] = jnp.concatenate(outs, axis=0).T.astype(BF)
        lse_ref[image, g] = jnp.concatenate(logs, axis=0)
        return c

    loop(0, width // BS, group, 0)


def attention_backward(qkv_ref, datt_ref, lse_ref, dqkv_ref, image, seq, width, head_size, valid):
    rows = pl.ds(pl.multiple_of(image * seq, 16), seq)
    per = BS // head_size
    scale = head_size**-0.5

    def group(g, c):
        def cols(which):
            return pl.ds(pl.multiple_of(which * width + g * BS, BS), BS)

        q, k, v = qkv_ref[rows, cols(0)], qkv_ref[rows, cols(1)], qkv_ref[rows, cols(2)]
        d_out = datt_ref[rows, cols(0)]
        lse = lse_ref[image, g]
        q_t, k_t, d_out_t = q.T, k.T, d_out.T
        d_q, d_k, d_v = [], [], []
        for h in range(per):
            mask = head_mask(h, head_size)
            part = slice(h * head_size, (h + 1) * head_size)
            probs = jnp.exp2(scores_of(k * mask, q, head_size, valid) - lse[h : h + 1, :])
            d_probs = mm_nt(v * mask, d_out)
            delta = jnp.sum(probs * d_probs, axis=0, keepdims=True)
            d_scores = (probs * (d_probs - delta)).astype(BF)
            d_v.append(mm_nt(d_out_t[part, :], probs.astype(BF)))
            d_k.append(mm_nt(q_t[part, :], d_scores))
            d_q.append(mm(k_t[part, :], d_scores))
        dqkv_ref[rows, cols(0)] = (jnp.concatenate(d_q, axis=0).T * scale).astype(BF)
        dqkv_ref[rows, cols(1)] = (jnp.concatenate(d_k, axis=0).T * scale).astype(BF)
        dqkv_ref[rows, cols(2)] = jnp.concatenate(d_v, axis=0).T.astype(BF)
        return c

    loop(0, width // BS, group, 0)


def fetch_tiles(row_ref, wg_ref, first, dst, sem):
    row_tiles, col_tiles = dst.shape[0] // BS, dst.shape[1] // BS
    for i in range(row_tiles):
        for j in range(col_tiles):
            start = pl.multiple_of(row_ref[first + i * col_tiles + j], 16)
            pltpu.make_async_copy(
                wg_ref.at[pl.ds(start, BS), :],
                dst.at[i * BS : (i + 1) * BS, j * BS : (j + 1) * BS],
                sem,
            ).start()


def await_tiles(dst, sem):
    pltpu.make_async_copy(dst, dst, sem).wait()


def fetch_all(first_step, row_ref, wg_ref, sems, matrices):
    @pl.when(first_step)
    def _():
        for i, (first, dst) in enumerate(matrices):
            fetch_tiles(row_ref, wg_ref, first, dst, sems.at[i])

    def ready(i):
        @pl.when(first_step)
        def _():
            await_tiles(matrices[i][1], sems.at[i])

    return ready


def qkv_forward(h_ref, w_ref, vec_ref, start, out_ref):
    def body(j, cols):
        out_ref[:, cols] = (mm(h_ref[...], w_ref[:, cols]) + vec_at(vec_ref, start, j)).astype(BF)

    col_loop(w_ref.shape[1] // BS, body)


def add_linear(x_ref, h_ref, w_ref, vec_ref, start, out_ref):
    def body(j, cols):
        out_ref[:, cols] = x_ref[:, cols] + (mm(h_ref[...], w_ref[:, cols]) + vec_at(vec_ref, start, j))

    col_loop(w_ref.shape[1] // BS, body)


def up_forward(h_ref, w_ref, vec_ref, start, act_ref, slope_ref):
    def body(j, cols):
        act, slope = gelu_pair(mm(h_ref[...], w_ref[:, cols]) + vec_at(vec_ref, start, j))
        act_ref[:, cols] = act.astype(BF)
        slope_ref[:, cols] = slope.astype(BF)

    col_loop(w_ref.shape[1] // BS, body)


def back_linear(g_ref, w_ref, out_ref):
    def body(j, cols):
        out_ref[:, cols] = mm_nt(g_ref[...], w_ref[cols, :])

    col_loop(w_ref.shape[0] // BS, body)


def back_up(g_ref, w_ref, slope_ref, du_ref, sum_ref, start):
    def body(j, cols):
        du = (mm_nt(g_ref[...], w_ref[cols, :]) * slope_ref[:, cols].astype(F32)).astype(BF)
        du_ref[:, cols] = du
        at = pl.ds(pl.multiple_of(start + j * BS, BS), BS)
        sum_ref[:, at] = sum_ref[:, at] + fold8(du.astype(F32))

    col_loop(w_ref.shape[0] // BS, body)


def round_and_sum(x_ref, out_ref, sum_ref, start):
    width = x_ref.shape[1]

    def body(sl, c):
        low = x_ref[sl, :].astype(BF)
        out_ref[sl, :] = low
        return c + fold8(low.astype(F32))

    total = row_loop(x_ref.shape[0], 16, body, jnp.zeros((8, width), F32))
    sum_ref[:, start : start + width] = sum_ref[:, start : start + width] + total


def sum_rows(x_ref, sum_ref, start):
    width = x_ref.shape[1]

    def body(sl, c):
        return c + fold8(x_ref[sl, :].astype(F32))

    total = row_loop(x_ref.shape[0], 16, body, jnp.zeros((8, width), F32))
    sum_ref[:, start : start + width] = sum_ref[:, start : start + width] + total


def add_sum(sum_ref, start, value):
    stop = start + value.shape[1]
    sum_ref[:, start:stop] = sum_ref[:, start:stop] + value


def order_kernel(shuffle_ref, pixels_ref, sin_d_ref, sin_e_ref, all_ref, visible_ref, pos_d_ref, pos_e_ref):
    ids = shuffle_ref[0]
    pick = jnp.where(ids == lax.broadcasted_iota(jnp.int32, (SD, POS), 1), 1.0, 0.0).astype(BF)
    ordered = mm(pick, pixels_ref[0]).astype(BF)
    all_ref[0] = ordered
    visible_ref[0] = ordered[:VMAX, :]
    few = pick[:VMAX, :]
    pos_d_ref[0] = mm(few, sin_d_ref[0]) + mm(few, sin_d_ref[1])
    pos_e_ref[0] = mm(pick, sin_e_ref[0]) + mm(pick, sin_e_ref[1])


def sinusoid_parts(count, width):
    half = width // 2
    frequency = np.exp(np.arange(half) * (-np.log(10000.0) / half))
    angles = np.arange(count)[:, None] * frequency[None, :]
    table = np.concatenate([np.sin(angles), np.cos(angles)], axis=1).astype(np.float32)
    high = table.astype(jnp.bfloat16)
    low = (table - high.astype(np.float32)).astype(jnp.bfloat16)
    return np.stack([high, low])


def order_patches(pixels, shuffle):
    images = pixels.shape[0]
    ids = jnp.pad(shuffle, ((0, 0), (0, SD - POS)), constant_values=-1)[:, :, None]

    def image(*dims):
        return pl.BlockSpec((1,) + dims, lambda b: (b,) + (0,) * len(dims))

    def whole(*dims):
        return pl.BlockSpec(dims, lambda b: (0,) * len(dims))

    return pl.pallas_call(
        order_kernel,
        grid=(images,),
        in_specs=[image(SD, 1), image(POS, PIX), whole(2, POS, D), whole(2, POS, E)],
        out_specs=[image(SD, PIX), image(VMAX, PIX), image(VMAX, D), image(SD, E)],
        out_shape=[
            jax.ShapeDtypeStruct((images, SD, PIX), BF),
            jax.ShapeDtypeStruct((images, VMAX, PIX), BF),
            jax.ShapeDtypeStruct((images, VMAX, D), F32),
            jax.ShapeDtypeStruct((images, SD, E), F32),
        ],
        compiler_params=pltpu.CompilerParams(vmem_limit_bytes=VMEM_LIMIT),
        name="order_patches",
    )(ids, pixels, jnp.asarray(sinusoid_parts(POS, D)), jnp.asarray(sinusoid_parts(POS, E)))


def group_call(kernel, steps, prefetch, in_arrays, out_list, scratch, name, flops):
    def spec(shape, kind):
        if kind == "any":
            return pl.BlockSpec(memory_space=pl.ANY)
        if kind == "rows":
            block = (shape[0] // steps,) + tuple(shape[1:])
            return pl.BlockSpec(block, lambda i, *_: (i,) + (0,) * (len(shape) - 1))
        return pl.BlockSpec(tuple(shape), lambda i, *_: (0,) * len(shape))

    return pl.pallas_call(
        kernel,
        grid_spec=pltpu.PrefetchScalarGridSpec(
            num_scalar_prefetch=len(prefetch),
            grid=(steps,),
            in_specs=[spec(a.shape, kind) for a, kind in in_arrays],
            out_specs=[spec(shape, kind) for shape, _, kind in out_list],
            scratch_shapes=scratch,
        ),
        out_shape=[jax.ShapeDtypeStruct(shape, dtype) for shape, dtype, _ in out_list],
        compiler_params=pltpu.CompilerParams(
            vmem_limit_bytes=VMEM_LIMIT, dimension_semantics=("arbitrary",)
        ),
        cost_estimate=pl.CostEstimate(
            flops=flops,
            bytes_accessed=sum(math.prod(s) * jnp.dtype(t).itemsize for s, t, _ in out_list) * 2,
            transcendentals=0,
        ),
        name=name,
    )(*prefetch, *[a for a, _ in in_arrays])


ENC = layer_offsets(V_ENC, D, FE)
DEC = layer_offsets(V_DEC, E, FD)


def encoder_forward_kernel(
    row_ref, len_ref, wg_ref, vec_ref, pix_ref, pos_ref,
    x0_ref, h1_ref, qkv_ref, lse_ref, att_ref, mid_ref, h2_ref, act_ref, slope_ref, x1_ref, hn_ref, latent_ref,
    w_embed, w_qkv, w_out, w_up, w_down, w_proj, sems,
):
    step = pl.program_id(0)
    images = lse_ref.shape[0]
    ready = fetch_all(
        step == 0,
        row_ref,
        wg_ref,
        sems,
        [
            (T_EMBED, w_embed),
            (T_EQKV, w_qkv),
            (T_EOUT, w_out),
            (T_EUP, w_up),
            (T_EDOWN, w_down),
            (T_PROJ, w_proj),
        ],
    )

    def vec(start, size=D):
        return vec_ref[:, start : start + size]

    ready(0)
    add_linear(pos_ref, pix_ref, w_embed, vec_ref, V_EMBED, x0_ref)
    norm_forward(x0_ref, vec(ENC["g1"]), vec(ENC["s1"]), h1_ref)
    ready(1)
    qkv_forward(h1_ref, w_qkv, vec_ref, ENC["bqkv"], qkv_ref)

    def one(image, c):
        valid = lax.broadcasted_iota(jnp.int32, (VMAX, 1), 0) < len_ref[step * images + image]
        attention_forward(qkv_ref, att_ref, lse_ref, image, VMAX, D, D // HE, valid)
        return c

    lax.fori_loop(0, images, one, 0)
    ready(2)
    add_linear(x0_ref, att_ref, w_out, vec_ref, ENC["bo"], mid_ref)
    norm_forward(mid_ref, vec(ENC["g2"]), vec(ENC["s2"]), h2_ref)
    ready(3)
    up_forward(h2_ref, w_up, vec_ref, ENC["bu"], act_ref, slope_ref)
    ready(4)
    add_linear(mid_ref, act_ref, w_down, vec_ref, ENC["bd"], x1_ref)
    norm_forward(x1_ref, vec(V_ENORM), vec(V_ENORM + D), hn_ref)
    ready(5)

    def project(j, cols):
        latent_ref[:, cols] = mm(hn_ref[...], w_proj[:, cols]) + vec_at(vec_ref, V_PROJ, j)

    col_loop(E // BS, project)


def encoder_forward(tile_rows, vis_len, gathered, vector, visible_pix, pos_d, steps):
    images = vis_len.shape[0]
    rows = images * VMAX
    outs = [
        ((rows, D), F32, "rows"),
        ((rows, D), BF, "rows"),
        ((rows, 3 * D), BF, "rows"),
        ((images, D // BS, BS * HE // D, VMAX), F32, "rows"),
        ((rows, D), BF, "rows"),
        ((rows, D), F32, "rows"),
        ((rows, D), BF, "rows"),
        ((rows, FE), BF, "rows"),
        ((rows, FE), BF, "rows"),
        ((rows, D), F32, "rows"),
        ((rows, D), BF, "rows"),
        ((rows, E), F32, "rows"),
    ]
    scratch = [pltpu.VMEM(s, BF) for s in [(PIX, D), (D, 3 * D), (D, D), (D, FE), (FE, D), (D, E)]]
    return group_call(
        encoder_forward_kernel,
        steps,
        (tile_rows, vis_len),
        [
            (gathered, "any"),
            (vector, "whole"),
            (visible_pix.reshape(rows, PIX), "rows"),
            (pos_d.reshape(rows, D), "rows"),
        ],
        outs,
        scratch + [pltpu.SemaphoreType.DMA((6,))],
        "encoder_forward",
        2 * rows * (PIX * D + 4 * D * D + 2 * D * FE + D * E),
    )


DM_BO, DM_G2, DM_S2, DM_BU, DM_BD = 0, E, 2 * E, 3 * E, 3 * E + FD
DM_NORM = 4 * E + FD
DM_HEAD = DM_NORM + 2 * E
DM_LOSS = DM_HEAD + PIX
DM_ALL = DM_LOSS + PIX
DA_QKV, DA_G1, DA_S1, DA_MASK, DA_ALL = 0, 3 * E, 4 * E, 5 * E, 6 * E
CHUNK = 16


def decoder_kernel(
    row_ref, len_ref, wg_ref, vec_ref, latent_ref, pos_ref, pix_ref,
    x0, h1_ref, qkv, lse, att_ref, gproj_ref, grad, h2_ref, du_ref, act_ref, gdown_ref, hn_ref, gpred_ref, sum_ref,
    w_qkv, w_out, w_up, w_down, w_head, mid, slope, x1, pred, dy, sems,
):
    step = pl.program_id(0)
    images = lse.shape[0]
    ready = fetch_all(
        step == 0,
        row_ref,
        wg_ref,
        sems,
        [(T_DQKV, w_qkv), (T_DOUT, w_out), (T_DUP, w_up), (T_DDOWN, w_down), (T_HEAD, w_head)],
    )

    @pl.when(step == 0)
    def _():
        sum_ref[...] = jnp.zeros_like(sum_ref)

    def vec(start, size=E):
        return vec_ref[:, start : start + size]

    def length(image):
        return len_ref[step * images + image]

    order = lax.broadcasted_iota(jnp.int32, (CHUNK, 1), 0)
    token = vec(V_MASK)

    def place(image, c):
        def head_rows(i, c):
            at = pl.ds(pl.multiple_of(image * SD + i * CHUNK, CHUNK), CHUNK)
            got = latent_ref[pl.ds(pl.multiple_of(image * VMAX + i * CHUNK, CHUNK), CHUNK), :]
            x0[at, :] = jnp.where(i * CHUNK + order < length(image), got, token) + pos_ref[at, :]
            return c

        def tail_rows(i, c):
            at = pl.ds(pl.multiple_of(image * SD + i * CHUNK, CHUNK), CHUNK)
            x0[at, :] = token + pos_ref[at, :]
            return c

        loop(0, VMAX // CHUNK, head_rows, 0)
        loop(VMAX // CHUNK, SD // CHUNK, tail_rows, 0)
        return c

    lax.fori_loop(0, images, place, 0)
    norm_forward(x0, vec(DEC["g1"]), vec(DEC["s1"]), h1_ref)
    ready(0)
    qkv_forward(h1_ref, w_qkv, vec_ref, DEC["bqkv"], qkv)
    valid = lax.broadcasted_iota(jnp.int32, (SD, 1), 0) < POS

    def attend(image, c):
        attention_forward(qkv, att_ref, lse, image, SD, E, E // HD, valid)
        return c

    lax.fori_loop(0, images, attend, 0)
    ready(1)
    add_linear(x0, att_ref, w_out, vec_ref, DEC["bo"], mid)
    norm_forward(mid, vec(DEC["g2"]), vec(DEC["s2"]), h2_ref)
    ready(2)
    up_forward(h2_ref, w_up, vec_ref, DEC["bu"], act_ref, slope)
    ready(3)
    add_linear(mid, act_ref, w_down, vec_ref, DEC["bd"], x1)
    norm_forward(x1, vec(V_DNORM), vec(V_DNORM + E), hn_ref)
    ready(4)

    def predict(j, cols):
        pred[:, cols] = mm(hn_ref[...], w_head[:, cols]) + vec_at(vec_ref, V_HEAD, j)

    col_loop(PIX // BS, predict)

    def errors(image, c):
        def one(i, c):
            loss, bias = c
            at = pl.ds(pl.multiple_of(image * SD + i * CHUNK, CHUNK), CHUNK)
            target, _ = norm_parts(pix_ref[at, :].astype(F32))
            place_in = i * CHUNK + order
            masked = (place_in >= length(image)) & (place_in < POS)
            residual = jnp.where(masked, pred[at, :] - target, 0.0)
            low = (residual * (2.0 / PIX)).astype(BF)
            gpred_ref[at, :] = low
            return (loss + fold8(residual * residual), bias + fold8(low.astype(F32)))

        return loop(0, SD // CHUNK, one, c)

    zero = jnp.zeros((8, PIX), F32)
    loss, bias = lax.fori_loop(0, images, errors, (zero, zero))
    add_sum(sum_ref, DM_LOSS, loss)
    add_sum(sum_ref, DM_HEAD, bias)

    back_linear(gpred_ref, w_head, dy)
    d_gain, d_shift = norm_backward(x1, dy, vec(V_DNORM), grad, False)
    add_sum(sum_ref, DM_NORM, d_gain)
    add_sum(sum_ref, DM_NORM + E, d_shift)
    round_and_sum(grad, gdown_ref, sum_ref, DM_BD)
    back_up(gdown_ref, w_down, slope, du_ref, sum_ref, DM_BU)
    back_linear(du_ref, w_up, dy)
    d_gain, d_shift = norm_backward(mid, dy, vec(DEC["g2"]), grad, True)
    add_sum(sum_ref, DM_G2, d_gain)
    add_sum(sum_ref, DM_S2, d_shift)
    round_and_sum(grad, gproj_ref, sum_ref, DM_BO)


def decoder(tile_rows, vis_len, gathered, vector, latent, pos_e, ordered, steps):
    images = vis_len.shape[0]
    rows = images * SD
    part = rows // steps
    outs = [
        ((rows, E), F32, "rows"),
        ((rows, E), BF, "rows"),
        ((rows, 3 * E), BF, "rows"),
        ((images, E // BS, BS * HD // E, SD), F32, "rows"),
        ((rows, E), BF, "rows"),
        ((rows, E), BF, "rows"),
        ((rows, E), F32, "rows"),
        ((rows, E), BF, "rows"),
        ((rows, FD), BF, "rows"),
        ((rows, FD), BF, "rows"),
        ((rows, E), BF, "rows"),
        ((rows, E), BF, "rows"),
        ((rows, PIX), BF, "rows"),
        ((8, DM_ALL), F32, "whole"),
    ]
    scratch = [pltpu.VMEM(s, BF) for s in [(E, 3 * E), (E, E), (E, FD), (FD, E), (E, PIX)]]
    scratch += [
        pltpu.VMEM((part, E), F32),
        pltpu.VMEM((part, FD), BF),
        pltpu.VMEM((part, E), F32),
        pltpu.VMEM((part, PIX), F32),
        pltpu.VMEM((part, E), F32),
        pltpu.SemaphoreType.DMA((5,)),
    ]
    return group_call(
        decoder_kernel,
        steps,
        (tile_rows, vis_len),
        [
            (gathered, "any"),
            (vector, "whole"),
            (latent, "rows"),
            (pos_e.reshape(rows, E), "rows"),
            (ordered.reshape(rows, PIX), "rows"),
        ],
        outs,
        scratch,
        "decoder",
        2 * rows * (4 * E * E + 4 * E * FD + 2 * E * PIX),
    )


def decoder_attention_back_kernel(
    row_ref, len_ref, wg_ref, vec_ref, gproj_ref, grad_in_ref, qkv_ref, lse_ref, x0_ref,
    dqkv_ref, glat_ref, sum_ref,
    w_out, w_qkv, dy, grad, datt, sems,
):
    step = pl.program_id(0)
    images = lse_ref.shape[0]
    ready = fetch_all(step == 0, row_ref, wg_ref, sems, [(T_DOUT, w_out), (T_DQKV, w_qkv)])

    @pl.when(step == 0)
    def _():
        sum_ref[...] = jnp.zeros_like(sum_ref)

    valid = lax.broadcasted_iota(jnp.int32, (SD, 1), 0) < POS
    order = lax.broadcasted_iota(jnp.int32, (CHUNK, 1), 0)
    ready(0)

    def back_out(j, cols):
        datt[:, cols] = mm_nt(gproj_ref[...], w_out[cols, :]).astype(BF)

    col_loop(E // BS, back_out)

    def attend_back(image, c):
        attention_backward(qkv_ref, datt, lse_ref, dqkv_ref, image, SD, E, E // HD, valid)
        return c

    lax.fori_loop(0, images, attend_back, 0)
    sum_rows(dqkv_ref, sum_ref, DA_QKV)
    ready(1)
    back_linear(dqkv_ref, w_qkv, dy)
    grad[...] = grad_in_ref[...]
    gain = vec_ref[:, DEC["g1"] : DEC["g1"] + E]
    d_gain, d_shift = norm_backward(x0_ref, dy, gain, grad, True)
    add_sum(sum_ref, DA_G1, d_gain)
    add_sum(sum_ref, DA_S1, d_shift)

    def unplace(image, c):
        length = len_ref[step * images + image]

        def head_rows(i, c):
            got = grad[pl.ds(pl.multiple_of(image * SD + i * CHUNK, CHUNK), CHUNK), :]
            seen = i * CHUNK + order < length
            at = pl.ds(pl.multiple_of(image * VMAX + i * CHUNK, CHUNK), CHUNK)
            glat_ref[at, :] = jnp.where(seen, got, 0.0).astype(BF)
            return c + fold8(jnp.where(seen, 0.0, got))

        def tail_rows(i, c):
            got = grad[pl.ds(pl.multiple_of(image * SD + i * CHUNK, CHUNK), CHUNK), :]
            return c + fold8(jnp.where(i * CHUNK + order < POS, got, 0.0))

        c = loop(0, VMAX // CHUNK, head_rows, c)
        return loop(VMAX // CHUNK, SD // CHUNK, tail_rows, c)

    add_sum(sum_ref, DA_MASK, lax.fori_loop(0, images, unplace, jnp.zeros((8, E), F32)))


def decoder_attention_back(tile_rows, vis_len, gathered, vector, gproj, grad, qkv, lse, x0, steps):
    images = vis_len.shape[0]
    rows = x0.shape[0]
    part = rows // steps
    outs = [
        ((rows, 3 * E), BF, "rows"),
        ((images * VMAX, E), BF, "rows"),
        ((8, DA_ALL), F32, "whole"),
    ]
    scratch = [pltpu.VMEM(s, BF) for s in [(E, E), (E, 3 * E)]]
    scratch += [pltpu.VMEM((part, E), F32), pltpu.VMEM((part, E), F32), pltpu.VMEM((part, E), BF)]
    return group_call(
        decoder_attention_back_kernel,
        steps,
        (tile_rows, vis_len),
        [
            (gathered, "any"),
            (vector, "whole"),
            (gproj, "rows"),
            (grad, "rows"),
            (qkv, "rows"),
            (lse, "rows"),
            (x0, "rows"),
        ],
        outs,
        scratch + [pltpu.SemaphoreType.DMA((2,))],
        "decoder_attention_back",
        2 * rows * 4 * E * E,
    )


EM_BD, EM_BU = 0, D
EM_G2, EM_S2 = D + FE, 2 * D + FE
EM_BO, EM_NORM = 3 * D + FE, 4 * D + FE
EM_PROJ = 6 * D + FE
EM_ALL = EM_PROJ + E
EA_QKV, EA_G1, EA_S1, EA_EMBED, EA_ALL = 0, 3 * D, 4 * D, 5 * D, 6 * D


def encoder_mlp_back_kernel(
    row_ref, wg_ref, vec_ref, glat_ref, x1_ref, mid_ref, slope_ref,
    gdown_ref, du_ref, grad_ref, gproj_ref, sum_ref,
    w_proj, w_down, w_up, dy, sems,
):
    step = pl.program_id(0)
    ready = fetch_all(
        step == 0, row_ref, wg_ref, sems, [(T_PROJ, w_proj), (T_EDOWN, w_down), (T_EUP, w_up)]
    )

    @pl.when(step == 0)
    def _():
        sum_ref[...] = jnp.zeros_like(sum_ref)

    def vec(start):
        return vec_ref[:, start : start + D]

    sum_rows(glat_ref, sum_ref, EM_PROJ)
    ready(0)
    back_linear(glat_ref, w_proj, dy)
    d_gain, d_shift = norm_backward(x1_ref, dy, vec(V_ENORM), grad_ref, False)
    add_sum(sum_ref, EM_NORM, d_gain)
    add_sum(sum_ref, EM_NORM + D, d_shift)
    round_and_sum(grad_ref, gdown_ref, sum_ref, EM_BD)
    ready(1)
    back_up(gdown_ref, w_down, slope_ref, du_ref, sum_ref, EM_BU)
    ready(2)
    back_linear(du_ref, w_up, dy)
    d_gain, d_shift = norm_backward(mid_ref, dy, vec(ENC["g2"]), grad_ref, True)
    add_sum(sum_ref, EM_G2, d_gain)
    add_sum(sum_ref, EM_S2, d_shift)
    round_and_sum(grad_ref, gproj_ref, sum_ref, EM_BO)


def encoder_mlp_back(tile_rows, gathered, vector, glat, x1, mid, slope, steps):
    rows = x1.shape[0]
    part = rows // steps
    outs = [
        ((rows, D), BF, "rows"),
        ((rows, FE), BF, "rows"),
        ((rows, D), F32, "rows"),
        ((rows, D), BF, "rows"),
        ((8, EM_ALL), F32, "whole"),
    ]
    scratch = [pltpu.VMEM(s, BF) for s in [(D, E), (FE, D), (D, FE)]]
    scratch += [pltpu.VMEM((part, D), F32), pltpu.SemaphoreType.DMA((3,))]
    return group_call(
        encoder_mlp_back_kernel,
        steps,
        (tile_rows,),
        [
            (gathered, "any"),
            (vector, "whole"),
            (glat, "rows"),
            (x1, "rows"),
            (mid, "rows"),
            (slope, "rows"),
        ],
        outs,
        scratch,
        "encoder_mlp_back",
        2 * rows * (D * E + 2 * D * FE),
    )


def encoder_attention_back_kernel(
    row_ref, len_ref, wg_ref, vec_ref, gproj_ref, grad_in_ref, qkv_ref, lse_ref, x0_ref,
    dqkv_ref, gembed_ref, sum_ref,
    w_out, w_qkv, dy, grad, datt, sems,
):
    step = pl.program_id(0)
    images = lse_ref.shape[0]
    ready = fetch_all(step == 0, row_ref, wg_ref, sems, [(T_EOUT, w_out), (T_EQKV, w_qkv)])

    @pl.when(step == 0)
    def _():
        sum_ref[...] = jnp.zeros_like(sum_ref)

    ready(0)

    def back_out(j, cols):
        datt[:, cols] = mm_nt(gproj_ref[...], w_out[cols, :]).astype(BF)

    col_loop(D // BS, back_out)

    def attend_back(image, c):
        valid = lax.broadcasted_iota(jnp.int32, (VMAX, 1), 0) < len_ref[step * images + image]
        attention_backward(qkv_ref, datt, lse_ref, dqkv_ref, image, VMAX, D, D // HE, valid)
        return c

    lax.fori_loop(0, images, attend_back, 0)
    sum_rows(dqkv_ref, sum_ref, EA_QKV)
    ready(1)
    back_linear(dqkv_ref, w_qkv, dy)
    grad[...] = grad_in_ref[...]
    gain = vec_ref[:, ENC["g1"] : ENC["g1"] + D]
    d_gain, d_shift = norm_backward(x0_ref, dy, gain, grad, True)
    add_sum(sum_ref, EA_G1, d_gain)
    add_sum(sum_ref, EA_S1, d_shift)
    round_and_sum(grad, gembed_ref, sum_ref, EA_EMBED)


def encoder_attention_back(tile_rows, vis_len, gathered, vector, gproj, grad, qkv, lse, x0, steps):
    rows = x0.shape[0]
    part = rows // steps
    outs = [((rows, 3 * D), BF, "rows"), ((rows, D), BF, "rows"), ((8, EA_ALL), F32, "whole")]
    scratch = [pltpu.VMEM(s, BF) for s in [(D, D), (D, 3 * D)]]
    scratch += [pltpu.VMEM((part, D), F32), pltpu.VMEM((part, D), F32), pltpu.VMEM((part, D), BF)]
    return group_call(
        encoder_attention_back_kernel,
        steps,
        (tile_rows, vis_len),
        [
            (gathered, "any"),
            (vector, "whole"),
            (gproj, "rows"),
            (grad, "rows"),
            (qkv, "rows"),
            (lse, "rows"),
            (x0, "rows"),
        ],
        outs,
        scratch + [pltpu.SemaphoreType.DMA((2,))],
        "encoder_attention_back",
        2 * rows * 4 * D * D,
    )


def weight_grad_kernel(parts, cut, extra, index_ref, x_ref, g_ref, *refs):
    outs = refs[extra : extra + min(parts, 2)]
    x_t, total = refs[-2:]
    row_tiles, col_tiles = x_ref.shape[1] // BS, g_ref.shape[1] // BS

    @pl.when(pl.program_id(1) == 0)
    def _():
        x_t[...] = x_ref[...].T

    total[...] = mm(x_t[...], g_ref[...])
    for p in range(parts):
        for i in range(row_tiles):
            start = pl.multiple_of(i * BS + (p ^ index_ref[0]) * cut, cut)
            for j in range(col_tiles):
                got = total[pl.ds(start, cut), j * BS : (j + 1) * BS]
                outs[p % 2][p // 2, i * col_tiles + j] = got.astype(BF)


def weight_grad(index, parts, count, first, x, g, block, buffers):
    cut = BS // parts
    rows, width = x.shape
    row_tiles, col_tiles = block
    size = row_tiles * col_tiles
    across = g.shape[1] // (col_tiles * BS)
    assert first % size == 0
    held = min(parts, 2)
    shape = jax.ShapeDtypeStruct((parts // held, count, cut, BS), BF)
    given = list(buffers or [])
    out_spec = pl.BlockSpec(
        (parts // held, size, cut, BS), lambda i, j, *_: (0, first // size + i * across + j, 0, 0)
    )
    return pl.pallas_call(
        functools.partial(weight_grad_kernel, parts, cut, len(given)),
        grid_spec=pltpu.PrefetchScalarGridSpec(
            num_scalar_prefetch=1,
            grid=(width // (row_tiles * BS), across),
            in_specs=[
                pl.BlockSpec((rows, row_tiles * BS), lambda i, j, *_: (0, i)),
                pl.BlockSpec((rows, col_tiles * BS), lambda i, j, *_: (0, j)),
            ]
            + [pl.BlockSpec(memory_space=pl.ANY)] * len(given),
            out_specs=[out_spec] * held,
            scratch_shapes=[
                pltpu.VMEM((row_tiles * BS, rows), BF),
                pltpu.VMEM((row_tiles * BS, col_tiles * BS), F32),
            ],
        ),
        out_shape=[shape] * held,
        input_output_aliases={3 + i: i for i in range(len(given))},
        compiler_params=pltpu.CompilerParams(vmem_limit_bytes=VMEM_LIMIT),
        cost_estimate=pl.CostEstimate(
            flops=2 * rows * width * g.shape[1],
            bytes_accessed=2 * rows * (width + g.shape[1]) + 2 * width * g.shape[1],
            transcendentals=0,
        ),
        name="weight_grad",
    )(index, x, g, *given)


def seed_kernel(parts, index_ref, vec_ref, *outs):
    first = pl.program_id(0) == 0
    for p in range(parts):
        got = vec_ref[p ^ index_ref[0]]
        out = outs[p % 2]
        for t in range(out.shape[1]):
            out[p // 2, t] = (jnp.where(first, got, 0.0) if t == 0 else jnp.zeros_like(got)).astype(BF)


def seed_buffers(index, parts, count, first, vector_tile):
    cut = BS // parts
    held = min(parts, 2)
    size = math.gcd(first, count - first)
    shape = jax.ShapeDtypeStruct((parts // held, count, cut, BS), BF)
    block = (parts // held, size, cut, BS)
    return pl.pallas_call(
        functools.partial(seed_kernel, parts),
        grid_spec=pltpu.PrefetchScalarGridSpec(
            num_scalar_prefetch=1,
            grid=((count - first) // size,),
            in_specs=[pl.BlockSpec(vector_tile.shape, lambda i, *_: (0, 0, 0))],
            out_specs=[pl.BlockSpec(block, lambda i, *_: (0, first // size + i, 0, 0))] * held,
        ),
        out_shape=[shape] * held,
        name="seed_buffers",
    )(index, vector_tile)


def low_sum(a, b):
    return (a.astype(F32) + b.astype(F32)).astype(BF)


def swap_bit(x, bit, size):
    return lax.ppermute(x, "dp", [(i, i ^ (1 << bit)) for i in range(size)])


def reduce_core(buffers, parts):
    if parts == 1:
        return [buffers[0][0]] * 2, []
    whole = low_sum(buffers[0], swap_bit(buffers[1], 0, parts))
    bits = list(range(parts.bit_length() - 2, 0, -1))
    whole = whole.reshape((2,) * len(bits) + whole.shape[1:])
    count = whole.shape[-3]
    return [whole[..., : count // 2, :, :], whole[..., count // 2 :, :, :]], [bits, bits]


def reduce_chips(state, parts, steps):
    halves, left = list(state[0]), list(state[1])
    for half in range(2 if parts > 1 else 0):
        for _ in range(min(steps, len(left[half]))):
            bit = left[half][-1 if half == 0 else 0]
            axis = left[half].index(bit)
            keep = lax.index_in_dim(halves[half], 0, axis, keepdims=False)
            send = lax.index_in_dim(halves[half], 1, axis, keepdims=False)
            halves[half] = low_sum(keep, swap_bit(send, bit, parts))
            left[half] = [b for b in left[half] if b != bit]
    return halves, left


def reduce_join(state, parts):
    halves, _ = reduce_chips(state, parts, 99)
    return jnp.concatenate(halves, axis=0) if parts > 1 else halves[0]


def shift_patch(x, shift, size):
    return lax.ppermute(x, "patch", [(i, (i + shift) % size) for i in range(size)])


def scatter_patch(x, groups):
    if groups == 1:
        return x
    me = lax.axis_index("patch")
    pieces = x.reshape((groups, x.shape[0] // groups) + x.shape[1:])
    total = lax.dynamic_index_in_dim(pieces, me, 0, keepdims=False).astype(F32)
    for k in range(1, groups):
        piece = lax.dynamic_index_in_dim(pieces, (me + k) % groups, 0, keepdims=False)
        total = total + shift_patch(piece, k, groups).astype(F32)
    return total.astype(BF)


def gather_patch(total, groups):
    return jnp.concatenate([total] + [shift_patch(total, k, groups) for k in range(1, groups)], axis=0)


def place_after(position, count, groups):
    if groups == 1:
        return position
    size = count // groups
    me = lax.axis_index("patch")
    return (me - position // size) % groups * size + position % size


def sum_all(x, parts, groups):
    for bit in range(groups.bit_length() - 1):
        x = x + lax.ppermute(x, "patch", [(i, i ^ (1 << bit)) for i in range(groups)])
    return sum_dp(x, parts)


def sum_dp(x, parts):
    for bit in range(parts.bit_length() - 1):
        x = x + swap_bit(x, bit, parts)
    return x


def split_low(x):
    high = x.astype(BF)
    return high, (x - high.astype(F32)).astype(BF)


def tile_kernel(
    scale_ref, grad_ref, w_ref, left_stat_ref, right_stat_ref, left_root_ref, right_root_ref,
    clipped_ref, left_new_ref, right_new_ref, w_new_ref,
):
    scale = scale_ref[0]
    for t in range(w_ref.shape[0]):
        grad = grad_ref[:, t].reshape(BS, BS)
        clipped_ref[t] = grad.astype(F32) * scale
        square = (1.0 - BETA_STAT) * scale * scale
        left_new_ref[t] = BETA_STAT * left_stat_ref[t] + square * mm_nt(grad, grad)
        right_new_ref[t] = BETA_STAT * right_stat_ref[t] + square * mm_tn(grad, grad)
        high, low = split_low(left_root_ref[t])
        half = (mm(high, grad) + mm(low, grad)) * scale
        half_high, half_low = split_low(half)
        high, low = split_low(right_root_ref[t])
        direction = mm(half_high, high) + (mm(half_high, low) + mm(half_low, high))
        direction = direction * lax.rsqrt(jnp.mean(direction * direction) + EPS_ROOT)
        w_new_ref[t] = w_ref[t] - RATE_MATRIX * (direction + DECAY_MATRIX * w_ref[t])


def tile_update(scale, grads, states):
    parts, slots, cut, _ = grads.shape
    per = 2 if slots % 2 == 0 else 1
    tile = pl.BlockSpec((per, BS, BS), lambda i, *_: (i, 0, 0))
    return pl.pallas_call(
        tile_kernel,
        grid_spec=pltpu.PrefetchScalarGridSpec(
            num_scalar_prefetch=1,
            grid=(slots // per,),
            in_specs=[pl.BlockSpec((parts, per, cut, BS), lambda i, *_: (0, i, 0, 0))] + [tile] * 5,
            out_specs=[tile] * 4,
        ),
        out_shape=[jax.ShapeDtypeStruct((slots, BS, BS), F32)] * 4,
        compiler_params=pltpu.CompilerParams(vmem_limit_bytes=VMEM_LIMIT),
        name="tile_update",
    )(scale.reshape(1), grads, *states)


def vector_update(clipped, vectors, moment, second):
    moment_new = BETA_FIRST * moment + (1.0 - BETA_FIRST) * clipped
    second_new = BETA_SECOND * second + (1.0 - BETA_SECOND) * clipped * clipped
    corrected = moment_new / (1.0 - BETA_FIRST**STEP)
    scaled = second_new / (1.0 - BETA_SECOND**STEP)
    vectors_new = vectors - RATE_VECTOR * corrected / (jnp.sqrt(scaled) + EPS_ADAM)
    return moment_new, second_new, vectors_new


CHUNKS = [
    [(T_DUP, 2, 8, (2, 4)), (T_DDOWN, 8, 2, (4, 2)), (T_DOUT, 2, 2, (2, 2))],
    [(T_DQKV, 2, 6, (2, 3)), (T_HEAD, 2, 3, (2, 3)), (T_PROJ, 3, 2, (3, 2))],
    [(T_EUP, 3, 12, (3, 4))],
    [(T_EDOWN, 12, 3, (4, 3)), (T_EOUT, 3, 3, (3, 3))],
    [(T_EQKV, 3, 9, (3, 3)), (T_EMBED, 3, 3, (3, 3))],
]


def chunk_sizes(groups):
    unit = max(2, groups)
    sizes = []
    for i, chunk in enumerate(CHUNKS):
        used = sum(r * c for _, r, c, _ in chunk) + (2 if i == len(CHUNKS) - 1 else 0)
        sizes.append(-(-used // unit) * unit)
    return sizes


def tile_places(sizes):
    chunk_of = np.zeros(NBLK + 2, np.int32)
    place_of = np.zeros(NBLK + 2, np.int32)
    for i, chunk in enumerate(CHUNKS):
        at = 0
        for first, row_tiles, col_tiles, (high, wide) in chunk:
            for r in range(row_tiles):
                for c in range(col_tiles):
                    block = r // high * (col_tiles // wide) + c // wide
                    chunk_of[first + r * col_tiles + c] = i
                    place_of[first + r * col_tiles + c] = at + block * high * wide + r % high * wide + c % wide
            at += row_tiles * col_tiles
    chunk_of[NBLK:] = len(CHUNKS) - 1
    place_of[NBLK + 1] = at
    place_of[NBLK] = at + 1
    return chunk_of, place_of


def shards(parts, groups, pixels, shuffle, vis_len, block_owner, weights, vectors, vec_moment, vec_second,
           left_stat, right_stat, left_root, right_root):
    slots = weights.shape[0]
    own = vectors.shape[0]
    index = lax.axis_index("dp").astype(jnp.int32).reshape(1)
    images = pixels.shape[0]

    vector_rows = -(-own // (16 * BS)) * 16
    mine = jnp.concatenate(
        [
            weights.astype(BF).reshape(slots * BS, BS),
            jnp.pad(vectors.astype(BF), (0, vector_rows * BS - own)).reshape(vector_rows, BS),
        ]
    )
    gathered = lax.all_gather(mine, "dp", axis=0, tiled=True)
    stride = mine.shape[0]
    slot_index = jnp.arange(block_owner.shape[0], dtype=jnp.int32)
    slot_of_block = jnp.sum(
        jnp.where(block_owner[None, :] == jnp.arange(NBLK, dtype=jnp.int32)[:, None], slot_index[None, :], 0),
        axis=1,
    )
    tile_rows = slot_of_block // slots * stride + slot_of_block % slots * BS
    vector = gathered.reshape(parts, stride, BS)[:, slots * BS :].reshape(parts, vector_rows * BS)
    vector = vector[:, :own].reshape(-1).astype(F32)
    enc_key, dec_key = 4 * D, 4 * D + (8 * D + FE - 3 * D) + 2 * D + 2 * E + 3 * E
    vector = jnp.concatenate(
        [vector[:enc_key], jnp.zeros(D, F32), vector[enc_key:dec_key], jnp.zeros(E, F32), vector[dec_key:]]
    ).reshape(1, V_ALL)

    ordered, visible_pix, pos_d, pos_e = order_patches(pixels, shuffle)
    (x0, h1, qkv, lse, att, mid, h2, act, slope, x1, hn, latent) = encoder_forward(
        tile_rows, vis_len, gathered, vector, visible_pix, pos_d, 2
    )
    (
        d_x0, d_h1, d_qkv, d_lse, d_att, d_gproj, d_grad, d_h2, d_du, d_act, d_gdown, d_hn, d_gpred, dm_sums,
    ) = decoder(tile_rows, vis_len, gathered, vector, latent, pos_e, ordered, 4)
    sizes = chunk_sizes(groups)
    chunk_of, place_of = tile_places(sizes)

    rows_cut = BS // parts

    def gradients(chunk, pairs, vector_tile=None):
        used = sum(r * c for _, r, c, _ in CHUNKS[chunk])
        at, buffers = 0, None
        if sizes[chunk] > used:
            if vector_tile is None:
                vector_tile = jnp.zeros((parts, rows_cut, BS), F32)
            buffers = seed_buffers(index, parts, sizes[chunk], used, vector_tile)
        for (x, g), (_, row_tiles, col_tiles, block) in zip(pairs, CHUNKS[chunk]):
            buffers = weight_grad(index, parts, sizes[chunk], at, x, g, block, buffers)
            at += row_tiles * col_tiles
        return buffers

    def core(buffers):
        return reduce_core(buffers, parts)

    def chips(state, steps=1):
        return reduce_chips(state, parts, steps)

    after = lax.optimization_barrier
    buf0 = gradients(0, [(d_h2, d_du), (d_act, d_gdown), (d_att, d_gproj)])
    d_grad, buf0 = after((d_grad, buf0))
    d_dqkv, glat, da_sums = decoder_attention_back(
        tile_rows, vis_len, gathered, vector, d_gproj, d_grad, d_qkv, d_lse, d_x0, 4
    )
    half0, left0 = core(buf0)
    d_dqkv, glat, half0 = after((d_dqkv, glat, half0))
    buf1 = gradients(1, [(d_h1, d_dqkv), (d_hn, d_gpred), (hn, glat)])
    half0, left0 = chips((half0, left0))
    glat, buf1 = after((glat, buf1))
    gdown, du, grad_mid, gproj, m_sums = encoder_mlp_back(tile_rows, gathered, vector, glat, x1, mid, slope, 2)
    half1, left1 = core(buf1)
    du, half0, half1 = after((du, half0, half1))
    buf2 = gradients(2, [(h2, du)])
    half0, left0 = chips((half0, left0), 99)
    half1, left1 = chips((half1, left1))
    gdown, buf2, half0, half1 = after((gdown, buf2, half0, half1))
    buf3 = gradients(3, [(act, gdown), (att, gproj)])
    own0 = scatter_patch(reduce_join((half0, left0), parts), groups)
    half1, left1 = chips((half1, left1), 99)
    half2, left2 = core(buf2)
    grad_mid, buf3, half1, half2, own0 = after((grad_mid, buf3, half1, half2, own0))
    dqkv, gembed, a_sums = encoder_attention_back(
        tile_rows, vis_len, gathered, vector, gproj, grad_mid, qkv, lse, x0, 2
    )
    own1 = scatter_patch(reduce_join((half1, left1), parts), groups)
    full0 = gather_patch(own0, groups)
    half2, left2 = chips((half2, left2))
    half3, left3 = core(buf3)
    dqkv, gembed, half2, half3, own1 = after((dqkv, gembed, half2, half3, own1))

    dm_sums, da_sums, m_sums, a_sums = (jnp.sum(s, axis=0) for s in (dm_sums, da_sums, m_sums, a_sums))

    def cut(sums, start, size):
        return sums[start : start + size]

    grad_vector = jnp.concatenate(
        [
            cut(a_sums, EA_EMBED, D),
            cut(a_sums, EA_G1, 2 * D),
            cut(a_sums, EA_QKV, D),
            cut(a_sums, EA_QKV + 2 * D, D),
            cut(m_sums, EM_BO, D),
            cut(m_sums, EM_G2, 2 * D),
            cut(m_sums, EM_BU, FE),
            cut(m_sums, EM_BD, D),
            cut(m_sums, EM_NORM, 2 * D),
            cut(m_sums, EM_PROJ, E),
            cut(da_sums, DA_MASK, E),
            cut(da_sums, DA_G1, 2 * E),
            cut(da_sums, DA_QKV, E),
            cut(da_sums, DA_QKV + 2 * E, E),
            cut(dm_sums, DM_BO, E),
            cut(dm_sums, DM_G2, 2 * E),
            cut(dm_sums, DM_BU, FD),
            cut(dm_sums, DM_BD, E),
            cut(dm_sums, DM_NORM, 2 * E),
            cut(dm_sums, DM_HEAD, PIX),
        ]
    )
    vector_tile = jnp.pad(grad_vector.reshape(parts, own), ((0, 0), (0, rows_cut * BS - own)))
    vector_tile = vector_tile.reshape(parts, rows_cut, BS)
    buf4 = gradients(4, [(h1, dqkv), (visible_pix.reshape(-1, PIX), gembed)], vector_tile)
    own2 = scatter_patch(reduce_join((half2, left2), parts), groups)
    own3 = scatter_patch(reduce_join((half3, left3), parts), groups)
    own4 = scatter_patch(reduce_join(core(buf4), parts), groups)
    owns = [own0, own1, own2, own3, own4]
    fulls = [full0] + [gather_patch(o, groups) for o in owns[1:]]

    def squares(x):
        wide = x.astype(F32)
        return jnp.sum(wide * wide)

    totals = jnp.stack(
        [
            jnp.sum(cut(dm_sums, DM_LOSS, PIX)) / PIX,
            jnp.sum(POS - vis_len).astype(F32),
            sum(squares(o) for o in owns),
        ]
    )
    totals = sum_all(totals, parts, groups)
    loss_sum, masked_count = totals[0], totals[1]
    grad_norm = jnp.sqrt(totals[2]) / masked_count
    scale = jnp.minimum(1.0, CLIP_NORM / grad_norm) / masked_count

    reduced = jnp.concatenate(fulls, axis=0)
    starts = np.cumsum([0] + sizes)
    where = jnp.zeros(NBLK + 2, jnp.int32)
    for i, size in enumerate(sizes):
        here = starts[i] + place_after(jnp.asarray(place_of), size, groups)
        where = jnp.where(jnp.asarray(chunk_of == i), here, where)
    reduced, scale = after((reduced, scale))
    slot_rows = reduced[where[jnp.minimum(block_owner, NBLK)]]
    if parts > 1:
        slot_rows = lax.all_to_all(slot_rows, "dp", 0, 0, tiled=True)
    grads = slot_rows.reshape(parts, slots, rows_cut, BS)
    clipped, left_new, right_new, weights_new = tile_update(
        scale, grads, (weights, left_stat, right_stat, left_root, right_root)
    )
    own_vector = lax.dynamic_index_in_dim(reduced, where[NBLK + 1], 0, keepdims=False)
    own_vector = own_vector.reshape(-1)[:own].astype(F32) * scale
    moment_new, second_new, vectors_new = vector_update(own_vector, vectors, vec_moment, vec_second)
    return (
        loss_sum,
        masked_count,
        grad_norm,
        clipped,
        left_new,
        right_new,
        weights_new,
        moment_new,
        second_new,
        vectors_new,
    )


def solution(mesh):
    both = ("dp", "patch")
    tiles = P("dp", None, None)
    return jax.shard_map(
        functools.partial(shards, mesh.shape["dp"], mesh.shape["patch"]),
        mesh=mesh,
        in_specs=(P(both, None, None), P(both, None), P(both), P())
        + (tiles, P("dp"), P("dp"), P("dp"))
        + (tiles,) * 4,
        out_specs=(P(), P(), P()) + (tiles,) * 4 + (P("dp"),) * 3,
        check_vma=False,
    )
```

```python
import functools
import math

import jax
import jax.numpy as jnp
import numpy as np
from jax import lax
from jax.experimental import pallas as pl
from jax.experimental.pallas import tpu as pltpu
from jax.sharding import PartitionSpec as P

D = 768
HE = 12
FE = 3072
E = 512
HD = 16
FD = 2048
PIX = 768
POS = 196
VMAX = 80
BS = 256
STEP = 10
NBLK = 177

SD = 208

EPS_NORM = 1e-06
EPS_ROOT = 1e-06
EPS_ADAM = 1e-08
CLIP_NORM = 0.01
RATE_MATRIX = 0.03
DECAY_MATRIX = 0.05
BETA_STAT = 0.5
BETA_FIRST = 0.9
BETA_SECOND = 0.999
RATE_VECTOR = 0.1
NEG_LARGE = -1e30
LOG2E = math.log2(math.e)

BF = jnp.bfloat16
F32 = jnp.float32
VMEM_LIMIT = 60 * 1024 * 1024

T_EMBED, T_EQKV, T_EOUT, T_EUP, T_EDOWN, T_PROJ = 0, 9, 36, 45, 81, 117
T_DQKV, T_DOUT, T_DUP, T_DDOWN, T_HEAD = 123, 135, 139, 155, 171

V_EMBED = 0
V_ENC = D
V_ENORM = V_ENC + 9 * D + FE
V_PROJ = V_ENORM + 2 * D
V_MASK = V_PROJ + E
V_DEC = V_MASK + E
V_DNORM = V_DEC + 9 * E + FD
V_HEAD = V_DNORM + 2 * E
V_ALL = V_HEAD + PIX


def layer_offsets(start, width, hidden):
    names = ["g1", "s1", "bqkv", "bo", "g2", "s2", "bu", "bd"]
    sizes = [width, width, 3 * width, width, width, width, hidden, width]
    offsets = {}
    for name, size in zip(names, sizes):
        offsets[name] = start
        start += size
    return offsets


def mm(a, b):
    return jnp.dot(a, b, preferred_element_type=F32)


def mm_nt(a, b):
    return lax.dot_general(a, b, (((1,), (1,)), ((), ())), preferred_element_type=F32)


def mm_tn(a, b):
    return lax.dot_general(a, b, (((0,), (0,)), ((), ())), preferred_element_type=F32)


def fold8(x):
    rows, cols = x.shape
    return jnp.sum(x.reshape(rows // 8, 8, cols), axis=0)


def gelu_pair(u):
    t = 1.0 / (1.0 + (0.3275911 * math.sqrt(0.5)) * jnp.abs(u))
    e = jnp.exp2((-0.5 * LOG2E) * (u * u))
    poly = t * (
        0.5 * 0.254829592
        + t * (-0.5 * 0.284496736 + t * (0.5 * 1.421413741 + t * (-0.5 * 1.453152027 + t * (0.5 * 1.061405429))))
    )
    tail = poly * e
    phi = jnp.where(u >= 0, 1.0 - tail, tail)
    return u * phi, phi + u * (e * (1.0 / math.sqrt(2.0 * math.pi)))


def norm_parts(x):
    centred = x - jnp.mean(x, axis=-1, keepdims=True)
    inverse = lax.rsqrt(jnp.mean(centred * centred, axis=-1, keepdims=True) + EPS_NORM)
    return centred * inverse, inverse


def loop(lower, upper, body, carry, most=26):
    count = upper - lower
    unroll = max(u for u in range(1, min(most, count) + 1) if count % u == 0)
    return lax.fori_loop(lower, upper, body, carry, unroll=unroll)


def row_loop(rows, step, body, carry=0):
    count = rows // step

    def one(i, c):
        return body(pl.ds(pl.multiple_of(i * step, step), step), c)

    return loop(0, count, one, carry)


def norm_forward(x_ref, gain, shift, out_ref):
    def body(sl, c):
        normed, _ = norm_parts(x_ref[sl, :])
        out_ref[sl, :] = (normed * gain + shift).astype(BF)
        return c

    row_loop(x_ref.shape[0], 16, body)


def norm_backward(x_ref, dy_ref, gain, out_ref, add):
    width = x_ref.shape[1]

    def body(sl, c):
        d_gain, d_shift = c
        normed, inverse = norm_parts(x_ref[sl, :])
        dy = dy_ref[sl, :]
        dn = dy * gain
        mean_one = jnp.mean(dn, axis=-1, keepdims=True)
        mean_two = jnp.mean(dn * normed, axis=-1, keepdims=True)
        dx = inverse * (dn - mean_one - normed * mean_two)
        out_ref[sl, :] = out_ref[sl, :] + dx if add else dx
        return (d_gain + fold8(dy * normed), d_shift + fold8(dy))

    zero = jnp.zeros((8, width), F32)
    return row_loop(x_ref.shape[0], 16, body, (zero, zero))


def col_loop(count, body):
    def one(j, c):
        body(j, pl.ds(pl.multiple_of(j * BS, BS), BS))
        return c

    loop(0, count, one, 0, 4)


def vec_at(vec_ref, start, j):
    return vec_ref[:, pl.ds(pl.multiple_of(start + j * BS, BS), BS)]


def head_mask(head, head_size):
    lane = lax.broadcasted_iota(jnp.int32, (1, BS), 1)
    inside = (lane >= head * head_size) & (lane < (head + 1) * head_size)
    return jnp.where(inside, 1.0, 0.0).astype(BF)


def masked_scores(k_masked, q, head_size, count):
    scores = mm(k_masked, q) * (head_size**-0.5 * LOG2E)
    if isinstance(count, int):
        whole = count // 8 * 8
        tail = scores[whole:]
        row = lax.broadcasted_iota(jnp.int32, tail.shape, 0) + whole
        return jnp.concatenate([scores[:whole], jnp.where(row < count, tail, NEG_LARGE)], axis=0)
    row = lax.broadcasted_iota(jnp.int32, (scores.shape[0], 1), 0)
    return jnp.where(row < count, scores, NEG_LARGE)


def scores_bounded(qkv_ref, width, head_size):
    lane = lax.broadcasted_iota(jnp.int32, (BS, 128), 0) // head_size
    pick = jnp.where(lane == lax.broadcasted_iota(jnp.int32, (BS, 128), 1), 1.0, 0.0).astype(BF)
    tops = []
    for which in range(2):
        top = None
        for g in range(width // BS):
            x = qkv_ref[:, which * width + g * BS : which * width + (g + 1) * BS]
            norms = mm(x * x, pick)
            top = norms if top is None else jnp.maximum(top, norms)
        tops.append(jnp.max(top))
    limit = 60.0 / (1.05 * head_size**-0.5 * LOG2E)
    return tops[0] * tops[1] < limit * limit


def attention_forward(qkv_ref, att_ref, out_t_ref, lse_ref, image, seq, width, head_size, count, bounded):
    rows = pl.ds(pl.multiple_of(image * seq, 16), seq)
    per = BS // head_size

    def group(g, c):
        def part(which):
            return qkv_ref[rows, pl.ds(pl.multiple_of(which * width + g * BS, BS), BS)]

        q, k, v = part(0), part(1), part(2)
        v_t = v.T
        q = q.T
        ones = jnp.ones((16, seq), BF)
        outs, logs = [], []
        for h in range(per):
            scores = masked_scores(k * head_mask(h, head_size), q, head_size, count)
            top = 0.0
            if not bounded:
                top = jnp.max(scores, axis=0, keepdims=True)
                scores = scores - top
            e = jnp.exp2(scores).astype(BF)
            both = mm(jnp.concatenate([v_t[h * head_size : (h + 1) * head_size, :], ones], axis=0), e)
            total = both[head_size : head_size + 1, :]
            outs.append(both[:head_size, :] * (1.0 / total))
            logs.append(top + jnp.log2(total))
        out_t = jnp.concatenate(outs, axis=0)
        out_t_ref[image, g] = out_t
        att_ref[rows, pl.ds(pl.multiple_of(g * BS, BS), BS)] = out_t.T.astype(BF)
        lse_ref[image, g] = jnp.concatenate(logs, axis=0)
        return c

    loop(0, width // BS, group, 0)


def attend_all(qkv_ref, att_ref, out_t_ref, lse_ref, images, seq, width, head_size, count_of):
    safe = scores_bounded(qkv_ref, width, head_size)

    def run(bounded):
        def one(image, c):
            count = count_of(image)
            attention_forward(
                qkv_ref, att_ref, out_t_ref, lse_ref, image, seq, width, head_size, count, bounded
            )
            return c

        lax.fori_loop(0, images, one, 0)

    @pl.when(safe)
    def _():
        run(True)

    @pl.when(jnp.logical_not(safe))
    def _():
        run(False)


def attention_backward(qkv_ref, datt_ref, out_t_ref, lse_ref, dqkv_ref, image, seq, width, head_size, count):
    rows = pl.ds(pl.multiple_of(image * seq, 16), seq)
    per = BS // head_size
    scale = head_size**-0.5

    def group(g, c):
        def cols(which):
            return pl.ds(pl.multiple_of(which * width + g * BS, BS), BS)

        q, k, v = qkv_ref[rows, cols(0)], qkv_ref[rows, cols(1)], qkv_ref[rows, cols(2)]
        d_out = datt_ref[rows, cols(0)]
        lse = lse_ref[image, g]
        q_t, k_t, d_out_t = q.T, k.T, d_out.T
        along = d_out_t.astype(F32) * out_t_ref[image, g]
        d_q, d_k, d_v = [], jnp.zeros((seq, BS), F32), jnp.zeros((seq, BS), F32)
        for h in range(per):
            mask = head_mask(h, head_size)
            part = slice(h * head_size, (h + 1) * head_size)
            delta = jnp.sum(along[part, :], axis=0, keepdims=True)
            probs = jnp.exp2(masked_scores(k * mask, q_t, head_size, count) - lse[h : h + 1, :])
            d_scores = (probs * (mm(v * mask, d_out_t) - delta)).astype(BF)
            d_v = d_v + mm(probs.astype(BF), d_out * mask)
            d_k = d_k + mm(d_scores, q * mask)
            d_q.append(mm(k_t[part, :], d_scores))
        dqkv_ref[rows, cols(0)] = (jnp.concatenate(d_q, axis=0).T * scale).astype(BF)
        dqkv_ref[rows, cols(1)] = (d_k * scale).astype(BF)
        dqkv_ref[rows, cols(2)] = d_v.astype(BF)
        return c

    loop(0, width // BS, group, 0)


def fetch_tiles(row_ref, wg_ref, first, dst, sem):
    row_tiles, col_tiles = dst.shape[0] // BS, dst.shape[1] // BS
    for i in range(row_tiles):
        for j in range(col_tiles):
            start = pl.multiple_of(row_ref[first + i * col_tiles + j], 16)
            pltpu.make_async_copy(
                wg_ref.at[pl.ds(start, BS), :],
                dst.at[i * BS : (i + 1) * BS, j * BS : (j + 1) * BS],
                sem,
            ).start()


def await_tiles(dst, sem):
    pltpu.make_async_copy(dst, dst, sem).wait()


def fetch_all(first_step, row_ref, wg_ref, sems, matrices):
    @pl.when(first_step)
    def _():
        for i, (first, dst) in enumerate(matrices):
            fetch_tiles(row_ref, wg_ref, first, dst, sems.at[i])

    def ready(i):
        @pl.when(first_step)
        def _():
            await_tiles(matrices[i][1], sems.at[i])

    return ready


def qkv_forward(h_ref, w_ref, vec_ref, start, out_ref):
    def body(j, cols):
        out_ref[:, cols] = (mm(h_ref[...], w_ref[:, cols]) + vec_at(vec_ref, start, j)).astype(BF)

    col_loop(w_ref.shape[1] // BS, body)


def add_linear(x_ref, h_ref, w_ref, vec_ref, start, out_ref):
    def body(j, cols):
        out_ref[:, cols] = x_ref[:, cols] + (mm(h_ref[...], w_ref[:, cols]) + vec_at(vec_ref, start, j))

    col_loop(w_ref.shape[1] // BS, body)


def up_forward(h_ref, w_ref, vec_ref, start, act_ref, slope_ref):
    def body(j, cols):
        act, slope = gelu_pair(mm(h_ref[...], w_ref[:, cols]) + vec_at(vec_ref, start, j))
        act_ref[:, cols] = act.astype(BF)
        slope_ref[:, cols] = slope.astype(BF)

    col_loop(w_ref.shape[1] // BS, body)


def back_linear(g_ref, w_ref, out_ref):
    def body(j, cols):
        out_ref[:, cols] = mm_nt(g_ref[...], w_ref[cols, :])

    col_loop(w_ref.shape[0] // BS, body)


def back_up(g_ref, w_ref, slope_ref, du_ref, sum_ref, start):
    def body(j, cols):
        du = (mm_nt(g_ref[...], w_ref[cols, :]) * slope_ref[:, cols].astype(F32)).astype(BF)
        du_ref[:, cols] = du
        at = pl.ds(pl.multiple_of(start + j * BS, BS), BS)
        sum_ref[:, at] = sum_ref[:, at] + fold8(du.astype(F32))

    col_loop(w_ref.shape[0] // BS, body)


def round_and_sum(x_ref, out_ref, sum_ref, start):
    width = x_ref.shape[1]

    def body(sl, c):
        low = x_ref[sl, :].astype(BF)
        out_ref[sl, :] = low
        return c + fold8(low.astype(F32))

    total = row_loop(x_ref.shape[0], 16, body, jnp.zeros((8, width), F32))
    sum_ref[:, start : start + width] = sum_ref[:, start : start + width] + total


def sum_rows(x_ref, sum_ref, start):
    width = x_ref.shape[1]

    def body(sl, c):
        return c + fold8(x_ref[sl, :].astype(F32))

    total = row_loop(x_ref.shape[0], 16, body, jnp.zeros((8, width), F32))
    sum_ref[:, start : start + width] = sum_ref[:, start : start + width] + total


def add_sum(sum_ref, start, value):
    stop = start + value.shape[1]
    sum_ref[:, start:stop] = sum_ref[:, start:stop] + value


def order_kernel(shuffle_ref, pixels_ref, sin_d_ref, sin_e_ref, all_ref, visible_ref, pos_d_ref, pos_e_ref):
    ids = shuffle_ref[0]
    pick = jnp.where(ids == lax.broadcasted_iota(jnp.int32, (SD, POS), 1), 1.0, 0.0).astype(BF)
    ordered = mm(pick, pixels_ref[0]).astype(BF)
    all_ref[0] = ordered
    visible_ref[0] = ordered[:VMAX, :]
    few = pick[:VMAX, :]
    pos_d_ref[0] = mm(few, sin_d_ref[0]) + mm(few, sin_d_ref[1])
    pos_e_ref[0] = mm(pick, sin_e_ref[0]) + mm(pick, sin_e_ref[1])


def sinusoid_parts(count, width):
    half = width // 2
    frequency = np.exp(np.arange(half) * (-np.log(10000.0) / half))
    angles = np.arange(count)[:, None] * frequency[None, :]
    table = np.concatenate([np.sin(angles), np.cos(angles)], axis=1).astype(np.float32)
    high = table.astype(jnp.bfloat16)
    low = (table - high.astype(np.float32)).astype(jnp.bfloat16)
    return np.stack([high, low])


def order_patches(pixels, shuffle):
    images = pixels.shape[0]
    ids = jnp.pad(shuffle, ((0, 0), (0, SD - POS)), constant_values=-1)[:, :, None]

    def image(*dims):
        return pl.BlockSpec((1,) + dims, lambda b: (b,) + (0,) * len(dims))

    def whole(*dims):
        return pl.BlockSpec(dims, lambda b: (0,) * len(dims))

    return pl.pallas_call(
        order_kernel,
        grid=(images,),
        in_specs=[image(SD, 1), image(POS, PIX), whole(2, POS, D), whole(2, POS, E)],
        out_specs=[image(SD, PIX), image(VMAX, PIX), image(VMAX, D), image(SD, E)],
        out_shape=[
            jax.ShapeDtypeStruct((images, SD, PIX), BF),
            jax.ShapeDtypeStruct((images, VMAX, PIX), BF),
            jax.ShapeDtypeStruct((images, VMAX, D), F32),
            jax.ShapeDtypeStruct((images, SD, E), F32),
        ],
        compiler_params=pltpu.CompilerParams(vmem_limit_bytes=VMEM_LIMIT),
        name="order_patches",
    )(ids, pixels, jnp.asarray(sinusoid_parts(POS, D)), jnp.asarray(sinusoid_parts(POS, E)))


def group_call(kernel, steps, prefetch, in_arrays, out_list, scratch, name, flops, share=(0, 1), given=()):
    count = steps // share[1]
    start = share[0] * count

    def spec(shape, kind):
        if kind == "any":
            return pl.BlockSpec(memory_space=pl.ANY)
        if kind == "rows":
            block = (shape[0] // steps,) + tuple(shape[1:])
            return pl.BlockSpec(block, lambda i, *_: (start + i,) + (0,) * (len(shape) - 1))
        return pl.BlockSpec(tuple(shape), lambda i, *_: (0,) * len(shape))

    first_given = len(prefetch) + len(in_arrays)
    return pl.pallas_call(
        functools.partial(kernel, start, len(given)),
        grid_spec=pltpu.PrefetchScalarGridSpec(
            num_scalar_prefetch=len(prefetch),
            grid=(count,),
            in_specs=[spec(a.shape, kind) for a, kind in in_arrays] + [pl.BlockSpec(memory_space=pl.ANY)] * len(given),
            out_specs=[spec(shape, kind) for shape, _, kind in out_list],
            scratch_shapes=scratch,
        ),
        out_shape=[jax.ShapeDtypeStruct(shape, dtype) for shape, dtype, _ in out_list],
        input_output_aliases={first_given + i: i for i in range(len(given))},
        compiler_params=pltpu.CompilerParams(
            vmem_limit_bytes=VMEM_LIMIT, dimension_semantics=("arbitrary",)
        ),
        cost_estimate=pl.CostEstimate(
            flops=flops // share[1],
            bytes_accessed=sum(math.prod(s) * jnp.dtype(t).itemsize for s, t, _ in out_list) * 2 // share[1],
            transcendentals=0,
        ),
        name=name,
    )(*prefetch, *[a for a, _ in in_arrays], *given)


ENC = layer_offsets(V_ENC, D, FE)
DEC = layer_offsets(V_DEC, E, FD)


def encoder_forward_kernel(
    start, given, row_ref, len_ref, wg_ref, vec_ref, pix_ref, pos_ref,
    x0_ref, h1_ref, qkv_ref, lse_ref, out_t_ref, att_ref, mid_ref, h2_ref, act_ref, slope_ref, x1_ref, hn_ref, latent_ref,
    w_embed, w_qkv, w_out, w_up, w_down, w_proj, sems,
):
    step = pl.program_id(0)
    images = lse_ref.shape[0]
    ready = fetch_all(
        step == 0,
        row_ref,
        wg_ref,
        sems,
        [
            (T_EMBED, w_embed),
            (T_EQKV, w_qkv),
            (T_EOUT, w_out),
            (T_EUP, w_up),
            (T_EDOWN, w_down),
            (T_PROJ, w_proj),
        ],
    )

    def vec(start, size=D):
        return vec_ref[:, start : start + size]

    ready(0)
    add_linear(pos_ref, pix_ref, w_embed, vec_ref, V_EMBED, x0_ref)
    norm_forward(x0_ref, vec(ENC["g1"]), vec(ENC["s1"]), h1_ref)
    ready(1)
    qkv_forward(h1_ref, w_qkv, vec_ref, ENC["bqkv"], qkv_ref)

    attend_all(
        qkv_ref, att_ref, out_t_ref, lse_ref, images, VMAX, D, D // HE, lambda i: len_ref[step * images + i]
    )
    ready(2)
    add_linear(x0_ref, att_ref, w_out, vec_ref, ENC["bo"], mid_ref)
    norm_forward(mid_ref, vec(ENC["g2"]), vec(ENC["s2"]), h2_ref)
    ready(3)
    up_forward(h2_ref, w_up, vec_ref, ENC["bu"], act_ref, slope_ref)
    ready(4)
    add_linear(mid_ref, act_ref, w_down, vec_ref, ENC["bd"], x1_ref)
    norm_forward(x1_ref, vec(V_ENORM), vec(V_ENORM + D), hn_ref)
    ready(5)

    def project(j, cols):
        latent_ref[:, cols] = mm(hn_ref[...], w_proj[:, cols]) + vec_at(vec_ref, V_PROJ, j)

    col_loop(E // BS, project)


def encoder_forward(tile_rows, vis_len, gathered, vector, visible_pix, pos_d, steps):
    images = vis_len.shape[0]
    rows = images * VMAX
    outs = [
        ((rows, D), F32, "rows"),
        ((rows, D), BF, "rows"),
        ((rows, 3 * D), BF, "rows"),
        ((images, D // BS, BS * HE // D, VMAX), F32, "rows"),
        ((images, D // BS, BS, VMAX), F32, "rows"),
        ((rows, D), BF, "rows"),
        ((rows, D), F32, "rows"),
        ((rows, D), BF, "rows"),
        ((rows, FE), BF, "rows"),
        ((rows, FE), BF, "rows"),
        ((rows, D), F32, "rows"),
        ((rows, D), BF, "rows"),
        ((rows, E), F32, "rows"),
    ]
    scratch = [pltpu.VMEM(s, BF) for s in [(PIX, D), (D, 3 * D), (D, D), (D, FE), (FE, D), (D, E)]]
    return group_call(
        encoder_forward_kernel,
        steps,
        (tile_rows, vis_len),
        [
            (gathered, "any"),
            (vector, "whole"),
            (visible_pix.reshape(rows, PIX), "rows"),
            (pos_d.reshape(rows, D), "rows"),
        ],
        outs,
        scratch + [pltpu.SemaphoreType.DMA((6,))],
        "encoder_forward",
        2 * rows * (PIX * D + 4 * D * D + 2 * D * FE + D * E),
    )


DS = layer_offsets(0, E, FD)
DS_NORM = 9 * E + FD
DS_HEAD = DS_NORM + 2 * E
DS_MASK = DS_HEAD + PIX
DS_LOSS = DS_MASK + E
DS_ALL = DS_LOSS + PIX


def decoder_kernel(
    start, given, row_ref, len_ref, wg_ref, vec_ref, latent_ref, pos_ref, pix_ref,
    h1_ref, dqkv_ref, att_ref, gproj_ref, h2_ref, du_ref, act_ref, gdown_ref, hn_ref, gpred_ref, glat_ref, sum_ref,
    w_qkv, w_out, w_up, w_down, w_head, x0, qkv, lse, out_t, mid, slope, x1, pred, dy, grad, datt, sems,
):
    step = pl.program_id(0)
    images = lse.shape[0]
    ready = fetch_all(
        step == 0,
        row_ref,
        wg_ref,
        sems,
        [(T_DQKV, w_qkv), (T_DOUT, w_out), (T_DUP, w_up), (T_DDOWN, w_down), (T_HEAD, w_head)],
    )

    @pl.when(step == 0)
    def _():
        sum_ref[...] = jnp.zeros_like(sum_ref)

    def vec(start, size=E):
        return vec_ref[:, start : start + size]

    def length(image):
        return len_ref[step * images + image]

    chunk = 16
    order = lax.broadcasted_iota(jnp.int32, (chunk, 1), 0)
    token = vec(V_MASK)

    def place(image, c):
        def head_rows(i, c):
            at = pl.ds(pl.multiple_of(image * SD + i * chunk, chunk), chunk)
            got = latent_ref[pl.ds(pl.multiple_of(image * VMAX + i * chunk, chunk), chunk), :]
            x0[at, :] = jnp.where(i * chunk + order < length(image), got, token) + pos_ref[at, :]
            return c

        def tail_rows(i, c):
            at = pl.ds(pl.multiple_of(image * SD + i * chunk, chunk), chunk)
            x0[at, :] = token + pos_ref[at, :]
            return c

        loop(0, VMAX // chunk, head_rows, 0)
        loop(VMAX // chunk, SD // chunk, tail_rows, 0)
        return c

    lax.fori_loop(0, images, place, 0)
    norm_forward(x0, vec(DEC["g1"]), vec(DEC["s1"]), h1_ref)
    ready(0)
    qkv_forward(h1_ref, w_qkv, vec_ref, DEC["bqkv"], qkv)
    attend_all(qkv, att_ref, out_t, lse, images, SD, E, E // HD, lambda i: POS)
    ready(1)
    add_linear(x0, att_ref, w_out, vec_ref, DEC["bo"], mid)
    norm_forward(mid, vec(DEC["g2"]), vec(DEC["s2"]), h2_ref)
    ready(2)
    up_forward(h2_ref, w_up, vec_ref, DEC["bu"], act_ref, slope)
    ready(3)
    add_linear(mid, act_ref, w_down, vec_ref, DEC["bd"], x1)
    norm_forward(x1, vec(V_DNORM), vec(V_DNORM + E), hn_ref)
    ready(4)

    def predict(j, cols):
        pred[:, cols] = mm(hn_ref[...], w_head[:, cols]) + vec_at(vec_ref, V_HEAD, j)

    col_loop(PIX // BS, predict)

    def errors(image, c):
        def one(i, c):
            loss, bias = c
            at = pl.ds(pl.multiple_of(image * SD + i * chunk, chunk), chunk)
            target, _ = norm_parts(pix_ref[at, :].astype(F32))
            place_in = i * chunk + order
            masked = (place_in >= length(image)) & (place_in < POS)
            residual = jnp.where(masked, pred[at, :] - target, 0.0)
            low = (residual * (2.0 / PIX)).astype(BF)
            gpred_ref[at, :] = low
            return (loss + fold8(residual * residual), bias + fold8(low.astype(F32)))

        return loop(0, SD // chunk, one, c)

    zero = jnp.zeros((8, PIX), F32)
    loss, bias = lax.fori_loop(0, images, errors, (zero, zero))
    add_sum(sum_ref, DS_LOSS, loss)
    add_sum(sum_ref, DS_HEAD, bias)

    back_linear(gpred_ref, w_head, dy)
    d_gain, d_shift = norm_backward(x1, dy, vec(V_DNORM), grad, False)
    add_sum(sum_ref, DS_NORM, d_gain)
    add_sum(sum_ref, DS_NORM + E, d_shift)
    round_and_sum(grad, gdown_ref, sum_ref, DS["bd"])
    back_up(gdown_ref, w_down, slope, du_ref, sum_ref, DS["bu"])
    back_linear(du_ref, w_up, dy)
    d_gain, d_shift = norm_backward(mid, dy, vec(DEC["g2"]), grad, True)
    add_sum(sum_ref, DS["g2"], d_gain)
    add_sum(sum_ref, DS["s2"], d_shift)
    round_and_sum(grad, gproj_ref, sum_ref, DS["bo"])

    def back_out(j, cols):
        datt[:, cols] = mm_nt(gproj_ref[...], w_out[cols, :]).astype(BF)

    col_loop(E // BS, back_out)

    def attend_back(image, c):
        attention_backward(qkv, datt, out_t, lse, dqkv_ref, image, SD, E, E // HD, POS)
        return c

    lax.fori_loop(0, images, attend_back, 0)
    sum_rows(dqkv_ref, sum_ref, DS["bqkv"])
    back_linear(dqkv_ref, w_qkv, dy)
    d_gain, d_shift = norm_backward(x0, dy, vec(DEC["g1"]), grad, True)
    add_sum(sum_ref, DS["g1"], d_gain)
    add_sum(sum_ref, DS["s1"], d_shift)

    def unplace(image, c):
        def head_rows(i, c):
            got = grad[pl.ds(pl.multiple_of(image * SD + i * chunk, chunk), chunk), :]
            seen = i * chunk + order < length(image)
            at = pl.ds(pl.multiple_of(image * VMAX + i * chunk, chunk), chunk)
            glat_ref[at, :] = jnp.where(seen, got, 0.0).astype(BF)
            return c + fold8(jnp.where(seen, 0.0, got))

        def tail_rows(i, c):
            got = grad[pl.ds(pl.multiple_of(image * SD + i * chunk, chunk), chunk), :]
            return c + fold8(jnp.where(i * chunk + order < POS, got, 0.0))

        c = loop(0, VMAX // chunk, head_rows, c)
        return loop(VMAX // chunk, SD // chunk, tail_rows, c)

    add_sum(sum_ref, DS_MASK, lax.fori_loop(0, images, unplace, jnp.zeros((8, E), F32)))


def decoder(tile_rows, vis_len, gathered, vector, latent, pos_e, ordered, steps):
    images = vis_len.shape[0]
    rows = images * SD
    part = rows // steps
    outs = [
        ((rows, E), BF, "rows"),
        ((rows, 3 * E), BF, "rows"),
        ((rows, E), BF, "rows"),
        ((rows, E), BF, "rows"),
        ((rows, E), BF, "rows"),
        ((rows, FD), BF, "rows"),
        ((rows, FD), BF, "rows"),
        ((rows, E), BF, "rows"),
        ((rows, E), BF, "rows"),
        ((rows, PIX), BF, "rows"),
        ((images * VMAX, E), BF, "rows"),
        ((8, DS_ALL), F32, "whole"),
    ]
    scratch = [pltpu.VMEM(s, BF) for s in [(E, 3 * E), (E, E), (E, FD), (FD, E), (E, PIX)]]
    scratch += [
        pltpu.VMEM((part, E), F32),
        pltpu.VMEM((part, 3 * E), BF),
        pltpu.VMEM((images // steps, E // BS, BS * HD // E, SD), F32),
        pltpu.VMEM((images // steps, E // BS, BS, SD), F32),
        pltpu.VMEM((part, E), F32),
        pltpu.VMEM((part, FD), BF),
        pltpu.VMEM((part, E), F32),
        pltpu.VMEM((part, PIX), F32),
        pltpu.VMEM((part, E), F32),
        pltpu.VMEM((part, E), F32),
        pltpu.VMEM((part, E), BF),
        pltpu.SemaphoreType.DMA((5,)),
    ]
    return group_call(
        decoder_kernel,
        steps,
        (tile_rows, vis_len),
        [
            (gathered, "any"),
            (vector, "whole"),
            (latent, "rows"),
            (pos_e.reshape(rows, E), "rows"),
            (ordered.reshape(rows, PIX), "rows"),
        ],
        outs,
        scratch,
        "decoder",
        4 * rows * (4 * E * E + 2 * E * FD + E * PIX),
    )


EM_BD, EM_BU = 0, D
EM_G2, EM_S2 = D + FE, 2 * D + FE
EM_BO, EM_NORM = 3 * D + FE, 4 * D + FE
EM_PROJ = 6 * D + FE
EM_ALL = EM_PROJ + E
EA_QKV, EA_G1, EA_S1, EA_EMBED, EA_ALL = 0, 3 * D, 4 * D, 5 * D, 6 * D


def encoder_mlp_back_kernel(
    start, given, row_ref, wg_ref, vec_ref, glat_ref, x1_ref, mid_ref, slope_ref,
    gdown_ref, du_ref, grad_ref, gproj_ref, sum_ref,
    w_proj, w_down, w_up, dy, sems,
):
    step = pl.program_id(0)
    ready = fetch_all(
        step == 0, row_ref, wg_ref, sems, [(T_PROJ, w_proj), (T_EDOWN, w_down), (T_EUP, w_up)]
    )

    @pl.when(step == 0)
    def _():
        sum_ref[...] = jnp.zeros_like(sum_ref)

    def vec(start):
        return vec_ref[:, start : start + D]

    sum_rows(glat_ref, sum_ref, EM_PROJ)
    ready(0)
    back_linear(glat_ref, w_proj, dy)
    d_gain, d_shift = norm_backward(x1_ref, dy, vec(V_ENORM), grad_ref, False)
    add_sum(sum_ref, EM_NORM, d_gain)
    add_sum(sum_ref, EM_NORM + D, d_shift)
    round_and_sum(grad_ref, gdown_ref, sum_ref, EM_BD)
    ready(1)
    back_up(gdown_ref, w_down, slope_ref, du_ref, sum_ref, EM_BU)
    ready(2)
    back_linear(du_ref, w_up, dy)
    d_gain, d_shift = norm_backward(mid_ref, dy, vec(ENC["g2"]), grad_ref, True)
    add_sum(sum_ref, EM_G2, d_gain)
    add_sum(sum_ref, EM_S2, d_shift)
    round_and_sum(grad_ref, gproj_ref, sum_ref, EM_BO)


def encoder_mlp_back(tile_rows, gathered, vector, glat, x1, mid, slope, steps):
    rows = x1.shape[0]
    part = rows // steps
    outs = [
        ((rows, D), BF, "rows"),
        ((rows, FE), BF, "rows"),
        ((rows, D), F32, "rows"),
        ((rows, D), BF, "rows"),
        ((8, EM_ALL), F32, "whole"),
    ]
    scratch = [pltpu.VMEM(s, BF) for s in [(D, E), (FE, D), (D, FE)]]
    scratch += [pltpu.VMEM((part, D), F32), pltpu.SemaphoreType.DMA((3,))]
    return group_call(
        encoder_mlp_back_kernel,
        steps,
        (tile_rows,),
        [
            (gathered, "any"),
            (vector, "whole"),
            (glat, "rows"),
            (x1, "rows"),
            (mid, "rows"),
            (slope, "rows"),
        ],
        outs,
        scratch,
        "encoder_mlp_back",
        2 * rows * (D * E + 2 * D * FE),
    )


def encoder_attention_back_kernel(
    start, given, row_ref, len_ref, wg_ref, vec_ref, gproj_ref, grad_in_ref, qkv_ref, lse_ref, out_t_ref, x0_ref, *refs
):
    dqkv_ref, gembed_ref, sum_ref, w_out, w_qkv, dy, grad, datt, sems = refs[given:]
    step = pl.program_id(0)
    images = lse_ref.shape[0]
    ready = fetch_all(step == 0, row_ref, wg_ref, sems, [(T_EOUT, w_out), (T_EQKV, w_qkv)])

    @pl.when(step == 0)
    def _():
        sum_ref[...] = jnp.zeros_like(sum_ref)

    ready(0)

    def back_out(j, cols):
        datt[:, cols] = mm_nt(gproj_ref[...], w_out[cols, :]).astype(BF)

    col_loop(D // BS, back_out)

    def attend_back(image, c):
        count = len_ref[(start + step) * images + image]
        attention_backward(qkv_ref, datt, out_t_ref, lse_ref, dqkv_ref, image, VMAX, D, D // HE, count)
        return c

    lax.fori_loop(0, images, attend_back, 0)
    sum_rows(dqkv_ref, sum_ref, EA_QKV)
    ready(1)
    back_linear(dqkv_ref, w_qkv, dy)
    grad[...] = grad_in_ref[...]
    gain = vec_ref[:, ENC["g1"] : ENC["g1"] + D]
    d_gain, d_shift = norm_backward(x0_ref, dy, gain, grad, True)
    add_sum(sum_ref, EA_G1, d_gain)
    add_sum(sum_ref, EA_S1, d_shift)
    round_and_sum(grad, gembed_ref, sum_ref, EA_EMBED)


def encoder_attention_back(tile_rows, vis_len, gathered, vector, gproj, grad, qkv, lse, out_t, x0, steps, share, given):
    rows = x0.shape[0]
    part = rows // steps
    outs = [((rows, 3 * D), BF, "rows"), ((rows, D), BF, "rows"), ((8, EA_ALL), F32, "whole")]
    scratch = [pltpu.VMEM(s, BF) for s in [(D, D), (D, 3 * D)]]
    scratch += [pltpu.VMEM((part, D), F32), pltpu.VMEM((part, D), F32), pltpu.VMEM((part, D), BF)]
    return group_call(
        encoder_attention_back_kernel,
        steps,
        (tile_rows, vis_len),
        [
            (gathered, "any"),
            (vector, "whole"),
            (gproj, "rows"),
            (grad, "rows"),
            (qkv, "rows"),
            (lse, "rows"),
            (out_t, "rows"),
            (x0, "rows"),
        ],
        outs,
        scratch + [pltpu.SemaphoreType.DMA((2,))],
        "encoder_attention_back",
        2 * rows * 4 * D * D,
        share,
        given,
    )


def weight_grad_kernel(parts, cut, extra, index_ref, x_ref, g_ref, *refs):
    outs = refs[extra : extra + min(parts, 2)]
    x_t, total = refs[-2:]
    row_tiles, col_tiles = x_ref.shape[1] // BS, g_ref.shape[1] // BS

    @pl.when(pl.program_id(1) == 0)
    def _():
        x_t[...] = x_ref[...].T

    total[...] = mm(x_t[...], g_ref[...])
    for p in range(parts):
        for i in range(row_tiles):
            start = pl.multiple_of(i * BS + (p ^ index_ref[0]) * cut, cut)
            for j in range(col_tiles):
                got = total[pl.ds(start, cut), j * BS : (j + 1) * BS]
                outs[p % 2][p // 2, i * col_tiles + j] = got.astype(BF)


def weight_grad(index, parts, count, first, x, g, block, buffers):
    cut = BS // parts
    rows, width = x.shape
    row_tiles, col_tiles = block
    size = row_tiles * col_tiles
    across = g.shape[1] // (col_tiles * BS)
    assert first % size == 0
    held = min(parts, 2)
    shape = jax.ShapeDtypeStruct((parts // held, count, cut, BS), BF)
    given = list(buffers or [])
    out_spec = pl.BlockSpec(
        (parts // held, size, cut, BS), lambda i, j, *_: (0, first // size + i * across + j, 0, 0)
    )
    return pl.pallas_call(
        functools.partial(weight_grad_kernel, parts, cut, len(given)),
        grid_spec=pltpu.PrefetchScalarGridSpec(
            num_scalar_prefetch=1,
            grid=(width // (row_tiles * BS), across),
            in_specs=[
                pl.BlockSpec((rows, row_tiles * BS), lambda i, j, *_: (0, i)),
                pl.BlockSpec((rows, col_tiles * BS), lambda i, j, *_: (0, j)),
            ]
            + [pl.BlockSpec(memory_space=pl.ANY)] * len(given),
            out_specs=[out_spec] * held,
            scratch_shapes=[
                pltpu.VMEM((row_tiles * BS, rows), BF),
                pltpu.VMEM((row_tiles * BS, col_tiles * BS), F32),
            ],
        ),
        out_shape=[shape] * held,
        input_output_aliases={3 + i: i for i in range(len(given))},
        compiler_params=pltpu.CompilerParams(vmem_limit_bytes=VMEM_LIMIT),
        cost_estimate=pl.CostEstimate(
            flops=2 * rows * width * g.shape[1],
            bytes_accessed=2 * rows * (width + g.shape[1]) + 2 * width * g.shape[1],
            transcendentals=0,
        ),
        name="weight_grad",
    )(index, x, g, *given)


def seed_kernel(parts, index_ref, vec_ref, *outs):
    at = pl.program_id(0)
    for p in range(parts):
        got = vec_ref[p ^ index_ref[0]]
        outs[p % 2][p // 2, 0] = jnp.where(at == 0, got, 0.0).astype(BF)


def seed_buffers(index, parts, count, first, vector_tile):
    cut = BS // parts
    held = min(parts, 2)
    shape = jax.ShapeDtypeStruct((parts // held, count, cut, BS), BF)
    return pl.pallas_call(
        functools.partial(seed_kernel, parts),
        grid_spec=pltpu.PrefetchScalarGridSpec(
            num_scalar_prefetch=1,
            grid=(count - first,),
            in_specs=[pl.BlockSpec(vector_tile.shape, lambda i, *_: (0, 0, 0))],
            out_specs=[pl.BlockSpec((parts // held, 1, cut, BS), lambda i, *_: (0, first + i, 0, 0))] * held,
        ),
        out_shape=[shape] * held,
        name="seed_buffers",
    )(index, vector_tile)


def low_sum(a, b):
    return (a.astype(F32) + b.astype(F32)).astype(BF)


def swap_bit(x, bit, size):
    return lax.ppermute(x, "dp", [(i, i ^ (1 << bit)) for i in range(size)])


def reduce_core(buffers, parts):
    if parts == 1:
        return [buffers[0][0]] * 2, []
    whole = low_sum(buffers[0], swap_bit(buffers[1], 0, parts))
    bits = list(range(parts.bit_length() - 2, 0, -1))
    whole = whole.reshape((2,) * len(bits) + whole.shape[1:])
    count = whole.shape[-3]
    return [whole[..., : count // 2, :, :], whole[..., count // 2 :, :, :]], [bits, bits]


def reduce_chips(state, parts, steps):
    halves, left = list(state[0]), list(state[1])
    for half in range(2 if parts > 1 else 0):
        for _ in range(min(steps, len(left[half]))):
            bit = left[half][-1 if half == 0 else 0]
            axis = left[half].index(bit)
            keep = lax.index_in_dim(halves[half], 0, axis, keepdims=False)
            send = lax.index_in_dim(halves[half], 1, axis, keepdims=False)
            halves[half] = low_sum(keep, swap_bit(send, bit, parts))
            left[half] = [b for b in left[half] if b != bit]
    return halves, left


def reduce_join(state, parts):
    halves, _ = reduce_chips(state, parts, 99)
    return jnp.concatenate(halves, axis=0) if parts > 1 else halves[0]


def scatter_patch(x, groups):
    if groups == 1:
        return x
    pieces = lax.all_to_all(x, "patch", 0, 0, tiled=True).reshape((groups, x.shape[0] // groups) + x.shape[1:])
    return jnp.sum(pieces.astype(F32), axis=0).astype(BF)


def gather_patch(own, groups):
    if groups == 1:
        return own
    copies = jnp.broadcast_to(own[None], (groups,) + own.shape).reshape((groups * own.shape[0],) + own.shape[1:])
    return lax.all_to_all(copies, "patch", 0, 0, tiled=True)


def sum_all(x, parts, groups):
    for bit in range(groups.bit_length() - 1):
        x = x + lax.ppermute(x, "patch", [(i, i ^ (1 << bit)) for i in range(groups)])
    return sum_dp(x, parts)


def sum_dp(x, parts):
    for bit in range(parts.bit_length() - 1):
        x = x + swap_bit(x, bit, parts)
    return x


def split_low(x):
    high = x.astype(BF)
    return high, (x - high.astype(F32)).astype(BF)


def tile_kernel(
    scale_ref, grad_ref, w_ref, left_stat_ref, right_stat_ref, left_root_ref, right_root_ref,
    clipped_ref, left_new_ref, right_new_ref, w_new_ref,
):
    scale = scale_ref[0]
    for t in range(w_ref.shape[0]):
        grad = grad_ref[:, t].reshape(BS, BS)
        clipped_ref[t] = grad.astype(F32) * scale
        square = (1.0 - BETA_STAT) * scale * scale
        left_new_ref[t] = BETA_STAT * left_stat_ref[t] + square * mm_nt(grad, grad)
        right_new_ref[t] = BETA_STAT * right_stat_ref[t] + square * mm_tn(grad, grad)
        high, low = split_low(left_root_ref[t])
        half = (mm(high, grad) + mm(low, grad)) * scale
        half_high, half_low = split_low(half)
        high, low = split_low(right_root_ref[t])
        direction = mm(half_high, high) + (mm(half_high, low) + mm(half_low, high))
        direction = direction * lax.rsqrt(jnp.mean(direction * direction) + EPS_ROOT)
        w_new_ref[t] = w_ref[t] - RATE_MATRIX * (direction + DECAY_MATRIX * w_ref[t])


def tile_update(scale, grads, states):
    parts, slots, cut, _ = grads.shape
    per = max(p for p in range(1, 7) if slots % p == 0)
    tile = pl.BlockSpec((per, BS, BS), lambda i, *_: (i, 0, 0))
    return pl.pallas_call(
        tile_kernel,
        grid_spec=pltpu.PrefetchScalarGridSpec(
            num_scalar_prefetch=1,
            grid=(slots // per,),
            in_specs=[pl.BlockSpec((parts, per, cut, BS), lambda i, *_: (0, i, 0, 0))] + [tile] * 5,
            out_specs=[tile] * 4,
        ),
        out_shape=[jax.ShapeDtypeStruct((slots, BS, BS), F32)] * 4,
        compiler_params=pltpu.CompilerParams(vmem_limit_bytes=VMEM_LIMIT),
        name="tile_update",
    )(scale.reshape(1), grads, *states)


def vector_update(clipped, vectors, moment, second):
    moment_new = BETA_FIRST * moment + (1.0 - BETA_FIRST) * clipped
    second_new = BETA_SECOND * second + (1.0 - BETA_SECOND) * clipped * clipped
    corrected = moment_new / (1.0 - BETA_FIRST**STEP)
    scaled = second_new / (1.0 - BETA_SECOND**STEP)
    vectors_new = vectors - RATE_VECTOR * corrected / (jnp.sqrt(scaled) + EPS_ADAM)
    return moment_new, second_new, vectors_new


CHUNKS = [
    [
        (T_DUP, 2, 8, (2, 4)),
        (T_DDOWN, 8, 2, (4, 2)),
        (T_DOUT, 2, 2, (2, 2)),
        (T_DQKV, 2, 6, (2, 3)),
        (T_HEAD, 2, 3, (2, 3)),
        (T_PROJ, 3, 2, (3, 2)),
    ],
    [(T_EUP, 3, 12, (3, 4)), (T_EDOWN, 12, 3, (4, 3)), (T_EOUT, 3, 3, (3, 3))],
    [(T_EQKV, 3, 9, (3, 3)), (T_EMBED, 3, 3, (3, 3))],
]


def chunk_sizes(groups):
    unit = max(2, groups)
    sizes = []
    for i, chunk in enumerate(CHUNKS):
        used = sum(r * c for _, r, c, _ in chunk) + (2 if i == len(CHUNKS) - 1 else 0)
        sizes.append(-(-used // unit) * unit)
    return sizes


def tile_places(sizes):
    chunk_of = np.zeros(NBLK + 2, np.int32)
    place_of = np.zeros(NBLK + 2, np.int32)
    for i, chunk in enumerate(CHUNKS):
        at = 0
        for first, row_tiles, col_tiles, (high, wide) in chunk:
            for r in range(row_tiles):
                for c in range(col_tiles):
                    block = r // high * (col_tiles // wide) + c // wide
                    chunk_of[first + r * col_tiles + c] = i
                    place_of[first + r * col_tiles + c] = at + block * high * wide + r % high * wide + c % wide
            at += row_tiles * col_tiles
    chunk_of[NBLK:] = len(CHUNKS) - 1
    place_of[NBLK + 1] = at
    place_of[NBLK] = at + 1
    return chunk_of, place_of


def shards(parts, groups, pixels, shuffle, vis_len, block_owner, weights, vectors, vec_moment, vec_second,
           left_stat, right_stat, left_root, right_root):
    slots = weights.shape[0]
    own = vectors.shape[0]
    index = lax.axis_index("dp").astype(jnp.int32).reshape(1)
    images = pixels.shape[0]

    vector_rows = -(-own // (16 * BS)) * 16
    mine = jnp.concatenate(
        [
            weights.astype(BF).reshape(slots * BS, BS),
            jnp.pad(vectors.astype(BF), (0, vector_rows * BS - own)).reshape(vector_rows, BS),
        ]
    )
    gathered = lax.all_gather(mine, "dp", axis=0, tiled=True)
    stride = mine.shape[0]
    slot_index = jnp.arange(block_owner.shape[0], dtype=jnp.int32)
    slot_of_block = jnp.sum(
        jnp.where(block_owner[None, :] == jnp.arange(NBLK, dtype=jnp.int32)[:, None], slot_index[None, :], 0),
        axis=1,
    )
    tile_rows = slot_of_block // slots * stride + slot_of_block % slots * BS
    vector = gathered.reshape(parts, stride, BS)[:, slots * BS :].reshape(parts, vector_rows * BS)
    vector = vector[:, :own].reshape(-1).astype(F32)
    enc_key, dec_key = 4 * D, 4 * D + (8 * D + FE - 3 * D) + 2 * D + 2 * E + 3 * E
    vector = jnp.concatenate(
        [vector[:enc_key], jnp.zeros(D, F32), vector[enc_key:dec_key], jnp.zeros(E, F32), vector[dec_key:]]
    ).reshape(1, V_ALL)

    ordered, visible_pix, pos_d, pos_e = order_patches(pixels, shuffle)
    (x0, h1, qkv, lse, out_t, att, mid, h2, act, slope, x1, hn, latent) = encoder_forward(
        tile_rows, vis_len, gathered, vector, visible_pix, pos_d, 2
    )
    (d_h1, d_dqkv, d_att, d_gproj, d_h2, d_du, d_act, d_gdown, d_hn, d_gpred, glat, d_sums) = decoder(
        tile_rows, vis_len, gathered, vector, latent, pos_e, ordered, 4
    )
    sizes = chunk_sizes(groups)
    chunk_of, place_of = tile_places(sizes)

    rows_cut = BS // parts

    def gradients(chunk, pairs, vector_tile=None):
        used = sum(r * c for _, r, c, _ in CHUNKS[chunk])
        at, buffers = 0, None
        if sizes[chunk] > used:
            if vector_tile is None:
                vector_tile = jnp.zeros((parts, rows_cut, BS), F32)
            buffers = seed_buffers(index, parts, sizes[chunk], used, vector_tile)
        for (x, g), (_, row_tiles, col_tiles, block) in zip(pairs, CHUNKS[chunk]):
            buffers = weight_grad(index, parts, sizes[chunk], at, x, g, block, buffers)
            at += row_tiles * col_tiles
        return buffers

    after = lax.optimization_barrier
    buf0 = gradients(
        0, [(d_h2, d_du), (d_act, d_gdown), (d_att, d_gproj), (d_h1, d_dqkv), (d_hn, d_gpred), (hn, glat)]
    )
    glat, buf0 = after((glat, buf0))
    gdown, du, grad_mid, gproj, m_sums = encoder_mlp_back(tile_rows, gathered, vector, glat, x1, mid, slope, 2)
    half0, left0 = reduce_core(buf0, parts)
    gdown, du, gproj, half0 = after((gdown, du, gproj, half0))
    buf1 = gradients(1, [(h2, du), (act, gdown), (att, gproj)])
    half0, left0 = reduce_chips((half0, left0), parts, 1)
    gproj, buf1, half0 = after((gproj, buf1, half0))

    def attention_back(gproj, k, given):
        return encoder_attention_back(
            tile_rows, vis_len, gathered, vector, gproj, grad_mid, qkv, lse, out_t, x0, 2, (k, 2), given
        )

    dqkv, gembed, a_sums = attention_back(gproj, 0, ())
    sum0 = reduce_join((half0, left0), parts)
    half1, left1 = reduce_core(buf1, parts)
    gproj, dqkv, gembed, sum0, half1 = after((gproj, dqkv, gembed, sum0, half1))
    dqkv, gembed, b_sums = attention_back(gproj, 1, (dqkv, gembed))
    own0 = scatter_patch(sum0, groups)
    half1, left1 = reduce_chips((half1, left1), parts, 1)
    dqkv, gembed, own0, half1 = after((dqkv, gembed, own0, half1))
    a_sums = a_sums + b_sums
    d_sums, m_sums, a_sums = (jnp.sum(s, axis=0) for s in (d_sums, m_sums, a_sums))

    def cut(sums, start, size):
        return sums[start : start + size]

    grad_vector = jnp.concatenate(
        [
            cut(a_sums, EA_EMBED, D),
            cut(a_sums, EA_G1, 2 * D),
            cut(a_sums, EA_QKV, D),
            cut(a_sums, EA_QKV + 2 * D, D),
            cut(m_sums, EM_BO, D),
            cut(m_sums, EM_G2, 2 * D),
            cut(m_sums, EM_BU, FE),
            cut(m_sums, EM_BD, D),
            cut(m_sums, EM_NORM, 2 * D),
            cut(m_sums, EM_PROJ, E),
            cut(d_sums, DS_MASK, E),
            cut(d_sums, DS["g1"], 2 * E),
            cut(d_sums, DS["bqkv"], E),
            cut(d_sums, DS["bqkv"] + 2 * E, E),
            cut(d_sums, DS["bo"], E),
            cut(d_sums, DS["g2"], 2 * E),
            cut(d_sums, DS["bu"], FD),
            cut(d_sums, DS["bd"], E),
            cut(d_sums, DS_NORM, 2 * E),
            cut(d_sums, DS_HEAD, PIX),
        ]
    )
    vector_tile = jnp.pad(grad_vector.reshape(parts, own), ((0, 0), (0, rows_cut * BS - own)))
    vector_tile = vector_tile.reshape(parts, rows_cut, BS)
    buf2 = gradients(2, [(h1, dqkv), (visible_pix.reshape(-1, PIX), gembed)], vector_tile)
    own1 = scatter_patch(reduce_join((half1, left1), parts), groups)
    own2 = scatter_patch(reduce_join(reduce_core(buf2, parts), parts), groups)
    owns = [own0, own1, own2]

    def squares(x):
        wide = x.astype(F32)
        return jnp.sum(wide * wide)

    totals = jnp.stack(
        [
            jnp.sum(cut(d_sums, DS_LOSS, PIX)) / PIX,
            jnp.sum(POS - vis_len).astype(F32),
            sum(squares(o) for o in owns),
        ]
    )
    totals = sum_all(totals, parts, groups)
    loss_sum, masked_count = totals[0], totals[1]
    grad_norm = jnp.sqrt(totals[2]) / masked_count
    scale = jnp.minimum(1.0, CLIP_NORM / grad_norm) / masked_count

    reduced = jnp.concatenate([gather_patch(o, groups) for o in owns], axis=0)
    where = jnp.asarray(np.cumsum([0] + sizes)[chunk_of] + place_of, jnp.int32)
    slot_rows = reduced[where[jnp.minimum(block_owner, NBLK)]]
    if parts > 1:
        slot_rows = lax.all_to_all(slot_rows, "dp", 0, 0, tiled=True)
    grads = slot_rows.reshape(parts, slots, rows_cut, BS)
    clipped, left_new, right_new, weights_new = tile_update(
        scale, grads, (weights, left_stat, right_stat, left_root, right_root)
    )
    own_vector = lax.dynamic_index_in_dim(reduced, where[NBLK + 1], 0, keepdims=False)
    own_vector = own_vector.reshape(-1)[:own].astype(F32) * scale
    moment_new, second_new, vectors_new = vector_update(own_vector, vectors, vec_moment, vec_second)
    return (
        loss_sum,
        masked_count,
        grad_norm,
        clipped,
        left_new,
        right_new,
        weights_new,
        moment_new,
        second_new,
        vectors_new,
    )


def solution(mesh):
    both = ("dp", "patch")
    tiles = P("dp", None, None)
    return jax.shard_map(
        functools.partial(shards, mesh.shape["dp"], mesh.shape["patch"]),
        mesh=mesh,
        in_specs=(P(both, None, None), P(both, None), P(both), P())
        + (tiles, P("dp"), P("dp"), P("dp"))
        + (tiles,) * 4,
        out_specs=(P(), P(), P()) + (tiles,) * 4 + (P("dp"),) * 3,
        check_vma=False,
    )
```

```python
import functools
import math

import jax
import jax.numpy as jnp
import numpy as np
from jax import lax
from jax.experimental import pallas as pl
from jax.experimental.pallas import tpu as pltpu
from jax.sharding import PartitionSpec as P

D = 768
HE = 12
FE = 3072
E = 512
HD = 16
FD = 2048
PIX = 768
POS = 196
VMAX = 80
BS = 256
STEP = 10
NBLK = 177

SD = 208

EPS_NORM = 1e-06
EPS_ROOT = 1e-06
EPS_ADAM = 1e-08
CLIP_NORM = 0.01
RATE_MATRIX = 0.03
DECAY_MATRIX = 0.05
BETA_STAT = 0.5
BETA_FIRST = 0.9
BETA_SECOND = 0.999
RATE_VECTOR = 0.1
NEG_LARGE = -1e30
LOG2E = math.log2(math.e)

BF = jnp.bfloat16
F32 = jnp.float32
VMEM_LIMIT = 60 * 1024 * 1024
SMALL = pl.CostEstimate(flops=1000, bytes_accessed=1000, transcendentals=0)

T_EMBED, T_EQKV, T_EOUT, T_EUP, T_EDOWN, T_PROJ = 0, 9, 36, 45, 81, 117
T_DQKV, T_DOUT, T_DUP, T_DDOWN, T_HEAD = 123, 135, 139, 155, 171

V_EMBED = 0
V_ENC = D
V_ENORM = V_ENC + 9 * D + FE
V_PROJ = V_ENORM + 2 * D
V_MASK = V_PROJ + E
V_DEC = V_MASK + E
V_DNORM = V_DEC + 9 * E + FD
V_HEAD = V_DNORM + 2 * E
V_ALL = V_HEAD + PIX


def layer_offsets(start, width, hidden):
    names = ["g1", "s1", "bqkv", "bo", "g2", "s2", "bu", "bd"]
    sizes = [width, width, 3 * width, width, width, width, hidden, width]
    offsets = {}
    for name, size in zip(names, sizes):
        offsets[name] = start
        start += size
    return offsets


def mm(a, b):
    return jnp.dot(a, b, preferred_element_type=F32)


def mm_nt(a, b):
    return lax.dot_general(a, b, (((1,), (1,)), ((), ())), preferred_element_type=F32)


def mm_tn(a, b):
    return lax.dot_general(a, b, (((0,), (0,)), ((), ())), preferred_element_type=F32)


def fold8(x):
    rows, cols = x.shape
    return jnp.sum(x.reshape(rows // 8, 8, cols), axis=0)


def gelu_pair(u):
    t = 1.0 / (1.0 + (0.3275911 * math.sqrt(0.5)) * jnp.abs(u))
    e = jnp.exp2((-0.5 * LOG2E) * (u * u))
    poly = t * (
        0.5 * 0.254829592
        + t * (-0.5 * 0.284496736 + t * (0.5 * 1.421413741 + t * (-0.5 * 1.453152027 + t * (0.5 * 1.061405429))))
    )
    tail = poly * e
    phi = jnp.where(u >= 0, 1.0 - tail, tail)
    return u * phi, phi + u * (e * (1.0 / math.sqrt(2.0 * math.pi)))


def norm_parts(x):
    centred = x - jnp.mean(x, axis=-1, keepdims=True)
    inverse = lax.rsqrt(jnp.mean(centred * centred, axis=-1, keepdims=True) + EPS_NORM)
    return centred * inverse, inverse


def loop(lower, upper, body, carry, most=26):
    count = upper - lower
    unroll = max(u for u in range(1, min(most, count) + 1) if count % u == 0)
    return lax.fori_loop(lower, upper, body, carry, unroll=unroll)


def row_loop(rows, step, body, carry=0):
    count = rows // step

    def one(i, c):
        return body(pl.ds(pl.multiple_of(i * step, step), step), c)

    return loop(0, count, one, carry)


def norm_forward(x_ref, gain, shift, out_ref):
    def body(sl, c):
        normed, _ = norm_parts(x_ref[sl, :])
        out_ref[sl, :] = (normed * gain + shift).astype(BF)
        return c

    row_loop(x_ref.shape[0], 16, body)


def norm_backward(x_ref, dy_ref, gain, out_ref, add):
    width = x_ref.shape[1]

    def body(sl, c):
        d_gain, d_shift = c
        normed, inverse = norm_parts(x_ref[sl, :])
        dy = dy_ref[sl, :]
        dn = dy * gain
        mean_one = jnp.mean(dn, axis=-1, keepdims=True)
        mean_two = jnp.mean(dn * normed, axis=-1, keepdims=True)
        dx = inverse * (dn - mean_one - normed * mean_two)
        out_ref[sl, :] = out_ref[sl, :] + dx if add else dx
        return (d_gain + fold8(dy * normed), d_shift + fold8(dy))

    zero = jnp.zeros((8, width), F32)
    return row_loop(x_ref.shape[0], 16, body, (zero, zero))


def col_loop(count, body):
    def one(j, c):
        body(j, pl.ds(pl.multiple_of(j * BS, BS), BS))
        return c

    loop(0, count, one, 0, 4)


def vec_at(vec_ref, start, j):
    return vec_ref[:, pl.ds(pl.multiple_of(start + j * BS, BS), BS)]


def head_mask(head, head_size):
    lane = lax.broadcasted_iota(jnp.int32, (1, BS), 1)
    inside = (lane >= head * head_size) & (lane < (head + 1) * head_size)
    return jnp.where(inside, 1.0, 0.0).astype(BF)


def masked_scores(k_masked, q, head_size, count):
    scores = mm(k_masked, q) * (head_size**-0.5 * LOG2E)
    if isinstance(count, int):
        whole = count // 8 * 8
        tail = scores[whole:]
        row = lax.broadcasted_iota(jnp.int32, tail.shape, 0) + whole
        return jnp.concatenate([scores[:whole], jnp.where(row < count, tail, NEG_LARGE)], axis=0)
    row = lax.broadcasted_iota(jnp.int32, (scores.shape[0], 1), 0)
    return jnp.where(row < count, scores, NEG_LARGE)


def scores_bounded(qkv_ref, width, head_size):
    lane = lax.broadcasted_iota(jnp.int32, (BS, 128), 0) // head_size
    pick = jnp.where(lane == lax.broadcasted_iota(jnp.int32, (BS, 128), 1), 1.0, 0.0).astype(BF)
    tops = []
    for which in range(2):
        top = None
        for g in range(width // BS):
            x = qkv_ref[:, which * width + g * BS : which * width + (g + 1) * BS]
            norms = mm(x * x, pick)
            top = norms if top is None else jnp.maximum(top, norms)
        tops.append(jnp.max(top))
    limit = 60.0 / (1.05 * head_size**-0.5 * LOG2E)
    return tops[0] * tops[1] < limit * limit


def attention_forward(qkv_ref, att_ref, out_t_ref, lse_ref, image, seq, width, head_size, count, bounded):
    rows = pl.ds(pl.multiple_of(image * seq, 16), seq)
    per = BS // head_size

    def group(g, c):
        def part(which):
            return qkv_ref[rows, pl.ds(pl.multiple_of(which * width + g * BS, BS), BS)]

        q, k, v = part(0), part(1), part(2)
        v_t = v.T
        q = q.T
        ones = jnp.ones((16, seq), BF)
        outs, logs = [], []
        for h in range(per):
            scores = masked_scores(k * head_mask(h, head_size), q, head_size, count)
            top = 0.0
            if not bounded:
                top = jnp.max(scores, axis=0, keepdims=True)
                scores = scores - top
            e = jnp.exp2(scores).astype(BF)
            both = mm(jnp.concatenate([v_t[h * head_size : (h + 1) * head_size, :], ones], axis=0), e)
            total = both[head_size : head_size + 1, :]
            outs.append(both[:head_size, :] * (1.0 / total))
            logs.append(top + jnp.log2(total))
        out_t = jnp.concatenate(outs, axis=0)
        out_t_ref[image, g] = out_t
        att_ref[rows, pl.ds(pl.multiple_of(g * BS, BS), BS)] = out_t.T.astype(BF)
        lse_ref[image, g] = jnp.concatenate(logs, axis=0)
        return c

    loop(0, width // BS, group, 0)


def attend_all(qkv_ref, att_ref, out_t_ref, lse_ref, images, seq, width, head_size, count_of):
    safe = scores_bounded(qkv_ref, width, head_size)

    def run(bounded):
        def one(image, c):
            count = count_of(image)
            attention_forward(
                qkv_ref, att_ref, out_t_ref, lse_ref, image, seq, width, head_size, count, bounded
            )
            return c

        lax.fori_loop(0, images, one, 0)

    @pl.when(safe)
    def _():
        run(True)

    @pl.when(jnp.logical_not(safe))
    def _():
        run(False)


def attention_backward(qkv_ref, datt_ref, out_t_ref, lse_ref, dqkv_ref, image, seq, width, head_size, count):
    rows = pl.ds(pl.multiple_of(image * seq, 16), seq)
    per = BS // head_size
    scale = head_size**-0.5

    def group(g, c):
        def cols(which):
            return pl.ds(pl.multiple_of(which * width + g * BS, BS), BS)

        q, k, v = qkv_ref[rows, cols(0)], qkv_ref[rows, cols(1)], qkv_ref[rows, cols(2)]
        d_out = datt_ref[rows, cols(0)]
        lse = lse_ref[image, g]
        q_t, k_t, d_out_t = q.T, k.T, d_out.T
        along = d_out_t.astype(F32) * out_t_ref[image, g]
        d_q, d_k, d_v = [], jnp.zeros((seq, BS), F32), jnp.zeros((seq, BS), F32)
        for h in range(per):
            mask = head_mask(h, head_size)
            part = slice(h * head_size, (h + 1) * head_size)
            delta = jnp.sum(along[part, :], axis=0, keepdims=True)
            probs = jnp.exp2(masked_scores(k * mask, q_t, head_size, count) - lse[h : h + 1, :])
            d_scores = (probs * (mm(v * mask, d_out_t) - delta)).astype(BF)
            d_v = d_v + mm(probs.astype(BF), d_out * mask)
            d_k = d_k + mm(d_scores, q * mask)
            d_q.append(mm(k_t[part, :], d_scores))
        dqkv_ref[rows, cols(0)] = (jnp.concatenate(d_q, axis=0).T * scale).astype(BF)
        dqkv_ref[rows, cols(1)] = (d_k * scale).astype(BF)
        dqkv_ref[rows, cols(2)] = d_v.astype(BF)
        return c

    loop(0, width // BS, group, 0)


def fetch_tiles(row_ref, wg_ref, first, dst, sem):
    row_tiles, col_tiles = dst.shape[0] // BS, dst.shape[1] // BS
    for i in range(row_tiles):
        for j in range(col_tiles):
            start = pl.multiple_of(row_ref[first + i * col_tiles + j], 16)
            pltpu.make_async_copy(
                wg_ref.at[pl.ds(start, BS), :],
                dst.at[i * BS : (i + 1) * BS, j * BS : (j + 1) * BS],
                sem,
            ).start()


def await_tiles(dst, sem):
    pltpu.make_async_copy(dst, dst, sem).wait()


def fetch_all(first_step, row_ref, wg_ref, sems, matrices):
    @pl.when(first_step)
    def _():
        for i, (first, dst) in enumerate(matrices):
            fetch_tiles(row_ref, wg_ref, first, dst, sems.at[i])

    def ready(i):
        @pl.when(first_step)
        def _():
            await_tiles(matrices[i][1], sems.at[i])

    return ready


def qkv_forward(h_ref, w_ref, vec_ref, start, out_ref):
    def body(j, cols):
        out_ref[:, cols] = (mm(h_ref[...], w_ref[:, cols]) + vec_at(vec_ref, start, j)).astype(BF)

    col_loop(w_ref.shape[1] // BS, body)


def add_linear(x_ref, h_ref, w_ref, vec_ref, start, out_ref):
    def body(j, cols):
        out_ref[:, cols] = x_ref[:, cols] + (mm(h_ref[...], w_ref[:, cols]) + vec_at(vec_ref, start, j))

    col_loop(w_ref.shape[1] // BS, body)


def up_forward(h_ref, w_ref, vec_ref, start, act_ref, slope_ref):
    def body(j, cols):
        act, slope = gelu_pair(mm(h_ref[...], w_ref[:, cols]) + vec_at(vec_ref, start, j))
        act_ref[:, cols] = act.astype(BF)
        slope_ref[:, cols] = slope.astype(BF)

    col_loop(w_ref.shape[1] // BS, body)


def back_linear(g_ref, w_ref, out_ref):
    def body(j, cols):
        out_ref[:, cols] = mm_nt(g_ref[...], w_ref[cols, :])

    col_loop(w_ref.shape[0] // BS, body)


def back_up(g_ref, w_ref, slope_ref, du_ref, sum_ref, start):
    def body(j, cols):
        du = (mm_nt(g_ref[...], w_ref[cols, :]) * slope_ref[:, cols].astype(F32)).astype(BF)
        du_ref[:, cols] = du
        at = pl.ds(pl.multiple_of(start + j * BS, BS), BS)
        sum_ref[:, at] = sum_ref[:, at] + fold8(du.astype(F32))

    col_loop(w_ref.shape[0] // BS, body)


def round_and_sum(x_ref, out_ref, sum_ref, start):
    width = x_ref.shape[1]

    def body(sl, c):
        low = x_ref[sl, :].astype(BF)
        out_ref[sl, :] = low
        return c + fold8(low.astype(F32))

    total = row_loop(x_ref.shape[0], 16, body, jnp.zeros((8, width), F32))
    sum_ref[:, start : start + width] = sum_ref[:, start : start + width] + total


def sum_rows(x_ref, sum_ref, start):
    width = x_ref.shape[1]

    def body(sl, c):
        return c + fold8(x_ref[sl, :].astype(F32))

    total = row_loop(x_ref.shape[0], 16, body, jnp.zeros((8, width), F32))
    sum_ref[:, start : start + width] = sum_ref[:, start : start + width] + total


def add_sum(sum_ref, start, value):
    stop = start + value.shape[1]
    sum_ref[:, start:stop] = sum_ref[:, start:stop] + value


def order_kernel(shuffle_ref, pixels_ref, sin_d_ref, sin_e_ref, all_ref, visible_ref, pos_d_ref, pos_e_ref):
    ids = shuffle_ref[0]
    pick = jnp.where(ids == lax.broadcasted_iota(jnp.int32, (SD, POS), 1), 1.0, 0.0).astype(BF)
    ordered = mm(pick, pixels_ref[0]).astype(BF)
    all_ref[0] = ordered
    visible_ref[0] = ordered[:VMAX, :]
    few = pick[:VMAX, :]
    pos_d_ref[0] = mm(few, sin_d_ref[0]) + mm(few, sin_d_ref[1])
    pos_e_ref[0] = mm(pick, sin_e_ref[0]) + mm(pick, sin_e_ref[1])


def sinusoid_parts(count, width):
    half = width // 2
    frequency = np.exp(np.arange(half) * (-np.log(10000.0) / half))
    angles = np.arange(count)[:, None] * frequency[None, :]
    table = np.concatenate([np.sin(angles), np.cos(angles)], axis=1).astype(np.float32)
    high = table.astype(jnp.bfloat16)
    low = (table - high.astype(np.float32)).astype(jnp.bfloat16)
    return np.stack([high, low])


def order_patches(pixels, shuffle):
    images = pixels.shape[0]
    ids = jnp.pad(shuffle, ((0, 0), (0, SD - POS)), constant_values=-1)[:, :, None]

    def image(*dims):
        return pl.BlockSpec((1,) + dims, lambda b: (b,) + (0,) * len(dims))

    def whole(*dims):
        return pl.BlockSpec(dims, lambda b: (0,) * len(dims))

    return pl.pallas_call(
        order_kernel,
        grid=(images,),
        in_specs=[image(SD, 1), image(POS, PIX), whole(2, POS, D), whole(2, POS, E)],
        out_specs=[image(SD, PIX), image(VMAX, PIX), image(VMAX, D), image(SD, E)],
        out_shape=[
            jax.ShapeDtypeStruct((images, SD, PIX), BF),
            jax.ShapeDtypeStruct((images, VMAX, PIX), BF),
            jax.ShapeDtypeStruct((images, VMAX, D), F32),
            jax.ShapeDtypeStruct((images, SD, E), F32),
        ],
        compiler_params=pltpu.CompilerParams(vmem_limit_bytes=VMEM_LIMIT),
        name="order_patches",
    )(ids, pixels, jnp.asarray(sinusoid_parts(POS, D)), jnp.asarray(sinusoid_parts(POS, E)))


def group_call(kernel, steps, prefetch, in_arrays, out_list, scratch, name, share=(0, 1), given=()):
    count = steps // share[1]
    start = share[0] * count

    def spec(shape, kind):
        if kind == "any":
            return pl.BlockSpec(memory_space=pl.ANY)
        if kind == "rows":
            block = (shape[0] // steps,) + tuple(shape[1:])
            return pl.BlockSpec(block, lambda i, *_: (start + i,) + (0,) * (len(shape) - 1))
        return pl.BlockSpec(tuple(shape), lambda i, *_: (0,) * len(shape))

    first_given = len(prefetch) + len(in_arrays)
    return pl.pallas_call(
        functools.partial(kernel, start, len(given)),
        grid_spec=pltpu.PrefetchScalarGridSpec(
            num_scalar_prefetch=len(prefetch),
            grid=(count,),
            in_specs=[spec(a.shape, kind) for a, kind in in_arrays] + [pl.BlockSpec(memory_space=pl.ANY)] * len(given),
            out_specs=[spec(shape, kind) for shape, _, kind in out_list],
            scratch_shapes=scratch,
        ),
        out_shape=[jax.ShapeDtypeStruct(shape, dtype) for shape, dtype, _ in out_list],
        input_output_aliases={first_given + i: i for i in range(len(given))},
        compiler_params=pltpu.CompilerParams(
            vmem_limit_bytes=VMEM_LIMIT, dimension_semantics=("arbitrary",)
        ),
        cost_estimate=SMALL,
        name=name,
    )(*prefetch, *[a for a, _ in in_arrays], *given)


ENC = layer_offsets(V_ENC, D, FE)
DEC = layer_offsets(V_DEC, E, FD)


def encoder_forward_kernel(
    start, given, row_ref, len_ref, wg_ref, vec_ref, pix_ref, pos_ref,
    x0_ref, h1_ref, qkv_ref, lse_ref, out_t_ref, att_ref, mid_ref, h2_ref, act_ref, slope_ref, x1_ref, hn_ref, latent_ref,
    w_embed, w_qkv, w_out, w_up, w_down, w_proj, sems,
):
    step = pl.program_id(0)
    images = lse_ref.shape[0]
    ready = fetch_all(
        step == 0,
        row_ref,
        wg_ref,
        sems,
        [
            (T_EMBED, w_embed),
            (T_EQKV, w_qkv),
            (T_EOUT, w_out),
            (T_EUP, w_up),
            (T_EDOWN, w_down),
            (T_PROJ, w_proj),
        ],
    )

    def vec(start, size=D):
        return vec_ref[:, start : start + size]

    ready(0)
    add_linear(pos_ref, pix_ref, w_embed, vec_ref, V_EMBED, x0_ref)
    norm_forward(x0_ref, vec(ENC["g1"]), vec(ENC["s1"]), h1_ref)
    ready(1)
    qkv_forward(h1_ref, w_qkv, vec_ref, ENC["bqkv"], qkv_ref)

    attend_all(
        qkv_ref, att_ref, out_t_ref, lse_ref, images, VMAX, D, D // HE, lambda i: len_ref[step * images + i]
    )
    ready(2)
    add_linear(x0_ref, att_ref, w_out, vec_ref, ENC["bo"], mid_ref)
    norm_forward(mid_ref, vec(ENC["g2"]), vec(ENC["s2"]), h2_ref)
    ready(3)
    up_forward(h2_ref, w_up, vec_ref, ENC["bu"], act_ref, slope_ref)
    ready(4)
    add_linear(mid_ref, act_ref, w_down, vec_ref, ENC["bd"], x1_ref)
    norm_forward(x1_ref, vec(V_ENORM), vec(V_ENORM + D), hn_ref)
    ready(5)

    def project(j, cols):
        latent_ref[:, cols] = mm(hn_ref[...], w_proj[:, cols]) + vec_at(vec_ref, V_PROJ, j)

    col_loop(E // BS, project)


def encoder_forward(tile_rows, vis_len, gathered, vector, visible_pix, pos_d, steps):
    images = vis_len.shape[0]
    rows = images * VMAX
    outs = [
        ((rows, D), F32, "rows"),
        ((rows, D), BF, "rows"),
        ((rows, 3 * D), BF, "rows"),
        ((images, D // BS, BS * HE // D, VMAX), F32, "rows"),
        ((images, D // BS, BS, VMAX), F32, "rows"),
        ((rows, D), BF, "rows"),
        ((rows, D), F32, "rows"),
        ((rows, D), BF, "rows"),
        ((rows, FE), BF, "rows"),
        ((rows, FE), BF, "rows"),
        ((rows, D), F32, "rows"),
        ((rows, D), BF, "rows"),
        ((rows, E), F32, "rows"),
    ]
    scratch = [pltpu.VMEM(s, BF) for s in [(PIX, D), (D, 3 * D), (D, D), (D, FE), (FE, D), (D, E)]]
    return group_call(
        encoder_forward_kernel,
        steps,
        (tile_rows, vis_len),
        [
            (gathered, "any"),
            (vector, "whole"),
            (visible_pix.reshape(rows, PIX), "rows"),
            (pos_d.reshape(rows, D), "rows"),
        ],
        outs,
        scratch + [pltpu.SemaphoreType.DMA((6,))],
        "encoder_forward",
    )


DS = layer_offsets(0, E, FD)
DS_NORM = 9 * E + FD
DS_HEAD = DS_NORM + 2 * E
DS_MASK = DS_HEAD + PIX
DS_LOSS = DS_MASK + E
DS_ALL = DS_LOSS + PIX


def decoder_kernel(
    start, given, row_ref, len_ref, wg_ref, vec_ref, latent_ref, pos_ref, pix_ref,
    h1_ref, dqkv_ref, att_ref, gproj_ref, h2_ref, du_ref, act_ref, gdown_ref, hn_ref, gpred_ref, glat_ref, sum_ref,
    w_qkv, w_out, w_up, w_down, w_head, x0, qkv, lse, out_t, mid, slope, x1, pred, dy, grad, datt, sems,
):
    step = pl.program_id(0)
    images = lse.shape[0]
    ready = fetch_all(
        step == 0,
        row_ref,
        wg_ref,
        sems,
        [(T_DQKV, w_qkv), (T_DOUT, w_out), (T_DUP, w_up), (T_DDOWN, w_down), (T_HEAD, w_head)],
    )

    @pl.when(step == 0)
    def _():
        sum_ref[...] = jnp.zeros_like(sum_ref)

    def vec(start, size=E):
        return vec_ref[:, start : start + size]

    def length(image):
        return len_ref[step * images + image]

    chunk = 16
    order = lax.broadcasted_iota(jnp.int32, (chunk, 1), 0)
    token = vec(V_MASK)

    def place(image, c):
        def head_rows(i, c):
            at = pl.ds(pl.multiple_of(image * SD + i * chunk, chunk), chunk)
            got = latent_ref[pl.ds(pl.multiple_of(image * VMAX + i * chunk, chunk), chunk), :]
            x0[at, :] = jnp.where(i * chunk + order < length(image), got, token) + pos_ref[at, :]
            return c

        def tail_rows(i, c):
            at = pl.ds(pl.multiple_of(image * SD + i * chunk, chunk), chunk)
            x0[at, :] = token + pos_ref[at, :]
            return c

        loop(0, VMAX // chunk, head_rows, 0)
        loop(VMAX // chunk, SD // chunk, tail_rows, 0)
        return c

    lax.fori_loop(0, images, place, 0)
    norm_forward(x0, vec(DEC["g1"]), vec(DEC["s1"]), h1_ref)
    ready(0)
    qkv_forward(h1_ref, w_qkv, vec_ref, DEC["bqkv"], qkv)
    attend_all(qkv, att_ref, out_t, lse, images, SD, E, E // HD, lambda i: POS)
    ready(1)
    add_linear(x0, att_ref, w_out, vec_ref, DEC["bo"], mid)
    norm_forward(mid, vec(DEC["g2"]), vec(DEC["s2"]), h2_ref)
    ready(2)
    up_forward(h2_ref, w_up, vec_ref, DEC["bu"], act_ref, slope)
    ready(3)
    add_linear(mid, act_ref, w_down, vec_ref, DEC["bd"], x1)
    norm_forward(x1, vec(V_DNORM), vec(V_DNORM + E), hn_ref)
    ready(4)

    def predict(j, cols):
        pred[:, cols] = mm(hn_ref[...], w_head[:, cols]) + vec_at(vec_ref, V_HEAD, j)

    col_loop(PIX // BS, predict)

    def errors(image, c):
        def one(i, c):
            loss, bias = c
            at = pl.ds(pl.multiple_of(image * SD + i * chunk, chunk), chunk)
            target, _ = norm_parts(pix_ref[at, :].astype(F32))
            place_in = i * chunk + order
            masked = (place_in >= length(image)) & (place_in < POS)
            residual = jnp.where(masked, pred[at, :] - target, 0.0)
            low = (residual * (2.0 / PIX)).astype(BF)
            gpred_ref[at, :] = low
            return (loss + fold8(residual * residual), bias + fold8(low.astype(F32)))

        return loop(0, SD // chunk, one, c)

    zero = jnp.zeros((8, PIX), F32)
    loss, bias = lax.fori_loop(0, images, errors, (zero, zero))
    add_sum(sum_ref, DS_LOSS, loss)
    add_sum(sum_ref, DS_HEAD, bias)

    back_linear(gpred_ref, w_head, dy)
    d_gain, d_shift = norm_backward(x1, dy, vec(V_DNORM), grad, False)
    add_sum(sum_ref, DS_NORM, d_gain)
    add_sum(sum_ref, DS_NORM + E, d_shift)
    round_and_sum(grad, gdown_ref, sum_ref, DS["bd"])
    back_up(gdown_ref, w_down, slope, du_ref, sum_ref, DS["bu"])
    back_linear(du_ref, w_up, dy)
    d_gain, d_shift = norm_backward(mid, dy, vec(DEC["g2"]), grad, True)
    add_sum(sum_ref, DS["g2"], d_gain)
    add_sum(sum_ref, DS["s2"], d_shift)
    round_and_sum(grad, gproj_ref, sum_ref, DS["bo"])

    def back_out(j, cols):
        datt[:, cols] = mm_nt(gproj_ref[...], w_out[cols, :]).astype(BF)

    col_loop(E // BS, back_out)

    def attend_back(image, c):
        attention_backward(qkv, datt, out_t, lse, dqkv_ref, image, SD, E, E // HD, POS)
        return c

    lax.fori_loop(0, images, attend_back, 0)
    sum_rows(dqkv_ref, sum_ref, DS["bqkv"])
    back_linear(dqkv_ref, w_qkv, dy)
    d_gain, d_shift = norm_backward(x0, dy, vec(DEC["g1"]), grad, True)
    add_sum(sum_ref, DS["g1"], d_gain)
    add_sum(sum_ref, DS["s1"], d_shift)

    def unplace(image, c):
        def head_rows(i, c):
            got = grad[pl.ds(pl.multiple_of(image * SD + i * chunk, chunk), chunk), :]
            seen = i * chunk + order < length(image)
            at = pl.ds(pl.multiple_of(image * VMAX + i * chunk, chunk), chunk)
            glat_ref[at, :] = jnp.where(seen, got, 0.0).astype(BF)
            return c + fold8(jnp.where(seen, 0.0, got))

        def tail_rows(i, c):
            got = grad[pl.ds(pl.multiple_of(image * SD + i * chunk, chunk), chunk), :]
            return c + fold8(jnp.where(i * chunk + order < POS, got, 0.0))

        c = loop(0, VMAX // chunk, head_rows, c)
        return loop(VMAX // chunk, SD // chunk, tail_rows, c)

    add_sum(sum_ref, DS_MASK, lax.fori_loop(0, images, unplace, jnp.zeros((8, E), F32)))


def decoder(tile_rows, vis_len, gathered, vector, latent, pos_e, ordered, steps):
    images = vis_len.shape[0]
    rows = images * SD
    part = rows // steps
    outs = [
        ((rows, E), BF, "rows"),
        ((rows, 3 * E), BF, "rows"),
        ((rows, E), BF, "rows"),
        ((rows, E), BF, "rows"),
        ((rows, E), BF, "rows"),
        ((rows, FD), BF, "rows"),
        ((rows, FD), BF, "rows"),
        ((rows, E), BF, "rows"),
        ((rows, E), BF, "rows"),
        ((rows, PIX), BF, "rows"),
        ((images * VMAX, E), BF, "rows"),
        ((8, DS_ALL), F32, "whole"),
    ]
    scratch = [pltpu.VMEM(s, BF) for s in [(E, 3 * E), (E, E), (E, FD), (FD, E), (E, PIX)]]
    scratch += [
        pltpu.VMEM((part, E), F32),
        pltpu.VMEM((part, 3 * E), BF),
        pltpu.VMEM((images // steps, E // BS, BS * HD // E, SD), F32),
        pltpu.VMEM((images // steps, E // BS, BS, SD), F32),
        pltpu.VMEM((part, E), F32),
        pltpu.VMEM((part, FD), BF),
        pltpu.VMEM((part, E), F32),
        pltpu.VMEM((part, PIX), F32),
        pltpu.VMEM((part, E), F32),
        pltpu.VMEM((part, E), F32),
        pltpu.VMEM((part, E), BF),
        pltpu.SemaphoreType.DMA((5,)),
    ]
    return group_call(
        decoder_kernel,
        steps,
        (tile_rows, vis_len),
        [
            (gathered, "any"),
            (vector, "whole"),
            (latent, "rows"),
            (pos_e.reshape(rows, E), "rows"),
            (ordered.reshape(rows, PIX), "rows"),
        ],
        outs,
        scratch,
        "decoder",
    )


EM_BD, EM_BU = 0, D
EM_G2, EM_S2 = D + FE, 2 * D + FE
EM_BO, EM_NORM = 3 * D + FE, 4 * D + FE
EM_PROJ = 6 * D + FE
EM_ALL = EM_PROJ + E
EA_QKV, EA_G1, EA_S1, EA_EMBED, EA_ALL = 0, 3 * D, 4 * D, 5 * D, 6 * D


def encoder_mlp_back_kernel(
    start, given, row_ref, wg_ref, vec_ref, glat_ref, x1_ref, mid_ref, slope_ref,
    gdown_ref, du_ref, grad_ref, gproj_ref, sum_ref,
    w_proj, w_down, w_up, dy, sems,
):
    step = pl.program_id(0)
    ready = fetch_all(
        step == 0, row_ref, wg_ref, sems, [(T_PROJ, w_proj), (T_EDOWN, w_down), (T_EUP, w_up)]
    )

    @pl.when(step == 0)
    def _():
        sum_ref[...] = jnp.zeros_like(sum_ref)

    def vec(start):
        return vec_ref[:, start : start + D]

    sum_rows(glat_ref, sum_ref, EM_PROJ)
    ready(0)
    back_linear(glat_ref, w_proj, dy)
    d_gain, d_shift = norm_backward(x1_ref, dy, vec(V_ENORM), grad_ref, False)
    add_sum(sum_ref, EM_NORM, d_gain)
    add_sum(sum_ref, EM_NORM + D, d_shift)
    round_and_sum(grad_ref, gdown_ref, sum_ref, EM_BD)
    ready(1)
    back_up(gdown_ref, w_down, slope_ref, du_ref, sum_ref, EM_BU)
    ready(2)
    back_linear(du_ref, w_up, dy)
    d_gain, d_shift = norm_backward(mid_ref, dy, vec(ENC["g2"]), grad_ref, True)
    add_sum(sum_ref, EM_G2, d_gain)
    add_sum(sum_ref, EM_S2, d_shift)
    round_and_sum(grad_ref, gproj_ref, sum_ref, EM_BO)


def encoder_mlp_back(tile_rows, gathered, vector, glat, x1, mid, slope, steps):
    rows = x1.shape[0]
    part = rows // steps
    outs = [
        ((rows, D), BF, "rows"),
        ((rows, FE), BF, "rows"),
        ((rows, D), F32, "rows"),
        ((rows, D), BF, "rows"),
        ((8, EM_ALL), F32, "whole"),
    ]
    scratch = [pltpu.VMEM(s, BF) for s in [(D, E), (FE, D), (D, FE)]]
    scratch += [pltpu.VMEM((part, D), F32), pltpu.SemaphoreType.DMA((3,))]
    return group_call(
        encoder_mlp_back_kernel,
        steps,
        (tile_rows,),
        [
            (gathered, "any"),
            (vector, "whole"),
            (glat, "rows"),
            (x1, "rows"),
            (mid, "rows"),
            (slope, "rows"),
        ],
        outs,
        scratch,
        "encoder_mlp_back",
    )


def encoder_attention_back_kernel(
    start, given, row_ref, len_ref, wg_ref, vec_ref, gproj_ref, grad_in_ref, qkv_ref, lse_ref, out_t_ref, x0_ref, *refs
):
    dqkv_ref, gembed_ref, sum_ref, w_out, w_qkv, dy, grad, datt, sems = refs[given:]
    step = pl.program_id(0)
    images = lse_ref.shape[0]
    ready = fetch_all(step == 0, row_ref, wg_ref, sems, [(T_EOUT, w_out), (T_EQKV, w_qkv)])

    @pl.when(step == 0)
    def _():
        sum_ref[...] = jnp.zeros_like(sum_ref)

    ready(0)

    def back_out(j, cols):
        datt[:, cols] = mm_nt(gproj_ref[...], w_out[cols, :]).astype(BF)

    col_loop(D // BS, back_out)

    def attend_back(image, c):
        count = len_ref[(start + step) * images + image]
        attention_backward(qkv_ref, datt, out_t_ref, lse_ref, dqkv_ref, image, VMAX, D, D // HE, count)
        return c

    lax.fori_loop(0, images, attend_back, 0)
    sum_rows(dqkv_ref, sum_ref, EA_QKV)
    ready(1)
    back_linear(dqkv_ref, w_qkv, dy)
    grad[...] = grad_in_ref[...]
    gain = vec_ref[:, ENC["g1"] : ENC["g1"] + D]
    d_gain, d_shift = norm_backward(x0_ref, dy, gain, grad, True)
    add_sum(sum_ref, EA_G1, d_gain)
    add_sum(sum_ref, EA_S1, d_shift)
    round_and_sum(grad, gembed_ref, sum_ref, EA_EMBED)


def encoder_attention_back(tile_rows, vis_len, gathered, vector, gproj, grad, qkv, lse, out_t, x0, steps, share, given):
    rows = x0.shape[0]
    part = rows // steps
    outs = [((rows, 3 * D), BF, "rows"), ((rows, D), BF, "rows"), ((8, EA_ALL), F32, "whole")]
    scratch = [pltpu.VMEM(s, BF) for s in [(D, D), (D, 3 * D)]]
    scratch += [pltpu.VMEM((part, D), F32), pltpu.VMEM((part, D), F32), pltpu.VMEM((part, D), BF)]
    return group_call(
        encoder_attention_back_kernel,
        steps,
        (tile_rows, vis_len),
        [
            (gathered, "any"),
            (vector, "whole"),
            (gproj, "rows"),
            (grad, "rows"),
            (qkv, "rows"),
            (lse, "rows"),
            (out_t, "rows"),
            (x0, "rows"),
        ],
        outs,
        scratch + [pltpu.SemaphoreType.DMA((2,))],
        "encoder_attention_back",
        share,
        given,
    )


def weight_grad_kernel(parts, cut, extra, index_ref, x_ref, g_ref, *refs):
    outs = refs[extra : extra + min(parts, 2)]
    x_t, total = refs[-2:]
    row_tiles, col_tiles = x_ref.shape[1] // BS, g_ref.shape[1] // BS

    @pl.when(pl.program_id(1) == 0)
    def _():
        x_t[...] = x_ref[...].T

    total[...] = mm(x_t[...], g_ref[...])
    for p in range(parts):
        for i in range(row_tiles):
            start = pl.multiple_of(i * BS + (p ^ index_ref[0]) * cut, cut)
            for j in range(col_tiles):
                got = total[pl.ds(start, cut), j * BS : (j + 1) * BS]
                outs[p % 2][p // 2, i * col_tiles + j] = got.astype(BF)


def weight_grad(index, parts, count, first, x, g, block, buffers):
    cut = BS // parts
    rows, width = x.shape
    row_tiles, col_tiles = block
    size = row_tiles * col_tiles
    across = g.shape[1] // (col_tiles * BS)
    assert first % size == 0
    held = min(parts, 2)
    shape = jax.ShapeDtypeStruct((parts // held, count, cut, BS), BF)
    given = list(buffers or [])
    out_spec = pl.BlockSpec(
        (parts // held, size, cut, BS), lambda i, j, *_: (0, first // size + i * across + j, 0, 0)
    )
    return pl.pallas_call(
        functools.partial(weight_grad_kernel, parts, cut, len(given)),
        grid_spec=pltpu.PrefetchScalarGridSpec(
            num_scalar_prefetch=1,
            grid=(width // (row_tiles * BS), across),
            in_specs=[
                pl.BlockSpec((rows, row_tiles * BS), lambda i, j, *_: (0, i)),
                pl.BlockSpec((rows, col_tiles * BS), lambda i, j, *_: (0, j)),
            ]
            + [pl.BlockSpec(memory_space=pl.ANY)] * len(given),
            out_specs=[out_spec] * held,
            scratch_shapes=[
                pltpu.VMEM((row_tiles * BS, rows), BF),
                pltpu.VMEM((row_tiles * BS, col_tiles * BS), F32),
            ],
        ),
        out_shape=[shape] * held,
        input_output_aliases={3 + i: i for i in range(len(given))},
        compiler_params=pltpu.CompilerParams(vmem_limit_bytes=VMEM_LIMIT),
        cost_estimate=SMALL,
        name="weight_grad",
    )(index, x, g, *given)


def seed_kernel(parts, index_ref, vec_ref, *outs):
    at = pl.program_id(0)
    for p in range(parts):
        got = vec_ref[p ^ index_ref[0]]
        outs[p % 2][p // 2, 0] = jnp.where(at == 0, got, 0.0).astype(BF)


def seed_buffers(index, parts, count, first, vector_tile):
    cut = BS // parts
    held = min(parts, 2)
    shape = jax.ShapeDtypeStruct((parts // held, count, cut, BS), BF)
    return pl.pallas_call(
        functools.partial(seed_kernel, parts),
        grid_spec=pltpu.PrefetchScalarGridSpec(
            num_scalar_prefetch=1,
            grid=(count - first,),
            in_specs=[pl.BlockSpec(vector_tile.shape, lambda i, *_: (0, 0, 0))],
            out_specs=[pl.BlockSpec((parts // held, 1, cut, BS), lambda i, *_: (0, first + i, 0, 0))] * held,
        ),
        out_shape=[shape] * held,
        name="seed_buffers",
    )(index, vector_tile)


def low_sum(a, b):
    return (a.astype(F32) + b.astype(F32)).astype(BF)


def swap_bit(x, bit, size):
    return lax.ppermute(x, "dp", [(i, i ^ (1 << bit)) for i in range(size)])


def reduce_core(buffers, parts):
    if parts == 1:
        whole, count = buffers[0][0], buffers[0].shape[1]
        return [whole[: count // 2], whole[count // 2 :]], [[], []]
    whole = low_sum(buffers[0], swap_bit(buffers[1], 0, parts))
    bits = list(range(parts.bit_length() - 2, 0, -1))
    whole = whole.reshape((2,) * len(bits) + whole.shape[1:])
    count = whole.shape[-3]
    return [whole[..., : count // 2, :, :], whole[..., count // 2 :, :, :]], [bits, bits]


def reduce_chips(state, parts, steps):
    halves, left = list(state[0]), list(state[1])
    for half in range(2):
        for _ in range(min(steps, len(left[half]))):
            bit = left[half][-1 if half == 0 else 0]
            axis = left[half].index(bit)
            keep = lax.index_in_dim(halves[half], 0, axis, keepdims=False)
            send = lax.index_in_dim(halves[half], 1, axis, keepdims=False)
            halves[half] = low_sum(keep, swap_bit(send, bit, parts))
            left[half] = [b for b in left[half] if b != bit]
    return halves, left


def patch_steps(groups):
    middle = groups // 2 - 1

    def inwards(k, x):
        return low_sum(x, lax.ppermute(x, "patch", [(k, k + 1), (groups - 1 - k, groups - 2 - k)]))

    def across(x):
        return low_sum(x, lax.ppermute(x, "patch", [(middle, middle + 1), (middle + 1, middle)]))

    def outwards(k, x):
        got = lax.ppermute(x, "patch", [(k + 1, k), (groups - 2 - k, groups - 1 - k)])
        me = lax.axis_index("patch")
        return jnp.where((me == k) | (me == groups - 1 - k), got, x)

    if groups == 1:
        return []
    steps = [functools.partial(inwards, k) for k in range(middle)] + [across]
    return steps + [functools.partial(outwards, k) for k in reversed(range(middle))]


def sum_patch(x, steps):
    for step in steps:
        x = step(x)
    return x


def sum_all(x, parts, groups):
    for bit in range(groups.bit_length() - 1):
        x = x + lax.ppermute(x, "patch", [(i, i ^ (1 << bit)) for i in range(groups)])
    return sum_dp(x, parts)


def sum_dp(x, parts):
    for bit in range(parts.bit_length() - 1):
        x = x + swap_bit(x, bit, parts)
    return x


def split_low(x):
    high = x.astype(BF)
    return high, (x - high.astype(F32)).astype(BF)


def tile_kernel(
    scale_ref, grad_ref, w_ref, left_stat_ref, right_stat_ref, left_root_ref, right_root_ref,
    clipped_ref, left_new_ref, right_new_ref, w_new_ref,
):
    scale = scale_ref[0]
    for t in range(w_ref.shape[0]):
        grad = grad_ref[:, t].reshape(BS, BS)
        clipped_ref[t] = grad.astype(F32) * scale
        square = (1.0 - BETA_STAT) * scale * scale
        left_new_ref[t] = BETA_STAT * left_stat_ref[t] + square * mm_nt(grad, grad)
        right_new_ref[t] = BETA_STAT * right_stat_ref[t] + square * mm_tn(grad, grad)
        high, low = split_low(left_root_ref[t])
        half = (mm(high, grad) + mm(low, grad)) * scale
        half_high, half_low = split_low(half)
        high, low = split_low(right_root_ref[t])
        direction = mm(half_high, high) + (mm(half_high, low) + mm(half_low, high))
        direction = direction * lax.rsqrt(jnp.mean(direction * direction) + EPS_ROOT)
        w_new_ref[t] = w_ref[t] - RATE_MATRIX * (direction + DECAY_MATRIX * w_ref[t])


def tile_update(scale, grads, states):
    parts, slots, cut, _ = grads.shape
    per = max(p for p in range(1, 7) if slots % p == 0)
    tile = pl.BlockSpec((per, BS, BS), lambda i, *_: (i, 0, 0))
    return pl.pallas_call(
        tile_kernel,
        grid_spec=pltpu.PrefetchScalarGridSpec(
            num_scalar_prefetch=1,
            grid=(slots // per,),
            in_specs=[pl.BlockSpec((parts, per, cut, BS), lambda i, *_: (0, i, 0, 0))] + [tile] * 5,
            out_specs=[tile] * 4,
        ),
        out_shape=[jax.ShapeDtypeStruct((slots, BS, BS), F32)] * 4,
        compiler_params=pltpu.CompilerParams(vmem_limit_bytes=VMEM_LIMIT),
        name="tile_update",
    )(scale.reshape(1), grads, *states)


def vector_update(clipped, vectors, moment, second):
    moment_new = BETA_FIRST * moment + (1.0 - BETA_FIRST) * clipped
    second_new = BETA_SECOND * second + (1.0 - BETA_SECOND) * clipped * clipped
    corrected = moment_new / (1.0 - BETA_FIRST**STEP)
    scaled = second_new / (1.0 - BETA_SECOND**STEP)
    vectors_new = vectors - RATE_VECTOR * corrected / (jnp.sqrt(scaled) + EPS_ADAM)
    return moment_new, second_new, vectors_new


CHUNKS = [
    [
        (T_DUP, 2, 8, (2, 4)),
        (T_DDOWN, 8, 2, (4, 2)),
        (T_DOUT, 2, 2, (2, 2)),
        (T_DQKV, 2, 6, (2, 3)),
        (T_HEAD, 2, 3, (2, 3)),
        (T_PROJ, 3, 2, (3, 2)),
    ],
    [(T_EUP, 3, 12, (3, 4)), (T_EDOWN, 12, 3, (4, 3)), (T_EOUT, 3, 3, (3, 3))],
    [(T_EQKV, 3, 9, (3, 3)), (T_EMBED, 3, 3, (3, 3))],
]


def chunk_sizes(groups):
    unit = max(2, groups)
    sizes = []
    for i, chunk in enumerate(CHUNKS):
        used = sum(r * c for _, r, c, _ in chunk) + (2 if i == len(CHUNKS) - 1 else 0)
        sizes.append(-(-used // unit) * unit)
    return sizes


def tile_places(sizes):
    chunk_of = np.zeros(NBLK + 2, np.int32)
    place_of = np.zeros(NBLK + 2, np.int32)
    for i, chunk in enumerate(CHUNKS):
        at = 0
        for first, row_tiles, col_tiles, (high, wide) in chunk:
            for r in range(row_tiles):
                for c in range(col_tiles):
                    block = r // high * (col_tiles // wide) + c // wide
                    chunk_of[first + r * col_tiles + c] = i
                    place_of[first + r * col_tiles + c] = at + block * high * wide + r % high * wide + c % wide
            at += row_tiles * col_tiles
    chunk_of[NBLK:] = len(CHUNKS) - 1
    place_of[NBLK + 1] = at
    place_of[NBLK] = at + 1
    return chunk_of, place_of


def shards(parts, groups, pixels, shuffle, vis_len, block_owner, weights, vectors, vec_moment, vec_second,
           left_stat, right_stat, left_root, right_root):
    slots = weights.shape[0]
    own = vectors.shape[0]
    index = lax.axis_index("dp").astype(jnp.int32).reshape(1)
    images = pixels.shape[0]

    vector_rows = -(-own // (16 * BS)) * 16
    mine = jnp.concatenate(
        [
            weights.astype(BF).reshape(slots * BS, BS),
            jnp.pad(vectors.astype(BF), (0, vector_rows * BS - own)).reshape(vector_rows, BS),
        ]
    )
    gathered = lax.all_gather(mine, "dp", axis=0, tiled=True)
    stride = mine.shape[0]
    slot_index = jnp.arange(block_owner.shape[0], dtype=jnp.int32)
    slot_of_block = jnp.sum(
        jnp.where(block_owner[None, :] == jnp.arange(NBLK, dtype=jnp.int32)[:, None], slot_index[None, :], 0),
        axis=1,
    )
    tile_rows = slot_of_block // slots * stride + slot_of_block % slots * BS
    vector = gathered.reshape(parts, stride, BS)[:, slots * BS :].reshape(parts, vector_rows * BS)
    vector = vector[:, :own].reshape(-1).astype(F32)
    enc_key, dec_key = 4 * D, 4 * D + (8 * D + FE - 3 * D) + 2 * D + 2 * E + 3 * E
    vector = jnp.concatenate(
        [vector[:enc_key], jnp.zeros(D, F32), vector[enc_key:dec_key], jnp.zeros(E, F32), vector[dec_key:]]
    ).reshape(1, V_ALL)

    ordered, visible_pix, pos_d, pos_e = order_patches(pixels, shuffle)
    (x0, h1, qkv, lse, out_t, att, mid, h2, act, slope, x1, hn, latent) = encoder_forward(
        tile_rows, vis_len, gathered, vector, visible_pix, pos_d, 2
    )
    (d_h1, d_dqkv, d_att, d_gproj, d_h2, d_du, d_act, d_gdown, d_hn, d_gpred, glat, d_sums) = decoder(
        tile_rows, vis_len, gathered, vector, latent, pos_e, ordered, 4
    )
    sizes = chunk_sizes(groups)
    chunk_of, place_of = tile_places(sizes)

    rows_cut = BS // parts

    def gradients(chunk, pairs, vector_tile=None):
        used = sum(r * c for _, r, c, _ in CHUNKS[chunk])
        at, buffers = 0, None
        if sizes[chunk] > used:
            if vector_tile is None:
                vector_tile = jnp.zeros((parts, rows_cut, BS), F32)
            buffers = seed_buffers(index, parts, sizes[chunk], used, vector_tile)
        for (x, g), (_, row_tiles, col_tiles, block) in zip(pairs, CHUNKS[chunk]):
            buffers = weight_grad(index, parts, sizes[chunk], at, x, g, block, buffers)
            at += row_tiles * col_tiles
        return buffers

    after = lax.optimization_barrier
    buf0 = gradients(
        0, [(d_h2, d_du), (d_act, d_gdown), (d_att, d_gproj), (d_h1, d_dqkv), (d_hn, d_gpred), (hn, glat)]
    )
    glat, buf0 = after((glat, buf0))
    gdown, du, grad_mid, gproj, m_sums = encoder_mlp_back(tile_rows, gathered, vector, glat, x1, mid, slope, 2)
    half0, left0 = reduce_core(buf0, parts)
    gdown, du, gproj, half0 = after((gdown, du, gproj, half0))
    buf1 = gradients(1, [(h2, du), (act, gdown), (att, gproj)])
    half0, left0 = reduce_chips((half0, left0), parts, 1)
    gproj, buf1, half0 = after((gproj, buf1, half0))

    def attention_back(gproj, k, given):
        return encoder_attention_back(
            tile_rows, vis_len, gathered, vector, gproj, grad_mid, qkv, lse, out_t, x0, 2, (k, 2), given
        )

    dqkv, gembed, a_sums = attention_back(gproj, 0, ())
    half0, left0 = reduce_chips((half0, left0), parts, 99)
    half1, left1 = reduce_core(buf1, parts)
    gproj, dqkv, gembed, half0, half1 = after((gproj, dqkv, gembed, half0, half1))
    dqkv, gembed, b_sums = attention_back(gproj, 1, (dqkv, gembed))
    half1, left1 = reduce_chips((half1, left1), parts, 1)
    dqkv, gembed, b_sums, half0, half1 = after((dqkv, gembed, b_sums, half0, half1))
    a_sums = a_sums + b_sums
    d_sums, m_sums, a_sums = (jnp.sum(s, axis=0) for s in (d_sums, m_sums, a_sums))

    def cut(sums, start, size):
        return sums[start : start + size]

    grad_vector = jnp.concatenate(
        [
            cut(a_sums, EA_EMBED, D),
            cut(a_sums, EA_G1, 2 * D),
            cut(a_sums, EA_QKV, D),
            cut(a_sums, EA_QKV + 2 * D, D),
            cut(m_sums, EM_BO, D),
            cut(m_sums, EM_G2, 2 * D),
            cut(m_sums, EM_BU, FE),
            cut(m_sums, EM_BD, D),
            cut(m_sums, EM_NORM, 2 * D),
            cut(m_sums, EM_PROJ, E),
            cut(d_sums, DS_MASK, E),
            cut(d_sums, DS["g1"], 2 * E),
            cut(d_sums, DS["bqkv"], E),
            cut(d_sums, DS["bqkv"] + 2 * E, E),
            cut(d_sums, DS["bo"], E),
            cut(d_sums, DS["g2"], 2 * E),
            cut(d_sums, DS["bu"], FD),
            cut(d_sums, DS["bd"], E),
            cut(d_sums, DS_NORM, 2 * E),
            cut(d_sums, DS_HEAD, PIX),
        ]
    )
    vector_tile = jnp.pad(grad_vector.reshape(parts, own), ((0, 0), (0, rows_cut * BS - own)))
    vector_tile = vector_tile.reshape(parts, rows_cut, BS)
    buf2 = gradients(2, [(h1, dqkv), (visible_pix.reshape(-1, PIX), gembed)], vector_tile)
    half1, _ = reduce_chips((half1, left1), parts, 99)
    steps = patch_steps(groups)
    half0 = [sum_patch(x, steps[:1]) for x in half0]
    buf2, half0, half1 = after((buf2, half0, half1))
    half2, _ = reduce_chips(reduce_core(buf2, parts), parts, 99)
    pieces = [sum_patch(x, steps[1:]) for x in half0] + [sum_patch(x, steps) for x in half1 + half2]
    mine = jnp.where(lax.axis_index("patch") == 0, 1.0, 0.0)

    def squares(x):
        wide = x.astype(F32)
        return jnp.sum(wide * wide)

    totals = jnp.stack(
        [
            jnp.sum(cut(d_sums, DS_LOSS, PIX)) / PIX,
            jnp.sum(POS - vis_len).astype(F32),
            sum(squares(x) for x in pieces) * mine,
        ]
    )
    totals = sum_all(totals, parts, groups)
    loss_sum, masked_count = totals[0], totals[1]
    grad_norm = jnp.sqrt(totals[2]) / masked_count
    scale = jnp.minimum(1.0, CLIP_NORM / grad_norm) / masked_count

    reduced = jnp.concatenate(pieces, axis=0)
    where = jnp.asarray(np.cumsum([0] + sizes)[chunk_of] + place_of, jnp.int32)
    slot_rows = reduced[where[jnp.minimum(block_owner, NBLK)]]
    if parts > 1:
        slot_rows = lax.all_to_all(slot_rows, "dp", 0, 0, tiled=True)
    grads = slot_rows.reshape(parts, slots, rows_cut, BS)
    clipped, left_new, right_new, weights_new = tile_update(
        scale, grads, (weights, left_stat, right_stat, left_root, right_root)
    )
    own_vector = lax.dynamic_index_in_dim(reduced, where[NBLK + 1], 0, keepdims=False)
    own_vector = own_vector.reshape(-1)[:own].astype(F32) * scale
    moment_new, second_new, vectors_new = vector_update(own_vector, vectors, vec_moment, vec_second)
    return (
        loss_sum,
        masked_count,
        grad_norm,
        clipped,
        left_new,
        right_new,
        weights_new,
        moment_new,
        second_new,
        vectors_new,
    )


def solution(mesh):
    both = ("dp", "patch")
    tiles = P("dp", None, None)
    return jax.shard_map(
        functools.partial(shards, mesh.shape["dp"], mesh.shape["patch"]),
        mesh=mesh,
        in_specs=(P(both, None, None), P(both, None), P(both), P())
        + (tiles, P("dp"), P("dp"), P("dp"))
        + (tiles,) * 4,
        out_specs=(P(), P(), P()) + (tiles,) * 4 + (P("dp"),) * 3,
        check_vma=False,
    )
```

```python
import functools
import math

import jax
import jax.numpy as jnp
import numpy as np
from jax import lax
from jax.experimental import pallas as pl
from jax.experimental.pallas import tpu as pltpu
from jax.sharding import PartitionSpec as P

D = 768
HE = 12
FE = 3072
E = 512
HD = 16
FD = 2048
PIX = 768
POS = 196
VMAX = 80
BS = 256
STEP = 10
NBLK = 177

SD = 208

EPS_NORM = 1e-06
EPS_ROOT = 1e-06
EPS_ADAM = 1e-08
CLIP_NORM = 0.01
RATE_MATRIX = 0.03
DECAY_MATRIX = 0.05
BETA_STAT = 0.5
BETA_FIRST = 0.9
BETA_SECOND = 0.999
RATE_VECTOR = 0.1
NEG_LARGE = -1e30
LOG2E = math.log2(math.e)

BF = jnp.bfloat16
F32 = jnp.float32
VMEM_LIMIT = 60 * 1024 * 1024
SMALL = pl.CostEstimate(flops=1000, bytes_accessed=1000, transcendentals=0)

T_EMBED, T_EQKV, T_EOUT, T_EUP, T_EDOWN, T_PROJ = 0, 9, 36, 45, 81, 117
T_DQKV, T_DOUT, T_DUP, T_DDOWN, T_HEAD = 123, 135, 139, 155, 171

V_EMBED = 0
V_ENC = D
V_ENORM = V_ENC + 9 * D + FE
V_PROJ = V_ENORM + 2 * D
V_MASK = V_PROJ + E
V_DEC = V_MASK + E
V_DNORM = V_DEC + 9 * E + FD
V_HEAD = V_DNORM + 2 * E
V_ALL = V_HEAD + PIX


def layer_offsets(start, width, hidden):
    names = ["g1", "s1", "bqkv", "bo", "g2", "s2", "bu", "bd"]
    sizes = [width, width, 3 * width, width, width, width, hidden, width]
    offsets = {}
    for name, size in zip(names, sizes):
        offsets[name] = start
        start += size
    return offsets


def mm(a, b):
    return jnp.dot(a, b, preferred_element_type=F32)


def mm_nt(a, b):
    return lax.dot_general(a, b, (((1,), (1,)), ((), ())), preferred_element_type=F32)


def mm_tn(a, b):
    return lax.dot_general(a, b, (((0,), (0,)), ((), ())), preferred_element_type=F32)


def fold8(x):
    rows, cols = x.shape
    return jnp.sum(x.reshape(rows // 8, 8, cols), axis=0)


def gelu_pair(u):
    t = 1.0 / (1.0 + (0.3275911 * math.sqrt(0.5)) * jnp.abs(u))
    e = jnp.exp2((-0.5 * LOG2E) * (u * u))
    poly = t * (
        0.5 * 0.254829592
        + t * (-0.5 * 0.284496736 + t * (0.5 * 1.421413741 + t * (-0.5 * 1.453152027 + t * (0.5 * 1.061405429))))
    )
    tail = poly * e
    phi = jnp.where(u >= 0, 1.0 - tail, tail)
    return u * phi, phi + u * (e * (1.0 / math.sqrt(2.0 * math.pi)))


def norm_parts(x):
    centred = x - jnp.mean(x, axis=-1, keepdims=True)
    inverse = lax.rsqrt(jnp.mean(centred * centred, axis=-1, keepdims=True) + EPS_NORM)
    return centred * inverse, inverse


def loop(lower, upper, body, carry, most=26):
    count = upper - lower
    unroll = max(u for u in range(1, min(most, count) + 1) if count % u == 0)
    return lax.fori_loop(lower, upper, body, carry, unroll=unroll)


def row_loop(rows, step, body, carry=0):
    count = rows // step

    def one(i, c):
        return body(pl.ds(pl.multiple_of(i * step, step), step), c)

    return loop(0, count, one, carry)


def norm_forward(x_ref, gain, shift, out_ref):
    def body(sl, c):
        normed, _ = norm_parts(x_ref[sl, :])
        out_ref[sl, :] = (normed * gain + shift).astype(BF)
        return c

    row_loop(x_ref.shape[0], 16, body)


def norm_backward(x_ref, dy_ref, gain, out_ref, add):
    width = x_ref.shape[1]

    def body(sl, c):
        d_gain, d_shift = c
        normed, inverse = norm_parts(x_ref[sl, :])
        dy = dy_ref[sl, :]
        dn = dy * gain
        mean_one = jnp.mean(dn, axis=-1, keepdims=True)
        mean_two = jnp.mean(dn * normed, axis=-1, keepdims=True)
        dx = inverse * (dn - mean_one - normed * mean_two)
        out_ref[sl, :] = out_ref[sl, :] + dx if add else dx
        return (d_gain + fold8(dy * normed), d_shift + fold8(dy))

    zero = jnp.zeros((8, width), F32)
    return row_loop(x_ref.shape[0], 16, body, (zero, zero))


def col_loop(count, body):
    def one(j, c):
        body(j, pl.ds(pl.multiple_of(j * BS, BS), BS))
        return c

    loop(0, count, one, 0, 4)


def vec_at(vec_ref, start, j):
    return vec_ref[:, pl.ds(pl.multiple_of(start + j * BS, BS), BS)]


def head_mask(head, head_size):
    lane = lax.broadcasted_iota(jnp.int32, (1, BS), 1)
    inside = (lane >= head * head_size) & (lane < (head + 1) * head_size)
    return jnp.where(inside, 1.0, 0.0).astype(BF)


def masked_scores(k_masked, q, head_size, count):
    scores = mm(k_masked, q) * (head_size**-0.5 * LOG2E)
    if isinstance(count, int):
        whole = count // 8 * 8
        tail = scores[whole:]
        row = lax.broadcasted_iota(jnp.int32, tail.shape, 0) + whole
        return jnp.concatenate([scores[:whole], jnp.where(row < count, tail, NEG_LARGE)], axis=0)
    row = lax.broadcasted_iota(jnp.int32, (scores.shape[0], 1), 0)
    return jnp.where(row < count, scores, NEG_LARGE)


def scores_bounded(qkv_ref, width, head_size):
    lane = lax.broadcasted_iota(jnp.int32, (BS, 128), 0) // head_size
    pick = jnp.where(lane == lax.broadcasted_iota(jnp.int32, (BS, 128), 1), 1.0, 0.0).astype(BF)
    score, value = None, None
    for g in range(width // BS):
        tops = []
        for which in range(3):
            x = qkv_ref[:, which * width + g * BS : which * width + (g + 1) * BS]
            tops.append(jnp.max(mm(x * x, pick), axis=0, keepdims=True))
        one = tops[0] * tops[1]
        score = one if score is None else jnp.maximum(score, one)
        value = tops[2] if value is None else jnp.maximum(value, tops[2])
    limit = 90.0 / (1.05 * head_size**-0.5 * LOG2E)
    return (jnp.max(score) < limit * limit) & (jnp.max(value) < 2.0**40)


def attention_forward(qkv_ref, att_ref, out_t_ref, lse_ref, image, seq, width, head_size, count, bounded):
    rows = pl.ds(pl.multiple_of(image * seq, 16), seq)
    per = BS // head_size

    def group(g, c):
        def part(which):
            return qkv_ref[rows, pl.ds(pl.multiple_of(which * width + g * BS, BS), BS)]

        q, k, v = part(0), part(1), part(2)
        v_t = v.T
        q = q.T
        ones = jnp.ones((16, seq), BF)
        outs, logs = [], []
        for h in range(per):
            scores = masked_scores(k * head_mask(h, head_size), q, head_size, count)
            top = 0.0
            if not bounded:
                top = jnp.max(scores, axis=0, keepdims=True)
                scores = scores - top
            e = jnp.exp2(scores).astype(BF)
            both = mm(jnp.concatenate([v_t[h * head_size : (h + 1) * head_size, :], ones], axis=0), e)
            total = both[head_size : head_size + 1, :]
            outs.append(both[:head_size, :] * (1.0 / total))
            logs.append(top + jnp.log2(total))
        out_t = jnp.concatenate(outs, axis=0)
        out_t_ref[image, g] = out_t
        att_ref[rows, pl.ds(pl.multiple_of(g * BS, BS), BS)] = out_t.T.astype(BF)
        lse_ref[image, g] = jnp.concatenate(logs, axis=0)
        return c

    loop(0, width // BS, group, 0)


def attend_all(qkv_ref, att_ref, out_t_ref, lse_ref, images, seq, width, head_size, count_of):
    safe = scores_bounded(qkv_ref, width, head_size)

    def run(bounded):
        def one(image, c):
            count = count_of(image)
            attention_forward(
                qkv_ref, att_ref, out_t_ref, lse_ref, image, seq, width, head_size, count, bounded
            )
            return c

        lax.fori_loop(0, images, one, 0)

    @pl.when(safe)
    def _():
        run(True)

    @pl.when(jnp.logical_not(safe))
    def _():
        run(False)


def attention_backward(qkv_ref, datt_ref, out_t_ref, lse_ref, dqkv_ref, image, seq, width, head_size, count):
    rows = pl.ds(pl.multiple_of(image * seq, 16), seq)
    per = BS // head_size
    scale = head_size**-0.5

    def group(g, c):
        def cols(which):
            return pl.ds(pl.multiple_of(which * width + g * BS, BS), BS)

        q, k, v = qkv_ref[rows, cols(0)], qkv_ref[rows, cols(1)], qkv_ref[rows, cols(2)]
        d_out = datt_ref[rows, cols(0)]
        lse = lse_ref[image, g]
        q_t, k_t, d_out_t = q.T, k.T, d_out.T
        along = d_out_t.astype(F32) * out_t_ref[image, g]
        d_q, d_k, d_v = [], jnp.zeros((seq, BS), F32), jnp.zeros((seq, BS), F32)
        for h in range(per):
            mask = head_mask(h, head_size)
            part = slice(h * head_size, (h + 1) * head_size)
            delta = jnp.sum(along[part, :], axis=0, keepdims=True)
            probs = jnp.exp2(masked_scores(k * mask, q_t, head_size, count) - lse[h : h + 1, :])
            d_scores = (probs * (mm(v * mask, d_out_t) - delta)).astype(BF)
            d_v = d_v + mm(probs.astype(BF), d_out * mask)
            d_k = d_k + mm(d_scores, q * mask)
            d_q.append(mm(k_t[part, :], d_scores))
        dqkv_ref[rows, cols(0)] = (jnp.concatenate(d_q, axis=0).T * scale).astype(BF)
        dqkv_ref[rows, cols(1)] = (d_k * scale).astype(BF)
        dqkv_ref[rows, cols(2)] = d_v.astype(BF)
        return c

    loop(0, width // BS, group, 0)


def fetch_tiles(row_ref, wg_ref, first, dst, sem):
    row_tiles, col_tiles = dst.shape[0] // BS, dst.shape[1] // BS
    for i in range(row_tiles):
        for j in range(col_tiles):
            start = pl.multiple_of(row_ref[first + i * col_tiles + j], 16)
            pltpu.make_async_copy(
                wg_ref.at[pl.ds(start, BS), :],
                dst.at[i * BS : (i + 1) * BS, j * BS : (j + 1) * BS],
                sem,
            ).start()


def await_tiles(dst, sem):
    pltpu.make_async_copy(dst, dst, sem).wait()


def fetch_all(first_step, row_ref, wg_ref, sems, matrices):
    @pl.when(first_step)
    def _():
        for i, (first, dst) in enumerate(matrices):
            fetch_tiles(row_ref, wg_ref, first, dst, sems.at[i])

    def ready(i):
        @pl.when(first_step)
        def _():
            await_tiles(matrices[i][1], sems.at[i])

    return ready


def qkv_forward(h_ref, w_ref, vec_ref, start, out_ref):
    def body(j, cols):
        out_ref[:, cols] = (mm(h_ref[...], w_ref[:, cols]) + vec_at(vec_ref, start, j)).astype(BF)

    col_loop(w_ref.shape[1] // BS, body)


def add_linear(x_ref, h_ref, w_ref, vec_ref, start, out_ref):
    def body(j, cols):
        out_ref[:, cols] = x_ref[:, cols] + (mm(h_ref[...], w_ref[:, cols]) + vec_at(vec_ref, start, j))

    col_loop(w_ref.shape[1] // BS, body)


def up_forward(h_ref, w_ref, vec_ref, start, act_ref, slope_ref):
    def body(j, cols):
        act, slope = gelu_pair(mm(h_ref[...], w_ref[:, cols]) + vec_at(vec_ref, start, j))
        act_ref[:, cols] = act.astype(BF)
        slope_ref[:, cols] = slope.astype(BF)

    col_loop(w_ref.shape[1] // BS, body)


def back_linear(g_ref, w_ref, out_ref):
    def body(j, cols):
        out_ref[:, cols] = mm_nt(g_ref[...], w_ref[cols, :])

    col_loop(w_ref.shape[0] // BS, body)


def back_up(g_ref, w_ref, slope_ref, du_ref, sum_ref, start):
    def body(j, cols):
        du = (mm_nt(g_ref[...], w_ref[cols, :]) * slope_ref[:, cols].astype(F32)).astype(BF)
        du_ref[:, cols] = du
        at = pl.ds(pl.multiple_of(start + j * BS, BS), BS)
        sum_ref[:, at] = sum_ref[:, at] + fold8(du.astype(F32))

    col_loop(w_ref.shape[0] // BS, body)


def round_and_sum(x_ref, out_ref, sum_ref, start):
    width = x_ref.shape[1]

    def body(sl, c):
        low = x_ref[sl, :].astype(BF)
        out_ref[sl, :] = low
        return c + fold8(low.astype(F32))

    total = row_loop(x_ref.shape[0], 16, body, jnp.zeros((8, width), F32))
    sum_ref[:, start : start + width] = sum_ref[:, start : start + width] + total


def sum_rows(x_ref, sum_ref, start):
    width = x_ref.shape[1]

    def body(sl, c):
        return c + fold8(x_ref[sl, :].astype(F32))

    total = row_loop(x_ref.shape[0], 16, body, jnp.zeros((8, width), F32))
    sum_ref[:, start : start + width] = sum_ref[:, start : start + width] + total


def add_sum(sum_ref, start, value):
    stop = start + value.shape[1]
    sum_ref[:, start:stop] = sum_ref[:, start:stop] + value


def order_kernel(shuffle_ref, pixels_ref, sin_d_ref, sin_e_ref, all_ref, visible_ref, pos_d_ref, pos_e_ref):
    ids = shuffle_ref[0]
    pick = jnp.where(ids == lax.broadcasted_iota(jnp.int32, (SD, POS), 1), 1.0, 0.0).astype(BF)
    ordered = mm(pick, pixels_ref[0]).astype(BF)
    all_ref[0] = ordered
    visible_ref[0] = ordered[:VMAX, :]
    few = pick[:VMAX, :]
    pos_d_ref[0] = mm(few, sin_d_ref[0]) + mm(few, sin_d_ref[1])
    pos_e_ref[0] = mm(pick, sin_e_ref[0]) + mm(pick, sin_e_ref[1])


def sinusoid_parts(count, width):
    half = width // 2
    frequency = np.exp(np.arange(half) * (-np.log(10000.0) / half))
    angles = np.arange(count)[:, None] * frequency[None, :]
    table = np.concatenate([np.sin(angles), np.cos(angles)], axis=1).astype(np.float32)
    high = table.astype(jnp.bfloat16)
    low = (table - high.astype(np.float32)).astype(jnp.bfloat16)
    return np.stack([high, low])


def order_patches(pixels, shuffle):
    images = pixels.shape[0]
    ids = jnp.pad(shuffle, ((0, 0), (0, SD - POS)), constant_values=-1)[:, :, None]

    def image(*dims):
        return pl.BlockSpec((1,) + dims, lambda b: (b,) + (0,) * len(dims))

    def whole(*dims):
        return pl.BlockSpec(dims, lambda b: (0,) * len(dims))

    return pl.pallas_call(
        order_kernel,
        grid=(images,),
        in_specs=[image(SD, 1), image(POS, PIX), whole(2, POS, D), whole(2, POS, E)],
        out_specs=[image(SD, PIX), image(VMAX, PIX), image(VMAX, D), image(SD, E)],
        out_shape=[
            jax.ShapeDtypeStruct((images, SD, PIX), BF),
            jax.ShapeDtypeStruct((images, VMAX, PIX), BF),
            jax.ShapeDtypeStruct((images, VMAX, D), F32),
            jax.ShapeDtypeStruct((images, SD, E), F32),
        ],
        compiler_params=pltpu.CompilerParams(vmem_limit_bytes=VMEM_LIMIT),
        name="order_patches",
    )(ids, pixels, jnp.asarray(sinusoid_parts(POS, D)), jnp.asarray(sinusoid_parts(POS, E)))


def group_call(kernel, steps, prefetch, in_arrays, out_list, scratch, name, share=(0, 1), given=()):
    count = steps // share[1]
    start = share[0] * count

    def spec(shape, kind):
        if kind == "any":
            return pl.BlockSpec(memory_space=pl.ANY)
        if kind == "rows":
            block = (shape[0] // steps,) + tuple(shape[1:])
            return pl.BlockSpec(block, lambda i, *_: (start + i,) + (0,) * (len(shape) - 1))
        return pl.BlockSpec(tuple(shape), lambda i, *_: (0,) * len(shape))

    first_given = len(prefetch) + len(in_arrays)
    return pl.pallas_call(
        functools.partial(kernel, start, len(given)),
        grid_spec=pltpu.PrefetchScalarGridSpec(
            num_scalar_prefetch=len(prefetch),
            grid=(count,),
            in_specs=[spec(a.shape, kind) for a, kind in in_arrays] + [pl.BlockSpec(memory_space=pl.ANY)] * len(given),
            out_specs=[spec(shape, kind) for shape, _, kind in out_list],
            scratch_shapes=scratch,
        ),
        out_shape=[jax.ShapeDtypeStruct(shape, dtype) for shape, dtype, _ in out_list],
        input_output_aliases={first_given + i: i for i in range(len(given))},
        compiler_params=pltpu.CompilerParams(
            vmem_limit_bytes=VMEM_LIMIT, dimension_semantics=("arbitrary",)
        ),
        cost_estimate=SMALL,
        name=name,
    )(*prefetch, *[a for a, _ in in_arrays], *given)


ENC = layer_offsets(V_ENC, D, FE)
DEC = layer_offsets(V_DEC, E, FD)


def encoder_forward_kernel(
    start, given, row_ref, len_ref, wg_ref, vec_ref, pix_ref, pos_ref,
    x0_ref, h1_ref, qkv_ref, lse_ref, out_t_ref, att_ref, mid_ref, h2_ref, act_ref, slope_ref, x1_ref, hn_ref, latent_ref,
    w_embed, w_qkv, w_out, w_up, w_down, w_proj, sems,
):
    step = pl.program_id(0)
    images = lse_ref.shape[0]
    ready = fetch_all(
        step == 0,
        row_ref,
        wg_ref,
        sems,
        [
            (T_EMBED, w_embed),
            (T_EQKV, w_qkv),
            (T_EOUT, w_out),
            (T_EUP, w_up),
            (T_EDOWN, w_down),
            (T_PROJ, w_proj),
        ],
    )

    def vec(start, size=D):
        return vec_ref[:, start : start + size]

    ready(0)
    add_linear(pos_ref, pix_ref, w_embed, vec_ref, V_EMBED, x0_ref)
    norm_forward(x0_ref, vec(ENC["g1"]), vec(ENC["s1"]), h1_ref)
    ready(1)
    qkv_forward(h1_ref, w_qkv, vec_ref, ENC["bqkv"], qkv_ref)

    attend_all(
        qkv_ref, att_ref, out_t_ref, lse_ref, images, VMAX, D, D // HE, lambda i: len_ref[step * images + i]
    )
    ready(2)
    add_linear(x0_ref, att_ref, w_out, vec_ref, ENC["bo"], mid_ref)
    norm_forward(mid_ref, vec(ENC["g2"]), vec(ENC["s2"]), h2_ref)
    ready(3)
    up_forward(h2_ref, w_up, vec_ref, ENC["bu"], act_ref, slope_ref)
    ready(4)
    add_linear(mid_ref, act_ref, w_down, vec_ref, ENC["bd"], x1_ref)
    norm_forward(x1_ref, vec(V_ENORM), vec(V_ENORM + D), hn_ref)
    ready(5)

    def project(j, cols):
        latent_ref[:, cols] = mm(hn_ref[...], w_proj[:, cols]) + vec_at(vec_ref, V_PROJ, j)

    col_loop(E // BS, project)


def encoder_forward(tile_rows, vis_len, gathered, vector, visible_pix, pos_d, steps):
    images = vis_len.shape[0]
    rows = images * VMAX
    outs = [
        ((rows, D), F32, "rows"),
        ((rows, D), BF, "rows"),
        ((rows, 3 * D), BF, "rows"),
        ((images, D // BS, BS * HE // D, VMAX), F32, "rows"),
        ((images, D // BS, BS, VMAX), F32, "rows"),
        ((rows, D), BF, "rows"),
        ((rows, D), F32, "rows"),
        ((rows, D), BF, "rows"),
        ((rows, FE), BF, "rows"),
        ((rows, FE), BF, "rows"),
        ((rows, D), F32, "rows"),
        ((rows, D), BF, "rows"),
        ((rows, E), F32, "rows"),
    ]
    scratch = [pltpu.VMEM(s, BF) for s in [(PIX, D), (D, 3 * D), (D, D), (D, FE), (FE, D), (D, E)]]
    return group_call(
        encoder_forward_kernel,
        steps,
        (tile_rows, vis_len),
        [
            (gathered, "any"),
            (vector, "whole"),
            (visible_pix.reshape(rows, PIX), "rows"),
            (pos_d.reshape(rows, D), "rows"),
        ],
        outs,
        scratch + [pltpu.SemaphoreType.DMA((6,))],
        "encoder_forward",
    )


DS = layer_offsets(0, E, FD)
DS_NORM = 9 * E + FD
DS_HEAD = DS_NORM + 2 * E
DS_MASK = DS_HEAD + PIX
DS_LOSS = DS_MASK + E
DS_ALL = DS_LOSS + PIX


def decoder_kernel(
    start, given, row_ref, len_ref, wg_ref, vec_ref, latent_ref, pos_ref, pix_ref,
    h1_ref, dqkv_ref, att_ref, gproj_ref, h2_ref, du_ref, act_ref, gdown_ref, hn_ref, gpred_ref, glat_ref, sum_ref,
    w_qkv, w_out, w_up, w_down, w_head, x0, qkv, lse, out_t, mid, slope, x1, pred, dy, grad, datt, sems,
):
    step = pl.program_id(0)
    images = lse.shape[0]
    ready = fetch_all(
        step == 0,
        row_ref,
        wg_ref,
        sems,
        [(T_DQKV, w_qkv), (T_DOUT, w_out), (T_DUP, w_up), (T_DDOWN, w_down), (T_HEAD, w_head)],
    )

    @pl.when(step == 0)
    def _():
        sum_ref[...] = jnp.zeros_like(sum_ref)

    def vec(start, size=E):
        return vec_ref[:, start : start + size]

    def length(image):
        return len_ref[step * images + image]

    chunk = 16
    order = lax.broadcasted_iota(jnp.int32, (chunk, 1), 0)
    token = vec(V_MASK)

    def place(image, c):
        def head_rows(i, c):
            at = pl.ds(pl.multiple_of(image * SD + i * chunk, chunk), chunk)
            got = latent_ref[pl.ds(pl.multiple_of(image * VMAX + i * chunk, chunk), chunk), :]
            x0[at, :] = jnp.where(i * chunk + order < length(image), got, token) + pos_ref[at, :]
            return c

        def tail_rows(i, c):
            at = pl.ds(pl.multiple_of(image * SD + i * chunk, chunk), chunk)
            x0[at, :] = token + pos_ref[at, :]
            return c

        loop(0, VMAX // chunk, head_rows, 0)
        loop(VMAX // chunk, SD // chunk, tail_rows, 0)
        return c

    lax.fori_loop(0, images, place, 0)
    norm_forward(x0, vec(DEC["g1"]), vec(DEC["s1"]), h1_ref)
    ready(0)
    qkv_forward(h1_ref, w_qkv, vec_ref, DEC["bqkv"], qkv)
    attend_all(qkv, att_ref, out_t, lse, images, SD, E, E // HD, lambda i: POS)
    ready(1)
    add_linear(x0, att_ref, w_out, vec_ref, DEC["bo"], mid)
    norm_forward(mid, vec(DEC["g2"]), vec(DEC["s2"]), h2_ref)
    ready(2)
    up_forward(h2_ref, w_up, vec_ref, DEC["bu"], act_ref, slope)
    ready(3)
    add_linear(mid, act_ref, w_down, vec_ref, DEC["bd"], x1)
    norm_forward(x1, vec(V_DNORM), vec(V_DNORM + E), hn_ref)
    ready(4)

    def predict(j, cols):
        pred[:, cols] = mm(hn_ref[...], w_head[:, cols]) + vec_at(vec_ref, V_HEAD, j)

    col_loop(PIX // BS, predict)

    def errors(image, c):
        def one(i, c):
            loss, bias = c
            at = pl.ds(pl.multiple_of(image * SD + i * chunk, chunk), chunk)
            target, _ = norm_parts(pix_ref[at, :].astype(F32))
            place_in = i * chunk + order
            masked = (place_in >= length(image)) & (place_in < POS)
            residual = jnp.where(masked, pred[at, :] - target, 0.0)
            low = (residual * (2.0 / PIX)).astype(BF)
            gpred_ref[at, :] = low
            return (loss + fold8(residual * residual), bias + fold8(low.astype(F32)))

        return loop(0, SD // chunk, one, c)

    zero = jnp.zeros((8, PIX), F32)
    loss, bias = lax.fori_loop(0, images, errors, (zero, zero))
    add_sum(sum_ref, DS_LOSS, loss)
    add_sum(sum_ref, DS_HEAD, bias)

    back_linear(gpred_ref, w_head, dy)
    d_gain, d_shift = norm_backward(x1, dy, vec(V_DNORM), grad, False)
    add_sum(sum_ref, DS_NORM, d_gain)
    add_sum(sum_ref, DS_NORM + E, d_shift)
    round_and_sum(grad, gdown_ref, sum_ref, DS["bd"])
    back_up(gdown_ref, w_down, slope, du_ref, sum_ref, DS["bu"])
    back_linear(du_ref, w_up, dy)
    d_gain, d_shift = norm_backward(mid, dy, vec(DEC["g2"]), grad, True)
    add_sum(sum_ref, DS["g2"], d_gain)
    add_sum(sum_ref, DS["s2"], d_shift)
    round_and_sum(grad, gproj_ref, sum_ref, DS["bo"])

    def back_out(j, cols):
        datt[:, cols] = mm_nt(gproj_ref[...], w_out[cols, :]).astype(BF)

    col_loop(E // BS, back_out)

    def attend_back(image, c):
        attention_backward(qkv, datt, out_t, lse, dqkv_ref, image, SD, E, E // HD, POS)
        return c

    lax.fori_loop(0, images, attend_back, 0)
    sum_rows(dqkv_ref, sum_ref, DS["bqkv"])
    back_linear(dqkv_ref, w_qkv, dy)
    d_gain, d_shift = norm_backward(x0, dy, vec(DEC["g1"]), grad, True)
    add_sum(sum_ref, DS["g1"], d_gain)
    add_sum(sum_ref, DS["s1"], d_shift)

    def unplace(image, c):
        def head_rows(i, c):
            got = grad[pl.ds(pl.multiple_of(image * SD + i * chunk, chunk), chunk), :]
            seen = i * chunk + order < length(image)
            at = pl.ds(pl.multiple_of(image * VMAX + i * chunk, chunk), chunk)
            glat_ref[at, :] = jnp.where(seen, got, 0.0).astype(BF)
            return c + fold8(jnp.where(seen, 0.0, got))

        def tail_rows(i, c):
            got = grad[pl.ds(pl.multiple_of(image * SD + i * chunk, chunk), chunk), :]
            return c + fold8(jnp.where(i * chunk + order < POS, got, 0.0))

        c = loop(0, VMAX // chunk, head_rows, c)
        return loop(VMAX // chunk, SD // chunk, tail_rows, c)

    add_sum(sum_ref, DS_MASK, lax.fori_loop(0, images, unplace, jnp.zeros((8, E), F32)))


def decoder(tile_rows, vis_len, gathered, vector, latent, pos_e, ordered, steps):
    images = vis_len.shape[0]
    rows = images * SD
    part = rows // steps
    outs = [
        ((rows, E), BF, "rows"),
        ((rows, 3 * E), BF, "rows"),
        ((rows, E), BF, "rows"),
        ((rows, E), BF, "rows"),
        ((rows, E), BF, "rows"),
        ((rows, FD), BF, "rows"),
        ((rows, FD), BF, "rows"),
        ((rows, E), BF, "rows"),
        ((rows, E), BF, "rows"),
        ((rows, PIX), BF, "rows"),
        ((images * VMAX, E), BF, "rows"),
        ((8, DS_ALL), F32, "whole"),
    ]
    scratch = [pltpu.VMEM(s, BF) for s in [(E, 3 * E), (E, E), (E, FD), (FD, E), (E, PIX)]]
    scratch += [
        pltpu.VMEM((part, E), F32),
        pltpu.VMEM((part, 3 * E), BF),
        pltpu.VMEM((images // steps, E // BS, BS * HD // E, SD), F32),
        pltpu.VMEM((images // steps, E // BS, BS, SD), F32),
        pltpu.VMEM((part, E), F32),
        pltpu.VMEM((part, FD), BF),
        pltpu.VMEM((part, E), F32),
        pltpu.VMEM((part, PIX), F32),
        pltpu.VMEM((part, E), F32),
        pltpu.VMEM((part, E), F32),
        pltpu.VMEM((part, E), BF),
        pltpu.SemaphoreType.DMA((5,)),
    ]
    return group_call(
        decoder_kernel,
        steps,
        (tile_rows, vis_len),
        [
            (gathered, "any"),
            (vector, "whole"),
            (latent, "rows"),
            (pos_e.reshape(rows, E), "rows"),
            (ordered.reshape(rows, PIX), "rows"),
        ],
        outs,
        scratch,
        "decoder",
    )


EM_BD, EM_BU = 0, D
EM_G2, EM_S2 = D + FE, 2 * D + FE
EM_BO, EM_NORM = 3 * D + FE, 4 * D + FE
EM_PROJ = 6 * D + FE
EM_ALL = EM_PROJ + E
EA_QKV, EA_G1, EA_S1, EA_EMBED, EA_ALL = 0, 3 * D, 4 * D, 5 * D, 6 * D


def encoder_mlp_back_kernel(
    start, given, row_ref, wg_ref, vec_ref, glat_ref, x1_ref, mid_ref, slope_ref,
    gdown_ref, du_ref, grad_ref, gproj_ref, sum_ref,
    w_proj, w_down, w_up, dy, sems,
):
    step = pl.program_id(0)
    ready = fetch_all(
        step == 0, row_ref, wg_ref, sems, [(T_PROJ, w_proj), (T_EDOWN, w_down), (T_EUP, w_up)]
    )

    @pl.when(step == 0)
    def _():
        sum_ref[...] = jnp.zeros_like(sum_ref)

    def vec(start):
        return vec_ref[:, start : start + D]

    sum_rows(glat_ref, sum_ref, EM_PROJ)
    ready(0)
    back_linear(glat_ref, w_proj, dy)
    d_gain, d_shift = norm_backward(x1_ref, dy, vec(V_ENORM), grad_ref, False)
    add_sum(sum_ref, EM_NORM, d_gain)
    add_sum(sum_ref, EM_NORM + D, d_shift)
    round_and_sum(grad_ref, gdown_ref, sum_ref, EM_BD)
    ready(1)
    back_up(gdown_ref, w_down, slope_ref, du_ref, sum_ref, EM_BU)
    ready(2)
    back_linear(du_ref, w_up, dy)
    d_gain, d_shift = norm_backward(mid_ref, dy, vec(ENC["g2"]), grad_ref, True)
    add_sum(sum_ref, EM_G2, d_gain)
    add_sum(sum_ref, EM_S2, d_shift)
    round_and_sum(grad_ref, gproj_ref, sum_ref, EM_BO)


def encoder_mlp_back(tile_rows, gathered, vector, glat, x1, mid, slope, steps):
    rows = x1.shape[0]
    part = rows // steps
    outs = [
        ((rows, D), BF, "rows"),
        ((rows, FE), BF, "rows"),
        ((rows, D), F32, "rows"),
        ((rows, D), BF, "rows"),
        ((8, EM_ALL), F32, "whole"),
    ]
    scratch = [pltpu.VMEM(s, BF) for s in [(D, E), (FE, D), (D, FE)]]
    scratch += [pltpu.VMEM((part, D), F32), pltpu.SemaphoreType.DMA((3,))]
    return group_call(
        encoder_mlp_back_kernel,
        steps,
        (tile_rows,),
        [
            (gathered, "any"),
            (vector, "whole"),
            (glat, "rows"),
            (x1, "rows"),
            (mid, "rows"),
            (slope, "rows"),
        ],
        outs,
        scratch,
        "encoder_mlp_back",
    )


def encoder_attention_back_kernel(
    start, given, row_ref, len_ref, wg_ref, vec_ref, gproj_ref, grad_in_ref, qkv_ref, lse_ref, out_t_ref, x0_ref, *refs
):
    dqkv_ref, gembed_ref, sum_ref, w_out, w_qkv, dy, grad, datt, sems = refs[given:]
    step = pl.program_id(0)
    images = lse_ref.shape[0]
    ready = fetch_all(step == 0, row_ref, wg_ref, sems, [(T_EOUT, w_out), (T_EQKV, w_qkv)])

    @pl.when(step == 0)
    def _():
        sum_ref[...] = jnp.zeros_like(sum_ref)

    ready(0)

    def back_out(j, cols):
        datt[:, cols] = mm_nt(gproj_ref[...], w_out[cols, :]).astype(BF)

    col_loop(D // BS, back_out)

    def attend_back(image, c):
        count = len_ref[(start + step) * images + image]
        attention_backward(qkv_ref, datt, out_t_ref, lse_ref, dqkv_ref, image, VMAX, D, D // HE, count)
        return c

    lax.fori_loop(0, images, attend_back, 0)
    sum_rows(dqkv_ref, sum_ref, EA_QKV)
    ready(1)
    back_linear(dqkv_ref, w_qkv, dy)
    grad[...] = grad_in_ref[...]
    gain = vec_ref[:, ENC["g1"] : ENC["g1"] + D]
    d_gain, d_shift = norm_backward(x0_ref, dy, gain, grad, True)
    add_sum(sum_ref, EA_G1, d_gain)
    add_sum(sum_ref, EA_S1, d_shift)
    round_and_sum(grad, gembed_ref, sum_ref, EA_EMBED)


def encoder_attention_back(tile_rows, vis_len, gathered, vector, gproj, grad, qkv, lse, out_t, x0, steps, share, given):
    rows = x0.shape[0]
    part = rows // steps
    outs = [((rows, 3 * D), BF, "rows"), ((rows, D), BF, "rows"), ((8, EA_ALL), F32, "whole")]
    scratch = [pltpu.VMEM(s, BF) for s in [(D, D), (D, 3 * D)]]
    scratch += [pltpu.VMEM((part, D), F32), pltpu.VMEM((part, D), F32), pltpu.VMEM((part, D), BF)]
    return group_call(
        encoder_attention_back_kernel,
        steps,
        (tile_rows, vis_len),
        [
            (gathered, "any"),
            (vector, "whole"),
            (gproj, "rows"),
            (grad, "rows"),
            (qkv, "rows"),
            (lse, "rows"),
            (out_t, "rows"),
            (x0, "rows"),
        ],
        outs,
        scratch + [pltpu.SemaphoreType.DMA((2,))],
        "encoder_attention_back",
        share,
        given,
    )


def weight_grad_kernel(parts, cut, extra, index_ref, x_ref, g_ref, *refs):
    outs = refs[extra : extra + min(parts, 2)]
    x_t, total = refs[-2:]
    row_tiles, col_tiles = x_ref.shape[1] // BS, g_ref.shape[1] // BS

    @pl.when(pl.program_id(1) == 0)
    def _():
        x_t[...] = x_ref[...].T

    total[...] = mm(x_t[...], g_ref[...])
    for p in range(parts):
        for i in range(row_tiles):
            start = pl.multiple_of(i * BS + (p ^ index_ref[0]) * cut, cut)
            for j in range(col_tiles):
                got = total[pl.ds(start, cut), j * BS : (j + 1) * BS]
                outs[p % 2][p // 2, i * col_tiles + j] = got.astype(BF)


def weight_grad(index, parts, count, first, x, g, block, buffers):
    cut = BS // parts
    rows, width = x.shape
    row_tiles, col_tiles = block
    size = row_tiles * col_tiles
    across = g.shape[1] // (col_tiles * BS)
    assert first % size == 0
    held = min(parts, 2)
    shape = jax.ShapeDtypeStruct((parts // held, count, cut, BS), BF)
    given = list(buffers or [])
    out_spec = pl.BlockSpec(
        (parts // held, size, cut, BS), lambda i, j, *_: (0, first // size + i * across + j, 0, 0)
    )
    return pl.pallas_call(
        functools.partial(weight_grad_kernel, parts, cut, len(given)),
        grid_spec=pltpu.PrefetchScalarGridSpec(
            num_scalar_prefetch=1,
            grid=(width // (row_tiles * BS), across),
            in_specs=[
                pl.BlockSpec((rows, row_tiles * BS), lambda i, j, *_: (0, i)),
                pl.BlockSpec((rows, col_tiles * BS), lambda i, j, *_: (0, j)),
            ]
            + [pl.BlockSpec(memory_space=pl.ANY)] * len(given),
            out_specs=[out_spec] * held,
            scratch_shapes=[
                pltpu.VMEM((row_tiles * BS, rows), BF),
                pltpu.VMEM((row_tiles * BS, col_tiles * BS), F32),
            ],
        ),
        out_shape=[shape] * held,
        input_output_aliases={3 + i: i for i in range(len(given))},
        compiler_params=pltpu.CompilerParams(vmem_limit_bytes=VMEM_LIMIT),
        cost_estimate=SMALL,
        name="weight_grad",
    )(index, x, g, *given)


def seed_kernel(parts, parcels, own, index_ref, *refs):
    sums, outs, rows = refs[: -1 - min(parts, 2)], refs[-1 - min(parts, 2) : -1], refs[-1]
    rows[...] = jnp.zeros_like(rows)
    at = 0
    for source, start, size in parcels:
        for k in range(0, size, 128):
            piece = sum(jnp.sum(sums[i][:, start + k : start + k + 128], axis=0, keepdims=True) for i in source)
            row, col = at % own // BS, at % own % BS
            rows[at // own, row : row + 1, col : col + 128] = piece
            at += 128
    for p in range(parts):
        out = outs[p % 2]
        out[p // 2, 0] = rows[p ^ index_ref[0]].astype(BF)
        for t in range(1, out.shape[1]):
            out[p // 2, t] = jnp.zeros(rows.shape[1:], BF)


def seed_buffers(index, parts, count, first, sums=(), parcels=(), own=1):
    cut = BS // parts
    held = min(parts, 2)
    size = count - first
    assert first % size == 0
    shape = jax.ShapeDtypeStruct((parts // held, count, cut, BS), BF)
    return pl.pallas_call(
        functools.partial(seed_kernel, parts, parcels, own),
        grid_spec=pltpu.PrefetchScalarGridSpec(
            num_scalar_prefetch=1,
            grid=(1,),
            in_specs=[pl.BlockSpec(x.shape, lambda i, *_: (0, 0)) for x in sums],
            out_specs=[pl.BlockSpec((parts // held, size, cut, BS), lambda i, *_: (0, first // size, 0, 0))] * held,
            scratch_shapes=[pltpu.VMEM((parts, cut, BS), F32)],
        ),
        out_shape=[shape] * held,
        cost_estimate=SMALL,
        name="seed_buffers",
    )(index, *sums)


def low_sum(a, b):
    return (a.astype(F32) + b.astype(F32)).astype(BF)


def swap_bit(x, bit, size):
    return lax.ppermute(x, "dp", [(i, i ^ (1 << bit)) for i in range(size)])


def reduce_core(buffers, parts):
    if parts == 1:
        whole, count = buffers[0][0], buffers[0].shape[1]
        return [whole[: count // 2], whole[count // 2 :]], [[], []]
    whole = low_sum(buffers[0], swap_bit(buffers[1], 0, parts))
    bits = list(range(parts.bit_length() - 2, 0, -1))
    whole = whole.reshape((2,) * len(bits) + whole.shape[1:])
    count = whole.shape[-3]
    return [whole[..., : count // 2, :, :], whole[..., count // 2 :, :, :]], [bits, bits]


def reduce_chips(state, parts, steps):
    halves, left = list(state[0]), list(state[1])
    for half in range(2):
        for _ in range(min(steps, len(left[half]))):
            bit = left[half][-1 if half == 0 else 0]
            axis = left[half].index(bit)
            keep = lax.index_in_dim(halves[half], 0, axis, keepdims=False)
            send = lax.index_in_dim(halves[half], 1, axis, keepdims=False)
            halves[half] = low_sum(keep, swap_bit(send, bit, parts))
            left[half] = [b for b in left[half] if b != bit]
    return halves, left


def patch_steps(groups):
    middle = groups // 2 - 1

    def inwards(k, x):
        return low_sum(x, lax.ppermute(x, "patch", [(k, k + 1), (groups - 1 - k, groups - 2 - k)]))

    def across(x):
        return low_sum(x, lax.ppermute(x, "patch", [(middle, middle + 1), (middle + 1, middle)]))

    def outwards(k, x):
        got = lax.ppermute(x, "patch", [(k + 1, k), (groups - 2 - k, groups - 1 - k)])
        me = lax.axis_index("patch")
        return jnp.where((me == k) | (me == groups - 1 - k), got, x)

    if groups == 1:
        return []
    steps = [functools.partial(inwards, k) for k in range(middle)] + [across]
    return steps + [functools.partial(outwards, k) for k in reversed(range(middle))]


def sum_patch(x, steps):
    for step in steps:
        x = step(x)
    return x


def sum_all(x, parts, groups):
    for bit in range(groups.bit_length() - 1):
        x = x + lax.ppermute(x, "patch", [(i, i ^ (1 << bit)) for i in range(groups)])
    return sum_dp(x, parts)


def sum_dp(x, parts):
    for bit in range(parts.bit_length() - 1):
        x = x + swap_bit(x, bit, parts)
    return x


def split_low(x):
    high = x.astype(BF)
    return high, (x - high.astype(F32)).astype(BF)


def tile_kernel(
    scale_ref, grad_ref, w_ref, left_stat_ref, right_stat_ref, left_root_ref, right_root_ref,
    clipped_ref, left_new_ref, right_new_ref, w_new_ref,
):
    scale = scale_ref[0]
    for t in range(w_ref.shape[0]):
        grad = grad_ref[:, t].reshape(BS, BS)
        clipped_ref[t] = grad.astype(F32) * scale
        square = (1.0 - BETA_STAT) * scale * scale
        left_new_ref[t] = BETA_STAT * left_stat_ref[t] + square * mm_nt(grad, grad)
        right_new_ref[t] = BETA_STAT * right_stat_ref[t] + square * mm_tn(grad, grad)
        high, low = split_low(left_root_ref[t])
        half = (mm(high, grad) + mm(low, grad)) * scale
        half_high, half_low = split_low(half)
        high, low = split_low(right_root_ref[t])
        direction = mm(half_high, high) + (mm(half_high, low) + mm(half_low, high))
        direction = direction * lax.rsqrt(jnp.mean(direction * direction) + EPS_ROOT)
        w_new_ref[t] = w_ref[t] - RATE_MATRIX * (direction + DECAY_MATRIX * w_ref[t])


def tile_update(scale, grads, states):
    parts, slots, cut, _ = grads.shape
    per = max(p for p in range(1, 7) if slots % p == 0)
    tile = pl.BlockSpec((per, BS, BS), lambda i, *_: (i, 0, 0))
    return pl.pallas_call(
        tile_kernel,
        grid_spec=pltpu.PrefetchScalarGridSpec(
            num_scalar_prefetch=1,
            grid=(slots // per,),
            in_specs=[pl.BlockSpec((parts, per, cut, BS), lambda i, *_: (0, i, 0, 0))] + [tile] * 5,
            out_specs=[tile] * 4,
        ),
        out_shape=[jax.ShapeDtypeStruct((slots, BS, BS), F32)] * 4,
        compiler_params=pltpu.CompilerParams(vmem_limit_bytes=VMEM_LIMIT),
        name="tile_update",
    )(scale.reshape(1), grads, *states)


def vector_update(clipped, vectors, moment, second):
    moment_new = BETA_FIRST * moment + (1.0 - BETA_FIRST) * clipped
    second_new = BETA_SECOND * second + (1.0 - BETA_SECOND) * clipped * clipped
    corrected = moment_new / (1.0 - BETA_FIRST**STEP)
    scaled = second_new / (1.0 - BETA_SECOND**STEP)
    vectors_new = vectors - RATE_VECTOR * corrected / (jnp.sqrt(scaled) + EPS_ADAM)
    return moment_new, second_new, vectors_new


CHUNKS = [
    [
        (T_DUP, 2, 8, (2, 4)),
        (T_DDOWN, 8, 2, (4, 2)),
        (T_DOUT, 2, 2, (2, 2)),
        (T_DQKV, 2, 6, (2, 3)),
        (T_HEAD, 2, 3, (2, 3)),
        (T_PROJ, 3, 2, (3, 2)),
    ],
    [(T_EUP, 3, 12, (3, 4)), (T_EDOWN, 12, 3, (4, 3)), (T_EOUT, 3, 3, (3, 3))],
    [(T_EQKV, 3, 9, (3, 3)), (T_EMBED, 3, 3, (3, 3))],
]


def chunk_sizes():
    sizes = [sum(r * c for _, r, c, _ in chunk) for chunk in CHUNKS]
    return sizes[:-1] + [sizes[-1] + 2]


def tile_places(sizes):
    chunk_of = np.zeros(NBLK + 2, np.int32)
    place_of = np.zeros(NBLK + 2, np.int32)
    for i, chunk in enumerate(CHUNKS):
        at = 0
        for first, row_tiles, col_tiles, (high, wide) in chunk:
            for r in range(row_tiles):
                for c in range(col_tiles):
                    block = r // high * (col_tiles // wide) + c // wide
                    chunk_of[first + r * col_tiles + c] = i
                    place_of[first + r * col_tiles + c] = at + block * high * wide + r % high * wide + c % wide
            at += row_tiles * col_tiles
    chunk_of[NBLK:] = len(CHUNKS) - 1
    place_of[NBLK + 1] = at
    place_of[NBLK] = at + 1
    return chunk_of, place_of


def shards(parts, groups, pixels, shuffle, vis_len, block_owner, weights, vectors, vec_moment, vec_second,
           left_stat, right_stat, left_root, right_root):
    slots = weights.shape[0]
    own = vectors.shape[0]
    index = lax.axis_index("dp").astype(jnp.int32).reshape(1)
    images = pixels.shape[0]

    vector_rows = -(-own // (16 * BS)) * 16
    mine = jnp.concatenate(
        [
            weights.astype(BF).reshape(slots * BS, BS),
            jnp.pad(vectors.astype(BF), (0, vector_rows * BS - own)).reshape(vector_rows, BS),
        ]
    )
    gathered = lax.all_gather(mine, "dp", axis=0, tiled=True)
    stride = mine.shape[0]
    slot_index = jnp.arange(block_owner.shape[0], dtype=jnp.int32)
    slot_of_block = jnp.sum(
        jnp.where(block_owner[None, :] == jnp.arange(NBLK, dtype=jnp.int32)[:, None], slot_index[None, :], 0),
        axis=1,
    )
    tile_rows = slot_of_block // slots * stride + slot_of_block % slots * BS
    vector = gathered.reshape(parts, stride, BS)[:, slots * BS :].reshape(parts, vector_rows * BS)
    vector = vector[:, :own].reshape(-1).astype(F32)
    enc_key, dec_key = 4 * D, 4 * D + (8 * D + FE - 3 * D) + 2 * D + 2 * E + 3 * E
    vector = jnp.concatenate(
        [vector[:enc_key], jnp.zeros(D, F32), vector[enc_key:dec_key], jnp.zeros(E, F32), vector[dec_key:]]
    ).reshape(1, V_ALL)

    ordered, visible_pix, pos_d, pos_e = order_patches(pixels, shuffle)
    (x0, h1, qkv, lse, out_t, att, mid, h2, act, slope, x1, hn, latent) = encoder_forward(
        tile_rows, vis_len, gathered, vector, visible_pix, pos_d, 2
    )
    (d_h1, d_dqkv, d_att, d_gproj, d_h2, d_du, d_act, d_gdown, d_hn, d_gpred, glat, d_sums) = decoder(
        tile_rows, vis_len, gathered, vector, latent, pos_e, ordered, 4
    )
    sizes = chunk_sizes()
    chunk_of, place_of = tile_places(sizes)

    rows_cut = BS // parts

    def gradients(chunk, pairs, *vector):
        used = sum(r * c for _, r, c, _ in CHUNKS[chunk])
        at, buffers = 0, None
        if sizes[chunk] > used:
            buffers = seed_buffers(index, parts, sizes[chunk], used, *vector)
        for (x, g), (_, row_tiles, col_tiles, block) in zip(pairs, CHUNKS[chunk]):
            buffers = weight_grad(index, parts, sizes[chunk], at, x, g, block, buffers)
            at += row_tiles * col_tiles
        return buffers

    after = lax.optimization_barrier
    buf0 = gradients(
        0, [(d_h2, d_du), (d_act, d_gdown), (d_att, d_gproj), (d_h1, d_dqkv), (d_hn, d_gpred), (hn, glat)]
    )
    glat, buf0 = after((glat, buf0))
    gdown, du, grad_mid, gproj, m_sums = encoder_mlp_back(tile_rows, gathered, vector, glat, x1, mid, slope, 2)
    half0, left0 = reduce_core(buf0, parts)
    gdown, du, gproj, half0 = after((gdown, du, gproj, half0))
    buf1 = gradients(1, [(h2, du), (act, gdown), (att, gproj)])
    half0, left0 = reduce_chips((half0, left0), parts, 1)
    gproj, buf1, half0 = after((gproj, buf1, half0))

    def attention_back(gproj, k, given):
        return encoder_attention_back(
            tile_rows, vis_len, gathered, vector, gproj, grad_mid, qkv, lse, out_t, x0, 2, (k, 2), given
        )

    dqkv, gembed, a_sums = attention_back(gproj, 0, ())
    half0, left0 = reduce_chips((half0, left0), parts, 99)
    half1, left1 = reduce_core(buf1, parts)
    gproj, dqkv, gembed, half0, half1 = after((gproj, dqkv, gembed, half0, half1))
    dqkv, gembed, b_sums = attention_back(gproj, 1, (dqkv, gembed))
    half1, left1 = reduce_chips((half1, left1), parts, 1)
    dqkv, gembed, b_sums, half0, half1 = after((dqkv, gembed, b_sums, half0, half1))

    late, early, dec = (0, 1), (2,), (3,)
    parcels = [
        (late, EA_EMBED, D),
        (late, EA_G1, 2 * D),
        (late, EA_QKV, D),
        (late, EA_QKV + 2 * D, D),
        (early, EM_BO, D),
        (early, EM_G2, 2 * D),
        (early, EM_BU, FE),
        (early, EM_BD, D),
        (early, EM_NORM, 2 * D),
        (early, EM_PROJ, E),
        (dec, DS_MASK, E),
        (dec, DS["g1"], 2 * E),
        (dec, DS["bqkv"], E),
        (dec, DS["bqkv"] + 2 * E, E),
        (dec, DS["bo"], E),
        (dec, DS["g2"], 2 * E),
        (dec, DS["bu"], FD),
        (dec, DS["bd"], E),
        (dec, DS_NORM, 2 * E),
        (dec, DS_HEAD, PIX),
    ]
    buf2 = gradients(2, [(h1, dqkv), (visible_pix.reshape(-1, PIX), gembed)], (a_sums, b_sums, m_sums, d_sums), parcels, own)
    half1, _ = reduce_chips((half1, left1), parts, 99)
    steps = patch_steps(groups)
    half0 = [sum_patch(x, steps[:1]) for x in half0]
    buf2, half0, half1 = after((buf2, half0, half1))
    half2, left2 = reduce_core(buf2, parts)
    half1, half2 = after((half1, half2))
    half2, _ = reduce_chips((half2, left2), parts, 99)
    pieces = [sum_patch(x, steps[1:]) for x in half0] + [sum_patch(x, steps) for x in half1 + half2]
    mine = jnp.where(lax.axis_index("patch") == 0, 1.0, 0.0)

    def squares(x):
        wide = x.astype(F32)
        return jnp.sum(wide * wide)

    totals = jnp.stack(
        [
            jnp.sum(d_sums[:, DS_LOSS : DS_LOSS + PIX]) / PIX,
            jnp.sum(POS - vis_len).astype(F32),
            sum(squares(x) for x in pieces) * mine,
        ]
    )
    totals = sum_all(totals, parts, groups)
    loss_sum, masked_count = totals[0], totals[1]
    grad_norm = jnp.sqrt(totals[2]) / masked_count
    scale = jnp.minimum(1.0, CLIP_NORM / grad_norm) / masked_count

    reduced = jnp.concatenate(pieces, axis=0)
    where = jnp.asarray(np.cumsum([0] + sizes)[chunk_of] + place_of, jnp.int32)
    slot_rows = reduced[where[jnp.minimum(block_owner, NBLK)]]
    if parts > 1:
        slot_rows = lax.all_to_all(slot_rows, "dp", 0, 0, tiled=True)
    grads = slot_rows.reshape(parts, slots, rows_cut, BS)
    clipped, left_new, right_new, weights_new = tile_update(
        scale, grads, (weights, left_stat, right_stat, left_root, right_root)
    )
    own_vector = lax.dynamic_index_in_dim(reduced, where[NBLK + 1], 0, keepdims=False)
    own_vector = own_vector.reshape(-1)[:own].astype(F32) * scale
    moment_new, second_new, vectors_new = vector_update(own_vector, vectors, vec_moment, vec_second)
    return (
        loss_sum,
        masked_count,
        grad_norm,
        clipped,
        left_new,
        right_new,
        weights_new,
        moment_new,
        second_new,
        vectors_new,
    )


def solution(mesh):
    both = ("dp", "patch")
    tiles = P("dp", None, None)
    return jax.shard_map(
        functools.partial(shards, mesh.shape["dp"], mesh.shape["patch"]),
        mesh=mesh,
        in_specs=(P(both, None, None), P(both, None), P(both), P())
        + (tiles, P("dp"), P("dp"), P("dp"))
        + (tiles,) * 4,
        out_specs=(P(), P(), P()) + (tiles,) * 4 + (P("dp"),) * 3,
        check_vma=False,
    )
```

```python
import functools
import math

import jax
import jax.numpy as jnp
import numpy as np
from jax import lax
from jax.experimental import pallas as pl
from jax.experimental.pallas import tpu as pltpu
from jax.sharding import PartitionSpec as P

D = 768
HE = 12
FE = 3072
E = 512
HD = 16
FD = 2048
PIX = 768
POS = 196
VMAX = 80
BS = 256
STEP = 10
NBLK = 177

SD = 208

EPS_NORM = 1e-06
EPS_ROOT = 1e-06
EPS_ADAM = 1e-08
CLIP_NORM = 0.01
RATE_MATRIX = 0.03
DECAY_MATRIX = 0.05
BETA_STAT = 0.5
BETA_FIRST = 0.9
BETA_SECOND = 0.999
RATE_VECTOR = 0.1
NEG_LARGE = -1e30
LOG2E = math.log2(math.e)

BF = jnp.bfloat16
F32 = jnp.float32
VMEM_LIMIT = 60 * 1024 * 1024
SMALL = pl.CostEstimate(flops=1000, bytes_accessed=1000, transcendentals=0)

T_EMBED, T_EQKV, T_EOUT, T_EUP, T_EDOWN, T_PROJ = 0, 9, 36, 45, 81, 117
T_DQKV, T_DOUT, T_DUP, T_DDOWN, T_HEAD = 123, 135, 139, 155, 171

V_EMBED = 0
V_ENC = D
V_ENORM = V_ENC + 9 * D + FE
V_PROJ = V_ENORM + 2 * D
V_MASK = V_PROJ + E
V_DEC = V_MASK + E
V_DNORM = V_DEC + 9 * E + FD
V_HEAD = V_DNORM + 2 * E
V_ALL = V_HEAD + PIX


def layer_offsets(start, width, hidden):
    names = ["g1", "s1", "bqkv", "bo", "g2", "s2", "bu", "bd"]
    sizes = [width, width, 3 * width, width, width, width, hidden, width]
    offsets = {}
    for name, size in zip(names, sizes):
        offsets[name] = start
        start += size
    return offsets


def mm(a, b):
    return jnp.dot(a, b, preferred_element_type=F32)


def mm_nt(a, b):
    return lax.dot_general(a, b, (((1,), (1,)), ((), ())), preferred_element_type=F32)


def mm_tn(a, b):
    return lax.dot_general(a, b, (((0,), (0,)), ((), ())), preferred_element_type=F32)


def fold8(x):
    rows, cols = x.shape
    return jnp.sum(x.reshape(rows // 8, 8, cols), axis=0)


def gelu_pair(u):
    t = 1.0 / (1.0 + (0.3275911 * math.sqrt(0.5)) * jnp.abs(u))
    e = jnp.exp2((-0.5 * LOG2E) * (u * u))
    poly = t * (
        0.5 * 0.254829592
        + t * (-0.5 * 0.284496736 + t * (0.5 * 1.421413741 + t * (-0.5 * 1.453152027 + t * (0.5 * 1.061405429))))
    )
    tail = poly * e
    phi = jnp.where(u >= 0, 1.0 - tail, tail)
    return u * phi, phi + u * (e * (1.0 / math.sqrt(2.0 * math.pi)))


def norm_parts(x):
    centred = x - jnp.mean(x, axis=-1, keepdims=True)
    inverse = lax.rsqrt(jnp.mean(centred * centred, axis=-1, keepdims=True) + EPS_NORM)
    return centred * inverse, inverse


def loop(lower, upper, body, carry, most=26):
    count = upper - lower
    unroll = max(u for u in range(1, min(most, count) + 1) if count % u == 0)
    return lax.fori_loop(lower, upper, body, carry, unroll=unroll)


def row_loop(rows, step, body, carry=0):
    count = rows // step

    def one(i, c):
        return body(pl.ds(pl.multiple_of(i * step, step), step), c)

    return loop(0, count, one, carry)


def norm_forward(x_ref, gain, shift, out_ref):
    def body(sl, c):
        normed, _ = norm_parts(x_ref[sl, :])
        out_ref[sl, :] = (normed * gain + shift).astype(BF)
        return c

    row_loop(x_ref.shape[0], 16, body)


def norm_backward(x_ref, dy_ref, gain, out_ref, add):
    width = x_ref.shape[1]

    def body(sl, c):
        d_gain, d_shift = c
        normed, inverse = norm_parts(x_ref[sl, :])
        dy = dy_ref[sl, :]
        dn = dy * gain
        mean_one = jnp.mean(dn, axis=-1, keepdims=True)
        mean_two = jnp.mean(dn * normed, axis=-1, keepdims=True)
        dx = inverse * (dn - mean_one - normed * mean_two)
        out_ref[sl, :] = out_ref[sl, :] + dx if add else dx
        return (d_gain + fold8(dy * normed), d_shift + fold8(dy))

    zero = jnp.zeros((8, width), F32)
    return row_loop(x_ref.shape[0], 16, body, (zero, zero))


def col_loop(count, body):
    def one(j, c):
        body(j, pl.ds(pl.multiple_of(j * BS, BS), BS))
        return c

    loop(0, count, one, 0, 4)


def vec_at(vec_ref, start, j):
    return vec_ref[:, pl.ds(pl.multiple_of(start + j * BS, BS), BS)]


def head_mask(head, head_size):
    lane = lax.broadcasted_iota(jnp.int32, (1, BS), 1)
    inside = (lane >= head * head_size) & (lane < (head + 1) * head_size)
    return jnp.where(inside, 1.0, 0.0).astype(BF)


def masked_scores(k_masked, q, head_size, count):
    scores = mm(k_masked, q) * (head_size**-0.5 * LOG2E)
    if isinstance(count, int):
        whole = count // 8 * 8
        tail = scores[whole:]
        row = lax.broadcasted_iota(jnp.int32, tail.shape, 0) + whole
        return jnp.concatenate([scores[:whole], jnp.where(row < count, tail, NEG_LARGE)], axis=0)
    row = lax.broadcasted_iota(jnp.int32, (scores.shape[0], 1), 0)
    return jnp.where(row < count, scores, NEG_LARGE)


def scores_bounded(qkv_ref, width, head_size):
    lane = lax.broadcasted_iota(jnp.int32, (BS, 128), 0) // head_size
    pick = jnp.where(lane == lax.broadcasted_iota(jnp.int32, (BS, 128), 1), 1.0, 0.0).astype(BF)
    score, value = None, None
    for g in range(width // BS):
        tops = []
        for which in range(3):
            x = qkv_ref[:, which * width + g * BS : which * width + (g + 1) * BS]
            tops.append(jnp.max(mm(x * x, pick), axis=0, keepdims=True))
        one = tops[0] * tops[1]
        score = one if score is None else jnp.maximum(score, one)
        value = tops[2] if value is None else jnp.maximum(value, tops[2])
    limit = 90.0 / (1.05 * head_size**-0.5 * LOG2E)
    return (jnp.max(score) < limit * limit) & (jnp.max(value) < 2.0**40)


def attention_forward(qkv_ref, att_ref, out_t_ref, lse_ref, image, seq, width, head_size, count, bounded):
    rows = pl.ds(pl.multiple_of(image * seq, 16), seq)
    per = BS // head_size

    def group(g, c):
        def part(which):
            return qkv_ref[rows, pl.ds(pl.multiple_of(which * width + g * BS, BS), BS)]

        q, k, v = part(0), part(1), part(2)
        v_t = v.T
        q = q.T
        ones = jnp.ones((16, seq), BF)
        outs, logs = [], []
        for h in range(per):
            scores = masked_scores(k * head_mask(h, head_size), q, head_size, count)
            top = 0.0
            if not bounded:
                top = jnp.max(scores, axis=0, keepdims=True)
                scores = scores - top
            e = jnp.exp2(scores).astype(BF)
            both = mm(jnp.concatenate([v_t[h * head_size : (h + 1) * head_size, :], ones], axis=0), e)
            total = both[head_size : head_size + 1, :]
            outs.append(both[:head_size, :] * (1.0 / total))
            logs.append(top + jnp.log2(total))
        out_t = jnp.concatenate(outs, axis=0)
        out_t_ref[image, g] = out_t
        att_ref[rows, pl.ds(pl.multiple_of(g * BS, BS), BS)] = out_t.T.astype(BF)
        lse_ref[image, g] = jnp.concatenate(logs, axis=0)
        return c

    loop(0, width // BS, group, 0)


def attend_all(qkv_ref, att_ref, out_t_ref, lse_ref, images, seq, width, head_size, count_of):
    safe = scores_bounded(qkv_ref, width, head_size)

    def run(bounded):
        def one(image, c):
            count = count_of(image)
            attention_forward(
                qkv_ref, att_ref, out_t_ref, lse_ref, image, seq, width, head_size, count, bounded
            )
            return c

        lax.fori_loop(0, images, one, 0)

    @pl.when(safe)
    def _():
        run(True)

    @pl.when(jnp.logical_not(safe))
    def _():
        run(False)


def attention_backward(qkv_ref, datt_ref, out_t_ref, lse_ref, dqkv_ref, image, seq, width, head_size, count):
    rows = pl.ds(pl.multiple_of(image * seq, 16), seq)
    per = BS // head_size
    scale = head_size**-0.5

    def group(g, c):
        def cols(which):
            return pl.ds(pl.multiple_of(which * width + g * BS, BS), BS)

        q, k, v = qkv_ref[rows, cols(0)], qkv_ref[rows, cols(1)], qkv_ref[rows, cols(2)]
        d_out = datt_ref[rows, cols(0)]
        lse = lse_ref[image, g]
        q_t, k_t, d_out_t = q.T, k.T, d_out.T
        along = d_out_t.astype(F32) * out_t_ref[image, g]
        d_q, d_k, d_v = [], jnp.zeros((seq, BS), F32), jnp.zeros((seq, BS), F32)
        for h in range(per):
            mask = head_mask(h, head_size)
            part = slice(h * head_size, (h + 1) * head_size)
            delta = jnp.sum(along[part, :], axis=0, keepdims=True)
            probs = jnp.exp2(masked_scores(k * mask, q_t, head_size, count) - lse[h : h + 1, :])
            d_scores = (probs * (mm(v * mask, d_out_t) - delta)).astype(BF)
            d_v = d_v + mm(probs.astype(BF), d_out * mask)
            d_k = d_k + mm(d_scores, q * mask)
            d_q.append(mm(k_t[part, :], d_scores))
        dqkv_ref[rows, cols(0)] = (jnp.concatenate(d_q, axis=0).T * scale).astype(BF)
        dqkv_ref[rows, cols(1)] = (d_k * scale).astype(BF)
        dqkv_ref[rows, cols(2)] = d_v.astype(BF)
        return c

    loop(0, width // BS, group, 0)


def fetch_tiles(row_ref, wg_ref, first, dst, sem):
    row_tiles, col_tiles = dst.shape[0] // BS, dst.shape[1] // BS
    for i in range(row_tiles):
        for j in range(col_tiles):
            start = pl.multiple_of(row_ref[first + i * col_tiles + j], 16)
            pltpu.make_async_copy(
                wg_ref.at[pl.ds(start, BS), :],
                dst.at[i * BS : (i + 1) * BS, j * BS : (j + 1) * BS],
                sem,
            ).start()


def await_tiles(dst, sem):
    pltpu.make_async_copy(dst, dst, sem).wait()


def fetch_all(first_step, row_ref, wg_ref, sems, matrices):
    @pl.when(first_step)
    def _():
        for i, (first, dst) in enumerate(matrices):
            fetch_tiles(row_ref, wg_ref, first, dst, sems.at[i])

    def ready(i):
        @pl.when(first_step)
        def _():
            await_tiles(matrices[i][1], sems.at[i])

    return ready


def qkv_forward(h_ref, w_ref, vec_ref, start, out_ref):
    def body(j, cols):
        out_ref[:, cols] = (mm(h_ref[...], w_ref[:, cols]) + vec_at(vec_ref, start, j)).astype(BF)

    col_loop(w_ref.shape[1] // BS, body)


def add_linear(x_ref, h_ref, w_ref, vec_ref, start, out_ref):
    def body(j, cols):
        out_ref[:, cols] = x_ref[:, cols] + (mm(h_ref[...], w_ref[:, cols]) + vec_at(vec_ref, start, j))

    col_loop(w_ref.shape[1] // BS, body)


def up_forward(h_ref, w_ref, vec_ref, start, act_ref, slope_ref):
    def body(j, cols):
        act, slope = gelu_pair(mm(h_ref[...], w_ref[:, cols]) + vec_at(vec_ref, start, j))
        act_ref[:, cols] = act.astype(BF)
        slope_ref[:, cols] = slope.astype(BF)

    col_loop(w_ref.shape[1] // BS, body)


def back_linear(g_ref, w_ref, out_ref):
    def body(j, cols):
        out_ref[:, cols] = mm_nt(g_ref[...], w_ref[cols, :])

    col_loop(w_ref.shape[0] // BS, body)


def back_up(g_ref, w_ref, slope_ref, du_ref, sum_ref, start):
    def body(j, cols):
        du = (mm_nt(g_ref[...], w_ref[cols, :]) * slope_ref[:, cols].astype(F32)).astype(BF)
        du_ref[:, cols] = du
        at = pl.ds(pl.multiple_of(start + j * BS, BS), BS)
        sum_ref[:, at] = sum_ref[:, at] + fold8(du.astype(F32))

    col_loop(w_ref.shape[0] // BS, body)


def round_and_sum(x_ref, out_ref, sum_ref, start):
    width = x_ref.shape[1]

    def body(sl, c):
        low = x_ref[sl, :].astype(BF)
        out_ref[sl, :] = low
        return c + fold8(low.astype(F32))

    total = row_loop(x_ref.shape[0], 16, body, jnp.zeros((8, width), F32))
    sum_ref[:, start : start + width] = sum_ref[:, start : start + width] + total


def sum_rows(x_ref, sum_ref, start):
    width = x_ref.shape[1]

    def body(sl, c):
        return c + fold8(x_ref[sl, :].astype(F32))

    total = row_loop(x_ref.shape[0], 16, body, jnp.zeros((8, width), F32))
    sum_ref[:, start : start + width] = sum_ref[:, start : start + width] + total


def add_sum(sum_ref, start, value):
    stop = start + value.shape[1]
    sum_ref[:, start:stop] = sum_ref[:, start:stop] + value


def order_kernel(shuffle_ref, pixels_ref, sin_d_ref, sin_e_ref, all_ref, visible_ref, pos_d_ref, pos_e_ref):
    ids = shuffle_ref[0]
    pick = jnp.where(ids == lax.broadcasted_iota(jnp.int32, (SD, POS), 1), 1.0, 0.0).astype(BF)
    ordered = mm(pick, pixels_ref[0]).astype(BF)
    all_ref[0] = ordered
    visible_ref[0] = ordered[:VMAX, :]
    few = pick[:VMAX, :]
    pos_d_ref[0] = mm(few, sin_d_ref[0]) + mm(few, sin_d_ref[1])
    pos_e_ref[0] = mm(pick, sin_e_ref[0]) + mm(pick, sin_e_ref[1])


def sinusoid_parts(count, width):
    half = width // 2
    frequency = np.exp(np.arange(half) * (-np.log(10000.0) / half))
    angles = np.arange(count)[:, None] * frequency[None, :]
    table = np.concatenate([np.sin(angles), np.cos(angles)], axis=1).astype(np.float32)
    high = table.astype(jnp.bfloat16)
    low = (table - high.astype(np.float32)).astype(jnp.bfloat16)
    return np.stack([high, low])


def order_patches(pixels, shuffle):
    images = pixels.shape[0]
    ids = jnp.pad(shuffle, ((0, 0), (0, SD - POS)), constant_values=-1)[:, :, None]

    def image(*dims):
        return pl.BlockSpec((1,) + dims, lambda b: (b,) + (0,) * len(dims))

    def whole(*dims):
        return pl.BlockSpec(dims, lambda b: (0,) * len(dims))

    return pl.pallas_call(
        order_kernel,
        grid=(images,),
        in_specs=[image(SD, 1), image(POS, PIX), whole(2, POS, D), whole(2, POS, E)],
        out_specs=[image(SD, PIX), image(VMAX, PIX), image(VMAX, D), image(SD, E)],
        out_shape=[
            jax.ShapeDtypeStruct((images, SD, PIX), BF),
            jax.ShapeDtypeStruct((images, VMAX, PIX), BF),
            jax.ShapeDtypeStruct((images, VMAX, D), F32),
            jax.ShapeDtypeStruct((images, SD, E), F32),
        ],
        compiler_params=pltpu.CompilerParams(vmem_limit_bytes=VMEM_LIMIT),
        name="order_patches",
    )(ids, pixels, jnp.asarray(sinusoid_parts(POS, D)), jnp.asarray(sinusoid_parts(POS, E)))


def group_call(kernel, steps, prefetch, in_arrays, out_list, scratch, name, share=(0, 1), given=()):
    count = steps // share[1]
    start = share[0] * count

    def spec(shape, kind):
        if kind == "any":
            return pl.BlockSpec(memory_space=pl.ANY)
        if kind == "rows":
            block = (shape[0] // steps,) + tuple(shape[1:])
            return pl.BlockSpec(block, lambda i, *_: (start + i,) + (0,) * (len(shape) - 1))
        return pl.BlockSpec(tuple(shape), lambda i, *_: (0,) * len(shape))

    first_given = len(prefetch) + len(in_arrays)
    return pl.pallas_call(
        functools.partial(kernel, start, len(given)),
        grid_spec=pltpu.PrefetchScalarGridSpec(
            num_scalar_prefetch=len(prefetch),
            grid=(count,),
            in_specs=[spec(a.shape, kind) for a, kind in in_arrays] + [pl.BlockSpec(memory_space=pl.ANY)] * len(given),
            out_specs=[spec(shape, kind) for shape, _, kind in out_list],
            scratch_shapes=scratch,
        ),
        out_shape=[jax.ShapeDtypeStruct(shape, dtype) for shape, dtype, _ in out_list],
        input_output_aliases={first_given + i: i for i in range(len(given))},
        compiler_params=pltpu.CompilerParams(
            vmem_limit_bytes=VMEM_LIMIT, dimension_semantics=("arbitrary",)
        ),
        cost_estimate=SMALL,
        name=name,
    )(*prefetch, *[a for a, _ in in_arrays], *given)


ENC = layer_offsets(V_ENC, D, FE)
DEC = layer_offsets(V_DEC, E, FD)


def encoder_forward_kernel(
    start, given, row_ref, len_ref, wg_ref, vec_ref, pix_ref, pos_ref,
    x0_ref, h1_ref, qkv_ref, lse_ref, out_t_ref, att_ref, mid_ref, h2_ref, act_ref, slope_ref, x1_ref, hn_ref, latent_ref,
    w_embed, w_qkv, w_out, w_up, w_down, w_proj, sems,
):
    step = pl.program_id(0)
    images = lse_ref.shape[0]
    ready = fetch_all(
        step == 0,
        row_ref,
        wg_ref,
        sems,
        [
            (T_EMBED, w_embed),
            (T_EQKV, w_qkv),
            (T_EOUT, w_out),
            (T_EUP, w_up),
            (T_EDOWN, w_down),
            (T_PROJ, w_proj),
        ],
    )

    def vec(start, size=D):
        return vec_ref[:, start : start + size]

    ready(0)
    add_linear(pos_ref, pix_ref, w_embed, vec_ref, V_EMBED, x0_ref)
    norm_forward(x0_ref, vec(ENC["g1"]), vec(ENC["s1"]), h1_ref)
    ready(1)
    qkv_forward(h1_ref, w_qkv, vec_ref, ENC["bqkv"], qkv_ref)

    attend_all(
        qkv_ref, att_ref, out_t_ref, lse_ref, images, VMAX, D, D // HE, lambda i: len_ref[step * images + i]
    )
    ready(2)
    add_linear(x0_ref, att_ref, w_out, vec_ref, ENC["bo"], mid_ref)
    norm_forward(mid_ref, vec(ENC["g2"]), vec(ENC["s2"]), h2_ref)
    ready(3)
    up_forward(h2_ref, w_up, vec_ref, ENC["bu"], act_ref, slope_ref)
    ready(4)
    add_linear(mid_ref, act_ref, w_down, vec_ref, ENC["bd"], x1_ref)
    norm_forward(x1_ref, vec(V_ENORM), vec(V_ENORM + D), hn_ref)
    ready(5)

    def project(j, cols):
        latent_ref[:, cols] = mm(hn_ref[...], w_proj[:, cols]) + vec_at(vec_ref, V_PROJ, j)

    col_loop(E // BS, project)


def encoder_forward(tile_rows, vis_len, gathered, vector, visible_pix, pos_d, steps):
    images = vis_len.shape[0]
    rows = images * VMAX
    outs = [
        ((rows, D), F32, "rows"),
        ((rows, D), BF, "rows"),
        ((rows, 3 * D), BF, "rows"),
        ((images, D // BS, BS * HE // D, VMAX), F32, "rows"),
        ((images, D // BS, BS, VMAX), F32, "rows"),
        ((rows, D), BF, "rows"),
        ((rows, D), F32, "rows"),
        ((rows, D), BF, "rows"),
        ((rows, FE), BF, "rows"),
        ((rows, FE), BF, "rows"),
        ((rows, D), F32, "rows"),
        ((rows, D), BF, "rows"),
        ((rows, E), F32, "rows"),
    ]
    scratch = [pltpu.VMEM(s, BF) for s in [(PIX, D), (D, 3 * D), (D, D), (D, FE), (FE, D), (D, E)]]
    return group_call(
        encoder_forward_kernel,
        steps,
        (tile_rows, vis_len),
        [
            (gathered, "any"),
            (vector, "whole"),
            (visible_pix.reshape(rows, PIX), "rows"),
            (pos_d.reshape(rows, D), "rows"),
        ],
        outs,
        scratch + [pltpu.SemaphoreType.DMA((6,))],
        "encoder_forward",
    )


DS = layer_offsets(0, E, FD)
DS_NORM = 9 * E + FD
DS_HEAD = DS_NORM + 2 * E
DS_MASK = DS_HEAD + PIX
DS_LOSS = DS_MASK + E
DS_ALL = DS_LOSS + PIX


def decoder_kernel(
    start, given, row_ref, len_ref, wg_ref, vec_ref, latent_ref, pos_ref, pix_ref,
    h1_ref, dqkv_ref, att_ref, gproj_ref, h2_ref, du_ref, act_ref, gdown_ref, hn_ref, gpred_ref, glat_ref, sum_ref,
    w_qkv, w_out, w_up, w_down, w_head, x0, qkv, lse, out_t, mid, slope, x1, pred, dy, grad, datt, sems,
):
    step = pl.program_id(0)
    images = lse.shape[0]
    ready = fetch_all(
        step == 0,
        row_ref,
        wg_ref,
        sems,
        [(T_DQKV, w_qkv), (T_DOUT, w_out), (T_DUP, w_up), (T_DDOWN, w_down), (T_HEAD, w_head)],
    )

    @pl.when(step == 0)
    def _():
        sum_ref[...] = jnp.zeros_like(sum_ref)

    def vec(start, size=E):
        return vec_ref[:, start : start + size]

    def length(image):
        return len_ref[step * images + image]

    chunk = 16
    order = lax.broadcasted_iota(jnp.int32, (chunk, 1), 0)
    token = vec(V_MASK)

    def place(image, c):
        def head_rows(i, c):
            at = pl.ds(pl.multiple_of(image * SD + i * chunk, chunk), chunk)
            got = latent_ref[pl.ds(pl.multiple_of(image * VMAX + i * chunk, chunk), chunk), :]
            x0[at, :] = jnp.where(i * chunk + order < length(image), got, token) + pos_ref[at, :]
            return c

        def tail_rows(i, c):
            at = pl.ds(pl.multiple_of(image * SD + i * chunk, chunk), chunk)
            x0[at, :] = token + pos_ref[at, :]
            return c

        loop(0, VMAX // chunk, head_rows, 0)
        loop(VMAX // chunk, SD // chunk, tail_rows, 0)
        return c

    lax.fori_loop(0, images, place, 0)
    norm_forward(x0, vec(DEC["g1"]), vec(DEC["s1"]), h1_ref)
    ready(0)
    qkv_forward(h1_ref, w_qkv, vec_ref, DEC["bqkv"], qkv)
    attend_all(qkv, att_ref, out_t, lse, images, SD, E, E // HD, lambda i: POS)
    ready(1)
    add_linear(x0, att_ref, w_out, vec_ref, DEC["bo"], mid)
    norm_forward(mid, vec(DEC["g2"]), vec(DEC["s2"]), h2_ref)
    ready(2)
    up_forward(h2_ref, w_up, vec_ref, DEC["bu"], act_ref, slope)
    ready(3)
    add_linear(mid, act_ref, w_down, vec_ref, DEC["bd"], x1)
    norm_forward(x1, vec(V_DNORM), vec(V_DNORM + E), hn_ref)
    ready(4)

    def predict(j, cols):
        pred[:, cols] = mm(hn_ref[...], w_head[:, cols]) + vec_at(vec_ref, V_HEAD, j)

    col_loop(PIX // BS, predict)

    def errors(image, c):
        def one(i, c):
            loss, bias = c
            at = pl.ds(pl.multiple_of(image * SD + i * chunk, chunk), chunk)
            target, _ = norm_parts(pix_ref[at, :].astype(F32))
            place_in = i * chunk + order
            masked = (place_in >= length(image)) & (place_in < POS)
            residual = jnp.where(masked, pred[at, :] - target, 0.0)
            low = (residual * (2.0 / PIX)).astype(BF)
            gpred_ref[at, :] = low
            return (loss + fold8(residual * residual), bias + fold8(low.astype(F32)))

        return loop(0, SD // chunk, one, c)

    zero = jnp.zeros((8, PIX), F32)
    loss, bias = lax.fori_loop(0, images, errors, (zero, zero))
    add_sum(sum_ref, DS_LOSS, loss)
    add_sum(sum_ref, DS_HEAD, bias)

    back_linear(gpred_ref, w_head, dy)
    d_gain, d_shift = norm_backward(x1, dy, vec(V_DNORM), grad, False)
    add_sum(sum_ref, DS_NORM, d_gain)
    add_sum(sum_ref, DS_NORM + E, d_shift)
    round_and_sum(grad, gdown_ref, sum_ref, DS["bd"])
    back_up(gdown_ref, w_down, slope, du_ref, sum_ref, DS["bu"])
    back_linear(du_ref, w_up, dy)
    d_gain, d_shift = norm_backward(mid, dy, vec(DEC["g2"]), grad, True)
    add_sum(sum_ref, DS["g2"], d_gain)
    add_sum(sum_ref, DS["s2"], d_shift)
    round_and_sum(grad, gproj_ref, sum_ref, DS["bo"])

    def back_out(j, cols):
        datt[:, cols] = mm_nt(gproj_ref[...], w_out[cols, :]).astype(BF)

    col_loop(E // BS, back_out)

    def attend_back(image, c):
        attention_backward(qkv, datt, out_t, lse, dqkv_ref, image, SD, E, E // HD, POS)
        return c

    lax.fori_loop(0, images, attend_back, 0)
    sum_rows(dqkv_ref, sum_ref, DS["bqkv"])
    back_linear(dqkv_ref, w_qkv, dy)
    d_gain, d_shift = norm_backward(x0, dy, vec(DEC["g1"]), grad, True)
    add_sum(sum_ref, DS["g1"], d_gain)
    add_sum(sum_ref, DS["s1"], d_shift)

    def unplace(image, c):
        def head_rows(i, c):
            got = grad[pl.ds(pl.multiple_of(image * SD + i * chunk, chunk), chunk), :]
            seen = i * chunk + order < length(image)
            at = pl.ds(pl.multiple_of(image * VMAX + i * chunk, chunk), chunk)
            glat_ref[at, :] = jnp.where(seen, got, 0.0).astype(BF)
            return c + fold8(jnp.where(seen, 0.0, got))

        def tail_rows(i, c):
            got = grad[pl.ds(pl.multiple_of(image * SD + i * chunk, chunk), chunk), :]
            return c + fold8(jnp.where(i * chunk + order < POS, got, 0.0))

        c = loop(0, VMAX // chunk, head_rows, c)
        return loop(VMAX // chunk, SD // chunk, tail_rows, c)

    add_sum(sum_ref, DS_MASK, lax.fori_loop(0, images, unplace, jnp.zeros((8, E), F32)))


def decoder(tile_rows, vis_len, gathered, vector, latent, pos_e, ordered, steps):
    images = vis_len.shape[0]
    rows = images * SD
    part = rows // steps
    outs = [
        ((rows, E), BF, "rows"),
        ((rows, 3 * E), BF, "rows"),
        ((rows, E), BF, "rows"),
        ((rows, E), BF, "rows"),
        ((rows, E), BF, "rows"),
        ((rows, FD), BF, "rows"),
        ((rows, FD), BF, "rows"),
        ((rows, E), BF, "rows"),
        ((rows, E), BF, "rows"),
        ((rows, PIX), BF, "rows"),
        ((images * VMAX, E), BF, "rows"),
        ((8, DS_ALL), F32, "whole"),
    ]
    scratch = [pltpu.VMEM(s, BF) for s in [(E, 3 * E), (E, E), (E, FD), (FD, E), (E, PIX)]]
    scratch += [
        pltpu.VMEM((part, E), F32),
        pltpu.VMEM((part, 3 * E), BF),
        pltpu.VMEM((images // steps, E // BS, BS * HD // E, SD), F32),
        pltpu.VMEM((images // steps, E // BS, BS, SD), F32),
        pltpu.VMEM((part, E), F32),
        pltpu.VMEM((part, FD), BF),
        pltpu.VMEM((part, E), F32),
        pltpu.VMEM((part, PIX), F32),
        pltpu.VMEM((part, E), F32),
        pltpu.VMEM((part, E), F32),
        pltpu.VMEM((part, E), BF),
        pltpu.SemaphoreType.DMA((5,)),
    ]
    return group_call(
        decoder_kernel,
        steps,
        (tile_rows, vis_len),
        [
            (gathered, "any"),
            (vector, "whole"),
            (latent, "rows"),
            (pos_e.reshape(rows, E), "rows"),
            (ordered.reshape(rows, PIX), "rows"),
        ],
        outs,
        scratch,
        "decoder",
    )


EM_BD, EM_BU = 0, D
EM_G2, EM_S2 = D + FE, 2 * D + FE
EM_BO, EM_NORM = 3 * D + FE, 4 * D + FE
EM_PROJ = 6 * D + FE
EM_ALL = EM_PROJ + E
EA_QKV, EA_G1, EA_S1, EA_EMBED, EA_ALL = 0, 3 * D, 4 * D, 5 * D, 6 * D


def encoder_mlp_back_kernel(
    start, given, row_ref, wg_ref, vec_ref, glat_ref, x1_ref, mid_ref, slope_ref,
    gdown_ref, du_ref, grad_ref, gproj_ref, sum_ref,
    w_proj, w_down, w_up, dy, sems,
):
    step = pl.program_id(0)
    ready = fetch_all(
        step == 0, row_ref, wg_ref, sems, [(T_PROJ, w_proj), (T_EDOWN, w_down), (T_EUP, w_up)]
    )

    @pl.when(step == 0)
    def _():
        sum_ref[...] = jnp.zeros_like(sum_ref)

    def vec(start):
        return vec_ref[:, start : start + D]

    sum_rows(glat_ref, sum_ref, EM_PROJ)
    ready(0)
    back_linear(glat_ref, w_proj, dy)
    d_gain, d_shift = norm_backward(x1_ref, dy, vec(V_ENORM), grad_ref, False)
    add_sum(sum_ref, EM_NORM, d_gain)
    add_sum(sum_ref, EM_NORM + D, d_shift)
    round_and_sum(grad_ref, gdown_ref, sum_ref, EM_BD)
    ready(1)
    back_up(gdown_ref, w_down, slope_ref, du_ref, sum_ref, EM_BU)
    ready(2)
    back_linear(du_ref, w_up, dy)
    d_gain, d_shift = norm_backward(mid_ref, dy, vec(ENC["g2"]), grad_ref, True)
    add_sum(sum_ref, EM_G2, d_gain)
    add_sum(sum_ref, EM_S2, d_shift)
    round_and_sum(grad_ref, gproj_ref, sum_ref, EM_BO)


def encoder_mlp_back(tile_rows, gathered, vector, glat, x1, mid, slope, steps):
    rows = x1.shape[0]
    part = rows // steps
    outs = [
        ((rows, D), BF, "rows"),
        ((rows, FE), BF, "rows"),
        ((rows, D), F32, "rows"),
        ((rows, D), BF, "rows"),
        ((8, EM_ALL), F32, "whole"),
    ]
    scratch = [pltpu.VMEM(s, BF) for s in [(D, E), (FE, D), (D, FE)]]
    scratch += [pltpu.VMEM((part, D), F32), pltpu.SemaphoreType.DMA((3,))]
    return group_call(
        encoder_mlp_back_kernel,
        steps,
        (tile_rows,),
        [
            (gathered, "any"),
            (vector, "whole"),
            (glat, "rows"),
            (x1, "rows"),
            (mid, "rows"),
            (slope, "rows"),
        ],
        outs,
        scratch,
        "encoder_mlp_back",
    )


def encoder_attention_back_kernel(
    start, given, row_ref, len_ref, wg_ref, vec_ref, gproj_ref, grad_in_ref, qkv_ref, lse_ref, out_t_ref, x0_ref, *refs
):
    dqkv_ref, gembed_ref, sum_ref, w_out, w_qkv, dy, grad, datt, sems = refs[given:]
    step = pl.program_id(0)
    images = lse_ref.shape[0]
    ready = fetch_all(step == 0, row_ref, wg_ref, sems, [(T_EOUT, w_out), (T_EQKV, w_qkv)])

    @pl.when(step == 0)
    def _():
        sum_ref[...] = jnp.zeros_like(sum_ref)

    ready(0)

    def back_out(j, cols):
        datt[:, cols] = mm_nt(gproj_ref[...], w_out[cols, :]).astype(BF)

    col_loop(D // BS, back_out)

    def attend_back(image, c):
        count = len_ref[(start + step) * images + image]
        attention_backward(qkv_ref, datt, out_t_ref, lse_ref, dqkv_ref, image, VMAX, D, D // HE, count)
        return c

    lax.fori_loop(0, images, attend_back, 0)
    sum_rows(dqkv_ref, sum_ref, EA_QKV)
    ready(1)
    back_linear(dqkv_ref, w_qkv, dy)
    grad[...] = grad_in_ref[...]
    gain = vec_ref[:, ENC["g1"] : ENC["g1"] + D]
    d_gain, d_shift = norm_backward(x0_ref, dy, gain, grad, True)
    add_sum(sum_ref, EA_G1, d_gain)
    add_sum(sum_ref, EA_S1, d_shift)
    round_and_sum(grad, gembed_ref, sum_ref, EA_EMBED)


def encoder_attention_back(tile_rows, vis_len, gathered, vector, gproj, grad, qkv, lse, out_t, x0, steps, share, given):
    rows = x0.shape[0]
    part = rows // steps
    outs = [((rows, 3 * D), BF, "rows"), ((rows, D), BF, "rows"), ((8, EA_ALL), F32, "whole")]
    scratch = [pltpu.VMEM(s, BF) for s in [(D, D), (D, 3 * D)]]
    scratch += [pltpu.VMEM((part, D), F32), pltpu.VMEM((part, D), F32), pltpu.VMEM((part, D), BF)]
    return group_call(
        encoder_attention_back_kernel,
        steps,
        (tile_rows, vis_len),
        [
            (gathered, "any"),
            (vector, "whole"),
            (gproj, "rows"),
            (grad, "rows"),
            (qkv, "rows"),
            (lse, "rows"),
            (out_t, "rows"),
            (x0, "rows"),
        ],
        outs,
        scratch + [pltpu.SemaphoreType.DMA((2,))],
        "encoder_attention_back",
        share,
        given,
    )


def weight_grad_kernel(parts, cut, extra, index_ref, x_ref, g_ref, *refs):
    outs = refs[extra : extra + min(parts, 2)]
    x_t, total = refs[-2:]
    row_tiles, col_tiles = x_ref.shape[1] // BS, g_ref.shape[1] // BS

    @pl.when(pl.program_id(1) == 0)
    def _():
        x_t[...] = x_ref[...].T

    total[...] = mm(x_t[...], g_ref[...])
    for p in range(parts):
        for i in range(row_tiles):
            start = pl.multiple_of(i * BS + (p ^ index_ref[0]) * cut, cut)
            for j in range(col_tiles):
                got = total[pl.ds(start, cut), j * BS : (j + 1) * BS]
                outs[p % 2][p // 2, i * col_tiles + j] = got.astype(BF)


def weight_grad(index, parts, count, first, x, g, block, buffers):
    cut = BS // parts
    rows, width = x.shape
    row_tiles, col_tiles = block
    size = row_tiles * col_tiles
    across = g.shape[1] // (col_tiles * BS)
    assert first % size == 0
    held = min(parts, 2)
    shape = jax.ShapeDtypeStruct((parts // held, count, cut, BS), BF)
    given = list(buffers or [])
    out_spec = pl.BlockSpec(
        (parts // held, size, cut, BS), lambda i, j, *_: (0, first // size + i * across + j, 0, 0)
    )
    return pl.pallas_call(
        functools.partial(weight_grad_kernel, parts, cut, len(given)),
        grid_spec=pltpu.PrefetchScalarGridSpec(
            num_scalar_prefetch=1,
            grid=(width // (row_tiles * BS), across),
            in_specs=[
                pl.BlockSpec((rows, row_tiles * BS), lambda i, j, *_: (0, i)),
                pl.BlockSpec((rows, col_tiles * BS), lambda i, j, *_: (0, j)),
            ]
            + [pl.BlockSpec(memory_space=pl.ANY)] * len(given),
            out_specs=[out_spec] * held,
            scratch_shapes=[
                pltpu.VMEM((row_tiles * BS, rows), BF),
                pltpu.VMEM((row_tiles * BS, col_tiles * BS), F32),
            ],
        ),
        out_shape=[shape] * held,
        input_output_aliases={3 + i: i for i in range(len(given))},
        compiler_params=pltpu.CompilerParams(vmem_limit_bytes=VMEM_LIMIT),
        cost_estimate=SMALL,
        name="weight_grad",
    )(index, x, g, *given)


def seed_kernel(parts, parcels, own, index_ref, *refs):
    sums, outs, rows = refs[: -1 - min(parts, 2)], refs[-1 - min(parts, 2) : -1], refs[-1]
    rows[...] = jnp.zeros_like(rows)
    at = 0
    for source, start, size in parcels:
        for k in range(0, size, 128):
            piece = sum(jnp.sum(sums[i][:, start + k : start + k + 128], axis=0, keepdims=True) for i in source)
            row, col = at % own // BS, at % own % BS
            rows[at // own, row : row + 1, col : col + 128] = piece
            at += 128
    for p in range(parts):
        out = outs[p % 2]
        out[p // 2, 0] = rows[p ^ index_ref[0]].astype(BF)
        for t in range(1, out.shape[1]):
            out[p // 2, t] = jnp.zeros(rows.shape[1:], BF)


def seed_buffers(index, parts, count, first, sums=(), parcels=(), own=1):
    cut = BS // parts
    held = min(parts, 2)
    size = count - first
    assert first % size == 0
    shape = jax.ShapeDtypeStruct((parts // held, count, cut, BS), BF)
    return pl.pallas_call(
        functools.partial(seed_kernel, parts, parcels, own),
        grid_spec=pltpu.PrefetchScalarGridSpec(
            num_scalar_prefetch=1,
            grid=(1,),
            in_specs=[pl.BlockSpec(x.shape, lambda i, *_: (0, 0)) for x in sums],
            out_specs=[pl.BlockSpec((parts // held, size, cut, BS), lambda i, *_: (0, first // size, 0, 0))] * held,
            scratch_shapes=[pltpu.VMEM((parts, cut, BS), F32)],
        ),
        out_shape=[shape] * held,
        cost_estimate=SMALL,
        name="seed_buffers",
    )(index, *sums)


def low_sum(a, b):
    return (a.astype(F32) + b.astype(F32)).astype(BF)


def swap_bit(x, bit, size):
    return lax.ppermute(x, "dp", [(i, i ^ (1 << bit)) for i in range(size)])


def reduce_core(buffers, parts):
    if parts == 1:
        whole, count = buffers[0][0], buffers[0].shape[1]
        return [whole[: count // 2], whole[count // 2 :]], [[], []]
    whole = low_sum(buffers[0], swap_bit(buffers[1], 0, parts))
    bits = list(range(parts.bit_length() - 2, 0, -1))
    whole = whole.reshape((2,) * len(bits) + whole.shape[1:])
    count = whole.shape[-3]
    return [whole[..., : count // 2, :, :], whole[..., count // 2 :, :, :]], [bits, bits]


def reduce_chips(state, parts, steps):
    halves, left = list(state[0]), list(state[1])
    for half in range(2):
        for _ in range(min(steps, len(left[half]))):
            bit = left[half][-1 if half == 0 else 0]
            axis = left[half].index(bit)
            keep = lax.index_in_dim(halves[half], 0, axis, keepdims=False)
            send = lax.index_in_dim(halves[half], 1, axis, keepdims=False)
            halves[half] = low_sum(keep, swap_bit(send, bit, parts))
            left[half] = [b for b in left[half] if b != bit]
    return halves, left


def patch_steps(groups):
    middle = groups // 2 - 1

    def inwards(k, x):
        return low_sum(x, lax.ppermute(x, "patch", [(k, k + 1), (groups - 1 - k, groups - 2 - k)]))

    def across(x):
        return low_sum(x, lax.ppermute(x, "patch", [(middle, middle + 1), (middle + 1, middle)]))

    def outwards(k, x):
        got = lax.ppermute(x, "patch", [(k + 1, k), (groups - 2 - k, groups - 1 - k)])
        me = lax.axis_index("patch")
        return jnp.where((me == k) | (me == groups - 1 - k), got, x)

    if groups == 1:
        return []
    steps = [functools.partial(inwards, k) for k in range(middle)] + [across]
    return steps + [functools.partial(outwards, k) for k in reversed(range(middle))]


def sum_patch(x, steps):
    for step in steps:
        x = step(x)
    return x


def sum_all(x, parts, groups):
    for bit in range(groups.bit_length() - 1):
        x = x + lax.ppermute(x, "patch", [(i, i ^ (1 << bit)) for i in range(groups)])
    return sum_dp(x, parts)


def sum_dp(x, parts):
    for bit in range(parts.bit_length() - 1):
        x = x + swap_bit(x, bit, parts)
    return x


def split_low(x):
    high = x.astype(BF)
    return high, (x - high.astype(F32)).astype(BF)


def tile_kernel(
    scale_ref, grad_ref, w_ref, left_stat_ref, right_stat_ref, left_root_ref, right_root_ref,
    clipped_ref, left_new_ref, right_new_ref, w_new_ref,
):
    scale = scale_ref[0]
    for t in range(w_ref.shape[0]):
        grad = grad_ref[:, t].reshape(BS, BS)
        clipped_ref[t] = grad.astype(F32) * scale
        square = (1.0 - BETA_STAT) * scale * scale
        left_new_ref[t] = BETA_STAT * left_stat_ref[t] + square * mm_nt(grad, grad)
        right_new_ref[t] = BETA_STAT * right_stat_ref[t] + square * mm_tn(grad, grad)
        high, low = split_low(left_root_ref[t])
        half = (mm(high, grad) + mm(low, grad)) * scale
        half_high, half_low = split_low(half)
        high, low = split_low(right_root_ref[t])
        direction = mm(half_high, high) + (mm(half_high, low) + mm(half_low, high))
        direction = direction * lax.rsqrt(jnp.mean(direction * direction) + EPS_ROOT)
        w_new_ref[t] = w_ref[t] - RATE_MATRIX * (direction + DECAY_MATRIX * w_ref[t])


def tile_update(scale, grads, states):
    parts, slots, cut, _ = grads.shape
    per = max(p for p in range(1, 7) if slots % p == 0)
    tile = pl.BlockSpec((per, BS, BS), lambda i, *_: (i, 0, 0))
    return pl.pallas_call(
        tile_kernel,
        grid_spec=pltpu.PrefetchScalarGridSpec(
            num_scalar_prefetch=1,
            grid=(slots // per,),
            in_specs=[pl.BlockSpec((parts, per, cut, BS), lambda i, *_: (0, i, 0, 0))] + [tile] * 5,
            out_specs=[tile] * 4,
        ),
        out_shape=[jax.ShapeDtypeStruct((slots, BS, BS), F32)] * 4,
        compiler_params=pltpu.CompilerParams(vmem_limit_bytes=VMEM_LIMIT),
        name="tile_update",
    )(scale.reshape(1), grads, *states)


def vector_update(clipped, vectors, moment, second):
    moment_new = BETA_FIRST * moment + (1.0 - BETA_FIRST) * clipped
    second_new = BETA_SECOND * second + (1.0 - BETA_SECOND) * clipped * clipped
    corrected = moment_new / (1.0 - BETA_FIRST**STEP)
    scaled = second_new / (1.0 - BETA_SECOND**STEP)
    vectors_new = vectors - RATE_VECTOR * corrected / (jnp.sqrt(scaled) + EPS_ADAM)
    return moment_new, second_new, vectors_new


CHUNKS = [
    [
        (T_DUP, 2, 8, (2, 4)),
        (T_DDOWN, 8, 2, (4, 2)),
        (T_DOUT, 2, 2, (2, 2)),
        (T_DQKV, 2, 6, (2, 3)),
        (T_HEAD, 2, 3, (2, 3)),
        (T_PROJ, 3, 2, (3, 2)),
    ],
    [(T_EUP, 3, 12, (3, 4)), (T_EDOWN, 12, 3, (4, 3)), (T_EOUT, 3, 3, (3, 3))],
    [(T_EQKV, 3, 9, (3, 3)), (T_EMBED, 3, 3, (3, 3))],
]


def chunk_sizes():
    sizes = [sum(r * c for _, r, c, _ in chunk) for chunk in CHUNKS]
    return sizes[:-1] + [sizes[-1] + 2]


def tile_places(sizes):
    chunk_of = np.zeros(NBLK + 2, np.int32)
    place_of = np.zeros(NBLK + 2, np.int32)
    for i, chunk in enumerate(CHUNKS):
        at = 0
        for first, row_tiles, col_tiles, (high, wide) in chunk:
            for r in range(row_tiles):
                for c in range(col_tiles):
                    block = r // high * (col_tiles // wide) + c // wide
                    chunk_of[first + r * col_tiles + c] = i
                    place_of[first + r * col_tiles + c] = at + block * high * wide + r % high * wide + c % wide
            at += row_tiles * col_tiles
    chunk_of[NBLK:] = len(CHUNKS) - 1
    place_of[NBLK + 1] = at
    place_of[NBLK] = at + 1
    return chunk_of, place_of


def shards(parts, groups, pixels, shuffle, vis_len, block_owner, weights, vectors, vec_moment, vec_second,
           left_stat, right_stat, left_root, right_root):
    slots = weights.shape[0]
    own = vectors.shape[0]
    index = lax.axis_index("dp").astype(jnp.int32).reshape(1)
    images = pixels.shape[0]

    vector_rows = -(-own // (16 * BS)) * 16
    mine = jnp.concatenate(
        [
            weights.astype(BF).reshape(slots * BS, BS),
            jnp.pad(vectors.astype(BF), (0, vector_rows * BS - own)).reshape(vector_rows, BS),
        ]
    )
    gathered = lax.all_gather(mine, "dp", axis=0, tiled=True)
    stride = mine.shape[0]
    slot_index = jnp.arange(block_owner.shape[0], dtype=jnp.int32)
    slot_of_block = jnp.sum(
        jnp.where(block_owner[None, :] == jnp.arange(NBLK, dtype=jnp.int32)[:, None], slot_index[None, :], 0),
        axis=1,
    )
    tile_rows = slot_of_block // slots * stride + slot_of_block % slots * BS
    vector = gathered.reshape(parts, stride, BS)[:, slots * BS :].reshape(parts, vector_rows * BS)
    vector = vector[:, :own].reshape(-1).astype(F32)
    enc_key, dec_key = 4 * D, 4 * D + (8 * D + FE - 3 * D) + 2 * D + 2 * E + 3 * E
    vector = jnp.concatenate(
        [vector[:enc_key], jnp.zeros(D, F32), vector[enc_key:dec_key], jnp.zeros(E, F32), vector[dec_key:]]
    ).reshape(1, V_ALL)

    ordered, visible_pix, pos_d, pos_e = order_patches(pixels, shuffle)
    (x0, h1, qkv, lse, out_t, att, mid, h2, act, slope, x1, hn, latent) = encoder_forward(
        tile_rows, vis_len, gathered, vector, visible_pix, pos_d, 2
    )
    (d_h1, d_dqkv, d_att, d_gproj, d_h2, d_du, d_act, d_gdown, d_hn, d_gpred, glat, d_sums) = decoder(
        tile_rows, vis_len, gathered, vector, latent, pos_e, ordered, 4
    )
    sizes = chunk_sizes()
    chunk_of, place_of = tile_places(sizes)

    rows_cut = BS // parts

    def gradients(chunk, pairs, vector=(), first=0, buffers=None):
        used = sum(r * c for _, r, c, _ in CHUNKS[chunk])
        if sizes[chunk] > used and buffers is None:
            buffers = seed_buffers(index, parts, sizes[chunk], used, *vector)
        at = sum(r * c for _, r, c, _ in CHUNKS[chunk][:first])
        for (x, g), (_, row_tiles, col_tiles, block) in zip(pairs, CHUNKS[chunk][first:]):
            buffers = weight_grad(index, parts, sizes[chunk], at, x, g, block, buffers)
            at += row_tiles * col_tiles
        return buffers

    def attention_back(gproj, k, given):
        return encoder_attention_back(
            tile_rows, vis_len, gathered, vector, gproj, grad_mid, qkv, lse, out_t, x0, 2, (k, 2), given
        )

    def core(buffers):
        return reduce_core(buffers, parts)

    def chips(state, steps):
        return reduce_chips(state, parts, steps)

    after = lax.optimization_barrier
    steps = patch_steps(groups)
    gdown, du, grad_mid, gproj, m_sums = encoder_mlp_back(tile_rows, gathered, vector, glat, x1, mid, slope, 2)
    buf1 = gradients(1, [(h2, du), (act, gdown), (att, gproj)])
    d_h2, d_act, buf1 = after((d_h2, d_act, buf1))
    buf0 = gradients(0, [(d_h2, d_du), (d_act, d_gdown)])
    half1, left1 = core(buf1)
    d_att, d_h1, d_hn, hn, buf0, half1 = after((d_att, d_h1, d_hn, hn, buf0, half1))
    half1, left1 = chips((half1, left1), 1)
    buf0 = gradients(0, [(d_att, d_gproj), (d_h1, d_dqkv), (d_hn, d_gpred), (hn, glat)], (), 2, buf0)
    gproj, buf0 = after((gproj, buf0))
    dqkv, gembed, a_sums = attention_back(gproj, 0, ())
    gproj, dqkv, gembed, buf0, half1 = after((gproj, dqkv, gembed, buf0, half1))
    dqkv, gembed, b_sums = attention_back(gproj, 1, (dqkv, gembed))
    (one, two), _ = chips((half1, left1), 99)
    half0, left0 = core(buf0)
    dqkv, gembed, b_sums, half0, one, two = after((dqkv, gembed, b_sums, half0, one, two))

    late, early, dec = (0, 1), (2,), (3,)
    parcels = [
        (late, EA_EMBED, D),
        (late, EA_G1, 2 * D),
        (late, EA_QKV, D),
        (late, EA_QKV + 2 * D, D),
        (early, EM_BO, D),
        (early, EM_G2, 2 * D),
        (early, EM_BU, FE),
        (early, EM_BD, D),
        (early, EM_NORM, 2 * D),
        (early, EM_PROJ, E),
        (dec, DS_MASK, E),
        (dec, DS["g1"], 2 * E),
        (dec, DS["bqkv"], E),
        (dec, DS["bqkv"] + 2 * E, E),
        (dec, DS["bo"], E),
        (dec, DS["g2"], 2 * E),
        (dec, DS["bu"], FD),
        (dec, DS["bd"], E),
        (dec, DS_NORM, 2 * E),
        (dec, DS_HEAD, PIX),
    ]
    sums = (a_sums, b_sums, m_sums, d_sums)
    buf2 = gradients(2, [(h1, dqkv), (visible_pix.reshape(-1, PIX), gembed)], (sums, parcels, own))
    half0, left0 = chips((half0, left0), 1)
    one = sum_patch(one, steps[:1])
    two = sum_patch(two, steps[:1])
    buf2, half0, one = after((buf2, half0, one))
    half2, left2 = core(buf2)
    half0, _ = chips((half0, left0), 99)
    one = sum_patch(one, steps[1:2])
    half2, half0, one, two = after((half2, half0, one, two))
    half2, left2 = chips((half2, left2), 1)
    one = sum_patch(one, steps[2:])
    two = sum_patch(two, steps[1:2])
    half0 = [sum_patch(x, steps[:1]) for x in half0]
    half2, two = after((half2, two))
    half2, _ = chips((half2, left2), 99)
    two = sum_patch(two, steps[2:])
    half2, half0 = after((half2, half0))
    half2 = [sum_patch(x, steps) for x in half2]
    half0 = [sum_patch(x, steps[1:]) for x in half0]
    pieces = half0 + [one, two] + half2
    mine = jnp.where(lax.axis_index("patch") == 0, 1.0, 0.0)

    def squares(x):
        wide = x.astype(F32)
        return jnp.sum(wide * wide)

    totals = jnp.stack(
        [
            jnp.sum(d_sums[:, DS_LOSS : DS_LOSS + PIX]) / PIX,
            jnp.sum(POS - vis_len).astype(F32),
            sum(squares(x) for x in pieces) * mine,
        ]
    )
    totals = sum_all(totals, parts, groups)
    loss_sum, masked_count = totals[0], totals[1]
    grad_norm = jnp.sqrt(totals[2]) / masked_count
    scale = jnp.minimum(1.0, CLIP_NORM / grad_norm) / masked_count

    reduced = jnp.concatenate(pieces, axis=0)
    where = jnp.asarray(np.cumsum([0] + sizes)[chunk_of] + place_of, jnp.int32)
    slot_rows = reduced[where[jnp.minimum(block_owner, NBLK)]]
    if parts > 1:
        slot_rows = lax.all_to_all(slot_rows, "dp", 0, 0, tiled=True)
    grads = slot_rows.reshape(parts, slots, rows_cut, BS)
    clipped, left_new, right_new, weights_new = tile_update(
        scale, grads, (weights, left_stat, right_stat, left_root, right_root)
    )
    own_vector = lax.dynamic_index_in_dim(reduced, where[NBLK + 1], 0, keepdims=False)
    own_vector = own_vector.reshape(-1)[:own].astype(F32) * scale
    moment_new, second_new, vectors_new = vector_update(own_vector, vectors, vec_moment, vec_second)
    return (
        loss_sum,
        masked_count,
        grad_norm,
        clipped,
        left_new,
        right_new,
        weights_new,
        moment_new,
        second_new,
        vectors_new,
    )


def solution(mesh):
    both = ("dp", "patch")
    tiles = P("dp", None, None)
    return jax.shard_map(
        functools.partial(shards, mesh.shape["dp"], mesh.shape["patch"]),
        mesh=mesh,
        in_specs=(P(both, None, None), P(both, None), P(both), P())
        + (tiles, P("dp"), P("dp"), P("dp"))
        + (tiles,) * 4,
        out_specs=(P(), P(), P()) + (tiles,) * 4 + (P("dp"),) * 3,
        check_vma=False,
    )
```

```python
import functools
import math

import jax
import jax.numpy as jnp
import numpy as np
from jax import lax
from jax.experimental import pallas as pl
from jax.experimental.pallas import tpu as pltpu
from jax.sharding import PartitionSpec as P

D = 768
HE = 12
FE = 3072
E = 512
HD = 16
FD = 2048
PIX = 768
POS = 196
VMAX = 80
BS = 256
STEP = 10
NBLK = 177

SD = 208

EPS_NORM = 1e-06
EPS_ROOT = 1e-06
EPS_ADAM = 1e-08
CLIP_NORM = 0.01
RATE_MATRIX = 0.03
DECAY_MATRIX = 0.05
BETA_STAT = 0.5
BETA_FIRST = 0.9
BETA_SECOND = 0.999
RATE_VECTOR = 0.1
NEG_LARGE = -1e30
LOG2E = math.log2(math.e)

BF = jnp.bfloat16
F32 = jnp.float32
VMEM_LIMIT = 60 * 1024 * 1024
SMALL = pl.CostEstimate(flops=1000, bytes_accessed=1000, transcendentals=0)

T_EMBED, T_EQKV, T_EOUT, T_EUP, T_EDOWN, T_PROJ = 0, 9, 36, 45, 81, 117
T_DQKV, T_DOUT, T_DUP, T_DDOWN, T_HEAD = 123, 135, 139, 155, 171

V_EMBED = 0
V_ENC = D
V_ENORM = V_ENC + 9 * D + FE
V_PROJ = V_ENORM + 2 * D
V_MASK = V_PROJ + E
V_DEC = V_MASK + E
V_DNORM = V_DEC + 9 * E + FD
V_HEAD = V_DNORM + 2 * E
V_ALL = V_HEAD + PIX


def layer_offsets(start, width, hidden):
    names = ["g1", "s1", "bqkv", "bo", "g2", "s2", "bu", "bd"]
    sizes = [width, width, 3 * width, width, width, width, hidden, width]
    offsets = {}
    for name, size in zip(names, sizes):
        offsets[name] = start
        start += size
    return offsets


def mm(a, b):
    return jnp.dot(a, b, preferred_element_type=F32)


def mm_nt(a, b):
    return lax.dot_general(a, b, (((1,), (1,)), ((), ())), preferred_element_type=F32)


def mm_tn(a, b):
    return lax.dot_general(a, b, (((0,), (0,)), ((), ())), preferred_element_type=F32)


def fold8(x):
    rows, cols = x.shape
    return jnp.sum(x.reshape(rows // 8, 8, cols), axis=0)


def gelu_pair(u):
    t = 1.0 / (1.0 + (0.3275911 * math.sqrt(0.5)) * jnp.abs(u))
    e = jnp.exp2((-0.5 * LOG2E) * (u * u))
    poly = t * (
        0.5 * 0.254829592
        + t * (-0.5 * 0.284496736 + t * (0.5 * 1.421413741 + t * (-0.5 * 1.453152027 + t * (0.5 * 1.061405429))))
    )
    tail = poly * e
    phi = jnp.where(u >= 0, 1.0 - tail, tail)
    return u * phi, phi + u * (e * (1.0 / math.sqrt(2.0 * math.pi)))


def norm_parts(x):
    centred = x - jnp.mean(x, axis=-1, keepdims=True)
    inverse = lax.rsqrt(jnp.mean(centred * centred, axis=-1, keepdims=True) + EPS_NORM)
    return centred * inverse, inverse


def loop(lower, upper, body, carry, most=26):
    count = upper - lower
    unroll = max(u for u in range(1, min(most, count) + 1) if count % u == 0)
    return lax.fori_loop(lower, upper, body, carry, unroll=unroll)


def row_loop(rows, step, body, carry=0):
    count = rows // step

    def one(i, c):
        return body(pl.ds(pl.multiple_of(i * step, step), step), c)

    return loop(0, count, one, carry)


def norm_forward(x_ref, gain, shift, out_ref):
    def body(sl, c):
        normed, _ = norm_parts(x_ref[sl, :])
        out_ref[sl, :] = (normed * gain + shift).astype(BF)
        return c

    row_loop(x_ref.shape[0], 16, body)


def norm_backward(x_ref, dy_ref, gain, out_ref, add):
    width = x_ref.shape[1]

    def body(sl, c):
        d_gain, d_shift = c
        normed, inverse = norm_parts(x_ref[sl, :])
        dy = dy_ref[sl, :]
        dn = dy * gain
        mean_one = jnp.mean(dn, axis=-1, keepdims=True)
        mean_two = jnp.mean(dn * normed, axis=-1, keepdims=True)
        dx = inverse * (dn - mean_one - normed * mean_two)
        out_ref[sl, :] = out_ref[sl, :] + dx if add else dx
        return (d_gain + fold8(dy * normed), d_shift + fold8(dy))

    zero = jnp.zeros((8, width), F32)
    return row_loop(x_ref.shape[0], 16, body, (zero, zero))


def col_loop(count, body):
    def one(j, c):
        body(j, pl.ds(pl.multiple_of(j * BS, BS), BS))
        return c

    loop(0, count, one, 0, 12)


def vec_at(vec_ref, start, j):
    return vec_ref[:, pl.ds(pl.multiple_of(start + j * BS, BS), BS)]


def head_mask(head, head_size):
    lane = lax.broadcasted_iota(jnp.int32, (1, BS), 1)
    inside = (lane >= head * head_size) & (lane < (head + 1) * head_size)
    return jnp.where(inside, 1.0, 0.0).astype(BF)


def masked_scores(raw, head_size, count):
    scores = raw * (head_size**-0.5 * LOG2E)
    if isinstance(count, int):
        whole = count // 8 * 8
        tail = scores[whole:]
        row = lax.broadcasted_iota(jnp.int32, tail.shape, 0) + whole
        return jnp.concatenate([scores[:whole], jnp.where(row < count, tail, NEG_LARGE)], axis=0)
    row = lax.broadcasted_iota(jnp.int32, (scores.shape[0], 1), 0)
    return jnp.where(row < count, scores, NEG_LARGE)


def scores_bounded(qkv_ref, width, head_size):
    lane = lax.broadcasted_iota(jnp.int32, (BS, 128), 0) // head_size
    pick = jnp.where(lane == lax.broadcasted_iota(jnp.int32, (BS, 128), 1), 1.0, 0.0).astype(BF)
    score, value = None, None
    for g in range(width // BS):
        tops = []
        for which in range(3):
            x = qkv_ref[:, which * width + g * BS : which * width + (g + 1) * BS]
            tops.append(jnp.max(mm(x * x, pick), axis=0, keepdims=True))
        one = tops[0] * tops[1]
        score = one if score is None else jnp.maximum(score, one)
        value = tops[2] if value is None else jnp.maximum(value, tops[2])
    limit = 90.0 / (1.05 * head_size**-0.5 * LOG2E)
    return (jnp.max(score) < limit * limit) & (jnp.max(value) < 2.0**40)


def attention_forward(qkv_ref, att_ref, out_t_ref, lse_ref, image, seq, width, head_size, count, bounded):
    rows = pl.ds(pl.multiple_of(image * seq, 16), seq)
    per = BS // head_size
    most = min(8, per)

    def group(g, c):
        def part(which):
            return qkv_ref[rows, pl.ds(pl.multiple_of(which * width + g * BS, BS), BS)]

        q, k, v = part(0), part(1), part(2)
        v_t = v.T
        q = q.T
        ones = jnp.ones((16, seq), BF)
        outs, logs = [], []
        for h in range(per):
            if h % most == 0:
                stacked = jnp.concatenate([k * head_mask(i, head_size) for i in range(h, h + most)], axis=0)
                many = mm(stacked, q)
            scores = masked_scores(many[h % most * seq : (h % most + 1) * seq], head_size, count)
            top = 0.0
            if not bounded:
                top = jnp.max(scores, axis=0, keepdims=True)
                scores = scores - top
            e = jnp.exp2(scores).astype(BF)
            both = mm(jnp.concatenate([v_t[h * head_size : (h + 1) * head_size, :], ones], axis=0), e)
            total = both[head_size : head_size + 1, :]
            outs.append(both[:head_size, :] * (1.0 / total))
            logs.append(top + jnp.log2(total))
        out_t = jnp.concatenate(outs, axis=0)
        out_t_ref[image, g] = out_t
        att_ref[rows, pl.ds(pl.multiple_of(g * BS, BS), BS)] = out_t.T.astype(BF)
        lse_ref[image, g] = jnp.concatenate(logs, axis=0)
        return c

    loop(0, width // BS, group, 0)


def attend_all(qkv_ref, att_ref, out_t_ref, lse_ref, images, seq, width, head_size, count_of):
    safe = scores_bounded(qkv_ref, width, head_size)

    def run(bounded):
        def one(image, c):
            count = count_of(image)
            attention_forward(
                qkv_ref, att_ref, out_t_ref, lse_ref, image, seq, width, head_size, count, bounded
            )
            return c

        loop(0, images, one, 0)

    @pl.when(safe)
    def _():
        run(True)

    @pl.when(jnp.logical_not(safe))
    def _():
        run(False)


def attention_backward(qkv_ref, datt_ref, out_t_ref, lse_ref, dqkv_ref, image, seq, width, head_size, count):
    rows = pl.ds(pl.multiple_of(image * seq, 16), seq)
    per = BS // head_size
    scale = head_size**-0.5
    most = min(8, per)

    def group(g, c):
        def cols(which):
            return pl.ds(pl.multiple_of(which * width + g * BS, BS), BS)

        q, k, v = qkv_ref[rows, cols(0)], qkv_ref[rows, cols(1)], qkv_ref[rows, cols(2)]
        d_out = datt_ref[rows, cols(0)]
        lse = lse_ref[image, g]
        q_t, k_t, d_out_t = q.T, k.T, d_out.T
        along = d_out_t.astype(F32) * out_t_ref[image, g]
        lane = lax.broadcasted_iota(jnp.int32, (seq, BS), 1)
        d_q, d_k, d_v = [], None, None
        for start in range(0, per, most):
            heads = range(start, start + most)
            many = mm(jnp.concatenate([k * head_mask(h, head_size) for h in heads], axis=0), q_t)
            more = mm(jnp.concatenate([v * head_mask(h, head_size) for h in heads], axis=0), d_out_t)
            probs_all, scores_all = [], []
            for h in heads:
                part = slice(h * head_size, (h + 1) * head_size)
                at = slice((h - start) * seq, (h - start + 1) * seq)
                delta = jnp.sum(along[part, :], axis=0, keepdims=True)
                probs = jnp.exp2(masked_scores(many[at], head_size, count) - lse[h : h + 1, :])
                d_scores = (probs * (more[at] - delta)).astype(BF)
                d_q.append(mm(k_t[part, :], d_scores))
                probs_all.append(probs.astype(BF))
                scores_all.append(d_scores)
            for_v = mm(jnp.concatenate(probs_all, axis=0), d_out)
            for_k = mm(jnp.concatenate(scores_all, axis=0), q)
            for h in heads:
                at = slice((h - start) * seq, (h - start + 1) * seq)
                inside = (lane >= h * head_size) & (lane < (h + 1) * head_size)
                d_v = for_v[at] if d_v is None else jnp.where(inside, for_v[at], d_v)
                d_k = for_k[at] if d_k is None else jnp.where(inside, for_k[at], d_k)
        dqkv_ref[rows, cols(0)] = (jnp.concatenate(d_q, axis=0).T * scale).astype(BF)
        dqkv_ref[rows, cols(1)] = (d_k * scale).astype(BF)
        dqkv_ref[rows, cols(2)] = d_v.astype(BF)
        return c

    loop(0, width // BS, group, 0)


def fetch_tiles(row_ref, wg_ref, first, dst, sem):
    row_tiles, col_tiles = dst.shape[0] // BS, dst.shape[1] // BS
    for i in range(row_tiles):
        for j in range(col_tiles):
            start = pl.multiple_of(row_ref[first + i * col_tiles + j], 16)
            pltpu.make_async_copy(
                wg_ref.at[pl.ds(start, BS), :],
                dst.at[i * BS : (i + 1) * BS, j * BS : (j + 1) * BS],
                sem,
            ).start()


def await_tiles(dst, sem):
    pltpu.make_async_copy(dst, dst, sem).wait()


def fetch_all(first_step, row_ref, wg_ref, sems, matrices):
    @pl.when(first_step)
    def _():
        for i, (first, dst) in enumerate(matrices):
            fetch_tiles(row_ref, wg_ref, first, dst, sems.at[i])

    def ready(i):
        @pl.when(first_step)
        def _():
            await_tiles(matrices[i][1], sems.at[i])

    return ready


def qkv_forward(h_ref, w_ref, vec_ref, start, out_ref):
    def body(j, cols):
        out_ref[:, cols] = (mm(h_ref[...], w_ref[:, cols]) + vec_at(vec_ref, start, j)).astype(BF)

    col_loop(w_ref.shape[1] // BS, body)


def add_linear(x_ref, h_ref, w_ref, vec_ref, start, out_ref):
    def body(j, cols):
        out_ref[:, cols] = x_ref[:, cols] + (mm(h_ref[...], w_ref[:, cols]) + vec_at(vec_ref, start, j))

    col_loop(w_ref.shape[1] // BS, body)


def up_forward(h_ref, w_ref, vec_ref, start, act_ref, slope_ref):
    def body(j, cols):
        act, slope = gelu_pair(mm(h_ref[...], w_ref[:, cols]) + vec_at(vec_ref, start, j))
        act_ref[:, cols] = act.astype(BF)
        slope_ref[:, cols] = slope.astype(BF)

    col_loop(w_ref.shape[1] // BS, body)


def back_linear(g_ref, w_ref, out_ref):
    def body(j, cols):
        out_ref[:, cols] = mm_nt(g_ref[...], w_ref[cols, :])

    col_loop(w_ref.shape[0] // BS, body)


def back_up(g_ref, w_ref, slope_ref, du_ref, sum_ref, start):
    def body(j, cols):
        du = (mm_nt(g_ref[...], w_ref[cols, :]) * slope_ref[:, cols].astype(F32)).astype(BF)
        du_ref[:, cols] = du
        at = pl.ds(pl.multiple_of(start + j * BS, BS), BS)
        sum_ref[:, at] = sum_ref[:, at] + fold8(du.astype(F32))

    col_loop(w_ref.shape[0] // BS, body)


def round_and_sum(x_ref, out_ref, sum_ref, start):
    width = x_ref.shape[1]

    def body(sl, c):
        low = x_ref[sl, :].astype(BF)
        out_ref[sl, :] = low
        return c + fold8(low.astype(F32))

    total = row_loop(x_ref.shape[0], 16, body, jnp.zeros((8, width), F32))
    sum_ref[:, start : start + width] = sum_ref[:, start : start + width] + total


def sum_rows(x_ref, sum_ref, start):
    width = x_ref.shape[1]

    def body(sl, c):
        return c + fold8(x_ref[sl, :].astype(F32))

    total = row_loop(x_ref.shape[0], 16, body, jnp.zeros((8, width), F32))
    sum_ref[:, start : start + width] = sum_ref[:, start : start + width] + total


def add_sum(sum_ref, start, value):
    stop = start + value.shape[1]
    sum_ref[:, start:stop] = sum_ref[:, start:stop] + value


def order_kernel(shuffle_ref, pixels_ref, sin_d_ref, sin_e_ref, all_ref, visible_ref, pos_d_ref, pos_e_ref):
    ids = shuffle_ref[0]
    pick = jnp.where(ids == lax.broadcasted_iota(jnp.int32, (SD, POS), 1), 1.0, 0.0).astype(BF)
    ordered = mm(pick, pixels_ref[0]).astype(BF)
    all_ref[0] = ordered
    visible_ref[0] = ordered[:VMAX, :]
    few = pick[:VMAX, :]
    pos_d_ref[0] = mm(few, sin_d_ref[0]) + mm(few, sin_d_ref[1])
    pos_e_ref[0] = mm(pick, sin_e_ref[0]) + mm(pick, sin_e_ref[1])


def sinusoid_parts(count, width):
    half = width // 2
    frequency = np.exp(np.arange(half) * (-np.log(10000.0) / half))
    angles = np.arange(count)[:, None] * frequency[None, :]
    table = np.concatenate([np.sin(angles), np.cos(angles)], axis=1).astype(np.float32)
    high = table.astype(jnp.bfloat16)
    low = (table - high.astype(np.float32)).astype(jnp.bfloat16)
    return np.stack([high, low])


def order_patches(pixels, shuffle):
    images = pixels.shape[0]
    ids = jnp.pad(shuffle, ((0, 0), (0, SD - POS)), constant_values=-1)[:, :, None]

    def image(*dims):
        return pl.BlockSpec((1,) + dims, lambda b: (b,) + (0,) * len(dims))

    def whole(*dims):
        return pl.BlockSpec(dims, lambda b: (0,) * len(dims))

    return pl.pallas_call(
        order_kernel,
        grid=(images,),
        in_specs=[image(SD, 1), image(POS, PIX), whole(2, POS, D), whole(2, POS, E)],
        out_specs=[image(SD, PIX), image(VMAX, PIX), image(VMAX, D), image(SD, E)],
        out_shape=[
            jax.ShapeDtypeStruct((images, SD, PIX), BF),
            jax.ShapeDtypeStruct((images, VMAX, PIX), BF),
            jax.ShapeDtypeStruct((images, VMAX, D), F32),
            jax.ShapeDtypeStruct((images, SD, E), F32),
        ],
        compiler_params=pltpu.CompilerParams(vmem_limit_bytes=VMEM_LIMIT),
        name="order_patches",
    )(ids, pixels, jnp.asarray(sinusoid_parts(POS, D)), jnp.asarray(sinusoid_parts(POS, E)))


def group_call(kernel, steps, prefetch, in_arrays, out_list, scratch, name, share=(0, 1), given=()):
    count = steps // share[1]
    start = share[0] * count

    def spec(shape, kind):
        if kind == "any":
            return pl.BlockSpec(memory_space=pl.ANY)
        if kind == "rows":
            block = (shape[0] // steps,) + tuple(shape[1:])
            return pl.BlockSpec(block, lambda i, *_: (start + i,) + (0,) * (len(shape) - 1))
        return pl.BlockSpec(tuple(shape), lambda i, *_: (0,) * len(shape))

    first_given = len(prefetch) + len(in_arrays)
    return pl.pallas_call(
        functools.partial(kernel, start, len(given)),
        grid_spec=pltpu.PrefetchScalarGridSpec(
            num_scalar_prefetch=len(prefetch),
            grid=(count,),
            in_specs=[spec(a.shape, kind) for a, kind in in_arrays] + [pl.BlockSpec(memory_space=pl.ANY)] * len(given),
            out_specs=[spec(shape, kind) for shape, _, kind in out_list],
            scratch_shapes=scratch,
        ),
        out_shape=[jax.ShapeDtypeStruct(shape, dtype) for shape, dtype, _ in out_list],
        input_output_aliases={first_given + i: i for i in range(len(given))},
        compiler_params=pltpu.CompilerParams(
            vmem_limit_bytes=VMEM_LIMIT, dimension_semantics=("arbitrary",)
        ),
        cost_estimate=SMALL,
        name=name,
    )(*prefetch, *[a for a, _ in in_arrays], *given)


ENC = layer_offsets(V_ENC, D, FE)
DEC = layer_offsets(V_DEC, E, FD)


def encoder_forward_kernel(
    start, given, row_ref, len_ref, wg_ref, vec_ref, pix_ref, pos_ref,
    x0_ref, h1_ref, qkv_ref, lse_ref, out_t_ref, att_ref, mid_ref, h2_ref, act_ref, slope_ref, x1_ref, hn_ref, latent_ref,
    w_embed, w_qkv, w_out, w_up, w_down, w_proj, sems,
):
    step = pl.program_id(0)
    images = lse_ref.shape[0]
    ready = fetch_all(
        step == 0,
        row_ref,
        wg_ref,
        sems,
        [
            (T_EMBED, w_embed),
            (T_EQKV, w_qkv),
            (T_EOUT, w_out),
            (T_EUP, w_up),
            (T_EDOWN, w_down),
            (T_PROJ, w_proj),
        ],
    )

    def vec(start, size=D):
        return vec_ref[:, start : start + size]

    ready(0)
    add_linear(pos_ref, pix_ref, w_embed, vec_ref, V_EMBED, x0_ref)
    norm_forward(x0_ref, vec(ENC["g1"]), vec(ENC["s1"]), h1_ref)
    ready(1)
    qkv_forward(h1_ref, w_qkv, vec_ref, ENC["bqkv"], qkv_ref)

    attend_all(
        qkv_ref, att_ref, out_t_ref, lse_ref, images, VMAX, D, D // HE, lambda i: len_ref[step * images + i]
    )
    ready(2)
    add_linear(x0_ref, att_ref, w_out, vec_ref, ENC["bo"], mid_ref)
    norm_forward(mid_ref, vec(ENC["g2"]), vec(ENC["s2"]), h2_ref)
    ready(3)
    up_forward(h2_ref, w_up, vec_ref, ENC["bu"], act_ref, slope_ref)
    ready(4)
    add_linear(mid_ref, act_ref, w_down, vec_ref, ENC["bd"], x1_ref)
    norm_forward(x1_ref, vec(V_ENORM), vec(V_ENORM + D), hn_ref)
    ready(5)

    def project(j, cols):
        latent_ref[:, cols] = mm(hn_ref[...], w_proj[:, cols]) + vec_at(vec_ref, V_PROJ, j)

    col_loop(E // BS, project)


def encoder_forward(tile_rows, vis_len, gathered, vector, visible_pix, pos_d, steps):
    images = vis_len.shape[0]
    rows = images * VMAX
    outs = [
        ((rows, D), F32, "rows"),
        ((rows, D), BF, "rows"),
        ((rows, 3 * D), BF, "rows"),
        ((images, D // BS, BS * HE // D, VMAX), F32, "rows"),
        ((images, D // BS, BS, VMAX), F32, "rows"),
        ((rows, D), BF, "rows"),
        ((rows, D), F32, "rows"),
        ((rows, D), BF, "rows"),
        ((rows, FE), BF, "rows"),
        ((rows, FE), BF, "rows"),
        ((rows, D), F32, "rows"),
        ((rows, D), BF, "rows"),
        ((rows, E), F32, "rows"),
    ]
    scratch = [pltpu.VMEM(s, BF) for s in [(PIX, D), (D, 3 * D), (D, D), (D, FE), (FE, D), (D, E)]]
    return group_call(
        encoder_forward_kernel,
        steps,
        (tile_rows, vis_len),
        [
            (gathered, "any"),
            (vector, "whole"),
            (visible_pix.reshape(rows, PIX), "rows"),
            (pos_d.reshape(rows, D), "rows"),
        ],
        outs,
        scratch + [pltpu.SemaphoreType.DMA((6,))],
        "encoder_forward",
    )


DS = layer_offsets(0, E, FD)
DS_NORM = 9 * E + FD
DS_HEAD = DS_NORM + 2 * E
DS_MASK = DS_HEAD + PIX
DS_LOSS = DS_MASK + E
DS_ALL = DS_LOSS + PIX


def decoder_kernel(
    start, given, row_ref, len_ref, wg_ref, vec_ref, latent_ref, pos_ref, pix_ref,
    h1_ref, dqkv_ref, att_ref, gproj_ref, h2_ref, du_ref, act_ref, gdown_ref, hn_ref, gpred_ref, glat_ref, sum_ref,
    w_qkv, w_out, w_up, w_down, w_head, x0, qkv, lse, out_t, mid, slope, x1, pred, dy, grad, datt, sems,
):
    step = pl.program_id(0)
    images = lse.shape[0]
    ready = fetch_all(
        step == 0,
        row_ref,
        wg_ref,
        sems,
        [(T_DQKV, w_qkv), (T_DOUT, w_out), (T_DUP, w_up), (T_DDOWN, w_down), (T_HEAD, w_head)],
    )

    @pl.when(step == 0)
    def _():
        sum_ref[...] = jnp.zeros_like(sum_ref)

    def vec(start, size=E):
        return vec_ref[:, start : start + size]

    def length(image):
        return len_ref[step * images + image]

    chunk = 16
    order = lax.broadcasted_iota(jnp.int32, (chunk, 1), 0)
    token = vec(V_MASK)

    def place(image, c):
        def head_rows(i, c):
            at = pl.ds(pl.multiple_of(image * SD + i * chunk, chunk), chunk)
            got = latent_ref[pl.ds(pl.multiple_of(image * VMAX + i * chunk, chunk), chunk), :]
            x0[at, :] = jnp.where(i * chunk + order < length(image), got, token) + pos_ref[at, :]
            return c

        def tail_rows(i, c):
            at = pl.ds(pl.multiple_of(image * SD + i * chunk, chunk), chunk)
            x0[at, :] = token + pos_ref[at, :]
            return c

        loop(0, VMAX // chunk, head_rows, 0)
        loop(VMAX // chunk, SD // chunk, tail_rows, 0)
        return c

    loop(0, images, place, 0)
    norm_forward(x0, vec(DEC["g1"]), vec(DEC["s1"]), h1_ref)
    ready(0)
    qkv_forward(h1_ref, w_qkv, vec_ref, DEC["bqkv"], qkv)
    attend_all(qkv, att_ref, out_t, lse, images, SD, E, E // HD, lambda i: POS)
    ready(1)
    add_linear(x0, att_ref, w_out, vec_ref, DEC["bo"], mid)
    norm_forward(mid, vec(DEC["g2"]), vec(DEC["s2"]), h2_ref)
    ready(2)
    up_forward(h2_ref, w_up, vec_ref, DEC["bu"], act_ref, slope)
    ready(3)
    add_linear(mid, act_ref, w_down, vec_ref, DEC["bd"], x1)
    norm_forward(x1, vec(V_DNORM), vec(V_DNORM + E), hn_ref)
    ready(4)

    def predict(j, cols):
        pred[:, cols] = mm(hn_ref[...], w_head[:, cols]) + vec_at(vec_ref, V_HEAD, j)

    col_loop(PIX // BS, predict)

    def errors(image, c):
        def one(i, c):
            loss, bias = c
            at = pl.ds(pl.multiple_of(image * SD + i * chunk, chunk), chunk)
            target, _ = norm_parts(pix_ref[at, :].astype(F32))
            place_in = i * chunk + order
            masked = (place_in >= length(image)) & (place_in < POS)
            residual = jnp.where(masked, pred[at, :] - target, 0.0)
            low = (residual * (2.0 / PIX)).astype(BF)
            gpred_ref[at, :] = low
            return (loss + fold8(residual * residual), bias + fold8(low.astype(F32)))

        return loop(0, SD // chunk, one, c)

    zero = jnp.zeros((8, PIX), F32)
    loss, bias = loop(0, images, errors, (zero, zero))
    add_sum(sum_ref, DS_LOSS, loss)
    add_sum(sum_ref, DS_HEAD, bias)

    back_linear(gpred_ref, w_head, dy)
    d_gain, d_shift = norm_backward(x1, dy, vec(V_DNORM), grad, False)
    add_sum(sum_ref, DS_NORM, d_gain)
    add_sum(sum_ref, DS_NORM + E, d_shift)
    round_and_sum(grad, gdown_ref, sum_ref, DS["bd"])
    back_up(gdown_ref, w_down, slope, du_ref, sum_ref, DS["bu"])
    back_linear(du_ref, w_up, dy)
    d_gain, d_shift = norm_backward(mid, dy, vec(DEC["g2"]), grad, True)
    add_sum(sum_ref, DS["g2"], d_gain)
    add_sum(sum_ref, DS["s2"], d_shift)
    round_and_sum(grad, gproj_ref, sum_ref, DS["bo"])

    def back_out(j, cols):
        datt[:, cols] = mm_nt(gproj_ref[...], w_out[cols, :]).astype(BF)

    col_loop(E // BS, back_out)

    def attend_back(image, c):
        attention_backward(qkv, datt, out_t, lse, dqkv_ref, image, SD, E, E // HD, POS)
        return c

    loop(0, images, attend_back, 0)
    sum_rows(dqkv_ref, sum_ref, DS["bqkv"])
    back_linear(dqkv_ref, w_qkv, dy)
    d_gain, d_shift = norm_backward(x0, dy, vec(DEC["g1"]), grad, True)
    add_sum(sum_ref, DS["g1"], d_gain)
    add_sum(sum_ref, DS["s1"], d_shift)

    def unplace(image, c):
        def head_rows(i, c):
            got = grad[pl.ds(pl.multiple_of(image * SD + i * chunk, chunk), chunk), :]
            seen = i * chunk + order < length(image)
            at = pl.ds(pl.multiple_of(image * VMAX + i * chunk, chunk), chunk)
            glat_ref[at, :] = jnp.where(seen, got, 0.0).astype(BF)
            return c + fold8(jnp.where(seen, 0.0, got))

        def tail_rows(i, c):
            got = grad[pl.ds(pl.multiple_of(image * SD + i * chunk, chunk), chunk), :]
            return c + fold8(jnp.where(i * chunk + order < POS, got, 0.0))

        c = loop(0, VMAX // chunk, head_rows, c)
        return loop(VMAX // chunk, SD // chunk, tail_rows, c)

    add_sum(sum_ref, DS_MASK, loop(0, images, unplace, jnp.zeros((8, E), F32)))


def decoder(tile_rows, vis_len, gathered, vector, latent, pos_e, ordered, steps):
    images = vis_len.shape[0]
    rows = images * SD
    part = rows // steps
    outs = [
        ((rows, E), BF, "rows"),
        ((rows, 3 * E), BF, "rows"),
        ((rows, E), BF, "rows"),
        ((rows, E), BF, "rows"),
        ((rows, E), BF, "rows"),
        ((rows, FD), BF, "rows"),
        ((rows, FD), BF, "rows"),
        ((rows, E), BF, "rows"),
        ((rows, E), BF, "rows"),
        ((rows, PIX), BF, "rows"),
        ((images * VMAX, E), BF, "rows"),
        ((8, DS_ALL), F32, "whole"),
    ]
    scratch = [pltpu.VMEM(s, BF) for s in [(E, 3 * E), (E, E), (E, FD), (FD, E), (E, PIX)]]
    scratch += [
        pltpu.VMEM((part, E), F32),
        pltpu.VMEM((part, 3 * E), BF),
        pltpu.VMEM((images // steps, E // BS, BS * HD // E, SD), F32),
        pltpu.VMEM((images // steps, E // BS, BS, SD), F32),
        pltpu.VMEM((part, E), F32),
        pltpu.VMEM((part, FD), BF),
        pltpu.VMEM((part, E), F32),
        pltpu.VMEM((part, PIX), F32),
        pltpu.VMEM((part, E), F32),
        pltpu.VMEM((part, E), F32),
        pltpu.VMEM((part, E), BF),
        pltpu.SemaphoreType.DMA((5,)),
    ]
    return group_call(
        decoder_kernel,
        steps,
        (tile_rows, vis_len),
        [
            (gathered, "any"),
            (vector, "whole"),
            (latent, "rows"),
            (pos_e.reshape(rows, E), "rows"),
            (ordered.reshape(rows, PIX), "rows"),
        ],
        outs,
        scratch,
        "decoder",
    )


EM_BD, EM_BU = 0, D
EM_G2, EM_S2 = D + FE, 2 * D + FE
EM_BO, EM_NORM = 3 * D + FE, 4 * D + FE
EM_PROJ = 6 * D + FE
EM_ALL = EM_PROJ + E
EA_QKV, EA_G1, EA_S1, EA_EMBED, EA_ALL = 0, 3 * D, 4 * D, 5 * D, 6 * D


def encoder_mlp_back_kernel(
    start, given, row_ref, wg_ref, vec_ref, glat_ref, x1_ref, mid_ref, slope_ref,
    gdown_ref, du_ref, grad_ref, gproj_ref, sum_ref,
    w_proj, w_down, w_up, dy, sems,
):
    step = pl.program_id(0)
    ready = fetch_all(
        step == 0, row_ref, wg_ref, sems, [(T_PROJ, w_proj), (T_EDOWN, w_down), (T_EUP, w_up)]
    )

    @pl.when(step == 0)
    def _():
        sum_ref[...] = jnp.zeros_like(sum_ref)

    def vec(start):
        return vec_ref[:, start : start + D]

    sum_rows(glat_ref, sum_ref, EM_PROJ)
    ready(0)
    back_linear(glat_ref, w_proj, dy)
    d_gain, d_shift = norm_backward(x1_ref, dy, vec(V_ENORM), grad_ref, False)
    add_sum(sum_ref, EM_NORM, d_gain)
    add_sum(sum_ref, EM_NORM + D, d_shift)
    round_and_sum(grad_ref, gdown_ref, sum_ref, EM_BD)
    ready(1)
    back_up(gdown_ref, w_down, slope_ref, du_ref, sum_ref, EM_BU)
    ready(2)
    back_linear(du_ref, w_up, dy)
    d_gain, d_shift = norm_backward(mid_ref, dy, vec(ENC["g2"]), grad_ref, True)
    add_sum(sum_ref, EM_G2, d_gain)
    add_sum(sum_ref, EM_S2, d_shift)
    round_and_sum(grad_ref, gproj_ref, sum_ref, EM_BO)


def encoder_mlp_back(tile_rows, gathered, vector, glat, x1, mid, slope, steps):
    rows = x1.shape[0]
    part = rows // steps
    outs = [
        ((rows, D), BF, "rows"),
        ((rows, FE), BF, "rows"),
        ((rows, D), F32, "rows"),
        ((rows, D), BF, "rows"),
        ((8, EM_ALL), F32, "whole"),
    ]
    scratch = [pltpu.VMEM(s, BF) for s in [(D, E), (FE, D), (D, FE)]]
    scratch += [pltpu.VMEM((part, D), F32), pltpu.SemaphoreType.DMA((3,))]
    return group_call(
        encoder_mlp_back_kernel,
        steps,
        (tile_rows,),
        [
            (gathered, "any"),
            (vector, "whole"),
            (glat, "rows"),
            (x1, "rows"),
            (mid, "rows"),
            (slope, "rows"),
        ],
        outs,
        scratch,
        "encoder_mlp_back",
    )


def encoder_attention_back_kernel(
    start, given, row_ref, len_ref, wg_ref, vec_ref, gproj_ref, grad_in_ref, qkv_ref, lse_ref, out_t_ref, x0_ref, *refs
):
    dqkv_ref, gembed_ref, sum_ref, w_out, w_qkv, dy, grad, datt, sems = refs[given:]
    step = pl.program_id(0)
    images = lse_ref.shape[0]
    ready = fetch_all(step == 0, row_ref, wg_ref, sems, [(T_EOUT, w_out), (T_EQKV, w_qkv)])

    @pl.when(step == 0)
    def _():
        sum_ref[...] = jnp.zeros_like(sum_ref)

    ready(0)

    def back_out(j, cols):
        datt[:, cols] = mm_nt(gproj_ref[...], w_out[cols, :]).astype(BF)

    col_loop(D // BS, back_out)

    def attend_back(image, c):
        count = len_ref[(start + step) * images + image]
        attention_backward(qkv_ref, datt, out_t_ref, lse_ref, dqkv_ref, image, VMAX, D, D // HE, count)
        return c

    loop(0, images, attend_back, 0)
    sum_rows(dqkv_ref, sum_ref, EA_QKV)
    ready(1)
    back_linear(dqkv_ref, w_qkv, dy)
    grad[...] = grad_in_ref[...]
    gain = vec_ref[:, ENC["g1"] : ENC["g1"] + D]
    d_gain, d_shift = norm_backward(x0_ref, dy, gain, grad, True)
    add_sum(sum_ref, EA_G1, d_gain)
    add_sum(sum_ref, EA_S1, d_shift)
    round_and_sum(grad, gembed_ref, sum_ref, EA_EMBED)


def encoder_attention_back(tile_rows, vis_len, gathered, vector, gproj, grad, qkv, lse, out_t, x0, steps, share, given):
    rows = x0.shape[0]
    part = rows // steps
    outs = [((rows, 3 * D), BF, "rows"), ((rows, D), BF, "rows"), ((8, EA_ALL), F32, "whole")]
    scratch = [pltpu.VMEM(s, BF) for s in [(D, D), (D, 3 * D)]]
    scratch += [pltpu.VMEM((part, D), F32), pltpu.VMEM((part, D), F32), pltpu.VMEM((part, D), BF)]
    return group_call(
        encoder_attention_back_kernel,
        steps,
        (tile_rows, vis_len),
        [
            (gathered, "any"),
            (vector, "whole"),
            (gproj, "rows"),
            (grad, "rows"),
            (qkv, "rows"),
            (lse, "rows"),
            (out_t, "rows"),
            (x0, "rows"),
        ],
        outs,
        scratch + [pltpu.SemaphoreType.DMA((2,))],
        "encoder_attention_back",
        share,
        given,
    )


def weight_grad_kernel(parts, cut, extra, index_ref, x_ref, g_ref, *refs):
    outs = refs[extra : extra + min(parts, 2)]
    x_t, total = refs[-2:]
    row_tiles, col_tiles = x_ref.shape[1] // BS, g_ref.shape[1] // BS

    @pl.when(pl.program_id(1) == 0)
    def _():
        x_t[...] = x_ref[...].T

    total[...] = mm(x_t[...], g_ref[...])
    for p in range(parts):
        for i in range(row_tiles):
            start = pl.multiple_of(i * BS + (p ^ index_ref[0]) * cut, cut)
            for j in range(col_tiles):
                got = total[pl.ds(start, cut), j * BS : (j + 1) * BS]
                outs[p % 2][p // 2, i * col_tiles + j] = got.astype(BF)


def weight_grad(index, parts, count, first, x, g, block, buffers):
    cut = BS // parts
    rows, width = x.shape
    row_tiles, col_tiles = block
    size = row_tiles * col_tiles
    across = g.shape[1] // (col_tiles * BS)
    assert first % size == 0
    held = min(parts, 2)
    shape = jax.ShapeDtypeStruct((parts // held, count, cut, BS), BF)
    given = list(buffers or [])
    out_spec = pl.BlockSpec(
        (parts // held, size, cut, BS), lambda i, j, *_: (0, first // size + i * across + j, 0, 0)
    )
    return pl.pallas_call(
        functools.partial(weight_grad_kernel, parts, cut, len(given)),
        grid_spec=pltpu.PrefetchScalarGridSpec(
            num_scalar_prefetch=1,
            grid=(width // (row_tiles * BS), across),
            in_specs=[
                pl.BlockSpec((rows, row_tiles * BS), lambda i, j, *_: (0, i)),
                pl.BlockSpec((rows, col_tiles * BS), lambda i, j, *_: (0, j)),
            ]
            + [pl.BlockSpec(memory_space=pl.ANY)] * len(given),
            out_specs=[out_spec] * held,
            scratch_shapes=[
                pltpu.VMEM((row_tiles * BS, rows), BF),
                pltpu.VMEM((row_tiles * BS, col_tiles * BS), F32),
            ],
        ),
        out_shape=[shape] * held,
        input_output_aliases={3 + i: i for i in range(len(given))},
        compiler_params=pltpu.CompilerParams(vmem_limit_bytes=VMEM_LIMIT),
        cost_estimate=SMALL,
        name="weight_grad",
    )(index, x, g, *given)


def seed_kernel(parts, parcels, own, index_ref, *refs):
    sums, outs, rows = refs[: -1 - min(parts, 2)], refs[-1 - min(parts, 2) : -1], refs[-1]
    rows[...] = jnp.zeros_like(rows)
    at = 0
    for source, start, size in parcels:
        for k in range(0, size, 128):
            piece = sum(jnp.sum(sums[i][:, start + k : start + k + 128], axis=0, keepdims=True) for i in source)
            row, col = at % own // BS, at % own % BS
            rows[at // own, row : row + 1, col : col + 128] = piece
            at += 128
    for p in range(parts):
        out = outs[p % 2]
        out[p // 2, 0] = rows[p ^ index_ref[0]].astype(BF)
        for t in range(1, out.shape[1]):
            out[p // 2, t] = jnp.zeros(rows.shape[1:], BF)


def seed_buffers(index, parts, count, first, sums=(), parcels=(), own=1):
    cut = BS // parts
    held = min(parts, 2)
    size = count - first
    assert first % size == 0
    shape = jax.ShapeDtypeStruct((parts // held, count, cut, BS), BF)
    return pl.pallas_call(
        functools.partial(seed_kernel, parts, parcels, own),
        grid_spec=pltpu.PrefetchScalarGridSpec(
            num_scalar_prefetch=1,
            grid=(1,),
            in_specs=[pl.BlockSpec(x.shape, lambda i, *_: (0, 0)) for x in sums],
            out_specs=[pl.BlockSpec((parts // held, size, cut, BS), lambda i, *_: (0, first // size, 0, 0))] * held,
            scratch_shapes=[pltpu.VMEM((parts, cut, BS), F32)],
        ),
        out_shape=[shape] * held,
        cost_estimate=SMALL,
        name="seed_buffers",
    )(index, *sums)


def low_sum(a, b):
    return (a.astype(F32) + b.astype(F32)).astype(BF)


def swap_bit(x, bit, size):
    return lax.ppermute(x, "dp", [(i, i ^ (1 << bit)) for i in range(size)])


def reduce_core(buffers, parts):
    if parts == 1:
        whole, count = buffers[0][0], buffers[0].shape[1]
        return [whole[: count // 2], whole[count // 2 :]], [[], []]
    whole = low_sum(buffers[0], swap_bit(buffers[1], 0, parts))
    bits = list(range(parts.bit_length() - 2, 0, -1))
    whole = whole.reshape((2,) * len(bits) + whole.shape[1:])
    count = whole.shape[-3]
    return [whole[..., : count // 2, :, :], whole[..., count // 2 :, :, :]], [bits, bits]


def reduce_chips(state, parts, steps):
    halves, left = list(state[0]), list(state[1])
    for half in range(2):
        for _ in range(min(steps, len(left[half]))):
            bit = left[half][-1 if half == 0 else 0]
            axis = left[half].index(bit)
            keep = lax.index_in_dim(halves[half], 0, axis, keepdims=False)
            send = lax.index_in_dim(halves[half], 1, axis, keepdims=False)
            halves[half] = low_sum(keep, swap_bit(send, bit, parts))
            left[half] = [b for b in left[half] if b != bit]
    return halves, left


def patch_steps(groups):
    middle = groups // 2 - 1

    def inwards(k, x):
        return low_sum(x, lax.ppermute(x, "patch", [(k, k + 1), (groups - 1 - k, groups - 2 - k)]))

    def across(x):
        return low_sum(x, lax.ppermute(x, "patch", [(middle, middle + 1), (middle + 1, middle)]))

    def outwards(k, x):
        got = lax.ppermute(x, "patch", [(k + 1, k), (groups - 2 - k, groups - 1 - k)])
        me = lax.axis_index("patch")
        return jnp.where((me == k) | (me == groups - 1 - k), got, x)

    if groups == 1:
        return []
    steps = [functools.partial(inwards, k) for k in range(middle)] + [across]
    return steps + [functools.partial(outwards, k) for k in reversed(range(middle))]


def sum_patch(x, steps):
    for step in steps:
        x = step(x)
    return x


def sum_all(x, parts, groups):
    for bit in range(groups.bit_length() - 1):
        x = x + lax.ppermute(x, "patch", [(i, i ^ (1 << bit)) for i in range(groups)])
    return sum_dp(x, parts)


def sum_dp(x, parts):
    for bit in range(parts.bit_length() - 1):
        x = x + swap_bit(x, bit, parts)
    return x


def split_low(x):
    high = x.astype(BF)
    return high, (x - high.astype(F32)).astype(BF)


def tile_kernel(
    scale_ref, grad_ref, w_ref, left_stat_ref, right_stat_ref, left_root_ref, right_root_ref,
    clipped_ref, left_new_ref, right_new_ref, w_new_ref,
):
    scale = scale_ref[0]
    for t in range(w_ref.shape[0]):
        grad = grad_ref[:, t].reshape(BS, BS)
        clipped_ref[t] = grad.astype(F32) * scale
        square = (1.0 - BETA_STAT) * scale * scale
        left_new_ref[t] = BETA_STAT * left_stat_ref[t] + square * mm_nt(grad, grad)
        right_new_ref[t] = BETA_STAT * right_stat_ref[t] + square * mm_tn(grad, grad)
        high, low = split_low(left_root_ref[t])
        half = (mm(high, grad) + mm(low, grad)) * scale
        half_high, half_low = split_low(half)
        high, low = split_low(right_root_ref[t])
        direction = mm(half_high, high) + (mm(half_high, low) + mm(half_low, high))
        direction = direction * lax.rsqrt(jnp.mean(direction * direction) + EPS_ROOT)
        w_new_ref[t] = w_ref[t] - RATE_MATRIX * (direction + DECAY_MATRIX * w_ref[t])


def tile_update(scale, grads, states):
    parts, slots, cut, _ = grads.shape
    per = max(p for p in range(1, 7) if slots % p == 0)
    tile = pl.BlockSpec((per, BS, BS), lambda i, *_: (i, 0, 0))
    return pl.pallas_call(
        tile_kernel,
        grid_spec=pltpu.PrefetchScalarGridSpec(
            num_scalar_prefetch=1,
            grid=(slots // per,),
            in_specs=[pl.BlockSpec((parts, per, cut, BS), lambda i, *_: (0, i, 0, 0))] + [tile] * 5,
            out_specs=[tile] * 4,
        ),
        out_shape=[jax.ShapeDtypeStruct((slots, BS, BS), F32)] * 4,
        compiler_params=pltpu.CompilerParams(vmem_limit_bytes=VMEM_LIMIT),
        name="tile_update",
    )(scale.reshape(1), grads, *states)


def vector_update(clipped, vectors, moment, second):
    moment_new = BETA_FIRST * moment + (1.0 - BETA_FIRST) * clipped
    second_new = BETA_SECOND * second + (1.0 - BETA_SECOND) * clipped * clipped
    corrected = moment_new / (1.0 - BETA_FIRST**STEP)
    scaled = second_new / (1.0 - BETA_SECOND**STEP)
    vectors_new = vectors - RATE_VECTOR * corrected / (jnp.sqrt(scaled) + EPS_ADAM)
    return moment_new, second_new, vectors_new


CHUNKS = [
    [
        (T_DUP, 2, 8, (2, 4)),
        (T_DDOWN, 8, 2, (4, 2)),
        (T_DOUT, 2, 2, (2, 2)),
        (T_DQKV, 2, 6, (2, 3)),
        (T_HEAD, 2, 3, (2, 3)),
        (T_PROJ, 3, 2, (3, 2)),
    ],
    [(T_EUP, 3, 12, (3, 4)), (T_EDOWN, 12, 3, (4, 3)), (T_EOUT, 3, 3, (3, 3))],
    [(T_EQKV, 3, 9, (3, 3)), (T_EMBED, 3, 3, (3, 3))],
]


def chunk_sizes():
    sizes = [sum(r * c for _, r, c, _ in chunk) for chunk in CHUNKS]
    return sizes[:-1] + [sizes[-1] + 2]


def tile_places(sizes):
    chunk_of = np.zeros(NBLK + 2, np.int32)
    place_of = np.zeros(NBLK + 2, np.int32)
    for i, chunk in enumerate(CHUNKS):
        at = 0
        for first, row_tiles, col_tiles, (high, wide) in chunk:
            for r in range(row_tiles):
                for c in range(col_tiles):
                    block = r // high * (col_tiles // wide) + c // wide
                    chunk_of[first + r * col_tiles + c] = i
                    place_of[first + r * col_tiles + c] = at + block * high * wide + r % high * wide + c % wide
            at += row_tiles * col_tiles
    chunk_of[NBLK:] = len(CHUNKS) - 1
    place_of[NBLK + 1] = at
    place_of[NBLK] = at + 1
    return chunk_of, place_of


def shards(parts, groups, pixels, shuffle, vis_len, block_owner, weights, vectors, vec_moment, vec_second,
           left_stat, right_stat, left_root, right_root):
    slots = weights.shape[0]
    own = vectors.shape[0]
    index = lax.axis_index("dp").astype(jnp.int32).reshape(1)
    images = pixels.shape[0]

    vector_rows = -(-own // (16 * BS)) * 16
    mine = jnp.concatenate(
        [
            weights.astype(BF).reshape(slots * BS, BS),
            jnp.pad(vectors.astype(BF), (0, vector_rows * BS - own)).reshape(vector_rows, BS),
        ]
    )
    gathered = lax.all_gather(mine, "dp", axis=0, tiled=True)
    stride = mine.shape[0]
    slot_index = jnp.arange(block_owner.shape[0], dtype=jnp.int32)
    slot_of_block = jnp.sum(
        jnp.where(block_owner[None, :] == jnp.arange(NBLK, dtype=jnp.int32)[:, None], slot_index[None, :], 0),
        axis=1,
    )
    tile_rows = slot_of_block // slots * stride + slot_of_block % slots * BS
    vector = gathered.reshape(parts, stride, BS)[:, slots * BS :].reshape(parts, vector_rows * BS)
    vector = vector[:, :own].reshape(-1).astype(F32)
    enc_key, dec_key = 4 * D, 4 * D + (8 * D + FE - 3 * D) + 2 * D + 2 * E + 3 * E
    vector = jnp.concatenate(
        [vector[:enc_key], jnp.zeros(D, F32), vector[enc_key:dec_key], jnp.zeros(E, F32), vector[dec_key:]]
    ).reshape(1, V_ALL)

    ordered, visible_pix, pos_d, pos_e = order_patches(pixels, shuffle)
    (x0, h1, qkv, lse, out_t, att, mid, h2, act, slope, x1, hn, latent) = encoder_forward(
        tile_rows, vis_len, gathered, vector, visible_pix, pos_d, 2
    )
    (d_h1, d_dqkv, d_att, d_gproj, d_h2, d_du, d_act, d_gdown, d_hn, d_gpred, glat, d_sums) = decoder(
        tile_rows, vis_len, gathered, vector, latent, pos_e, ordered, 4
    )
    sizes = chunk_sizes()
    chunk_of, place_of = tile_places(sizes)

    rows_cut = BS // parts

    def gradients(chunk, pairs, vector=(), first=0, buffers=None):
        used = sum(r * c for _, r, c, _ in CHUNKS[chunk])
        if sizes[chunk] > used and buffers is None:
            buffers = seed_buffers(index, parts, sizes[chunk], used, *vector)
        at = sum(r * c for _, r, c, _ in CHUNKS[chunk][:first])
        for (x, g), (_, row_tiles, col_tiles, block) in zip(pairs, CHUNKS[chunk][first:]):
            buffers = weight_grad(index, parts, sizes[chunk], at, x, g, block, buffers)
            at += row_tiles * col_tiles
        return buffers

    def attention_back(gproj, k, given):
        return encoder_attention_back(
            tile_rows, vis_len, gathered, vector, gproj, grad_mid, qkv, lse, out_t, x0, 2, (k, 2), given
        )

    def core(buffers):
        return reduce_core(buffers, parts)

    def chips(state, steps):
        return reduce_chips(state, parts, steps)

    after = lax.optimization_barrier
    steps = patch_steps(groups)
    gdown, du, grad_mid, gproj, m_sums = encoder_mlp_back(tile_rows, gathered, vector, glat, x1, mid, slope, 2)
    buf1 = gradients(1, [(h2, du), (act, gdown), (att, gproj)])
    d_h2, d_act, buf1 = after((d_h2, d_act, buf1))
    buf0 = gradients(0, [(d_h2, d_du), (d_act, d_gdown)])
    half1, left1 = core(buf1)
    d_att, d_h1, d_hn, hn, buf0, half1 = after((d_att, d_h1, d_hn, hn, buf0, half1))
    half1, left1 = chips((half1, left1), 1)
    buf0 = gradients(0, [(d_att, d_gproj), (d_h1, d_dqkv), (d_hn, d_gpred), (hn, glat)], (), 2, buf0)
    gproj, buf0 = after((gproj, buf0))
    dqkv, gembed, a_sums = attention_back(gproj, 0, ())
    gproj, dqkv, gembed, buf0, half1 = after((gproj, dqkv, gembed, buf0, half1))
    dqkv, gembed, b_sums = attention_back(gproj, 1, (dqkv, gembed))
    (one, two), _ = chips((half1, left1), 99)
    half0, left0 = core(buf0)
    dqkv, gembed, b_sums, half0, one, two = after((dqkv, gembed, b_sums, half0, one, two))

    late, early, dec = (0, 1), (2,), (3,)
    parcels = [
        (late, EA_EMBED, D),
        (late, EA_G1, 2 * D),
        (late, EA_QKV, D),
        (late, EA_QKV + 2 * D, D),
        (early, EM_BO, D),
        (early, EM_G2, 2 * D),
        (early, EM_BU, FE),
        (early, EM_BD, D),
        (early, EM_NORM, 2 * D),
        (early, EM_PROJ, E),
        (dec, DS_MASK, E),
        (dec, DS["g1"], 2 * E),
        (dec, DS["bqkv"], E),
        (dec, DS["bqkv"] + 2 * E, E),
        (dec, DS["bo"], E),
        (dec, DS["g2"], 2 * E),
        (dec, DS["bu"], FD),
        (dec, DS["bd"], E),
        (dec, DS_NORM, 2 * E),
        (dec, DS_HEAD, PIX),
    ]
    sums = (a_sums, b_sums, m_sums, d_sums)
    buf2 = gradients(2, [(h1, dqkv), (visible_pix.reshape(-1, PIX), gembed)], (sums, parcels, own))
    half0, left0 = chips((half0, left0), 1)
    one = sum_patch(one, steps[:1])
    two = sum_patch(two, steps[:1])
    buf2, half0, one = after((buf2, half0, one))
    half2, left2 = core(buf2)
    half0, _ = chips((half0, left0), 99)
    one = sum_patch(one, steps[1:2])
    half2, half0, one, two = after((half2, half0, one, two))
    half2, left2 = chips((half2, left2), 1)
    one = sum_patch(one, steps[2:])
    two = sum_patch(two, steps[1:2])
    half0 = [sum_patch(x, steps[:1]) for x in half0]
    half2, one, two = after((half2, one, two))
    half2, _ = chips((half2, left2), 99)
    two = sum_patch(two, steps[2:])
    half2, half0, two = after((half2, half0, two))
    half2 = [sum_patch(x, steps) for x in half2]
    half0 = [sum_patch(x, steps[1:]) for x in half0]
    pieces = half0 + [one, two] + half2
    mine = jnp.where(lax.axis_index("patch") == 0, 1.0, 0.0)

    def squares(x):
        wide = x.astype(F32)
        return jnp.sum(wide * wide)

    totals = jnp.stack(
        [
            jnp.sum(d_sums[:, DS_LOSS : DS_LOSS + PIX]) / PIX,
            jnp.sum(POS - vis_len).astype(F32),
            sum(squares(x) for x in pieces) * mine,
        ]
    )
    totals = sum_all(totals, parts, groups)
    loss_sum, masked_count = totals[0], totals[1]
    grad_norm = jnp.sqrt(totals[2]) / masked_count
    scale = jnp.minimum(1.0, CLIP_NORM / grad_norm) / masked_count

    reduced = jnp.concatenate(pieces, axis=0)
    where = jnp.asarray(np.cumsum([0] + sizes)[chunk_of] + place_of, jnp.int32)
    slot_rows = reduced[where[jnp.minimum(block_owner, NBLK)]]
    if parts > 1:
        slot_rows = lax.all_to_all(slot_rows, "dp", 0, 0, tiled=True)
    grads = slot_rows.reshape(parts, slots, rows_cut, BS)
    clipped, left_new, right_new, weights_new = tile_update(
        scale, grads, (weights, left_stat, right_stat, left_root, right_root)
    )
    own_vector = lax.dynamic_index_in_dim(reduced, where[NBLK + 1], 0, keepdims=False)
    own_vector = own_vector.reshape(-1)[:own].astype(F32) * scale
    moment_new, second_new, vectors_new = vector_update(own_vector, vectors, vec_moment, vec_second)
    return (
        loss_sum,
        masked_count,
        grad_norm,
        clipped,
        left_new,
        right_new,
        weights_new,
        moment_new,
        second_new,
        vectors_new,
    )


def solution(mesh):
    both = ("dp", "patch")
    tiles = P("dp", None, None)
    return jax.shard_map(
        functools.partial(shards, mesh.shape["dp"], mesh.shape["patch"]),
        mesh=mesh,
        in_specs=(P(both, None, None), P(both, None), P(both), P())
        + (tiles, P("dp"), P("dp"), P("dp"))
        + (tiles,) * 4,
        out_specs=(P(), P(), P()) + (tiles,) * 4 + (P("dp"),) * 3,
        check_vma=False,
    )
```

```python
import functools
import math

import jax
import jax.numpy as jnp
import numpy as np
from jax import lax
from jax.experimental import pallas as pl
from jax.experimental.pallas import tpu as pltpu
from jax.sharding import PartitionSpec as P

D = 768
HE = 12
FE = 3072
E = 512
HD = 16
FD = 2048
PIX = 768
POS = 196
VMAX = 80
BS = 256
STEP = 10
NBLK = 177

SD = 208

EPS_NORM = 1e-06
EPS_ROOT = 1e-06
EPS_ADAM = 1e-08
CLIP_NORM = 0.01
RATE_MATRIX = 0.03
DECAY_MATRIX = 0.05
BETA_STAT = 0.5
BETA_FIRST = 0.9
BETA_SECOND = 0.999
RATE_VECTOR = 0.1
NEG_LARGE = -1e30
LOG2E = math.log2(math.e)

BF = jnp.bfloat16
F32 = jnp.float32
VMEM_LIMIT = 60 * 1024 * 1024
SMALL = pl.CostEstimate(flops=1000, bytes_accessed=1000, transcendentals=0)

T_EMBED, T_EQKV, T_EOUT, T_EUP, T_EDOWN, T_PROJ = 0, 9, 36, 45, 81, 117
T_DQKV, T_DOUT, T_DUP, T_DDOWN, T_HEAD = 123, 135, 139, 155, 171

V_EMBED = 0
V_ENC = D
V_ENORM = V_ENC + 9 * D + FE
V_PROJ = V_ENORM + 2 * D
V_MASK = V_PROJ + E
V_DEC = V_MASK + E
V_DNORM = V_DEC + 9 * E + FD
V_HEAD = V_DNORM + 2 * E
V_ALL = V_HEAD + PIX


def layer_offsets(start, width, hidden):
    names = ["g1", "s1", "bqkv", "bo", "g2", "s2", "bu", "bd"]
    sizes = [width, width, 3 * width, width, width, width, hidden, width]
    offsets = {}
    for name, size in zip(names, sizes):
        offsets[name] = start
        start += size
    return offsets


def mm(a, b):
    return jnp.dot(a, b, preferred_element_type=F32)


def mm_nt(a, b):
    return lax.dot_general(a, b, (((1,), (1,)), ((), ())), preferred_element_type=F32)


def mm_tn(a, b):
    return lax.dot_general(a, b, (((0,), (0,)), ((), ())), preferred_element_type=F32)


def fold8(x):
    rows, cols = x.shape
    return jnp.sum(x.reshape(rows // 8, 8, cols), axis=0)


def gelu_pair(u):
    t = 1.0 / (1.0 + (0.3275911 * math.sqrt(0.5)) * jnp.abs(u))
    e = jnp.exp2((-0.5 * LOG2E) * (u * u))
    poly = t * (
        0.5 * 0.254829592
        + t * (-0.5 * 0.284496736 + t * (0.5 * 1.421413741 + t * (-0.5 * 1.453152027 + t * (0.5 * 1.061405429))))
    )
    tail = poly * e
    phi = jnp.where(u >= 0, 1.0 - tail, tail)
    return u * phi, phi + u * (e * (1.0 / math.sqrt(2.0 * math.pi)))


def norm_parts(x):
    centred = x - jnp.mean(x, axis=-1, keepdims=True)
    inverse = lax.rsqrt(jnp.mean(centred * centred, axis=-1, keepdims=True) + EPS_NORM)
    return centred * inverse, inverse


def loop(lower, upper, body, carry, most=26):
    count = upper - lower
    unroll = max(u for u in range(1, min(most, count) + 1) if count % u == 0)
    return lax.fori_loop(lower, upper, body, carry, unroll=unroll)


def row_loop(rows, step, body, carry=0):
    count = rows // step

    def one(i, c):
        return body(pl.ds(pl.multiple_of(i * step, step), step), c)

    return loop(0, count, one, carry)


def norm_forward(x_ref, gain, shift, out_ref):
    def body(sl, c):
        normed, _ = norm_parts(x_ref[sl, :])
        out_ref[sl, :] = (normed * gain + shift).astype(BF)
        return c

    row_loop(x_ref.shape[0], 16, body)


def norm_backward(x_ref, dy_ref, gain, out_ref, add):
    width = x_ref.shape[1]

    def body(sl, c):
        d_gain, d_shift = c
        normed, inverse = norm_parts(x_ref[sl, :])
        dy = dy_ref[sl, :]
        dn = dy * gain
        mean_one = jnp.mean(dn, axis=-1, keepdims=True)
        mean_two = jnp.mean(dn * normed, axis=-1, keepdims=True)
        dx = inverse * (dn - mean_one - normed * mean_two)
        out_ref[sl, :] = out_ref[sl, :] + dx if add else dx
        return (d_gain + fold8(dy * normed), d_shift + fold8(dy))

    zero = jnp.zeros((8, width), F32)
    return row_loop(x_ref.shape[0], 16, body, (zero, zero))


def col_loop(count, body):
    def one(j, c):
        body(j, pl.ds(pl.multiple_of(j * BS, BS), BS))
        return c

    loop(0, count, one, 0, 12)


def vec_at(vec_ref, start, j):
    return vec_ref[:, pl.ds(pl.multiple_of(start + j * BS, BS), BS)]


def head_mask(head, head_size):
    lane = lax.broadcasted_iota(jnp.int32, (1, BS), 1)
    inside = (lane >= head * head_size) & (lane < (head + 1) * head_size)
    return jnp.where(inside, 1.0, 0.0).astype(BF)


def masked_scores(raw, head_size, count):
    scores = raw * (head_size**-0.5 * LOG2E)
    if isinstance(count, int):
        whole = count // 8 * 8
        tail = scores[whole:]
        row = lax.broadcasted_iota(jnp.int32, tail.shape, 0) + whole
        return jnp.concatenate([scores[:whole], jnp.where(row < count, tail, NEG_LARGE)], axis=0)
    row = lax.broadcasted_iota(jnp.int32, (scores.shape[0], 1), 0)
    return jnp.where(row < count, scores, NEG_LARGE)


def scores_bounded(qkv_ref, width, head_size):
    lane = lax.broadcasted_iota(jnp.int32, (BS, 128), 0) // head_size
    pick = jnp.where(lane == lax.broadcasted_iota(jnp.int32, (BS, 128), 1), 1.0, 0.0).astype(BF)
    score, value = None, None
    for g in range(width // BS):
        tops = []
        for which in range(3):
            x = qkv_ref[:, which * width + g * BS : which * width + (g + 1) * BS]
            tops.append(jnp.max(mm(x * x, pick), axis=0, keepdims=True))
        one = tops[0] * tops[1]
        score = one if score is None else jnp.maximum(score, one)
        value = tops[2] if value is None else jnp.maximum(value, tops[2])
    limit = 90.0 / (1.05 * head_size**-0.5 * LOG2E)
    return (jnp.max(score) < limit * limit) & (jnp.max(value) < 2.0**40)


def attention_forward(qkv_ref, att_ref, out_t_ref, lse_ref, image, seq, width, head_size, count, bounded):
    rows = pl.ds(pl.multiple_of(image * seq, 16), seq)
    per = BS // head_size
    most = min(8, per)

    def group(g, c):
        def part(which):
            return qkv_ref[rows, pl.ds(pl.multiple_of(which * width + g * BS, BS), BS)]

        q, k, v = part(0), part(1), part(2)
        v_t = v.T
        q = q.T
        ones = jnp.ones((16, seq), BF)
        outs, logs = [], []
        for h in range(per):
            if h % most == 0:
                stacked = jnp.concatenate([k * head_mask(i, head_size) for i in range(h, h + most)], axis=0)
                many = mm(stacked, q)
            scores = masked_scores(many[h % most * seq : (h % most + 1) * seq], head_size, count)
            top = 0.0
            if not bounded:
                top = jnp.max(scores, axis=0, keepdims=True)
                scores = scores - top
            e = jnp.exp2(scores).astype(BF)
            both = mm(jnp.concatenate([v_t[h * head_size : (h + 1) * head_size, :], ones], axis=0), e)
            total = both[head_size : head_size + 1, :]
            outs.append(both[:head_size, :] * (1.0 / total))
            logs.append(top + jnp.log2(total))
        out_t = jnp.concatenate(outs, axis=0)
        out_t_ref[image, g] = out_t
        att_ref[rows, pl.ds(pl.multiple_of(g * BS, BS), BS)] = out_t.T.astype(BF)
        lse_ref[image, g] = jnp.concatenate(logs, axis=0)
        return c

    loop(0, width // BS, group, 0)


def attend_all(qkv_ref, att_ref, out_t_ref, lse_ref, images, seq, width, head_size, count_of):
    safe = scores_bounded(qkv_ref, width, head_size)

    def run(bounded):
        def one(image, c):
            count = count_of(image)
            attention_forward(
                qkv_ref, att_ref, out_t_ref, lse_ref, image, seq, width, head_size, count, bounded
            )
            return c

        loop(0, images, one, 0)

    @pl.when(safe)
    def _():
        run(True)

    @pl.when(jnp.logical_not(safe))
    def _():
        run(False)


def attention_backward(qkv_ref, datt_ref, out_t_ref, lse_ref, dqkv_ref, image, seq, width, head_size, count):
    rows = pl.ds(pl.multiple_of(image * seq, 16), seq)
    per = BS // head_size
    scale = head_size**-0.5
    most = min(8, per)

    def group(g, c):
        def cols(which):
            return pl.ds(pl.multiple_of(which * width + g * BS, BS), BS)

        q, k, v = qkv_ref[rows, cols(0)], qkv_ref[rows, cols(1)], qkv_ref[rows, cols(2)]
        d_out = datt_ref[rows, cols(0)]
        lse = lse_ref[image, g]
        q_t, k_t, d_out_t = q.T, k.T, d_out.T
        along = d_out_t.astype(F32) * out_t_ref[image, g]
        lane = lax.broadcasted_iota(jnp.int32, (seq, BS), 1)
        d_q, d_k, d_v = [], None, None
        for start in range(0, per, most):
            heads = range(start, start + most)
            many = mm(jnp.concatenate([k * head_mask(h, head_size) for h in heads], axis=0), q_t)
            more = mm(jnp.concatenate([v * head_mask(h, head_size) for h in heads], axis=0), d_out_t)
            probs_all, scores_all = [], []
            for h in heads:
                part = slice(h * head_size, (h + 1) * head_size)
                at = slice((h - start) * seq, (h - start + 1) * seq)
                delta = jnp.sum(along[part, :], axis=0, keepdims=True)
                probs = jnp.exp2(masked_scores(many[at], head_size, count) - lse[h : h + 1, :])
                d_scores = (probs * (more[at] - delta)).astype(BF)
                d_q.append(mm(k_t[part, :], d_scores))
                probs_all.append(probs.astype(BF))
                scores_all.append(d_scores)
            for_v = mm(jnp.concatenate(probs_all, axis=0), d_out)
            for_k = mm(jnp.concatenate(scores_all, axis=0), q)
            for h in heads:
                at = slice((h - start) * seq, (h - start + 1) * seq)
                inside = (lane >= h * head_size) & (lane < (h + 1) * head_size)
                d_v = for_v[at] if d_v is None else jnp.where(inside, for_v[at], d_v)
                d_k = for_k[at] if d_k is None else jnp.where(inside, for_k[at], d_k)
        dqkv_ref[rows, cols(0)] = (jnp.concatenate(d_q, axis=0).T * scale).astype(BF)
        dqkv_ref[rows, cols(1)] = (d_k * scale).astype(BF)
        dqkv_ref[rows, cols(2)] = d_v.astype(BF)
        return c

    loop(0, width // BS, group, 0)


def fetch_tiles(row_ref, wg_ref, first, dst, sem):
    row_tiles, col_tiles = dst.shape[0] // BS, dst.shape[1] // BS
    for i in range(row_tiles):
        for j in range(col_tiles):
            start = pl.multiple_of(row_ref[first + i * col_tiles + j], 16)
            pltpu.make_async_copy(
                wg_ref.at[pl.ds(start, BS), :],
                dst.at[i * BS : (i + 1) * BS, j * BS : (j + 1) * BS],
                sem,
            ).start()


def await_tiles(dst, sem):
    pltpu.make_async_copy(dst, dst, sem).wait()


def fetch_all(first_step, row_ref, wg_ref, sems, matrices):
    @pl.when(first_step)
    def _():
        for i, (first, dst) in enumerate(matrices):
            fetch_tiles(row_ref, wg_ref, first, dst, sems.at[i])

    def ready(i):
        @pl.when(first_step)
        def _():
            await_tiles(matrices[i][1], sems.at[i])

    return ready


def qkv_forward(h_ref, w_ref, vec_ref, start, out_ref):
    def body(j, cols):
        out_ref[:, cols] = (mm(h_ref[...], w_ref[:, cols]) + vec_at(vec_ref, start, j)).astype(BF)

    col_loop(w_ref.shape[1] // BS, body)


def add_linear(x_ref, h_ref, w_ref, vec_ref, start, out_ref):
    def body(j, cols):
        out_ref[:, cols] = x_ref[:, cols] + (mm(h_ref[...], w_ref[:, cols]) + vec_at(vec_ref, start, j))

    col_loop(w_ref.shape[1] // BS, body)


def up_forward(h_ref, w_ref, vec_ref, start, act_ref, slope_ref):
    def body(j, cols):
        act, slope = gelu_pair(mm(h_ref[...], w_ref[:, cols]) + vec_at(vec_ref, start, j))
        act_ref[:, cols] = act.astype(BF)
        slope_ref[:, cols] = slope.astype(BF)

    col_loop(w_ref.shape[1] // BS, body)


def back_linear(g_ref, w_ref, out_ref):
    def body(j, cols):
        out_ref[:, cols] = mm_nt(g_ref[...], w_ref[cols, :])

    col_loop(w_ref.shape[0] // BS, body)


def back_up(g_ref, w_ref, slope_ref, du_ref, sum_ref, start):
    def body(j, cols):
        du = (mm_nt(g_ref[...], w_ref[cols, :]) * slope_ref[:, cols].astype(F32)).astype(BF)
        du_ref[:, cols] = du
        at = pl.ds(pl.multiple_of(start + j * BS, BS), BS)
        sum_ref[:, at] = sum_ref[:, at] + fold8(du.astype(F32))

    col_loop(w_ref.shape[0] // BS, body)


def round_and_sum(x_ref, out_ref, sum_ref, start):
    width = x_ref.shape[1]

    def body(sl, c):
        low = x_ref[sl, :].astype(BF)
        out_ref[sl, :] = low
        return c + fold8(low.astype(F32))

    total = row_loop(x_ref.shape[0], 16, body, jnp.zeros((8, width), F32))
    sum_ref[:, start : start + width] = sum_ref[:, start : start + width] + total


def sum_rows(x_ref, sum_ref, start):
    width = x_ref.shape[1]

    def body(sl, c):
        return c + fold8(x_ref[sl, :].astype(F32))

    total = row_loop(x_ref.shape[0], 16, body, jnp.zeros((8, width), F32))
    sum_ref[:, start : start + width] = sum_ref[:, start : start + width] + total


def add_sum(sum_ref, start, value):
    stop = start + value.shape[1]
    sum_ref[:, start:stop] = sum_ref[:, start:stop] + value


def order_kernel(shuffle_ref, pixels_ref, sin_d_ref, sin_e_ref, all_ref, visible_ref, pos_d_ref, pos_e_ref):
    ids = shuffle_ref[0]
    pick = jnp.where(ids == lax.broadcasted_iota(jnp.int32, (SD, POS), 1), 1.0, 0.0).astype(BF)
    ordered = mm(pick, pixels_ref[0]).astype(BF)
    all_ref[0] = ordered
    visible_ref[0] = ordered[:VMAX, :]
    few = pick[:VMAX, :]
    pos_d_ref[0] = mm(few, sin_d_ref[0]) + mm(few, sin_d_ref[1])
    pos_e_ref[0] = mm(pick, sin_e_ref[0]) + mm(pick, sin_e_ref[1])


def sinusoid_parts(count, width):
    half = width // 2
    frequency = np.exp(np.arange(half) * (-np.log(10000.0) / half))
    angles = np.arange(count)[:, None] * frequency[None, :]
    table = np.concatenate([np.sin(angles), np.cos(angles)], axis=1).astype(np.float32)
    high = table.astype(jnp.bfloat16)
    low = (table - high.astype(np.float32)).astype(jnp.bfloat16)
    return np.stack([high, low])


def order_patches(pixels, shuffle):
    images = pixels.shape[0]
    ids = jnp.pad(shuffle, ((0, 0), (0, SD - POS)), constant_values=-1)[:, :, None]

    def image(*dims):
        return pl.BlockSpec((1,) + dims, lambda b: (b,) + (0,) * len(dims))

    def whole(*dims):
        return pl.BlockSpec(dims, lambda b: (0,) * len(dims))

    return pl.pallas_call(
        order_kernel,
        grid=(images,),
        in_specs=[image(SD, 1), image(POS, PIX), whole(2, POS, D), whole(2, POS, E)],
        out_specs=[image(SD, PIX), image(VMAX, PIX), image(VMAX, D), image(SD, E)],
        out_shape=[
            jax.ShapeDtypeStruct((images, SD, PIX), BF),
            jax.ShapeDtypeStruct((images, VMAX, PIX), BF),
            jax.ShapeDtypeStruct((images, VMAX, D), F32),
            jax.ShapeDtypeStruct((images, SD, E), F32),
        ],
        compiler_params=pltpu.CompilerParams(vmem_limit_bytes=VMEM_LIMIT),
        name="order_patches",
    )(ids, pixels, jnp.asarray(sinusoid_parts(POS, D)), jnp.asarray(sinusoid_parts(POS, E)))


def group_call(kernel, steps, prefetch, in_arrays, out_list, scratch, name, share=(0, 1), given=()):
    count = steps // share[1]
    start = share[0] * count

    def spec(shape, kind):
        if kind == "any":
            return pl.BlockSpec(memory_space=pl.ANY)
        if kind == "rows":
            block = (shape[0] // steps,) + tuple(shape[1:])
            return pl.BlockSpec(block, lambda i, *_: (start + i,) + (0,) * (len(shape) - 1))
        return pl.BlockSpec(tuple(shape), lambda i, *_: (0,) * len(shape))

    first_given = len(prefetch) + len(in_arrays)
    return pl.pallas_call(
        functools.partial(kernel, start, len(given)),
        grid_spec=pltpu.PrefetchScalarGridSpec(
            num_scalar_prefetch=len(prefetch),
            grid=(count,),
            in_specs=[spec(a.shape, kind) for a, kind in in_arrays] + [pl.BlockSpec(memory_space=pl.ANY)] * len(given),
            out_specs=[spec(shape, kind) for shape, _, kind in out_list],
            scratch_shapes=scratch,
        ),
        out_shape=[jax.ShapeDtypeStruct(shape, dtype) for shape, dtype, _ in out_list],
        input_output_aliases={first_given + i: i for i in range(len(given))},
        compiler_params=pltpu.CompilerParams(
            vmem_limit_bytes=VMEM_LIMIT, dimension_semantics=("arbitrary",)
        ),
        cost_estimate=SMALL,
        name=name,
    )(*prefetch, *[a for a, _ in in_arrays], *given)


ENC = layer_offsets(V_ENC, D, FE)
DEC = layer_offsets(V_DEC, E, FD)


def encoder_forward_kernel(
    start, given, row_ref, len_ref, wg_ref, vec_ref, pix_ref, pos_ref,
    x0_ref, h1_ref, qkv_ref, lse_ref, out_t_ref, att_ref, mid_ref, h2_ref, act_ref, slope_ref, x1_ref, hn_ref, latent_ref,
    w_embed, w_qkv, w_out, w_up, w_down, w_proj, sems,
):
    step = pl.program_id(0)
    images = lse_ref.shape[0]
    ready = fetch_all(
        step == 0,
        row_ref,
        wg_ref,
        sems,
        [
            (T_EMBED, w_embed),
            (T_EQKV, w_qkv),
            (T_EOUT, w_out),
            (T_EUP, w_up),
            (T_EDOWN, w_down),
            (T_PROJ, w_proj),
        ],
    )

    def vec(start, size=D):
        return vec_ref[:, start : start + size]

    ready(0)
    add_linear(pos_ref, pix_ref, w_embed, vec_ref, V_EMBED, x0_ref)
    norm_forward(x0_ref, vec(ENC["g1"]), vec(ENC["s1"]), h1_ref)
    ready(1)
    qkv_forward(h1_ref, w_qkv, vec_ref, ENC["bqkv"], qkv_ref)

    attend_all(
        qkv_ref, att_ref, out_t_ref, lse_ref, images, VMAX, D, D // HE, lambda i: len_ref[step * images + i]
    )
    ready(2)
    add_linear(x0_ref, att_ref, w_out, vec_ref, ENC["bo"], mid_ref)
    norm_forward(mid_ref, vec(ENC["g2"]), vec(ENC["s2"]), h2_ref)
    ready(3)
    up_forward(h2_ref, w_up, vec_ref, ENC["bu"], act_ref, slope_ref)
    ready(4)
    add_linear(mid_ref, act_ref, w_down, vec_ref, ENC["bd"], x1_ref)
    norm_forward(x1_ref, vec(V_ENORM), vec(V_ENORM + D), hn_ref)
    ready(5)

    def project(j, cols):
        latent_ref[:, cols] = mm(hn_ref[...], w_proj[:, cols]) + vec_at(vec_ref, V_PROJ, j)

    col_loop(E // BS, project)


def encoder_forward(tile_rows, vis_len, gathered, vector, visible_pix, pos_d, steps):
    images = vis_len.shape[0]
    rows = images * VMAX
    outs = [
        ((rows, D), F32, "rows"),
        ((rows, D), BF, "rows"),
        ((rows, 3 * D), BF, "rows"),
        ((images, D // BS, BS * HE // D, VMAX), F32, "rows"),
        ((images, D // BS, BS, VMAX), F32, "rows"),
        ((rows, D), BF, "rows"),
        ((rows, D), F32, "rows"),
        ((rows, D), BF, "rows"),
        ((rows, FE), BF, "rows"),
        ((rows, FE), BF, "rows"),
        ((rows, D), F32, "rows"),
        ((rows, D), BF, "rows"),
        ((rows, E), F32, "rows"),
    ]
    scratch = [pltpu.VMEM(s, BF) for s in [(PIX, D), (D, 3 * D), (D, D), (D, FE), (FE, D), (D, E)]]
    return group_call(
        encoder_forward_kernel,
        steps,
        (tile_rows, vis_len),
        [
            (gathered, "any"),
            (vector, "whole"),
            (visible_pix.reshape(rows, PIX), "rows"),
            (pos_d.reshape(rows, D), "rows"),
        ],
        outs,
        scratch + [pltpu.SemaphoreType.DMA((6,))],
        "encoder_forward",
    )


DS = layer_offsets(0, E, FD)
DS_NORM = 9 * E + FD
DS_HEAD = DS_NORM + 2 * E
DS_MASK = DS_HEAD + PIX
DS_LOSS = DS_MASK + E
DS_ALL = DS_LOSS + PIX


def decoder_kernel(
    start, given, row_ref, len_ref, wg_ref, vec_ref, latent_ref, pos_ref, pix_ref,
    h1_ref, dqkv_ref, att_ref, gproj_ref, h2_ref, du_ref, act_ref, gdown_ref, hn_ref, gpred_ref, glat_ref, sum_ref,
    w_qkv, w_out, w_up, w_down, w_head, x0, qkv, lse, out_t, mid, slope, x1, pred, dy, grad, datt, sems,
):
    step = pl.program_id(0)
    images = lse.shape[0]
    ready = fetch_all(
        step == 0,
        row_ref,
        wg_ref,
        sems,
        [(T_DQKV, w_qkv), (T_DOUT, w_out), (T_DUP, w_up), (T_DDOWN, w_down), (T_HEAD, w_head)],
    )

    @pl.when(step == 0)
    def _():
        sum_ref[...] = jnp.zeros_like(sum_ref)

    def vec(start, size=E):
        return vec_ref[:, start : start + size]

    def length(image):
        return len_ref[step * images + image]

    chunk = 16
    order = lax.broadcasted_iota(jnp.int32, (chunk, 1), 0)
    token = vec(V_MASK)

    def place(image, c):
        def head_rows(i, c):
            at = pl.ds(pl.multiple_of(image * SD + i * chunk, chunk), chunk)
            got = latent_ref[pl.ds(pl.multiple_of(image * VMAX + i * chunk, chunk), chunk), :]
            x0[at, :] = jnp.where(i * chunk + order < length(image), got, token) + pos_ref[at, :]
            return c

        def tail_rows(i, c):
            at = pl.ds(pl.multiple_of(image * SD + i * chunk, chunk), chunk)
            x0[at, :] = token + pos_ref[at, :]
            return c

        loop(0, VMAX // chunk, head_rows, 0)
        loop(VMAX // chunk, SD // chunk, tail_rows, 0)
        return c

    loop(0, images, place, 0)
    norm_forward(x0, vec(DEC["g1"]), vec(DEC["s1"]), h1_ref)
    ready(0)
    qkv_forward(h1_ref, w_qkv, vec_ref, DEC["bqkv"], qkv)
    attend_all(qkv, att_ref, out_t, lse, images, SD, E, E // HD, lambda i: POS)
    ready(1)
    add_linear(x0, att_ref, w_out, vec_ref, DEC["bo"], mid)
    norm_forward(mid, vec(DEC["g2"]), vec(DEC["s2"]), h2_ref)
    ready(2)
    up_forward(h2_ref, w_up, vec_ref, DEC["bu"], act_ref, slope)
    ready(3)
    add_linear(mid, act_ref, w_down, vec_ref, DEC["bd"], x1)
    norm_forward(x1, vec(V_DNORM), vec(V_DNORM + E), hn_ref)
    ready(4)

    def predict(j, cols):
        pred[:, cols] = mm(hn_ref[...], w_head[:, cols]) + vec_at(vec_ref, V_HEAD, j)

    col_loop(PIX // BS, predict)

    def errors(image, c):
        def one(i, c):
            loss, bias = c
            at = pl.ds(pl.multiple_of(image * SD + i * chunk, chunk), chunk)
            target, _ = norm_parts(pix_ref[at, :].astype(F32))
            place_in = i * chunk + order
            masked = (place_in >= length(image)) & (place_in < POS)
            residual = jnp.where(masked, pred[at, :] - target, 0.0)
            low = (residual * (2.0 / PIX)).astype(BF)
            gpred_ref[at, :] = low
            return (loss + fold8(residual * residual), bias + fold8(low.astype(F32)))

        return loop(0, SD // chunk, one, c)

    zero = jnp.zeros((8, PIX), F32)
    loss, bias = loop(0, images, errors, (zero, zero))
    add_sum(sum_ref, DS_LOSS, loss)
    add_sum(sum_ref, DS_HEAD, bias)

    back_linear(gpred_ref, w_head, dy)
    d_gain, d_shift = norm_backward(x1, dy, vec(V_DNORM), grad, False)
    add_sum(sum_ref, DS_NORM, d_gain)
    add_sum(sum_ref, DS_NORM + E, d_shift)
    round_and_sum(grad, gdown_ref, sum_ref, DS["bd"])
    back_up(gdown_ref, w_down, slope, du_ref, sum_ref, DS["bu"])
    back_linear(du_ref, w_up, dy)
    d_gain, d_shift = norm_backward(mid, dy, vec(DEC["g2"]), grad, True)
    add_sum(sum_ref, DS["g2"], d_gain)
    add_sum(sum_ref, DS["s2"], d_shift)
    round_and_sum(grad, gproj_ref, sum_ref, DS["bo"])

    def back_out(j, cols):
        datt[:, cols] = mm_nt(gproj_ref[...], w_out[cols, :]).astype(BF)

    col_loop(E // BS, back_out)

    def attend_back(image, c):
        attention_backward(qkv, datt, out_t, lse, dqkv_ref, image, SD, E, E // HD, POS)
        return c

    loop(0, images, attend_back, 0)
    sum_rows(dqkv_ref, sum_ref, DS["bqkv"])
    back_linear(dqkv_ref, w_qkv, dy)
    d_gain, d_shift = norm_backward(x0, dy, vec(DEC["g1"]), grad, True)
    add_sum(sum_ref, DS["g1"], d_gain)
    add_sum(sum_ref, DS["s1"], d_shift)

    def unplace(image, c):
        def head_rows(i, c):
            got = grad[pl.ds(pl.multiple_of(image * SD + i * chunk, chunk), chunk), :]
            seen = i * chunk + order < length(image)
            at = pl.ds(pl.multiple_of(image * VMAX + i * chunk, chunk), chunk)
            glat_ref[at, :] = jnp.where(seen, got, 0.0).astype(BF)
            return c + fold8(jnp.where(seen, 0.0, got))

        def tail_rows(i, c):
            got = grad[pl.ds(pl.multiple_of(image * SD + i * chunk, chunk), chunk), :]
            return c + fold8(jnp.where(i * chunk + order < POS, got, 0.0))

        c = loop(0, VMAX // chunk, head_rows, c)
        return loop(VMAX // chunk, SD // chunk, tail_rows, c)

    add_sum(sum_ref, DS_MASK, loop(0, images, unplace, jnp.zeros((8, E), F32)))


def decoder(tile_rows, vis_len, gathered, vector, latent, pos_e, ordered, steps):
    images = vis_len.shape[0]
    rows = images * SD
    part = rows // steps
    outs = [
        ((rows, E), BF, "rows"),
        ((rows, 3 * E), BF, "rows"),
        ((rows, E), BF, "rows"),
        ((rows, E), BF, "rows"),
        ((rows, E), BF, "rows"),
        ((rows, FD), BF, "rows"),
        ((rows, FD), BF, "rows"),
        ((rows, E), BF, "rows"),
        ((rows, E), BF, "rows"),
        ((rows, PIX), BF, "rows"),
        ((images * VMAX, E), BF, "rows"),
        ((8, DS_ALL), F32, "whole"),
    ]
    scratch = [pltpu.VMEM(s, BF) for s in [(E, 3 * E), (E, E), (E, FD), (FD, E), (E, PIX)]]
    scratch += [
        pltpu.VMEM((part, E), F32),
        pltpu.VMEM((part, 3 * E), BF),
        pltpu.VMEM((images // steps, E // BS, BS * HD // E, SD), F32),
        pltpu.VMEM((images // steps, E // BS, BS, SD), F32),
        pltpu.VMEM((part, E), F32),
        pltpu.VMEM((part, FD), BF),
        pltpu.VMEM((part, E), F32),
        pltpu.VMEM((part, PIX), F32),
        pltpu.VMEM((part, E), F32),
        pltpu.VMEM((part, E), F32),
        pltpu.VMEM((part, E), BF),
        pltpu.SemaphoreType.DMA((5,)),
    ]
    return group_call(
        decoder_kernel,
        steps,
        (tile_rows, vis_len),
        [
            (gathered, "any"),
            (vector, "whole"),
            (latent, "rows"),
            (pos_e.reshape(rows, E), "rows"),
            (ordered.reshape(rows, PIX), "rows"),
        ],
        outs,
        scratch,
        "decoder",
    )


EM_BD, EM_BU = 0, D
EM_G2, EM_S2 = D + FE, 2 * D + FE
EM_BO, EM_NORM = 3 * D + FE, 4 * D + FE
EM_PROJ = 6 * D + FE
EM_ALL = EM_PROJ + E
EA_QKV, EA_G1, EA_S1, EA_EMBED, EA_ALL = 0, 3 * D, 4 * D, 5 * D, 6 * D


def encoder_mlp_back_kernel(
    start, given, row_ref, wg_ref, vec_ref, glat_ref, x1_ref, mid_ref, slope_ref,
    gdown_ref, du_ref, grad_ref, gproj_ref, sum_ref,
    w_proj, w_down, w_up, dy, sems,
):
    step = pl.program_id(0)
    ready = fetch_all(
        step == 0, row_ref, wg_ref, sems, [(T_PROJ, w_proj), (T_EDOWN, w_down), (T_EUP, w_up)]
    )

    @pl.when(step == 0)
    def _():
        sum_ref[...] = jnp.zeros_like(sum_ref)

    def vec(start):
        return vec_ref[:, start : start + D]

    sum_rows(glat_ref, sum_ref, EM_PROJ)
    ready(0)
    back_linear(glat_ref, w_proj, dy)
    d_gain, d_shift = norm_backward(x1_ref, dy, vec(V_ENORM), grad_ref, False)
    add_sum(sum_ref, EM_NORM, d_gain)
    add_sum(sum_ref, EM_NORM + D, d_shift)
    round_and_sum(grad_ref, gdown_ref, sum_ref, EM_BD)
    ready(1)
    back_up(gdown_ref, w_down, slope_ref, du_ref, sum_ref, EM_BU)
    ready(2)
    back_linear(du_ref, w_up, dy)
    d_gain, d_shift = norm_backward(mid_ref, dy, vec(ENC["g2"]), grad_ref, True)
    add_sum(sum_ref, EM_G2, d_gain)
    add_sum(sum_ref, EM_S2, d_shift)
    round_and_sum(grad_ref, gproj_ref, sum_ref, EM_BO)


def encoder_mlp_back(tile_rows, gathered, vector, glat, x1, mid, slope, steps):
    rows = x1.shape[0]
    part = rows // steps
    outs = [
        ((rows, D), BF, "rows"),
        ((rows, FE), BF, "rows"),
        ((rows, D), F32, "rows"),
        ((rows, D), BF, "rows"),
        ((8, EM_ALL), F32, "whole"),
    ]
    scratch = [pltpu.VMEM(s, BF) for s in [(D, E), (FE, D), (D, FE)]]
    scratch += [pltpu.VMEM((part, D), F32), pltpu.SemaphoreType.DMA((3,))]
    return group_call(
        encoder_mlp_back_kernel,
        steps,
        (tile_rows,),
        [
            (gathered, "any"),
            (vector, "whole"),
            (glat, "rows"),
            (x1, "rows"),
            (mid, "rows"),
            (slope, "rows"),
        ],
        outs,
        scratch,
        "encoder_mlp_back",
    )


def encoder_attention_back_kernel(
    start, given, row_ref, len_ref, wg_ref, vec_ref, gproj_ref, grad_in_ref, qkv_ref, lse_ref, out_t_ref, x0_ref, *refs
):
    dqkv_ref, gembed_ref, sum_ref, w_out, w_qkv, dy, grad, datt, sems = refs[given:]
    step = pl.program_id(0)
    images = lse_ref.shape[0]
    ready = fetch_all(step == 0, row_ref, wg_ref, sems, [(T_EOUT, w_out), (T_EQKV, w_qkv)])

    @pl.when(step == 0)
    def _():
        sum_ref[...] = jnp.zeros_like(sum_ref)

    ready(0)

    def back_out(j, cols):
        datt[:, cols] = mm_nt(gproj_ref[...], w_out[cols, :]).astype(BF)

    col_loop(D // BS, back_out)

    def attend_back(image, c):
        count = len_ref[(start + step) * images + image]
        attention_backward(qkv_ref, datt, out_t_ref, lse_ref, dqkv_ref, image, VMAX, D, D // HE, count)
        return c

    loop(0, images, attend_back, 0)
    sum_rows(dqkv_ref, sum_ref, EA_QKV)
    ready(1)
    back_linear(dqkv_ref, w_qkv, dy)
    grad[...] = grad_in_ref[...]
    gain = vec_ref[:, ENC["g1"] : ENC["g1"] + D]
    d_gain, d_shift = norm_backward(x0_ref, dy, gain, grad, True)
    add_sum(sum_ref, EA_G1, d_gain)
    add_sum(sum_ref, EA_S1, d_shift)
    round_and_sum(grad, gembed_ref, sum_ref, EA_EMBED)


def encoder_attention_back(tile_rows, vis_len, gathered, vector, gproj, grad, qkv, lse, out_t, x0, steps, share, given):
    rows = x0.shape[0]
    part = rows // steps
    outs = [((rows, 3 * D), BF, "rows"), ((rows, D), BF, "rows"), ((8, EA_ALL), F32, "whole")]
    scratch = [pltpu.VMEM(s, BF) for s in [(D, D), (D, 3 * D)]]
    scratch += [pltpu.VMEM((part, D), F32), pltpu.VMEM((part, D), F32), pltpu.VMEM((part, D), BF)]
    return group_call(
        encoder_attention_back_kernel,
        steps,
        (tile_rows, vis_len),
        [
            (gathered, "any"),
            (vector, "whole"),
            (gproj, "rows"),
            (grad, "rows"),
            (qkv, "rows"),
            (lse, "rows"),
            (out_t, "rows"),
            (x0, "rows"),
        ],
        outs,
        scratch + [pltpu.SemaphoreType.DMA((2,))],
        "encoder_attention_back",
        share,
        given,
    )


def weight_grad_kernel(parts, cut, jobs, count, extra, index_ref, *refs):
    held = min(parts, 2)
    arrays = refs[:count]
    outs = refs[count + extra : count + extra + held]
    x_buf, g_buf, x_t, total, o_buf, x_sem, g_sem, o_sem = refs[count + extra + held :]

    def fetch(array, rows, start, width, buf, sem, slot):
        return pltpu.make_async_copy(
            arrays[array].at[:, start : start + width], buf.at[slot, 0:rows, 0:width], sem.at[slot]
        )

    def send(j, h):
        size, first = jobs[j][-2:]
        return pltpu.make_async_copy(
            o_buf.at[j % 2, h, :, 0:size], outs[h].at[:, first : first + size], o_sem.at[j % 2, h]
        )

    x_slots = [0]
    for one, two in zip(jobs, jobs[1:]):
        x_slots.append(x_slots[-1] if one[:4] == two[:4] else 1 - x_slots[-1])

    def start_fetch(j):
        array, rows, x_start, x_width, g_start, g_width = jobs[j][:6]
        if j == 0 or x_slots[j] != x_slots[j - 1]:
            fetch(array, rows, x_start, x_width, x_buf, x_sem, x_slots[j]).start()
        fetch(array + 1, rows, g_start, g_width, g_buf, g_sem, j % 2).start()

    start_fetch(0)
    for j, (array, rows, x_start, x_width, g_start, g_width, size, first) in enumerate(jobs):
        if j + 1 < len(jobs):
            start_fetch(j + 1)
        if j == 0 or x_slots[j] != x_slots[j - 1]:
            fetch(array, rows, x_start, x_width, x_buf, x_sem, x_slots[j]).wait()
            x_t[0:x_width, 0:rows] = x_buf[x_slots[j], 0:rows, 0:x_width].T
        fetch(array + 1, rows, g_start, g_width, g_buf, g_sem, j % 2).wait()
        total[0:x_width, 0:g_width] = mm(x_t[0:x_width, 0:rows], g_buf[j % 2, 0:rows, 0:g_width])
        if j >= 2:
            for h in range(held):
                send(j - 2, h).wait()
        wide = g_width // BS
        for p in range(parts):
            for r in range(x_width // BS):
                start = pl.multiple_of(r * BS + (p ^ index_ref[0]) * cut, cut)
                for c in range(wide):
                    got = total[pl.ds(start, cut), c * BS : (c + 1) * BS]
                    o_buf[j % 2, p % 2, p // 2, r * wide + c] = got.astype(BF)
        for h in range(held):
            send(j, h).start()
    for j in range(max(0, len(jobs) - 2), len(jobs)):
        for h in range(held):
            send(j, h).wait()


def weight_grads(index, parts, count, first, pairs, blocks, buffers):
    cut = BS // parts
    held = min(parts, 2)
    shape = jax.ShapeDtypeStruct((parts // held, count, cut, BS), BF)
    given = list(buffers or [])
    jobs = []
    for i, ((x, g), (high, wide)) in enumerate(zip(pairs, blocks)):
        for x_start in range(0, x.shape[1], high * BS):
            for g_start in range(0, g.shape[1], wide * BS):
                jobs.append((2 * i, x.shape[0], x_start, high * BS, g_start, wide * BS, high * wide, first))
                first += high * wide
    most = [max(job[k] for job in jobs) for k in range(8)]
    any_spec = pl.BlockSpec(memory_space=pl.ANY)
    return pl.pallas_call(
        functools.partial(weight_grad_kernel, parts, cut, jobs, 2 * len(pairs), len(given)),
        grid_spec=pltpu.PrefetchScalarGridSpec(
            num_scalar_prefetch=1,
            grid=(1,),
            in_specs=[any_spec] * (2 * len(pairs) + len(given)),
            out_specs=[any_spec] * held,
            scratch_shapes=[
                pltpu.VMEM((2, most[1], most[3]), BF),
                pltpu.VMEM((2, most[1], most[5]), BF),
                pltpu.VMEM((most[3], most[1]), BF),
                pltpu.VMEM((most[3], most[5]), F32),
                pltpu.VMEM((2, held, parts // held, most[6], cut, BS), BF),
                pltpu.SemaphoreType.DMA((2,)),
                pltpu.SemaphoreType.DMA((2,)),
                pltpu.SemaphoreType.DMA((2, held)),
            ],
        ),
        out_shape=[shape] * held,
        input_output_aliases={1 + 2 * len(pairs) + i: i for i in range(len(given))},
        compiler_params=pltpu.CompilerParams(vmem_limit_bytes=VMEM_LIMIT),
        cost_estimate=SMALL,
        name="weight_grads",
    )(index, *[array for pair in pairs for array in pair], *given)


def seed_kernel(parts, parcels, own, index_ref, *refs):
    sums, outs, rows = refs[: -1 - min(parts, 2)], refs[-1 - min(parts, 2) : -1], refs[-1]
    rows[...] = jnp.zeros_like(rows)
    at = 0
    for source, start, size in parcels:
        for k in range(0, size, 128):
            piece = sum(jnp.sum(sums[i][:, start + k : start + k + 128], axis=0, keepdims=True) for i in source)
            row, col = at % own // BS, at % own % BS
            rows[at // own, row : row + 1, col : col + 128] = piece
            at += 128
    for p in range(parts):
        out = outs[p % 2]
        out[p // 2, 0] = rows[p ^ index_ref[0]].astype(BF)
        for t in range(1, out.shape[1]):
            out[p // 2, t] = jnp.zeros(rows.shape[1:], BF)


def seed_buffers(index, parts, count, first, sums=(), parcels=(), own=1):
    cut = BS // parts
    held = min(parts, 2)
    size = count - first
    assert first % size == 0
    shape = jax.ShapeDtypeStruct((parts // held, count, cut, BS), BF)
    return pl.pallas_call(
        functools.partial(seed_kernel, parts, parcels, own),
        grid_spec=pltpu.PrefetchScalarGridSpec(
            num_scalar_prefetch=1,
            grid=(1,),
            in_specs=[pl.BlockSpec(x.shape, lambda i, *_: (0, 0)) for x in sums],
            out_specs=[pl.BlockSpec((parts // held, size, cut, BS), lambda i, *_: (0, first // size, 0, 0))] * held,
            scratch_shapes=[pltpu.VMEM((parts, cut, BS), F32)],
        ),
        out_shape=[shape] * held,
        cost_estimate=SMALL,
        name="seed_buffers",
    )(index, *sums)


def low_sum(a, b):
    return (a.astype(F32) + b.astype(F32)).astype(BF)


def swap_bit(x, bit, size):
    return lax.ppermute(x, "dp", [(i, i ^ (1 << bit)) for i in range(size)])


def reduce_core(buffers, parts):
    if parts == 1:
        whole, count = buffers[0][0], buffers[0].shape[1]
        return [whole[: count // 2], whole[count // 2 :]], [[], []]
    whole = low_sum(buffers[0], swap_bit(buffers[1], 0, parts))
    bits = list(range(parts.bit_length() - 2, 0, -1))
    whole = whole.reshape((2,) * len(bits) + whole.shape[1:])
    count = whole.shape[-3]
    return [whole[..., : count // 2, :, :], whole[..., count // 2 :, :, :]], [bits, bits]


def reduce_chips(state, parts, steps):
    halves, left = list(state[0]), list(state[1])
    for half in range(2):
        for _ in range(min(steps, len(left[half]))):
            bit = left[half][-1 if half == 0 else 0]
            axis = left[half].index(bit)
            keep = lax.index_in_dim(halves[half], 0, axis, keepdims=False)
            send = lax.index_in_dim(halves[half], 1, axis, keepdims=False)
            halves[half] = low_sum(keep, swap_bit(send, bit, parts))
            left[half] = [b for b in left[half] if b != bit]
    return halves, left


def patch_steps(groups):
    middle = groups // 2 - 1

    def inwards(k, x):
        return low_sum(x, lax.ppermute(x, "patch", [(k, k + 1), (groups - 1 - k, groups - 2 - k)]))

    def across(x):
        return low_sum(x, lax.ppermute(x, "patch", [(middle, middle + 1), (middle + 1, middle)]))

    def outwards(k, x):
        got = lax.ppermute(x, "patch", [(k + 1, k), (groups - 2 - k, groups - 1 - k)])
        me = lax.axis_index("patch")
        return jnp.where((me == k) | (me == groups - 1 - k), got, x)

    if groups == 1:
        return []
    steps = [functools.partial(inwards, k) for k in range(middle)] + [across]
    return steps + [functools.partial(outwards, k) for k in reversed(range(middle))]


def sum_patch(x, steps):
    for step in steps:
        x = step(x)
    return x


def sum_all(x, parts, groups):
    for bit in range(groups.bit_length() - 1):
        x = x + lax.ppermute(x, "patch", [(i, i ^ (1 << bit)) for i in range(groups)])
    return sum_dp(x, parts)


def sum_dp(x, parts):
    for bit in range(parts.bit_length() - 1):
        x = x + swap_bit(x, bit, parts)
    return x


def split_low(x):
    high = x.astype(BF)
    return high, (x - high.astype(F32)).astype(BF)


def tile_kernel(
    scale_ref, grad_ref, w_ref, left_stat_ref, right_stat_ref, left_root_ref, right_root_ref,
    clipped_ref, left_new_ref, right_new_ref, w_new_ref,
):
    scale = scale_ref[0]
    for t in range(w_ref.shape[0]):
        grad = grad_ref[:, t].reshape(BS, BS)
        clipped_ref[t] = grad.astype(F32) * scale
        square = (1.0 - BETA_STAT) * scale * scale
        left_new_ref[t] = BETA_STAT * left_stat_ref[t] + square * mm_nt(grad, grad)
        right_new_ref[t] = BETA_STAT * right_stat_ref[t] + square * mm_tn(grad, grad)
        high, low = split_low(left_root_ref[t])
        half = (mm(high, grad) + mm(low, grad)) * scale
        half_high, half_low = split_low(half)
        high, low = split_low(right_root_ref[t])
        direction = mm(half_high, high) + (mm(half_high, low) + mm(half_low, high))
        direction = direction * lax.rsqrt(jnp.mean(direction * direction) + EPS_ROOT)
        w_new_ref[t] = w_ref[t] - RATE_MATRIX * (direction + DECAY_MATRIX * w_ref[t])


def tile_update(scale, grads, states):
    parts, slots, cut, _ = grads.shape
    per = max(p for p in range(1, 7) if slots % p == 0)
    tile = pl.BlockSpec((per, BS, BS), lambda i, *_: (i, 0, 0))
    return pl.pallas_call(
        tile_kernel,
        grid_spec=pltpu.PrefetchScalarGridSpec(
            num_scalar_prefetch=1,
            grid=(slots // per,),
            in_specs=[pl.BlockSpec((parts, per, cut, BS), lambda i, *_: (0, i, 0, 0))] + [tile] * 5,
            out_specs=[tile] * 4,
        ),
        out_shape=[jax.ShapeDtypeStruct((slots, BS, BS), F32)] * 4,
        compiler_params=pltpu.CompilerParams(vmem_limit_bytes=VMEM_LIMIT),
        name="tile_update",
    )(scale.reshape(1), grads, *states)


def vector_update(clipped, vectors, moment, second):
    moment_new = BETA_FIRST * moment + (1.0 - BETA_FIRST) * clipped
    second_new = BETA_SECOND * second + (1.0 - BETA_SECOND) * clipped * clipped
    corrected = moment_new / (1.0 - BETA_FIRST**STEP)
    scaled = second_new / (1.0 - BETA_SECOND**STEP)
    vectors_new = vectors - RATE_VECTOR * corrected / (jnp.sqrt(scaled) + EPS_ADAM)
    return moment_new, second_new, vectors_new


CHUNKS = [
    [
        (T_DUP, 2, 8, (2, 4)),
        (T_DDOWN, 8, 2, (4, 2)),
        (T_DOUT, 2, 2, (2, 2)),
        (T_DQKV, 2, 6, (2, 3)),
        (T_HEAD, 2, 3, (2, 3)),
        (T_PROJ, 3, 2, (3, 2)),
    ],
    [(T_EUP, 3, 12, (3, 4)), (T_EDOWN, 12, 3, (4, 3)), (T_EOUT, 3, 3, (3, 3))],
    [(T_EQKV, 3, 9, (3, 3)), (T_EMBED, 3, 3, (3, 3))],
]


def chunk_sizes():
    sizes = [sum(r * c for _, r, c, _ in chunk) for chunk in CHUNKS]
    return sizes[:-1] + [sizes[-1] + 2]


def tile_places(sizes):
    chunk_of = np.zeros(NBLK + 2, np.int32)
    place_of = np.zeros(NBLK + 2, np.int32)
    for i, chunk in enumerate(CHUNKS):
        at = 0
        for first, row_tiles, col_tiles, (high, wide) in chunk:
            for r in range(row_tiles):
                for c in range(col_tiles):
                    block = r // high * (col_tiles // wide) + c // wide
                    chunk_of[first + r * col_tiles + c] = i
                    place_of[first + r * col_tiles + c] = at + block * high * wide + r % high * wide + c % wide
            at += row_tiles * col_tiles
    chunk_of[NBLK:] = len(CHUNKS) - 1
    place_of[NBLK + 1] = at
    place_of[NBLK] = at + 1
    return chunk_of, place_of


def shards(parts, groups, pixels, shuffle, vis_len, block_owner, weights, vectors, vec_moment, vec_second,
           left_stat, right_stat, left_root, right_root):
    slots = weights.shape[0]
    own = vectors.shape[0]
    index = lax.axis_index("dp").astype(jnp.int32).reshape(1)
    images = pixels.shape[0]

    vector_rows = -(-own // (16 * BS)) * 16
    mine = jnp.concatenate(
        [
            weights.astype(BF).reshape(slots * BS, BS),
            jnp.pad(vectors.astype(BF), (0, vector_rows * BS - own)).reshape(vector_rows, BS),
        ]
    )
    gathered = lax.all_gather(mine, "dp", axis=0, tiled=True)
    stride = mine.shape[0]
    slot_index = jnp.arange(block_owner.shape[0], dtype=jnp.int32)
    slot_of_block = jnp.sum(
        jnp.where(block_owner[None, :] == jnp.arange(NBLK, dtype=jnp.int32)[:, None], slot_index[None, :], 0),
        axis=1,
    )
    tile_rows = slot_of_block // slots * stride + slot_of_block % slots * BS
    vector = gathered.reshape(parts, stride, BS)[:, slots * BS :].reshape(parts, vector_rows * BS)
    vector = vector[:, :own].reshape(-1).astype(F32)
    enc_key, dec_key = 4 * D, 4 * D + (8 * D + FE - 3 * D) + 2 * D + 2 * E + 3 * E
    vector = jnp.concatenate(
        [vector[:enc_key], jnp.zeros(D, F32), vector[enc_key:dec_key], jnp.zeros(E, F32), vector[dec_key:]]
    ).reshape(1, V_ALL)

    ordered, visible_pix, pos_d, pos_e = order_patches(pixels, shuffle)
    (x0, h1, qkv, lse, out_t, att, mid, h2, act, slope, x1, hn, latent) = encoder_forward(
        tile_rows, vis_len, gathered, vector, visible_pix, pos_d, 2
    )
    (d_h1, d_dqkv, d_att, d_gproj, d_h2, d_du, d_act, d_gdown, d_hn, d_gpred, glat, d_sums) = decoder(
        tile_rows, vis_len, gathered, vector, latent, pos_e, ordered, 4
    )
    sizes = chunk_sizes()
    chunk_of, place_of = tile_places(sizes)

    rows_cut = BS // parts

    def gradients(chunk, pairs, vector=(), first=0, buffers=None):
        used = sum(r * c for _, r, c, _ in CHUNKS[chunk])
        if sizes[chunk] > used and buffers is None:
            buffers = seed_buffers(index, parts, sizes[chunk], used, *vector)
        at = sum(r * c for _, r, c, _ in CHUNKS[chunk][:first])
        blocks = [block for _, _, _, block in CHUNKS[chunk][first : first + len(pairs)]]
        return weight_grads(index, parts, sizes[chunk], at, pairs, blocks, buffers)

    def attention_back(gproj, k, given):
        return encoder_attention_back(
            tile_rows, vis_len, gathered, vector, gproj, grad_mid, qkv, lse, out_t, x0, 2, (k, 2), given
        )

    def core(buffers):
        return reduce_core(buffers, parts)

    def chips(state, steps):
        return reduce_chips(state, parts, steps)

    after = lax.optimization_barrier
    steps = patch_steps(groups)
    gdown, du, grad_mid, gproj, m_sums = encoder_mlp_back(tile_rows, gathered, vector, glat, x1, mid, slope, 2)
    buf1 = gradients(1, [(h2, du), (act, gdown), (att, gproj)])
    d_h2, d_act, buf1 = after((d_h2, d_act, buf1))
    buf0 = gradients(0, [(d_h2, d_du), (d_act, d_gdown)])
    half1, left1 = core(buf1)
    d_att, d_h1, d_hn, hn, buf0, half1 = after((d_att, d_h1, d_hn, hn, buf0, half1))
    half1, left1 = chips((half1, left1), 1)
    buf0 = gradients(0, [(d_att, d_gproj), (d_h1, d_dqkv), (d_hn, d_gpred), (hn, glat)], (), 2, buf0)
    gproj, buf0 = after((gproj, buf0))
    dqkv, gembed, a_sums = attention_back(gproj, 0, ())
    gproj, dqkv, gembed, buf0, half1 = after((gproj, dqkv, gembed, buf0, half1))
    dqkv, gembed, b_sums = attention_back(gproj, 1, (dqkv, gembed))
    (one, two), _ = chips((half1, left1), 99)
    half0, left0 = core(buf0)
    dqkv, gembed, b_sums, half0, one, two = after((dqkv, gembed, b_sums, half0, one, two))

    late, early, dec = (0, 1), (2,), (3,)
    parcels = [
        (late, EA_EMBED, D),
        (late, EA_G1, 2 * D),
        (late, EA_QKV, D),
        (late, EA_QKV + 2 * D, D),
        (early, EM_BO, D),
        (early, EM_G2, 2 * D),
        (early, EM_BU, FE),
        (early, EM_BD, D),
        (early, EM_NORM, 2 * D),
        (early, EM_PROJ, E),
        (dec, DS_MASK, E),
        (dec, DS["g1"], 2 * E),
        (dec, DS["bqkv"], E),
        (dec, DS["bqkv"] + 2 * E, E),
        (dec, DS["bo"], E),
        (dec, DS["g2"], 2 * E),
        (dec, DS["bu"], FD),
        (dec, DS["bd"], E),
        (dec, DS_NORM, 2 * E),
        (dec, DS_HEAD, PIX),
    ]
    sums = (a_sums, b_sums, m_sums, d_sums)
    buf2 = gradients(2, [(h1, dqkv), (visible_pix.reshape(-1, PIX), gembed)], (sums, parcels, own))
    half0, left0 = chips((half0, left0), 1)
    one = sum_patch(one, steps[:1])
    two = sum_patch(two, steps[:1])
    buf2, half0, one, two = after((buf2, half0, one, two))
    half2, left2 = core(buf2)
    half0, _ = chips((half0, left0), 99)
    one = sum_patch(one, steps[1:2])
    half2, half0, one, two = after((half2, half0, one, two))
    half2, left2 = chips((half2, left2), 1)
    half0 = [sum_patch(x, steps[:1]) for x in half0]
    one = sum_patch(one, steps[2:])
    two = sum_patch(two, steps[1:2])
    half2, half0, one, two = after((half2, half0, one, two))
    half2, _ = chips((half2, left2), 99)
    two = sum_patch(two, steps[2:])
    half0 = [sum_patch(x, steps[1:2]) for x in half0]
    half2 = [sum_patch(x, steps[:1]) for x in half2]
    half2, half0, two = after((half2, half0, two))
    half2 = [sum_patch(x, steps[1:]) for x in half2]
    half0 = [sum_patch(x, steps[2:]) for x in half0]
    pieces = half0 + [one, two] + half2
    mine = jnp.where(lax.axis_index("patch") == 0, 1.0, 0.0)

    def squares(x):
        wide = x.astype(F32)
        return jnp.sum(wide * wide)

    totals = jnp.stack(
        [
            jnp.sum(d_sums[:, DS_LOSS : DS_LOSS + PIX]) / PIX,
            jnp.sum(POS - vis_len).astype(F32),
            sum(squares(x) for x in pieces) * mine,
        ]
    )
    totals = sum_all(totals, parts, groups)
    loss_sum, masked_count = totals[0], totals[1]
    grad_norm = jnp.sqrt(totals[2]) / masked_count
    scale = jnp.minimum(1.0, CLIP_NORM / grad_norm) / masked_count

    reduced = jnp.concatenate(pieces, axis=0)
    where = jnp.asarray(np.cumsum([0] + sizes)[chunk_of] + place_of, jnp.int32)
    slot_rows = reduced[where[jnp.minimum(block_owner, NBLK)]]
    if parts > 1:
        slot_rows = lax.all_to_all(slot_rows, "dp", 0, 0, tiled=True)
    grads = slot_rows.reshape(parts, slots, rows_cut, BS)
    clipped, left_new, right_new, weights_new = tile_update(
        scale, grads, (weights, left_stat, right_stat, left_root, right_root)
    )
    own_vector = lax.dynamic_index_in_dim(reduced, where[NBLK + 1], 0, keepdims=False)
    own_vector = own_vector.reshape(-1)[:own].astype(F32) * scale
    moment_new, second_new, vectors_new = vector_update(own_vector, vectors, vec_moment, vec_second)
    return (
        loss_sum,
        masked_count,
        grad_norm,
        clipped,
        left_new,
        right_new,
        weights_new,
        moment_new,
        second_new,
        vectors_new,
    )


def solution(mesh):
    both = ("dp", "patch")
    tiles = P("dp", None, None)
    return jax.shard_map(
        functools.partial(shards, mesh.shape["dp"], mesh.shape["patch"]),
        mesh=mesh,
        in_specs=(P(both, None, None), P(both, None), P(both), P())
        + (tiles, P("dp"), P("dp"), P("dp"))
        + (tiles,) * 4,
        out_specs=(P(), P(), P()) + (tiles,) * 4 + (P("dp"),) * 3,
        check_vma=False,
    )
```

```python
import functools
import math

import jax
import jax.numpy as jnp
import numpy as np
from jax import lax
from jax.experimental import pallas as pl
from jax.experimental.pallas import tpu as pltpu
from jax.sharding import PartitionSpec as P

D = 768
HE = 12
FE = 3072
E = 512
HD = 16
FD = 2048
PIX = 768
POS = 196
VMAX = 80
BS = 256
STEP = 10
NBLK = 177

SD = 208

EPS_NORM = 1e-06
EPS_ROOT = 1e-06
EPS_ADAM = 1e-08
CLIP_NORM = 0.01
RATE_MATRIX = 0.03
DECAY_MATRIX = 0.05
BETA_STAT = 0.5
BETA_FIRST = 0.9
BETA_SECOND = 0.999
RATE_VECTOR = 0.1
NEG_LARGE = -1e30
LOG2E = math.log2(math.e)

BF = jnp.bfloat16
F32 = jnp.float32
VMEM_LIMIT = 60 * 1024 * 1024
SMALL = pl.CostEstimate(flops=1000, bytes_accessed=1000, transcendentals=0)

T_EMBED, T_EQKV, T_EOUT, T_EUP, T_EDOWN, T_PROJ = 0, 9, 36, 45, 81, 117
T_DQKV, T_DOUT, T_DUP, T_DDOWN, T_HEAD = 123, 135, 139, 155, 171

V_EMBED = 0
V_ENC = D
V_ENORM = V_ENC + 9 * D + FE
V_PROJ = V_ENORM + 2 * D
V_MASK = V_PROJ + E
V_DEC = V_MASK + E
V_DNORM = V_DEC + 9 * E + FD
V_HEAD = V_DNORM + 2 * E
V_ALL = V_HEAD + PIX


def layer_offsets(start, width, hidden):
    names = ["g1", "s1", "bqkv", "bo", "g2", "s2", "bu", "bd"]
    sizes = [width, width, 3 * width, width, width, width, hidden, width]
    offsets = {}
    for name, size in zip(names, sizes):
        offsets[name] = start
        start += size
    return offsets


def mm(a, b):
    return jnp.dot(a, b, preferred_element_type=F32)


def mm_nt(a, b):
    return lax.dot_general(a, b, (((1,), (1,)), ((), ())), preferred_element_type=F32)


def mm_tn(a, b):
    return lax.dot_general(a, b, (((0,), (0,)), ((), ())), preferred_element_type=F32)


def fold8(x):
    rows, cols = x.shape
    return jnp.sum(x.reshape(rows // 8, 8, cols), axis=0)


def gelu_pair(u):
    t = 1.0 / (1.0 + (0.3275911 * math.sqrt(0.5)) * jnp.abs(u))
    e = jnp.exp2((-0.5 * LOG2E) * (u * u))
    poly = t * (
        0.5 * 0.254829592
        + t * (-0.5 * 0.284496736 + t * (0.5 * 1.421413741 + t * (-0.5 * 1.453152027 + t * (0.5 * 1.061405429))))
    )
    tail = poly * e
    phi = jnp.where(u >= 0, 1.0 - tail, tail)
    return u * phi, phi + u * (e * (1.0 / math.sqrt(2.0 * math.pi)))


def norm_parts(x):
    centred = x - jnp.mean(x, axis=-1, keepdims=True)
    inverse = lax.rsqrt(jnp.mean(centred * centred, axis=-1, keepdims=True) + EPS_NORM)
    return centred * inverse, inverse


def loop(lower, upper, body, carry, most=26):
    count = upper - lower
    unroll = max(u for u in range(1, min(most, count) + 1) if count % u == 0)
    return lax.fori_loop(lower, upper, body, carry, unroll=unroll)


def row_loop(rows, step, body, carry=0):
    count = rows // step

    def one(i, c):
        return body(pl.ds(pl.multiple_of(i * step, step), step), c)

    return loop(0, count, one, carry)


def norm_forward(x_ref, gain, shift, out_ref):
    def body(sl, c):
        normed, _ = norm_parts(x_ref[sl, :])
        out_ref[sl, :] = (normed * gain + shift).astype(BF)
        return c

    row_loop(x_ref.shape[0], 16, body)


def norm_backward(x_ref, dy_ref, gain, out_ref, add):
    width = x_ref.shape[1]

    def body(sl, c):
        d_gain, d_shift = c
        normed, inverse = norm_parts(x_ref[sl, :])
        dy = dy_ref[sl, :]
        dn = dy * gain
        mean_one = jnp.mean(dn, axis=-1, keepdims=True)
        mean_two = jnp.mean(dn * normed, axis=-1, keepdims=True)
        dx = inverse * (dn - mean_one - normed * mean_two)
        out_ref[sl, :] = out_ref[sl, :] + dx if add else dx
        return (d_gain + fold8(dy * normed), d_shift + fold8(dy))

    zero = jnp.zeros((8, width), F32)
    return row_loop(x_ref.shape[0], 16, body, (zero, zero))


def col_loop(count, body):
    def one(j, c):
        body(j, pl.ds(pl.multiple_of(j * BS, BS), BS))
        return c

    loop(0, count, one, 0, 12)


def vec_at(vec_ref, start, j):
    return vec_ref[:, pl.ds(pl.multiple_of(start + j * BS, BS), BS)]


def head_mask(head, head_size):
    lane = lax.broadcasted_iota(jnp.int32, (1, BS), 1)
    inside = (lane >= head * head_size) & (lane < (head + 1) * head_size)
    return jnp.where(inside, 1.0, 0.0).astype(BF)


def masked_scores(raw, head_size, count):
    scores = raw * (head_size**-0.5 * LOG2E)
    if isinstance(count, int):
        whole = count // 8 * 8
        tail = scores[whole:]
        row = lax.broadcasted_iota(jnp.int32, tail.shape, 0) + whole
        return jnp.concatenate([scores[:whole], jnp.where(row < count, tail, NEG_LARGE)], axis=0)
    row = lax.broadcasted_iota(jnp.int32, (scores.shape[0], 1), 0)
    return jnp.where(row < count, scores, NEG_LARGE)


def scores_bounded(qkv_ref, width, head_size):
    lane = lax.broadcasted_iota(jnp.int32, (BS, 128), 0) // head_size
    pick = jnp.where(lane == lax.broadcasted_iota(jnp.int32, (BS, 128), 1), 1.0, 0.0).astype(BF)
    score, value = None, None
    for g in range(width // BS):
        tops = []
        for which in range(3):
            x = qkv_ref[:, which * width + g * BS : which * width + (g + 1) * BS]
            tops.append(jnp.max(mm(x * x, pick), axis=0, keepdims=True))
        one = tops[0] * tops[1]
        score = one if score is None else jnp.maximum(score, one)
        value = tops[2] if value is None else jnp.maximum(value, tops[2])
    limit = 90.0 / (1.05 * head_size**-0.5 * LOG2E)
    return (jnp.max(score) < limit * limit) & (jnp.max(value) < 2.0**40)


def attention_forward(qkv_ref, att_ref, out_t_ref, lse_ref, image, seq, width, head_size, count, bounded):
    rows = pl.ds(pl.multiple_of(image * seq, 16), seq)
    per = BS // head_size
    most = min(8, per)

    def group(g, c):
        def part(which):
            return qkv_ref[rows, pl.ds(pl.multiple_of(which * width + g * BS, BS), BS)]

        q, k, v = part(0), part(1), part(2)
        v_t = v.T
        q = q.T
        ones = jnp.ones((16, seq), BF)
        outs, logs = [], []
        for h in range(per):
            if h % most == 0:
                stacked = jnp.concatenate([k * head_mask(i, head_size) for i in range(h, h + most)], axis=0)
                many = mm(stacked, q)
            scores = masked_scores(many[h % most * seq : (h % most + 1) * seq], head_size, count)
            top = 0.0
            if not bounded:
                top = jnp.max(scores, axis=0, keepdims=True)
                scores = scores - top
            e = jnp.exp2(scores).astype(BF)
            both = mm(jnp.concatenate([v_t[h * head_size : (h + 1) * head_size, :], ones], axis=0), e)
            total = both[head_size : head_size + 1, :]
            outs.append(both[:head_size, :] * (1.0 / total))
            logs.append(top + jnp.log2(total))
        out_t = jnp.concatenate(outs, axis=0)
        out_t_ref[image, g] = out_t
        att_ref[rows, pl.ds(pl.multiple_of(g * BS, BS), BS)] = out_t.T.astype(BF)
        lse_ref[image, g] = jnp.concatenate(logs, axis=0)
        return c

    loop(0, width // BS, group, 0)


def attend_all(qkv_ref, att_ref, out_t_ref, lse_ref, images, seq, width, head_size, count_of):
    safe = scores_bounded(qkv_ref, width, head_size)

    def run(bounded):
        def one(image, c):
            count = count_of(image)
            attention_forward(
                qkv_ref, att_ref, out_t_ref, lse_ref, image, seq, width, head_size, count, bounded
            )
            return c

        loop(0, images, one, 0)

    @pl.when(safe)
    def _():
        run(True)

    @pl.when(jnp.logical_not(safe))
    def _():
        run(False)


def attention_backward(qkv_ref, datt_ref, out_t_ref, lse_ref, dqkv_ref, image, seq, width, head_size, count):
    rows = pl.ds(pl.multiple_of(image * seq, 16), seq)
    per = BS // head_size
    scale = head_size**-0.5
    most = min(8, per)

    def group(g, c):
        def cols(which):
            return pl.ds(pl.multiple_of(which * width + g * BS, BS), BS)

        q, k, v = qkv_ref[rows, cols(0)], qkv_ref[rows, cols(1)], qkv_ref[rows, cols(2)]
        d_out = datt_ref[rows, cols(0)]
        lse = lse_ref[image, g]
        q_t, k_t, d_out_t = q.T, k.T, d_out.T
        along = d_out_t.astype(F32) * out_t_ref[image, g]
        lane = lax.broadcasted_iota(jnp.int32, (seq, BS), 1)
        d_q, d_k, d_v = [], None, None
        for start in range(0, per, most):
            heads = range(start, start + most)
            many = mm(jnp.concatenate([k * head_mask(h, head_size) for h in heads], axis=0), q_t)
            more = mm(jnp.concatenate([v * head_mask(h, head_size) for h in heads], axis=0), d_out_t)
            probs_all, scores_all = [], []
            for h in heads:
                part = slice(h * head_size, (h + 1) * head_size)
                at = slice((h - start) * seq, (h - start + 1) * seq)
                delta = jnp.sum(along[part, :], axis=0, keepdims=True)
                probs = jnp.exp2(masked_scores(many[at], head_size, count) - lse[h : h + 1, :])
                d_scores = (probs * (more[at] - delta)).astype(BF)
                d_q.append(mm(k_t[part, :], d_scores))
                probs_all.append(probs.astype(BF))
                scores_all.append(d_scores)
            for_v = mm(jnp.concatenate(probs_all, axis=0), d_out)
            for_k = mm(jnp.concatenate(scores_all, axis=0), q)
            for h in heads:
                at = slice((h - start) * seq, (h - start + 1) * seq)
                inside = (lane >= h * head_size) & (lane < (h + 1) * head_size)
                d_v = for_v[at] if d_v is None else jnp.where(inside, for_v[at], d_v)
                d_k = for_k[at] if d_k is None else jnp.where(inside, for_k[at], d_k)
        dqkv_ref[rows, cols(0)] = (jnp.concatenate(d_q, axis=0).T * scale).astype(BF)
        dqkv_ref[rows, cols(1)] = (d_k * scale).astype(BF)
        dqkv_ref[rows, cols(2)] = d_v.astype(BF)
        return c

    loop(0, width // BS, group, 0)


def fetch_tiles(row_ref, wg_ref, first, dst, sem):
    row_tiles, col_tiles = dst.shape[0] // BS, dst.shape[1] // BS
    for i in range(row_tiles):
        for j in range(col_tiles):
            start = pl.multiple_of(row_ref[first + i * col_tiles + j], 16)
            pltpu.make_async_copy(
                wg_ref.at[pl.ds(start, BS), :],
                dst.at[i * BS : (i + 1) * BS, j * BS : (j + 1) * BS],
                sem,
            ).start()


def await_tiles(dst, sem):
    pltpu.make_async_copy(dst, dst, sem).wait()


def fetch_all(first_step, row_ref, wg_ref, sems, matrices):
    @pl.when(first_step)
    def _():
        for i, (first, dst) in enumerate(matrices):
            fetch_tiles(row_ref, wg_ref, first, dst, sems.at[i])

    def ready(i):
        @pl.when(first_step)
        def _():
            await_tiles(matrices[i][1], sems.at[i])

    return ready


def qkv_forward(h_ref, w_ref, vec_ref, start, out_ref):
    def body(j, cols):
        out_ref[:, cols] = (mm(h_ref[...], w_ref[:, cols]) + vec_at(vec_ref, start, j)).astype(BF)

    col_loop(w_ref.shape[1] // BS, body)


def add_linear(x_ref, h_ref, w_ref, vec_ref, start, out_ref):
    def body(j, cols):
        out_ref[:, cols] = x_ref[:, cols] + (mm(h_ref[...], w_ref[:, cols]) + vec_at(vec_ref, start, j))

    col_loop(w_ref.shape[1] // BS, body)


def up_forward(h_ref, w_ref, vec_ref, start, act_ref, slope_ref):
    def body(j, cols):
        act, slope = gelu_pair(mm(h_ref[...], w_ref[:, cols]) + vec_at(vec_ref, start, j))
        act_ref[:, cols] = act.astype(BF)
        slope_ref[:, cols] = slope.astype(BF)

    col_loop(w_ref.shape[1] // BS, body)


def back_linear(g_ref, w_ref, out_ref):
    def body(j, cols):
        out_ref[:, cols] = mm_nt(g_ref[...], w_ref[cols, :])

    col_loop(w_ref.shape[0] // BS, body)


def back_up(g_ref, w_ref, slope_ref, du_ref, sum_ref, start):
    def body(j, cols):
        du = (mm_nt(g_ref[...], w_ref[cols, :]) * slope_ref[:, cols].astype(F32)).astype(BF)
        du_ref[:, cols] = du
        at = pl.ds(pl.multiple_of(start + j * BS, BS), BS)
        sum_ref[:, at] = sum_ref[:, at] + fold8(du.astype(F32))

    col_loop(w_ref.shape[0] // BS, body)


def round_and_sum(x_ref, out_ref, sum_ref, start):
    width = x_ref.shape[1]

    def body(sl, c):
        low = x_ref[sl, :].astype(BF)
        out_ref[sl, :] = low
        return c + fold8(low.astype(F32))

    total = row_loop(x_ref.shape[0], 16, body, jnp.zeros((8, width), F32))
    sum_ref[:, start : start + width] = sum_ref[:, start : start + width] + total


def sum_rows(x_ref, sum_ref, start):
    width = x_ref.shape[1]

    def body(sl, c):
        return c + fold8(x_ref[sl, :].astype(F32))

    total = row_loop(x_ref.shape[0], 16, body, jnp.zeros((8, width), F32))
    sum_ref[:, start : start + width] = sum_ref[:, start : start + width] + total


def add_sum(sum_ref, start, value):
    stop = start + value.shape[1]
    sum_ref[:, start:stop] = sum_ref[:, start:stop] + value


def order_kernel(shuffle_ref, pixels_ref, sin_d_ref, sin_e_ref, all_ref, visible_ref, pos_d_ref, pos_e_ref):
    ids = shuffle_ref[0]
    pick = jnp.where(ids == lax.broadcasted_iota(jnp.int32, (SD, POS), 1), 1.0, 0.0).astype(BF)
    ordered = mm(pick, pixels_ref[0]).astype(BF)
    all_ref[0] = ordered
    visible_ref[0] = ordered[:VMAX, :]
    few = pick[:VMAX, :]
    pos_d_ref[0] = mm(few, sin_d_ref[0]) + mm(few, sin_d_ref[1])
    pos_e_ref[0] = mm(pick, sin_e_ref[0]) + mm(pick, sin_e_ref[1])


def sinusoid_parts(count, width):
    half = width // 2
    frequency = np.exp(np.arange(half) * (-np.log(10000.0) / half))
    angles = np.arange(count)[:, None] * frequency[None, :]
    table = np.concatenate([np.sin(angles), np.cos(angles)], axis=1).astype(np.float32)
    high = table.astype(jnp.bfloat16)
    low = (table - high.astype(np.float32)).astype(jnp.bfloat16)
    return np.stack([high, low])


def order_patches(pixels, shuffle):
    images = pixels.shape[0]
    ids = jnp.pad(shuffle, ((0, 0), (0, SD - POS)), constant_values=-1)[:, :, None]

    def image(*dims):
        return pl.BlockSpec((1,) + dims, lambda b: (b,) + (0,) * len(dims))

    def whole(*dims):
        return pl.BlockSpec(dims, lambda b: (0,) * len(dims))

    return pl.pallas_call(
        order_kernel,
        grid=(images,),
        in_specs=[image(SD, 1), image(POS, PIX), whole(2, POS, D), whole(2, POS, E)],
        out_specs=[image(SD, PIX), image(VMAX, PIX), image(VMAX, D), image(SD, E)],
        out_shape=[
            jax.ShapeDtypeStruct((images, SD, PIX), BF),
            jax.ShapeDtypeStruct((images, VMAX, PIX), BF),
            jax.ShapeDtypeStruct((images, VMAX, D), F32),
            jax.ShapeDtypeStruct((images, SD, E), F32),
        ],
        compiler_params=pltpu.CompilerParams(vmem_limit_bytes=VMEM_LIMIT),
        name="order_patches",
    )(ids, pixels, jnp.asarray(sinusoid_parts(POS, D)), jnp.asarray(sinusoid_parts(POS, E)))


def group_call(kernel, steps, prefetch, in_arrays, out_list, scratch, name, share=(0, 1), given=()):
    count = steps // share[1]
    start = share[0] * count

    def spec(shape, kind):
        if kind == "any":
            return pl.BlockSpec(memory_space=pl.ANY)
        if kind == "rows":
            block = (shape[0] // steps,) + tuple(shape[1:])
            return pl.BlockSpec(block, lambda i, *_: (start + i,) + (0,) * (len(shape) - 1))
        return pl.BlockSpec(tuple(shape), lambda i, *_: (0,) * len(shape))

    first_given = len(prefetch) + len(in_arrays)
    return pl.pallas_call(
        functools.partial(kernel, start, len(given)),
        grid_spec=pltpu.PrefetchScalarGridSpec(
            num_scalar_prefetch=len(prefetch),
            grid=(count,),
            in_specs=[spec(a.shape, kind) for a, kind in in_arrays] + [pl.BlockSpec(memory_space=pl.ANY)] * len(given),
            out_specs=[spec(shape, kind) for shape, _, kind in out_list],
            scratch_shapes=scratch,
        ),
        out_shape=[jax.ShapeDtypeStruct(shape, dtype) for shape, dtype, _ in out_list],
        input_output_aliases={first_given + i: i for i in range(len(given))},
        compiler_params=pltpu.CompilerParams(
            vmem_limit_bytes=VMEM_LIMIT, dimension_semantics=("arbitrary",)
        ),
        cost_estimate=SMALL,
        name=name,
    )(*prefetch, *[a for a, _ in in_arrays], *given)


ENC = layer_offsets(V_ENC, D, FE)
DEC = layer_offsets(V_DEC, E, FD)


def encoder_forward_kernel(
    start, given, row_ref, len_ref, wg_ref, vec_ref, pix_ref, pos_ref,
    x0_ref, h1_ref, qkv_ref, lse_ref, out_t_ref, att_ref, mid_ref, h2_ref, act_ref, slope_ref, x1_ref, hn_ref, latent_ref,
    w_embed, w_qkv, w_out, w_up, w_down, w_proj, sems,
):
    step = pl.program_id(0)
    images = lse_ref.shape[0]
    ready = fetch_all(
        step == 0,
        row_ref,
        wg_ref,
        sems,
        [
            (T_EMBED, w_embed),
            (T_EQKV, w_qkv),
            (T_EOUT, w_out),
            (T_EUP, w_up),
            (T_EDOWN, w_down),
            (T_PROJ, w_proj),
        ],
    )

    def vec(start, size=D):
        return vec_ref[:, start : start + size]

    ready(0)
    add_linear(pos_ref, pix_ref, w_embed, vec_ref, V_EMBED, x0_ref)
    norm_forward(x0_ref, vec(ENC["g1"]), vec(ENC["s1"]), h1_ref)
    ready(1)
    qkv_forward(h1_ref, w_qkv, vec_ref, ENC["bqkv"], qkv_ref)

    attend_all(
        qkv_ref, att_ref, out_t_ref, lse_ref, images, VMAX, D, D // HE, lambda i: len_ref[step * images + i]
    )
    ready(2)
    add_linear(x0_ref, att_ref, w_out, vec_ref, ENC["bo"], mid_ref)
    norm_forward(mid_ref, vec(ENC["g2"]), vec(ENC["s2"]), h2_ref)
    ready(3)
    up_forward(h2_ref, w_up, vec_ref, ENC["bu"], act_ref, slope_ref)
    ready(4)
    add_linear(mid_ref, act_ref, w_down, vec_ref, ENC["bd"], x1_ref)
    norm_forward(x1_ref, vec(V_ENORM), vec(V_ENORM + D), hn_ref)
    ready(5)

    def project(j, cols):
        latent_ref[:, cols] = mm(hn_ref[...], w_proj[:, cols]) + vec_at(vec_ref, V_PROJ, j)

    col_loop(E // BS, project)


def encoder_forward(tile_rows, vis_len, gathered, vector, visible_pix, pos_d, steps):
    images = vis_len.shape[0]
    rows = images * VMAX
    outs = [
        ((rows, D), F32, "rows"),
        ((rows, D), BF, "rows"),
        ((rows, 3 * D), BF, "rows"),
        ((images, D // BS, BS * HE // D, VMAX), F32, "rows"),
        ((images, D // BS, BS, VMAX), F32, "rows"),
        ((rows, D), BF, "rows"),
        ((rows, D), F32, "rows"),
        ((rows, D), BF, "rows"),
        ((rows, FE), BF, "rows"),
        ((rows, FE), BF, "rows"),
        ((rows, D), F32, "rows"),
        ((rows, D), BF, "rows"),
        ((rows, E), F32, "rows"),
    ]
    scratch = [pltpu.VMEM(s, BF) for s in [(PIX, D), (D, 3 * D), (D, D), (D, FE), (FE, D), (D, E)]]
    return group_call(
        encoder_forward_kernel,
        steps,
        (tile_rows, vis_len),
        [
            (gathered, "any"),
            (vector, "whole"),
            (visible_pix.reshape(rows, PIX), "rows"),
            (pos_d.reshape(rows, D), "rows"),
        ],
        outs,
        scratch + [pltpu.SemaphoreType.DMA((6,))],
        "encoder_forward",
    )


DS = layer_offsets(0, E, FD)
DS_NORM = 9 * E + FD
DS_HEAD = DS_NORM + 2 * E
DS_MASK = DS_HEAD + PIX
DS_LOSS = DS_MASK + E
DS_ALL = DS_LOSS + PIX


def decoder_kernel(
    start, given, row_ref, len_ref, wg_ref, vec_ref, latent_ref, pos_ref, pix_ref,
    h1_ref, dqkv_ref, att_ref, gproj_ref, h2_ref, du_ref, act_ref, gdown_ref, hn_ref, gpred_ref, glat_ref, sum_ref,
    w_qkv, w_out, w_up, w_down, w_head, x0, qkv, lse, out_t, mid, slope, x1, pred, dy, grad, datt, sems,
):
    step = pl.program_id(0)
    images = lse.shape[0]
    ready = fetch_all(
        step == 0,
        row_ref,
        wg_ref,
        sems,
        [(T_DQKV, w_qkv), (T_DOUT, w_out), (T_DUP, w_up), (T_DDOWN, w_down), (T_HEAD, w_head)],
    )

    @pl.when(step == 0)
    def _():
        sum_ref[...] = jnp.zeros_like(sum_ref)

    def vec(start, size=E):
        return vec_ref[:, start : start + size]

    def length(image):
        return len_ref[step * images + image]

    chunk = 16
    order = lax.broadcasted_iota(jnp.int32, (chunk, 1), 0)
    token = vec(V_MASK)

    def place(image, c):
        def head_rows(i, c):
            at = pl.ds(pl.multiple_of(image * SD + i * chunk, chunk), chunk)
            got = latent_ref[pl.ds(pl.multiple_of(image * VMAX + i * chunk, chunk), chunk), :]
            x0[at, :] = jnp.where(i * chunk + order < length(image), got, token) + pos_ref[at, :]
            return c

        def tail_rows(i, c):
            at = pl.ds(pl.multiple_of(image * SD + i * chunk, chunk), chunk)
            x0[at, :] = token + pos_ref[at, :]
            return c

        loop(0, VMAX // chunk, head_rows, 0)
        loop(VMAX // chunk, SD // chunk, tail_rows, 0)
        return c

    loop(0, images, place, 0)
    norm_forward(x0, vec(DEC["g1"]), vec(DEC["s1"]), h1_ref)
    ready(0)
    qkv_forward(h1_ref, w_qkv, vec_ref, DEC["bqkv"], qkv)
    attend_all(qkv, att_ref, out_t, lse, images, SD, E, E // HD, lambda i: POS)
    ready(1)
    add_linear(x0, att_ref, w_out, vec_ref, DEC["bo"], mid)
    norm_forward(mid, vec(DEC["g2"]), vec(DEC["s2"]), h2_ref)
    ready(2)
    up_forward(h2_ref, w_up, vec_ref, DEC["bu"], act_ref, slope)
    ready(3)
    add_linear(mid, act_ref, w_down, vec_ref, DEC["bd"], x1)
    norm_forward(x1, vec(V_DNORM), vec(V_DNORM + E), hn_ref)
    ready(4)

    def predict(j, cols):
        pred[:, cols] = mm(hn_ref[...], w_head[:, cols]) + vec_at(vec_ref, V_HEAD, j)

    col_loop(PIX // BS, predict)

    def errors(image, c):
        def one(i, c):
            loss, bias = c
            at = pl.ds(pl.multiple_of(image * SD + i * chunk, chunk), chunk)
            target, _ = norm_parts(pix_ref[at, :].astype(F32))
            place_in = i * chunk + order
            masked = (place_in >= length(image)) & (place_in < POS)
            residual = jnp.where(masked, pred[at, :] - target, 0.0)
            low = (residual * (2.0 / PIX)).astype(BF)
            gpred_ref[at, :] = low
            return (loss + fold8(residual * residual), bias + fold8(low.astype(F32)))

        return loop(0, SD // chunk, one, c)

    zero = jnp.zeros((8, PIX), F32)
    loss, bias = loop(0, images, errors, (zero, zero))
    add_sum(sum_ref, DS_LOSS, loss)
    add_sum(sum_ref, DS_HEAD, bias)

    back_linear(gpred_ref, w_head, dy)
    d_gain, d_shift = norm_backward(x1, dy, vec(V_DNORM), grad, False)
    add_sum(sum_ref, DS_NORM, d_gain)
    add_sum(sum_ref, DS_NORM + E, d_shift)
    round_and_sum(grad, gdown_ref, sum_ref, DS["bd"])
    back_up(gdown_ref, w_down, slope, du_ref, sum_ref, DS["bu"])
    back_linear(du_ref, w_up, dy)
    d_gain, d_shift = norm_backward(mid, dy, vec(DEC["g2"]), grad, True)
    add_sum(sum_ref, DS["g2"], d_gain)
    add_sum(sum_ref, DS["s2"], d_shift)
    round_and_sum(grad, gproj_ref, sum_ref, DS["bo"])

    def back_out(j, cols):
        datt[:, cols] = mm_nt(gproj_ref[...], w_out[cols, :]).astype(BF)

    col_loop(E // BS, back_out)

    def attend_back(image, c):
        attention_backward(qkv, datt, out_t, lse, dqkv_ref, image, SD, E, E // HD, POS)
        return c

    loop(0, images, attend_back, 0)
    sum_rows(dqkv_ref, sum_ref, DS["bqkv"])
    back_linear(dqkv_ref, w_qkv, dy)
    d_gain, d_shift = norm_backward(x0, dy, vec(DEC["g1"]), grad, True)
    add_sum(sum_ref, DS["g1"], d_gain)
    add_sum(sum_ref, DS["s1"], d_shift)

    def unplace(image, c):
        def head_rows(i, c):
            got = grad[pl.ds(pl.multiple_of(image * SD + i * chunk, chunk), chunk), :]
            seen = i * chunk + order < length(image)
            at = pl.ds(pl.multiple_of(image * VMAX + i * chunk, chunk), chunk)
            glat_ref[at, :] = jnp.where(seen, got, 0.0).astype(BF)
            return c + fold8(jnp.where(seen, 0.0, got))

        def tail_rows(i, c):
            got = grad[pl.ds(pl.multiple_of(image * SD + i * chunk, chunk), chunk), :]
            return c + fold8(jnp.where(i * chunk + order < POS, got, 0.0))

        c = loop(0, VMAX // chunk, head_rows, c)
        return loop(VMAX // chunk, SD // chunk, tail_rows, c)

    add_sum(sum_ref, DS_MASK, loop(0, images, unplace, jnp.zeros((8, E), F32)))


def decoder(tile_rows, vis_len, gathered, vector, latent, pos_e, ordered, steps):
    images = vis_len.shape[0]
    rows = images * SD
    part = rows // steps
    outs = [
        ((rows, E), BF, "rows"),
        ((rows, 3 * E), BF, "rows"),
        ((rows, E), BF, "rows"),
        ((rows, E), BF, "rows"),
        ((rows, E), BF, "rows"),
        ((rows, FD), BF, "rows"),
        ((rows, FD), BF, "rows"),
        ((rows, E), BF, "rows"),
        ((rows, E), BF, "rows"),
        ((rows, PIX), BF, "rows"),
        ((images * VMAX, E), BF, "rows"),
        ((8, DS_ALL), F32, "whole"),
    ]
    scratch = [pltpu.VMEM(s, BF) for s in [(E, 3 * E), (E, E), (E, FD), (FD, E), (E, PIX)]]
    scratch += [
        pltpu.VMEM((part, E), F32),
        pltpu.VMEM((part, 3 * E), BF),
        pltpu.VMEM((images // steps, E // BS, BS * HD // E, SD), F32),
        pltpu.VMEM((images // steps, E // BS, BS, SD), F32),
        pltpu.VMEM((part, E), F32),
        pltpu.VMEM((part, FD), BF),
        pltpu.VMEM((part, E), F32),
        pltpu.VMEM((part, PIX), F32),
        pltpu.VMEM((part, E), F32),
        pltpu.VMEM((part, E), F32),
        pltpu.VMEM((part, E), BF),
        pltpu.SemaphoreType.DMA((5,)),
    ]
    return group_call(
        decoder_kernel,
        steps,
        (tile_rows, vis_len),
        [
            (gathered, "any"),
            (vector, "whole"),
            (latent, "rows"),
            (pos_e.reshape(rows, E), "rows"),
            (ordered.reshape(rows, PIX), "rows"),
        ],
        outs,
        scratch,
        "decoder",
    )


EM_BD, EM_BU = 0, D
EM_G2, EM_S2 = D + FE, 2 * D + FE
EM_BO, EM_NORM = 3 * D + FE, 4 * D + FE
EM_PROJ = 6 * D + FE
EM_ALL = EM_PROJ + E
EA_QKV, EA_G1, EA_S1, EA_EMBED, EA_ALL = 0, 3 * D, 4 * D, 5 * D, 6 * D


def encoder_mlp_back_kernel(
    start, given, row_ref, wg_ref, vec_ref, glat_ref, x1_ref, mid_ref, slope_ref,
    gdown_ref, du_ref, grad_ref, gproj_ref, sum_ref,
    w_proj, w_down, w_up, dy, sems,
):
    step = pl.program_id(0)
    ready = fetch_all(
        step == 0, row_ref, wg_ref, sems, [(T_PROJ, w_proj), (T_EDOWN, w_down), (T_EUP, w_up)]
    )

    @pl.when(step == 0)
    def _():
        sum_ref[...] = jnp.zeros_like(sum_ref)

    def vec(start):
        return vec_ref[:, start : start + D]

    sum_rows(glat_ref, sum_ref, EM_PROJ)
    ready(0)
    back_linear(glat_ref, w_proj, dy)
    d_gain, d_shift = norm_backward(x1_ref, dy, vec(V_ENORM), grad_ref, False)
    add_sum(sum_ref, EM_NORM, d_gain)
    add_sum(sum_ref, EM_NORM + D, d_shift)
    round_and_sum(grad_ref, gdown_ref, sum_ref, EM_BD)
    ready(1)
    back_up(gdown_ref, w_down, slope_ref, du_ref, sum_ref, EM_BU)
    ready(2)
    back_linear(du_ref, w_up, dy)
    d_gain, d_shift = norm_backward(mid_ref, dy, vec(ENC["g2"]), grad_ref, True)
    add_sum(sum_ref, EM_G2, d_gain)
    add_sum(sum_ref, EM_S2, d_shift)
    round_and_sum(grad_ref, gproj_ref, sum_ref, EM_BO)


def encoder_mlp_back(tile_rows, gathered, vector, glat, x1, mid, slope, steps):
    rows = x1.shape[0]
    part = rows // steps
    outs = [
        ((rows, D), BF, "rows"),
        ((rows, FE), BF, "rows"),
        ((rows, D), F32, "rows"),
        ((rows, D), BF, "rows"),
        ((8, EM_ALL), F32, "whole"),
    ]
    scratch = [pltpu.VMEM(s, BF) for s in [(D, E), (FE, D), (D, FE)]]
    scratch += [pltpu.VMEM((part, D), F32), pltpu.SemaphoreType.DMA((3,))]
    return group_call(
        encoder_mlp_back_kernel,
        steps,
        (tile_rows,),
        [
            (gathered, "any"),
            (vector, "whole"),
            (glat, "rows"),
            (x1, "rows"),
            (mid, "rows"),
            (slope, "rows"),
        ],
        outs,
        scratch,
        "encoder_mlp_back",
    )


def encoder_attention_back_kernel(
    start, given, row_ref, len_ref, wg_ref, vec_ref, gproj_ref, grad_in_ref, qkv_ref, lse_ref, out_t_ref, x0_ref, *refs
):
    dqkv_ref, gembed_ref, sum_ref, w_out, w_qkv, dy, grad, datt, sems = refs[given:]
    step = pl.program_id(0)
    images = lse_ref.shape[0]
    ready = fetch_all(step == 0, row_ref, wg_ref, sems, [(T_EOUT, w_out), (T_EQKV, w_qkv)])

    @pl.when(step == 0)
    def _():
        sum_ref[...] = jnp.zeros_like(sum_ref)

    ready(0)

    def back_out(j, cols):
        datt[:, cols] = mm_nt(gproj_ref[...], w_out[cols, :]).astype(BF)

    col_loop(D // BS, back_out)

    def attend_back(image, c):
        count = len_ref[(start + step) * images + image]
        attention_backward(qkv_ref, datt, out_t_ref, lse_ref, dqkv_ref, image, VMAX, D, D // HE, count)
        return c

    loop(0, images, attend_back, 0)
    sum_rows(dqkv_ref, sum_ref, EA_QKV)
    ready(1)
    back_linear(dqkv_ref, w_qkv, dy)
    grad[...] = grad_in_ref[...]
    gain = vec_ref[:, ENC["g1"] : ENC["g1"] + D]
    d_gain, d_shift = norm_backward(x0_ref, dy, gain, grad, True)
    add_sum(sum_ref, EA_G1, d_gain)
    add_sum(sum_ref, EA_S1, d_shift)
    round_and_sum(grad, gembed_ref, sum_ref, EA_EMBED)


def encoder_attention_back(tile_rows, vis_len, gathered, vector, gproj, grad, qkv, lse, out_t, x0, steps, share, given):
    rows = x0.shape[0]
    part = rows // steps
    outs = [((rows, 3 * D), BF, "rows"), ((rows, D), BF, "rows"), ((8, EA_ALL), F32, "whole")]
    scratch = [pltpu.VMEM(s, BF) for s in [(D, D), (D, 3 * D)]]
    scratch += [pltpu.VMEM((part, D), F32), pltpu.VMEM((part, D), F32), pltpu.VMEM((part, D), BF)]
    return group_call(
        encoder_attention_back_kernel,
        steps,
        (tile_rows, vis_len),
        [
            (gathered, "any"),
            (vector, "whole"),
            (gproj, "rows"),
            (grad, "rows"),
            (qkv, "rows"),
            (lse, "rows"),
            (out_t, "rows"),
            (x0, "rows"),
        ],
        outs,
        scratch + [pltpu.SemaphoreType.DMA((2,))],
        "encoder_attention_back",
        share,
        given,
    )


def weight_grad_kernel(parts, cut, jobs, count, extra, index_ref, *refs):
    held = min(parts, 2)
    arrays = refs[:count]
    outs = refs[count + extra : count + extra + held]
    x_buf, g_buf, x_t, total, o_buf, x_sem, g_sem, o_sem = refs[count + extra + held :]

    def fetch(array, rows, start, width, buf, sem, slot):
        return pltpu.make_async_copy(
            arrays[array].at[:, start : start + width], buf.at[slot, 0:rows, 0:width], sem.at[slot]
        )

    def send(j, h):
        size, first = jobs[j][-2:]
        return pltpu.make_async_copy(
            o_buf.at[j % 2, h, :, 0:size], outs[h].at[:, first : first + size], o_sem.at[j % 2, h]
        )

    x_slots = [0]
    for one, two in zip(jobs, jobs[1:]):
        x_slots.append(x_slots[-1] if one[:4] == two[:4] else 1 - x_slots[-1])

    def start_fetch(j):
        array, rows, x_start, x_width, g_start, g_width = jobs[j][:6]
        if j == 0 or x_slots[j] != x_slots[j - 1]:
            fetch(array, rows, x_start, x_width, x_buf, x_sem, x_slots[j]).start()
        fetch(array + 1, rows, g_start, g_width, g_buf, g_sem, j % 2).start()

    start_fetch(0)
    for j, (array, rows, x_start, x_width, g_start, g_width, size, first) in enumerate(jobs):
        if j + 1 < len(jobs):
            start_fetch(j + 1)
        if j == 0 or x_slots[j] != x_slots[j - 1]:
            fetch(array, rows, x_start, x_width, x_buf, x_sem, x_slots[j]).wait()
            x_t[0:x_width, 0:rows] = x_buf[x_slots[j], 0:rows, 0:x_width].T
        fetch(array + 1, rows, g_start, g_width, g_buf, g_sem, j % 2).wait()
        total[0:x_width, 0:g_width] = mm(x_t[0:x_width, 0:rows], g_buf[j % 2, 0:rows, 0:g_width])
        if j >= 2:
            for h in range(held):
                send(j - 2, h).wait()
        wide = g_width // BS
        for p in range(parts):
            for r in range(x_width // BS):
                start = pl.multiple_of(r * BS + (p ^ index_ref[0]) * cut, cut)
                for c in range(wide):
                    got = total[pl.ds(start, cut), c * BS : (c + 1) * BS]
                    o_buf[j % 2, p % 2, p // 2, r * wide + c] = got.astype(BF)
        for h in range(held):
            send(j, h).start()
    for j in range(max(0, len(jobs) - 2), len(jobs)):
        for h in range(held):
            send(j, h).wait()


def weight_grads(index, parts, count, first, pairs, blocks, buffers):
    cut = BS // parts
    held = min(parts, 2)
    shape = jax.ShapeDtypeStruct((parts // held, count, cut, BS), BF)
    given = list(buffers or [])
    jobs = []
    for i, ((x, g), (high, wide)) in enumerate(zip(pairs, blocks)):
        for x_start in range(0, x.shape[1], high * BS):
            for g_start in range(0, g.shape[1], wide * BS):
                jobs.append((2 * i, x.shape[0], x_start, high * BS, g_start, wide * BS, high * wide, first))
                first += high * wide
    most = [max(job[k] for job in jobs) for k in range(8)]
    any_spec = pl.BlockSpec(memory_space=pl.ANY)
    return pl.pallas_call(
        functools.partial(weight_grad_kernel, parts, cut, jobs, 2 * len(pairs), len(given)),
        grid_spec=pltpu.PrefetchScalarGridSpec(
            num_scalar_prefetch=1,
            grid=(1,),
            in_specs=[any_spec] * (2 * len(pairs) + len(given)),
            out_specs=[any_spec] * held,
            scratch_shapes=[
                pltpu.VMEM((2, most[1], most[3]), BF),
                pltpu.VMEM((2, most[1], most[5]), BF),
                pltpu.VMEM((most[3], most[1]), BF),
                pltpu.VMEM((most[3], most[5]), F32),
                pltpu.VMEM((2, held, parts // held, most[6], cut, BS), BF),
                pltpu.SemaphoreType.DMA((2,)),
                pltpu.SemaphoreType.DMA((2,)),
                pltpu.SemaphoreType.DMA((2, held)),
            ],
        ),
        out_shape=[shape] * held,
        input_output_aliases={1 + 2 * len(pairs) + i: i for i in range(len(given))},
        compiler_params=pltpu.CompilerParams(vmem_limit_bytes=VMEM_LIMIT),
        cost_estimate=SMALL,
        name="weight_grads",
    )(index, *[array for pair in pairs for array in pair], *given)


def seed_kernel(parts, parcels, own, index_ref, *refs):
    sums, outs, rows = refs[: -1 - min(parts, 2)], refs[-1 - min(parts, 2) : -1], refs[-1]
    rows[...] = jnp.zeros_like(rows)
    at = 0
    for source, start, size in parcels:
        for k in range(0, size, 128):
            piece = sum(jnp.sum(sums[i][:, start + k : start + k + 128], axis=0, keepdims=True) for i in source)
            row, col = at % own // BS, at % own % BS
            rows[at // own, row : row + 1, col : col + 128] = piece
            at += 128
    for p in range(parts):
        out = outs[p % 2]
        out[p // 2, 0] = rows[p ^ index_ref[0]].astype(BF)
        for t in range(1, out.shape[1]):
            out[p // 2, t] = jnp.zeros(rows.shape[1:], BF)


def seed_buffers(index, parts, count, first, sums=(), parcels=(), own=1):
    cut = BS // parts
    held = min(parts, 2)
    size = count - first
    assert first % size == 0
    shape = jax.ShapeDtypeStruct((parts // held, count, cut, BS), BF)
    return pl.pallas_call(
        functools.partial(seed_kernel, parts, parcels, own),
        grid_spec=pltpu.PrefetchScalarGridSpec(
            num_scalar_prefetch=1,
            grid=(1,),
            in_specs=[pl.BlockSpec(x.shape, lambda i, *_: (0, 0)) for x in sums],
            out_specs=[pl.BlockSpec((parts // held, size, cut, BS), lambda i, *_: (0, first // size, 0, 0))] * held,
            scratch_shapes=[pltpu.VMEM((parts, cut, BS), F32)],
        ),
        out_shape=[shape] * held,
        cost_estimate=SMALL,
        name="seed_buffers",
    )(index, *sums)


def low_sum(a, b):
    return (a.astype(F32) + b.astype(F32)).astype(BF)


def swap_bit(x, bit, size):
    return lax.ppermute(x, "dp", [(i, i ^ (1 << bit)) for i in range(size)])


def reduce_core(buffers, parts):
    if parts == 1:
        whole, count = buffers[0][0], buffers[0].shape[1]
        return [whole[: count // 2], whole[count // 2 :]], [[], []]
    whole = low_sum(buffers[0], swap_bit(buffers[1], 0, parts))
    bits = list(range(parts.bit_length() - 2, 0, -1))
    whole = whole.reshape((2,) * len(bits) + whole.shape[1:])
    count = whole.shape[-3]
    return [whole[..., : count // 2, :, :], whole[..., count // 2 :, :, :]], [bits, bits]


def reduce_chips(state, parts, steps):
    halves, left = list(state[0]), list(state[1])
    for half in range(2):
        for _ in range(min(steps, len(left[half]))):
            bit = left[half][-1 if half == 0 else 0]
            axis = left[half].index(bit)
            keep = lax.index_in_dim(halves[half], 0, axis, keepdims=False)
            send = lax.index_in_dim(halves[half], 1, axis, keepdims=False)
            halves[half] = low_sum(keep, swap_bit(send, bit, parts))
            left[half] = [b for b in left[half] if b != bit]
    return halves, left


def patch_steps(groups):
    middle = groups // 2 - 1

    def inwards(k, x):
        return low_sum(x, lax.ppermute(x, "patch", [(k, k + 1), (groups - 1 - k, groups - 2 - k)]))

    def across(x):
        return low_sum(x, lax.ppermute(x, "patch", [(middle, middle + 1), (middle + 1, middle)]))

    def outwards(k, x):
        got = lax.ppermute(x, "patch", [(k + 1, k), (groups - 2 - k, groups - 1 - k)])
        me = lax.axis_index("patch")
        return jnp.where((me == k) | (me == groups - 1 - k), got, x)

    if groups == 1:
        return []
    steps = [functools.partial(inwards, k) for k in range(middle)] + [across]
    return steps + [functools.partial(outwards, k) for k in reversed(range(middle))]


def sum_patch(x, steps):
    for step in steps:
        x = step(x)
    return x


def sum_all(x, parts, groups):
    for bit in range(groups.bit_length() - 1):
        x = x + lax.ppermute(x, "patch", [(i, i ^ (1 << bit)) for i in range(groups)])
    return sum_dp(x, parts)


def sum_dp(x, parts):
    for bit in range(parts.bit_length() - 1):
        x = x + swap_bit(x, bit, parts)
    return x


def split_low(x):
    high = x.astype(BF)
    return high, (x - high.astype(F32)).astype(BF)


def tile_kernel(
    scale_ref, grad_ref, w_ref, left_stat_ref, right_stat_ref, left_root_ref, right_root_ref,
    clipped_ref, left_new_ref, right_new_ref, w_new_ref,
):
    scale = scale_ref[0]
    for t in range(w_ref.shape[0]):
        grad = grad_ref[:, t].reshape(BS, BS)
        clipped_ref[t] = grad.astype(F32) * scale
        square = (1.0 - BETA_STAT) * scale * scale
        left_new_ref[t] = BETA_STAT * left_stat_ref[t] + square * mm_nt(grad, grad)
        right_new_ref[t] = BETA_STAT * right_stat_ref[t] + square * mm_tn(grad, grad)
        high, low = split_low(left_root_ref[t])
        half = (mm(high, grad) + mm(low, grad)) * scale
        half_high, half_low = split_low(half)
        high, low = split_low(right_root_ref[t])
        direction = mm(half_high, high) + (mm(half_high, low) + mm(half_low, high))
        direction = direction * lax.rsqrt(jnp.mean(direction * direction) + EPS_ROOT)
        w_new_ref[t] = w_ref[t] - RATE_MATRIX * (direction + DECAY_MATRIX * w_ref[t])


def tile_update(scale, grads, states):
    parts, slots, cut, _ = grads.shape
    per = max(p for p in range(1, 7) if slots % p == 0)
    tile = pl.BlockSpec((per, BS, BS), lambda i, *_: (i, 0, 0))
    return pl.pallas_call(
        tile_kernel,
        grid_spec=pltpu.PrefetchScalarGridSpec(
            num_scalar_prefetch=1,
            grid=(slots // per,),
            in_specs=[pl.BlockSpec((parts, per, cut, BS), lambda i, *_: (0, i, 0, 0))] + [tile] * 5,
            out_specs=[tile] * 4,
        ),
        out_shape=[jax.ShapeDtypeStruct((slots, BS, BS), F32)] * 4,
        compiler_params=pltpu.CompilerParams(vmem_limit_bytes=VMEM_LIMIT),
        name="tile_update",
    )(scale.reshape(1), grads, *states)


def vector_update(clipped, vectors, moment, second):
    moment_new = BETA_FIRST * moment + (1.0 - BETA_FIRST) * clipped
    second_new = BETA_SECOND * second + (1.0 - BETA_SECOND) * clipped * clipped
    corrected = moment_new / (1.0 - BETA_FIRST**STEP)
    scaled = second_new / (1.0 - BETA_SECOND**STEP)
    vectors_new = vectors - RATE_VECTOR * corrected / (jnp.sqrt(scaled) + EPS_ADAM)
    return moment_new, second_new, vectors_new


CHUNKS = [
    [
        (T_DUP, 2, 8, (2, 4)),
        (T_DDOWN, 8, 2, (4, 2)),
        (T_DOUT, 2, 2, (2, 2)),
        (T_DQKV, 2, 6, (2, 3)),
        (T_HEAD, 2, 3, (2, 3)),
        (T_PROJ, 3, 2, (3, 2)),
    ],
    [(T_EUP, 3, 12, (3, 4)), (T_EDOWN, 12, 3, (4, 3)), (T_EOUT, 3, 3, (3, 3))],
    [(T_EQKV, 3, 9, (3, 3)), (T_EMBED, 3, 3, (3, 3))],
]


def chunk_sizes():
    sizes = [sum(r * c for _, r, c, _ in chunk) for chunk in CHUNKS]
    return sizes[:-1] + [sizes[-1] + 2]


def tile_places(sizes):
    chunk_of = np.zeros(NBLK + 2, np.int32)
    place_of = np.zeros(NBLK + 2, np.int32)
    for i, chunk in enumerate(CHUNKS):
        at = 0
        for first, row_tiles, col_tiles, (high, wide) in chunk:
            for r in range(row_tiles):
                for c in range(col_tiles):
                    block = r // high * (col_tiles // wide) + c // wide
                    chunk_of[first + r * col_tiles + c] = i
                    place_of[first + r * col_tiles + c] = at + block * high * wide + r % high * wide + c % wide
            at += row_tiles * col_tiles
    chunk_of[NBLK:] = len(CHUNKS) - 1
    place_of[NBLK + 1] = at
    place_of[NBLK] = at + 1
    return chunk_of, place_of


def shards(parts, groups, pixels, shuffle, vis_len, block_owner, weights, vectors, vec_moment, vec_second,
           left_stat, right_stat, left_root, right_root):
    slots = weights.shape[0]
    own = vectors.shape[0]
    index = lax.axis_index("dp").astype(jnp.int32).reshape(1)
    images = pixels.shape[0]

    vector_rows = -(-own // (16 * BS)) * 16
    mine = jnp.concatenate(
        [
            weights.astype(BF).reshape(slots * BS, BS),
            jnp.pad(vectors.astype(BF), (0, vector_rows * BS - own)).reshape(vector_rows, BS),
        ]
    )
    gathered = lax.all_gather(mine, "dp", axis=0, tiled=True)
    stride = mine.shape[0]
    slot_index = jnp.arange(block_owner.shape[0], dtype=jnp.int32)
    slot_of_block = jnp.sum(
        jnp.where(block_owner[None, :] == jnp.arange(NBLK, dtype=jnp.int32)[:, None], slot_index[None, :], 0),
        axis=1,
    )
    tile_rows = slot_of_block // slots * stride + slot_of_block % slots * BS
    vector = gathered.reshape(parts, stride, BS)[:, slots * BS :].reshape(parts, vector_rows * BS)
    vector = vector[:, :own].reshape(-1).astype(F32)
    enc_key, dec_key = 4 * D, 4 * D + (8 * D + FE - 3 * D) + 2 * D + 2 * E + 3 * E
    vector = jnp.concatenate(
        [vector[:enc_key], jnp.zeros(D, F32), vector[enc_key:dec_key], jnp.zeros(E, F32), vector[dec_key:]]
    ).reshape(1, V_ALL)

    ordered, visible_pix, pos_d, pos_e = order_patches(pixels, shuffle)
    (x0, h1, qkv, lse, out_t, att, mid, h2, act, slope, x1, hn, latent) = encoder_forward(
        tile_rows, vis_len, gathered, vector, visible_pix, pos_d, 2
    )
    (d_h1, d_dqkv, d_att, d_gproj, d_h2, d_du, d_act, d_gdown, d_hn, d_gpred, glat, d_sums) = decoder(
        tile_rows, vis_len, gathered, vector, latent, pos_e, ordered, 4
    )
    sizes = chunk_sizes()
    chunk_of, place_of = tile_places(sizes)

    rows_cut = BS // parts

    def gradients(chunk, pairs, vector=(), first=0, buffers=None):
        used = sum(r * c for _, r, c, _ in CHUNKS[chunk])
        if sizes[chunk] > used and buffers is None:
            buffers = seed_buffers(index, parts, sizes[chunk], used, *vector)
        at = sum(r * c for _, r, c, _ in CHUNKS[chunk][:first])
        blocks = [block for _, _, _, block in CHUNKS[chunk][first : first + len(pairs)]]
        return weight_grads(index, parts, sizes[chunk], at, pairs, blocks, buffers)

    def attention_back(gproj, k, given):
        return encoder_attention_back(
            tile_rows, vis_len, gathered, vector, gproj, grad_mid, qkv, lse, out_t, x0, 2, (k, 2), given
        )

    def core(buffers):
        return reduce_core(buffers, parts)

    def chips(state, steps):
        return reduce_chips(state, parts, steps)

    after = lax.optimization_barrier
    steps = patch_steps(groups)
    gdown, du, grad_mid, gproj, m_sums = encoder_mlp_back(tile_rows, gathered, vector, glat, x1, mid, slope, 2)
    buf1 = gradients(1, [(h2, du), (act, gdown), (att, gproj)])
    d_h2, d_act, buf1 = after((d_h2, d_act, buf1))
    buf0 = gradients(0, [(d_h2, d_du), (d_act, d_gdown)])
    half1, left1 = core(buf1)
    d_att, d_h1, d_hn, hn, buf0, half1 = after((d_att, d_h1, d_hn, hn, buf0, half1))
    half1, left1 = chips((half1, left1), 1)
    buf0 = gradients(0, [(d_att, d_gproj), (d_h1, d_dqkv), (d_hn, d_gpred), (hn, glat)], (), 2, buf0)
    gproj, buf0 = after((gproj, buf0))
    dqkv, gembed, a_sums = attention_back(gproj, 0, ())
    gproj, dqkv, gembed, buf0, half1 = after((gproj, dqkv, gembed, buf0, half1))
    dqkv, gembed, b_sums = attention_back(gproj, 1, (dqkv, gembed))
    (one, two), _ = chips((half1, left1), 99)
    half0, left0 = core(buf0)
    dqkv, gembed, b_sums, half0, one, two = after((dqkv, gembed, b_sums, half0, one, two))

    late, early, dec = (0, 1), (2,), (3,)
    parcels = [
        (late, EA_EMBED, D),
        (late, EA_G1, 2 * D),
        (late, EA_QKV, D),
        (late, EA_QKV + 2 * D, D),
        (early, EM_BO, D),
        (early, EM_G2, 2 * D),
        (early, EM_BU, FE),
        (early, EM_BD, D),
        (early, EM_NORM, 2 * D),
        (early, EM_PROJ, E),
        (dec, DS_MASK, E),
        (dec, DS["g1"], 2 * E),
        (dec, DS["bqkv"], E),
        (dec, DS["bqkv"] + 2 * E, E),
        (dec, DS["bo"], E),
        (dec, DS["g2"], 2 * E),
        (dec, DS["bu"], FD),
        (dec, DS["bd"], E),
        (dec, DS_NORM, 2 * E),
        (dec, DS_HEAD, PIX),
    ]
    sums = (a_sums, b_sums, m_sums, d_sums)
    buf2 = gradients(2, [(h1, dqkv), (visible_pix.reshape(-1, PIX), gembed)], (sums, parcels, own))
    half0, left0 = chips((half0, left0), 1)
    one = sum_patch(one, steps[:1])
    two = sum_patch(two, steps[:1])
    buf2, half0, one = after((buf2, half0, one))
    half2, left2 = core(buf2)
    half0, _ = chips((half0, left0), 99)
    one = sum_patch(one, steps[1:2])
    half2, half0, one, two = after((half2, half0, one, two))
    half2, left2 = chips((half2, left2), 1)
    one = sum_patch(one, steps[2:])
    two = sum_patch(two, steps[1:2])
    half0 = [sum_patch(x, steps[:1]) for x in half0]
    half2, one, two = after((half2, one, two))
    half2, _ = chips((half2, left2), 99)
    two = sum_patch(two, steps[2:])
    half2, half0, two = after((half2, half0, two))
    half2 = [sum_patch(x, steps) for x in half2]
    half0 = [sum_patch(x, steps[1:]) for x in half0]
    pieces = half0 + [one, two] + half2
    mine = jnp.where(lax.axis_index("patch") == 0, 1.0, 0.0)

    def squares(x):
        wide = x.astype(F32)
        return jnp.sum(wide * wide)

    totals = jnp.stack(
        [
            jnp.sum(d_sums[:, DS_LOSS : DS_LOSS + PIX]) / PIX,
            jnp.sum(POS - vis_len).astype(F32),
            sum(squares(x) for x in pieces) * mine,
        ]
    )
    totals = sum_all(totals, parts, groups)
    loss_sum, masked_count = totals[0], totals[1]
    grad_norm = jnp.sqrt(totals[2]) / masked_count
    scale = jnp.minimum(1.0, CLIP_NORM / grad_norm) / masked_count

    reduced = jnp.concatenate(pieces, axis=0)
    where = jnp.asarray(np.cumsum([0] + sizes)[chunk_of] + place_of, jnp.int32)
    slot_rows = reduced[where[jnp.minimum(block_owner, NBLK)]]
    if parts > 1:
        slot_rows = lax.all_to_all(slot_rows, "dp", 0, 0, tiled=True)
    grads = slot_rows.reshape(parts, slots, rows_cut, BS)
    clipped, left_new, right_new, weights_new = tile_update(
        scale, grads, (weights, left_stat, right_stat, left_root, right_root)
    )
    own_vector = lax.dynamic_index_in_dim(reduced, where[NBLK + 1], 0, keepdims=False)
    own_vector = own_vector.reshape(-1)[:own].astype(F32) * scale
    moment_new, second_new, vectors_new = vector_update(own_vector, vectors, vec_moment, vec_second)
    return (
        loss_sum,
        masked_count,
        grad_norm,
        clipped,
        left_new,
        right_new,
        weights_new,
        moment_new,
        second_new,
        vectors_new,
    )


def solution(mesh):
    both = ("dp", "patch")
    tiles = P("dp", None, None)
    return jax.shard_map(
        functools.partial(shards, mesh.shape["dp"], mesh.shape["patch"]),
        mesh=mesh,
        in_specs=(P(both, None, None), P(both, None), P(both), P())
        + (tiles, P("dp"), P("dp"), P("dp"))
        + (tiles,) * 4,
        out_specs=(P(), P(), P()) + (tiles,) * 4 + (P("dp"),) * 3,
        check_vma=False,
    )
```
